32 devices in a mesh: gx: 4 (over z), gy: 2 (over y), gz: 4 (over x, core).
Axes of the slice: x: 2, y: 2, z: 4, core: 2. Of those that a mesh axis runs over, the one named last changes fastest.
Arguments:
- field: float32 [32, 512, 256], P('gz', 'gx', 'gy'), may hold values from -6 to 6
Outputs:
- coeffs_fine: float32 [32, 512, 256], P('gz', 'gx', 'gy')
- coeffs_middle: float32 [16, 256, 128], P('gz', 'gx', 'gy')
- coeffs_coarse: float32 [8, 128, 64], P('gz', 'gx', 'gy')
- coarsest: float32 [4, 64, 32], P('gz', 'gx', 'gy')
The draws below stay inside these ranges and needn't reach their ends.
All inputs are finite; a program needn't handle non-finite values.
Results may differ from the reference program's by a relative error of at most 0.0003.
Values sent between devices are 32-bit elements; how exact they have to be, the bound alone decides.
No kernel may reach another device: no remote copies, remote signals or barrier semaphores. Data moves between devices by JAX's collectives and lax.ppermute only.
A program may use at most 64 MiB of HBM per device.

```python
import math
import jax
import jax.numpy as jnp
from jax import lax

NZ = 32
NX = 512
NY = 256


def shard_levels(rng, extent, split, smallest, high):
    def one(position, blocks):
        draws = jax.random.uniform(jax.random.fold_in(jax.random.fold_in(rng, 6), position), (blocks,), jnp.float32, smallest / len(split), high / len(split))
        return jnp.repeat(jnp.exp(draws), extent[position] // blocks).reshape((-1,) + (1,) * (len(extent) - position - 1))

    loudness = one(*split[0])
    for cut in split[1:]:
        loudness = loudness * one(*cut)
    return loudness


def gaussian(rng, extent, spread, reach, shards=(), kind=jnp.bfloat16):
    array = jax.random.normal(rng, extent, jnp.float32) * spread
    if len(shards) > 0:
        array = shard_levels(rng, extent, shards, -0.22, 0.18) * array
    return jnp.clip(array, min=-reach, max=reach).astype(kind)


def setup_inputs(seed: int = 0) -> dict:
    key_list = jax.random.split(jax.random.key(seed), 2)
    return {
        "field": gaussian(key_list[0], (NZ, NX, NY), 1.0, 6.0, ((0, 4), (1, 4), (2, 2)), jnp.float32),
    }


band_ratio = 2.0 - math.sqrt(3.0)

def along_shape(length, dimension):
    new_shape = [1, 1, 1]
    new_shape[dimension] = length
    return new_shape

def prolong(coarse, dimension):
    length = coarse.shape[dimension]
    following = jnp.concatenate([lax.slice_in_dim(coarse, 1, length, axis=dimension), lax.slice_in_dim(coarse, length - 1, length, axis=dimension)], axis=dimension)
    middle = 0.5 * (coarse + following)
    stacked = jnp.stack([coarse, middle], axis=dimension + 1)
    new_shape = list(coarse.shape)
    new_shape[dimension] = 2 * length
    return stacked.reshape(new_shape)

def restrict_mass(coeffs, dimension):
    length = coeffs.shape[dimension]
    widths = [(0, 0), (0, 0), (0, 0)]
    widths[dimension] = (1, 1)
    padded = jnp.pad(coeffs, widths)
    mass = lax.slice_in_dim(padded, 0, length, axis=dimension) + 4.0 * lax.slice_in_dim(padded, 1, length + 1, axis=dimension) + lax.slice_in_dim(padded, 2, length + 2, axis=dimension)
    even_part = lax.slice_in_dim(mass, 0, length, 2, dimension)
    odd_part = lax.slice_in_dim(mass, 1, length, 2, dimension)
    half_len = length // 2
    weights = jnp.where(jnp.arange(half_len) == half_len - 1, 1.0, 0.5).astype(coeffs.dtype).reshape(along_shape(half_len, dimension))
    earlier = jnp.concatenate([jnp.zeros_like(lax.slice_in_dim(odd_part, 0, 1, axis=dimension)), lax.slice_in_dim(odd_part, 0, half_len - 1, axis=dimension)], axis=dimension)
    return 0.5 * band_ratio * (even_part + weights * odd_part + 0.5 * earlier)

def solve_band(source, dimension):
    moved_axis = jnp.moveaxis(source, dimension, 0)

    def advance(carried, row_values):
        updated = row_values - band_ratio * carried
        return (updated, updated)
    start_zero = jnp.zeros_like(moved_axis[0])
    unused_carry, lower = lax.scan(advance, start_zero, moved_axis)
    unused_back, upper = lax.scan(advance, start_zero, lower, reverse=True)
    return jnp.moveaxis(upper, 0, dimension)

def reference(field):
    current = field
    results = []
    for level_index in range(3):
        coarse = current[::2, ::2, ::2]
        interp = prolong(prolong(prolong(coarse, 2), 1), 0)
        coeffs = current - interp
        correction = coeffs
        for dimension in (1, 2, 0):
            correction = solve_band(restrict_mass(correction, dimension), dimension)
        results.append(coeffs)
        current = coarse + correction
    return (results[0], results[1], results[2], current)
```

```python
import functools
import math

import jax
import jax.numpy as jnp
import numpy as np
from jax import lax
from jax.experimental import pallas as pl
from jax.experimental.pallas import tpu as pltpu
from jax.sharding import PartitionSpec as P

band_ratio = 2.0 - math.sqrt(3.0)
f32 = np.float32


def round_up(value, unit):
    return -(-value // unit) * unit


def dense(fine):
    n = fine // 2
    steps = np.arange(n)[:, None] - np.arange(n)[None, :]
    lower = np.where(steps >= 0, (-band_ratio) ** np.maximum(steps, 0), 0.0)
    inverse = lower.T @ lower
    mass = 4.0 * np.eye(fine) + np.eye(fine, k=1) + np.eye(fine, k=-1)
    weights = np.where(np.arange(n) == n - 1, 1.0, 0.5)[:, None]
    earlier = np.concatenate([np.zeros((1, fine)), mass[1::2][:-1]])
    product = inverse @ (0.5 * band_ratio * (mass[0::2] + weights * mass[1::2] + 0.5 * earlier))
    return product, inverse[:, 0] * (3 * band_ratio - 1), inverse[:, -1] * (2 * band_ratio)


class Level:
    def __init__(self, whole, count, following):
        self.count, self.fine = count, whole // count
        self.n = self.fine // 2
        self.product, self.first, self.last = dense(whole)
        self.following = following
        self.kept = following.functional_count if following else 0
        self.functional_count = 4 + 2 * self.kept
        self.even = np.zeros((self.n, self.fine))
        self.even[np.arange(self.n), 2 * np.arange(self.n)] = 1.0
        self.v = [self.towards(i, i * self.n - 1) for i in range(count)]
        self.w = [self.towards(i, (i + 1) * self.n) for i in range(count)]
        self.functionals = []
        for i in range(count):
            own = np.zeros((4, self.fine))
            own[0, 0] = own[1, self.fine - 2] = 1.0
            own[2], own[3] = self.v[i], self.w[i]
            if following:
                inner = following.functionals[i]
                own = np.concatenate([own, inner @ self.even, inner @ self.block(i, i)])
            self.functionals.append(own)

    def rows(self, i):
        return slice(i * self.n, (i + 1) * self.n)

    def block(self, i, j):
        return self.product[self.rows(i), j * self.fine : (j + 1) * self.fine]

    def towards(self, i, row):
        if not 0 <= row < self.count * self.n:
            return np.zeros(self.fine)
        values = self.product[row, i * self.fine : (i + 1) * self.fine]
        return values / np.abs(values).max()

    def reach(self, i, j):
        side = self.v[j] if j > i else self.w[j]
        best = np.argmax(np.abs(side))
        return self.block(i, j)[:, best] / side[best]

    def side(self, i, j):
        return 2 if j > i else 3

    def tables(self, j):
        own, kept, many, n, fine = self.n, self.kept, self.functional_count, self.n, self.fine
        others = [j ^ k for k in range(1, self.count)]
        shape = (own + kept * len(others), fine + many * len(others))
        product, even = np.zeros(shape), np.zeros(shape)
        at = {i: fine + many * place for place, i in enumerate(others)}
        product[:n, :fine] = self.block(j, j)
        even[:n, :fine] = self.even
        first, last = [self.first[self.rows(j)]], [self.last[self.rows(j)]]
        for i in others:
            product[:n, at[i] + self.side(j, i)] = self.reach(j, i)
        for place, i in enumerate(others):
            if not kept:
                break
            inner = self.following.functionals[i]
            target = n + kept * place + np.arange(kept)
            product[target, :fine] = inner @ self.block(i, j)
            product[target, at[i] + 4 + kept + np.arange(kept)] = 1.0
            even[target, at[i] + 4 + np.arange(kept)] = 1.0
            for other in others:
                if other != i:
                    product[target, at[other] + self.side(i, other)] = inner @ self.reach(i, other)
            first.append(inner @ self.first[self.rows(i)])
            last.append(inner @ self.last[self.rows(i)])
        around = even.copy()
        around[:, 0 if j == 0 else at[0]] += np.concatenate(first)
        end = self.count - 1
        around[:, fine - 2 if j == end else at[end] + 1] += np.concatenate(last)
        return product, even, around

    def next_first(self, j, stride):
        if j == self.count - 1:
            return self.fine - 2
        return self.fine + stride * ((j ^ (j + 1)) - 1)


def interpolation(level, j, inputs, stride, coarse):
    table = np.zeros((level.fine, inputs))
    if coarse:
        places = list(range(level.n))
        last = level.n - 1 if j == level.count - 1 else level.n + stride * ((j ^ (j + 1)) - 1)
    else:
        places = [2 * c for c in range(level.n)]
        last = level.next_first(j, stride)
    places.append(last)
    for c in range(level.n):
        table[2 * c, places[c]] = 1.0
        table[2 * c + 1, places[c]] += 0.5
        table[2 * c + 1, places[c + 1]] += 0.5
    return table


def chain(whole, count, levels):
    made = None
    for depth in reversed(range(levels)):
        made = Level(whole >> depth, count, made)
    return made


def padded(table, rows, cols):
    out = np.zeros((rows, cols))
    out[: table.shape[0], : table.shape[1]] = table
    return out


highest = lax.Precision.HIGHEST


def dot(a, b, dims=((1,), (0,))):
    return lax.dot_general(a, b, (dims, ((), ())), precision=highest, preferred_element_type=jnp.float32)


def kernel_call(body, outs, arrays, scalars=0, scratch=()):
    specs = [pl.BlockSpec(memory_space=pltpu.VMEM)] * (len(arrays) - scalars)
    specs += [pl.BlockSpec(memory_space=pltpu.SMEM)] * scalars
    return pl.pallas_call(
        body,
        out_shape=[jax.ShapeDtypeStruct(shape, jnp.float32) for shape in outs],
        in_specs=specs,
        out_specs=[pl.BlockSpec(memory_space=pltpu.VMEM)] * len(outs),
        scratch_shapes=list(scratch),
        compiler_params=pltpu.CompilerParams(vmem_limit_bytes=40 << 20),
    )(*arrays)


def swapped(value, axis):
    count = lax.axis_size(axis)
    return [lax.ppermute(value, axis, [(i, i ^ k) for i in range(count)]) for k in range(1, count)]


def iota(shape, dim):
    return lax.broadcasted_iota(jnp.int32, shape, dim)


def shards(counts, field):
    dz, dx, dy = counts
    lz, lx, ly = field.shape
    nz, nx, ny = lz * dz, lx * dx, ly * dy

    yone = chain(ny, dy, 3)
    ytwo, ythree = yone.following, yone.following.following
    xone = chain(nx, dx, 1)
    xtwo = chain(nx // 2, dx, 2)
    xthree = xtwo.following
    zone = Level(nz, dz, None)

    ky, ky2, ky3 = yone.kept, ytwo.kept, ythree.kept
    kya = round_up(ky + 3, 16)
    kys = round_up(ky + 2, 16)
    wide = round_up(yone.n + ky * (dy - 1) + 1, 128)
    wide2 = ytwo.n + ky2 * (dy - 1)
    packed = round_up(3 * wide2, 128)
    kx = round_up(xtwo.functional_count, 8)
    rowsx = xtwo.fine + kx * (dx - 1)
    tall = round_up(xtwo.n + xtwo.kept * (dx - 1), 8)

    fya = np.zeros((dy, kya, ly))
    fys = np.zeros((dy, kys, ly))
    ta = np.zeros((dy, ly, wide))
    wa = np.zeros((dy, max(dy - 1, 1) * kya, wide))
    tsm = np.zeros((dy, ly, 2 * wide))
    wsm = np.zeros((dy, max(dy - 1, 1) * kys, 2 * wide))
    for j in range(dy):
        pick_a = [2, 3] + list(range(4 + ky, 4 + 2 * ky)) + [0]
        pick_s = [0, 1] + list(range(4, 4 + ky))
        fya[j, : len(pick_a)] = yone.functionals[j][pick_a]
        fys[j, : len(pick_s)] = yone.functionals[j][pick_s]
        product, even, around = yone.tables(j)
        used = product.shape[0]
        for source, to, across, pick, k in (
            (product, ta[j], wa[j], pick_a[:-1], kya),
            (even, tsm[j][:, :wide], wsm[j][:, :wide], pick_s, kys),
            (around, tsm[j][:, wide:], wsm[j][:, wide:], pick_s, kys),
        ):
            to[:, :used] = source[:, :ly].T
            for place in range(dy - 1):
                begin = ly + yone.functional_count * place
                part = source[:, begin : begin + yone.functional_count].T[pick]
                across[k * place : k * place + len(pick), :used] = part
        if j == dy - 1:
            ta[j, ly - 2, wide - 1] = 0.5
        else:
            wa[j, kya * ((j ^ (j + 1)) - 1) + len(pick_a) - 1, wide - 1] = 0.5

    fx = np.zeros((dx, 8, lx))
    txa = np.zeros((dx, xone.n, lx + 8 * (dx - 1)))
    txm = np.zeros((dx, xone.n, xone.n + 8 * (dx - 1)))
    hx = np.zeros((dx, dx))
    for j in range(dx):
        fx[j, :2] = xone.functionals[j][2:4]
        product, even, around = xone.tables(j)
        txa[j, :, :lx] = product[:, :lx]
        txm[j, :, : xone.n] = around[:, :lx:2]
        for place in range(dx - 1):
            txa[j, :, lx + 8 * place : lx + 8 * place + 2] = product[:, lx + 4 * place + 2 : lx + 4 * place + 4]
            begin = xone.n + 8 * place
            txm[j, :, begin + 2 : begin + 4] = around[:, lx + 4 * place : lx + 4 * place + 2]
        hx[j, 0 if j == dx - 1 else j ^ (j + 1)] = 1.0

    zn = zone.n
    zs = np.zeros((dz, 2 * lz + 2 + zn * (lz + dz + 1)))
    for j in range(dz):
        cv, cw = zone.v[j], zone.w[j]
        k_last = (zone.last[zone.rows(0)] / zone.reach(0, j))[0] if 0 < j == dz - 1 else 0.0
        k_first = (zone.first[zone.rows(dz - 1)] / zone.reach(dz - 1, j))[-1] if j == 0 and dz > 1 else 0.0
        parts = [cv, cw, [k_last, k_first], zone.block(j, j).reshape(-1)]
        parts += [zone.reach(j, j ^ k) for k in range(1, dz)]
        parts += [zone.first[zone.rows(j)] * (j == 0), zone.last[zone.rows(j)] * (j == dz - 1)]
        zs[j] = np.concatenate([np.asarray(p, np.float64) for p in parts])
    at_local = 2 * lz + 2
    at_reach = at_local + zn * lz
    at_first = at_reach + zn * (dz - 1)
    at_last = at_first + zn

    f2x = np.stack([padded(xtwo.functionals[j], kx, xtwo.fine) for j in range(dx)])
    tx2 = np.zeros((dx, 3 * tall, rowsx))
    qx2 = np.zeros((dx, xtwo.fine, rowsx))
    tx3 = np.zeros((dx, 3 * xthree.n, tall))
    qx3 = np.zeros((dx, xthree.fine, tall))
    px3 = np.zeros((dx, xtwo.fine, tall))
    for j in range(dx):
        for c, table in enumerate(xtwo.tables(j)):
            tx2[j, c * tall : c * tall + table.shape[0], : xtwo.fine] = table[:, : xtwo.fine]
            for place in range(dx - 1):
                begin = xtwo.fine + xtwo.functional_count * place
                target = xtwo.fine + kx * place
                tx2[j, c * tall : c * tall + table.shape[0], target : target + xtwo.functional_count] = table[
                    :, begin : begin + xtwo.functional_count
                ]
        qx2[j] = interpolation(xtwo, j, rowsx, kx, False)
        for c, table in enumerate(xthree.tables(j)):
            tx3[j, c * xthree.n : (c + 1) * xthree.n, : table.shape[1]] = table
        qx3[j] = interpolation(xthree, j, tall, xthree.functional_count, False)
        px3[j] = interpolation(xtwo, j, tall, xtwo.kept, True)

    ty2 = np.zeros((dy, 3 * wide, packed))
    qy2 = np.zeros((dy, wide, round_up(ytwo.fine, 128)))
    ty3 = np.zeros((dy, 3 * packed, 128))
    qy3 = np.zeros((dy, packed, 128))
    py3 = np.zeros((dy, packed, round_up(ytwo.fine, 128)))
    for j in range(dy):
        for c, table in enumerate(ytwo.tables(j)):
            ty2[j, c * wide : c * wide + table.shape[1], c * wide2 : c * wide2 + wide2] = table.T
        qy2[j, :, : ytwo.fine] = interpolation(ytwo, j, wide, ky, False).T
        for c, table in enumerate(ythree.tables(j)):
            ty3[j, c * packed : c * packed + table.shape[1], : ythree.n] = (-1.0 if c == 2 else 1.0) * table.T
        qy3[j, :, : ythree.fine] = interpolation(ythree, j, packed, ky2, False).T
        py3[j, wide2:, : ytwo.fine] = interpolation(ytwo, j, packed - wide2, ky2, True).T
    az2, first2, last2 = (t.tolist() for t in dense(nz // 2))
    az3, first3, last3 = dense(nz // 4)
    z2, z3 = nz // 2, nz // 4
    lz2, lz3 = lz // 2, lz // 4
    zt = np.concatenate([az3, first3[:, None], last3[:, None]], axis=1)
    zt = zt.reshape(dz, (lz // 8) * (z3 + 2))
    lz4 = lz // 8

    to32 = lambda *tables: [jnp.asarray(t, jnp.float32) for t in tables]
    hz, hx1 = lz // 2, lx // 2

    def y_messages(u_ref, fya_ref, fys_ref, out_ref):
        j = lax.axis_index("gy")
        nt = ((1,), (1,))
        out_ref[:kya, : lz * lx] = dot(fya_ref[j], u_ref[...].reshape(lz * lx, ly), nt)
        even = jnp.concatenate([u_ref[2 * z, pl.ds(0, hx1, stride=2), :] for z in range(hz)], axis=0)
        out_ref[:kys, lz * lx :] = dot(fys_ref[j], even, nt)

    def y_apply(*refs):
        u_ref, came = refs[0], refs[1:dy]
        ta_ref, wa_ref, tsm_ref, wsm_ref, fx_ref, ta_out, tsm_out, iy_out, xm_out = refs[dy:]
        j, jx = lax.axis_index("gy"), lax.axis_index("gx")
        tn = ((0,), (0,))
        ta_all = dot(u_ref[...].reshape(lz * lx, ly), ta_ref[j])
        even = jnp.concatenate([u_ref[2 * z, pl.ds(0, hx1, stride=2), :] for z in range(hz)], axis=0)
        tsm_all = dot(even, tsm_ref[j])
        for k, ref in enumerate(came):
            ta_all += dot(ref[:kya, : lz * lx], wa_ref[j, kya * k : kya * (k + 1), :], tn)
            tsm_all += dot(ref[:kys, lz * lx :], wsm_ref[j, kys * k : kys * (k + 1), :], tn)
        ta_out[...] = ta_all
        tsm_out[...] = tsm_all
        xm_out[...] = jnp.zeros_like(xm_out)
        lane = iota((lx, ly), 1)
        for z in range(lz):
            part = ta_all[z * lx : (z + 1) * lx]
            xm_out[z, 0:2, :wide] = dot(fx_ref[jx], part)[0:2]
            if z % 2 == 0:
                half = z // 2
                tm = tsm_all[half * hx1 : (half + 1) * hx1, wide:]
                xm_out[z, 2:3, :wide] = tm[0:1]
                xm_out[z, 3:4, :wide] = tm[hx1 - 1 : hx1]
                u = u_ref[z]
                before, after = pltpu.roll(u, 1, 1), pltpu.roll(u, ly - 1, 1)
                middle = 0.5 * (before + after)
                edge = 0.5 * before + jnp.broadcast_to(part[:, wide - 1 : wide], (lx, ly))
                iy = jnp.where(lane == ly - 1, edge, jnp.where(lane % 2 == 1, middle, u))
                iy_out[half] = iy
                xm_out[z, 4:5, :ly] = iy[0:1]

    def x_apply(*refs):
        ta_ref, tsm_ref, iy_ref, own_ref = refs[:4]
        came = refs[4 : 3 + dx]
        txa_ref, txm_ref, hx_ref, zs_ref = refs[3 + dx : 7 + dx]
        ixy_out, first_out, u1_out = refs[7 + dx : 10 + dx]
        planes_out = refs[10 + dx :]
        jx, jz = lax.axis_index("gx"), lax.axis_index("gz")
        xa, xm, diff = [], [], []
        for z in range(lz):
            stacked = jnp.concatenate([ta_ref[z * lx : (z + 1) * lx, :]] + [r[z, :, :wide] for r in came], axis=0)
            xa.append(dot(txa_ref[jx], stacked))
        row = iota((lx, ly), 0)
        for half in range(hz):
            part = tsm_ref[half * hx1 : (half + 1) * hx1, :]
            stacked = jnp.concatenate([part[:, wide:]] + [r[2 * half, :, :wide] for r in came], axis=0)
            xm.append(dot(txm_ref[jx], stacked))
            diff.append(part[:, :wide] - xm[-1])
            iy = iy_ref[half]
            halo = hx_ref[jx, 0] * iy[lx - 2 : lx - 1]
            for k, r in enumerate(came):
                halo += hx_ref[jx, k + 1] * r[2 * half, 4:5, :ly]
            before, after = pltpu.roll(iy, 1, 0), pltpu.roll(iy, lx - 1, 0)
            after = jnp.where(row == lx - 1, jnp.broadcast_to(halo, (lx, ly)), after)
            ixy = jnp.where(row % 2 == 1, 0.5 * (before + after), iy)
            ixy_out[half] = ixy
            if half == 0:
                first_out[...] = ixy
        scalar = lambda place: zs_ref[jz, place]
        for zc in range(zn):
            total = diff[zc] - scalar(at_first + zc) * xm[0] - scalar(at_last + zc) * xm[hz - 1]
            for z in range(lz):
                total += scalar(at_local + zc * lz + z) * xa[z]
            u1_out[zc] = total
        v = -scalar(2 * lz) * xm[hz - 1]
        w = -scalar(2 * lz + 1) * xm[0]
        for z in range(lz):
            v += scalar(z) * xa[z]
            w += scalar(lz + z) * xa[z]
        for k, out in enumerate(planes_out):
            out[...] = jnp.where((jz ^ (k + 1)) > jz, w, v)

    def z_apply(*refs):
        part_ref, came = refs[0], refs[1:dz]
        f2x_ref, zs_ref, u1_out, xt_out = refs[dz:]
        jx, jz = lax.axis_index("gx"), lax.axis_index("gz")
        for zc in range(zn):
            total = part_ref[zc]
            for k, r in enumerate(came):
                total += zs_ref[jz, at_reach + k * zn + zc] * r[...]
            u1_out[zc] = total
            xt_out[:, zc * wide : (zc + 1) * wide] = dot(f2x_ref[jx], total)

    def fine_coefficients(u_ref, ixy_ref, halo_ref, out_ref):
        jz = lax.axis_index("gz")
        for half in range(hz):
            here = ixy_ref[half]
            out_ref[2 * half] = u_ref[2 * half] - here
            after = ixy_ref[half + 1] if half + 1 < hz else jnp.where(jz == dz - 1, here, halo_ref[...])
            out_ref[2 * half + 1] = u_ref[2 * half + 1] - 0.5 * (here + after)

    def second_apply(*refs):
        u1_ref, came = refs[0], refs[1:dx]
        tx2_ref, qx2_ref, ty2_ref, qy2_ref, zt_out, i2_out = refs[dx:]
        jx, jy = lax.axis_index("gx"), lax.axis_index("gy")
        own = jnp.concatenate([u1_ref[z] for z in range(lz2)], axis=1)
        state = jnp.concatenate([own] + [r[...] for r in came], axis=0)
        across = dot(tx2_ref[jx], state)
        spread = dot(qx2_ref[jx], state)
        for z in range(lz2):
            cut = across[:, z * wide : (z + 1) * wide]
            joined = jnp.concatenate([cut[c * tall : (c + 1) * tall] for c in range(3)], axis=1)
            zt_out[z] = dot(joined, ty2_ref[jy])
            if z % 2 == 0:
                i2_out[z // 2] = dot(spread[:, z * wide : (z + 1) * wide], qy2_ref[jy])

    def third_apply(*refs):
        u1_ref, i2_ref, own_ref = refs[:3]
        came = refs[3 : 2 + dz]
        px3_ref, py3_ref, tx3_ref, ty3_ref, qx3_ref, qy3_ref, zt_ref = refs[2 + dz : 9 + dz]
        middle_out, coarse_out, coarsest_out, zbuf, ubuf = refs[9 + dz :]
        jx, jy, jz = lax.axis_index("gx"), lax.axis_index("gy"), lax.axis_index("gz")
        zbuf[pl.ds(jz * lz2, lz2)] = own_ref[...]
        for k, r in enumerate(came):
            zbuf[pl.ds((jz ^ (k + 1)) * lz2, lz2)] = r[...]
        at = jnp.minimum((jz + 1) * lz2, z2 - 2)
        halo = dot(dot(px3_ref[jx], zbuf[at]), py3_ref[jy])
        fy = ytwo.fine
        for half in range(lz2 // 2):
            here = i2_ref[half]
            after = i2_ref[half + 1] if half + 1 < lz2 // 2 else halo
            middle_out[2 * half] = (u1_ref[2 * half][:, :fy] - here[:, :fy])
            middle_out[2 * half + 1] = u1_ref[2 * half + 1][:, :fy] - (0.5 * (here + after))[:, :fy]
        everything = [zbuf[z] for z in range(z2)]
        evens = [pltpu.roll(everything[z], packed - wide2, 1) for z in range(0, z2, 2)]
        arounds = [pltpu.roll(everything[z], packed - 2 * wide2, 1) for z in range(0, z2, 2)]
        for zc in range(z3):
            total = evens[zc] - arounds[zc] - first2[zc] * arounds[0] - last2[zc] * arounds[-1]
            for z in range(z2):
                total += az2[zc][z] * everything[z]
            ubuf[zc] = total
        fy3 = ythree.fine
        spread = []
        for half in range(lz3 // 2 + 1):
            at = jnp.minimum(jz * lz3 + 2 * half, z3 - 2)
            spread.append(dot(dot(qx3_ref[jx], ubuf[at]), qy3_ref[jy])[:, :fy3])
        for half in range(lz3 // 2):
            at = jz * lz3 + 2 * half
            coarse_out[2 * half] = ubuf[at][: xthree.fine, :fy3] - spread[half]
            coarse_out[2 * half + 1] = ubuf[at + 1][: xthree.fine, :fy3] - 0.5 * (spread[half] + spread[half + 1])
        n3 = xthree.n
        for zc in range(lz4):
            base = zc * (z3 + 2)
            along = zt_ref[jz, base] * ubuf[0]
            for z in range(1, z3):
                along += zt_ref[jz, base + z] * ubuf[z]
            even = ubuf[2 * (jz * lz4 + zc)]
            around = even + zt_ref[jz, base + z3] * ubuf[0] + zt_ref[jz, base + z3 + 1] * ubuf[z3 - 2]
            joined = jnp.concatenate(
                [
                    dot(tx3_ref[jx, c * n3 : (c + 1) * n3, :], plane)
                    for c, plane in enumerate((along, even, around))
                ],
                axis=1,
            )
            coarsest_out[zc] = dot(joined, ty3_ref[jy])[:, : ythree.n]

    (ym,) = kernel_call(y_messages, [(max(kya, kys), lz * lx + hz * hx1)], [field, *to32(fya, fys)])
    ycame = swapped(ym, "gy")
    xw = max(wide, ly)
    ta_v, tsm_v, iy, xm = kernel_call(
        y_apply,
        [(lz * lx, wide), (hz * hx1, 2 * wide), (hz, lx, ly), (lz, 8, xw)],
        [field, *ycame, *to32(ta, wa, tsm, wsm, fx)],
    )
    xcame = swapped(xm, "gx")
    ixy, zfirst, u1_part, *planes = kernel_call(
        x_apply,
        [(hz, lx, ly), (lx, ly), (zn, xone.n, wide)] + [(xone.n, wide)] * (dz - 1),
        [ta_v, tsm_v, iy, xm, *xcame, *to32(txa, txm, hx, zs)],
        scalars=2,
    )
    zcame = [
        lax.ppermute(plane, "gz", [(i, i ^ (k + 1)) for i in range(dz)]) for k, plane in enumerate(planes)
    ]
    zhalo = lax.ppermute(zfirst, "gz", [(i + 1, i) for i in range(dz - 1)])
    u1, xt = kernel_call(
        z_apply,
        [(zn, xone.n, wide), (kx, zn * wide)],
        [u1_part, *zcame, *to32(f2x, zs)],
        scalars=1,
    )
    xtcame = swapped(xt, "gx")
    (fine,) = kernel_call(fine_coefficients, [(lz, lx, ly)], [field, ixy, zhalo])
    zmsg, i2 = kernel_call(
        second_apply,
        [(lz2, tall, packed), (lz2 // 2, xtwo.fine, round_up(ytwo.fine, 128))],
        [u1, *xtcame, *to32(tx2, qx2, ty2, qy2)],
    )
    ztcame = swapped(zmsg, "gz")
    middle, coarse, coarsest = kernel_call(
        third_apply,
        [(lz2, xtwo.fine, ytwo.fine), (lz3, xthree.fine, ythree.fine), (lz4, xthree.n, ythree.n)],
        [u1, i2, zmsg, *ztcame, *to32(px3, py3, tx3, ty3, qx3, qy3, zt)],
        scalars=1,
        scratch=[pltpu.VMEM((z2, tall, packed), jnp.float32), pltpu.VMEM((z3, tall, packed), jnp.float32)],
    )
    return fine, middle, coarse, coarsest


def solution(mesh):
    spec = P("gz", "gx", "gy")
    counts = tuple(mesh.shape[a] for a in ("gz", "gx", "gy"))
    return jax.shard_map(
        functools.partial(shards, counts), mesh=mesh, in_specs=(spec,), out_specs=(spec,) * 4, check_vma=False
    )
```

```python
import functools
import math

import jax
import jax.numpy as jnp
import numpy as np
from jax import lax
from jax.experimental import pallas as pl
from jax.experimental.pallas import tpu as pltpu
from jax.sharding import PartitionSpec as P

band_ratio = 2.0 - math.sqrt(3.0)
f32 = np.float32


def round_up(value, unit):
    return -(-value // unit) * unit


def dense(fine):
    n = fine // 2
    steps = np.arange(n)[:, None] - np.arange(n)[None, :]
    lower = np.where(steps >= 0, (-band_ratio) ** np.maximum(steps, 0), 0.0)
    inverse = lower.T @ lower
    mass = 4.0 * np.eye(fine) + np.eye(fine, k=1) + np.eye(fine, k=-1)
    weights = np.where(np.arange(n) == n - 1, 1.0, 0.5)[:, None]
    earlier = np.concatenate([np.zeros((1, fine)), mass[1::2][:-1]])
    product = inverse @ (0.5 * band_ratio * (mass[0::2] + weights * mass[1::2] + 0.5 * earlier))
    return product, inverse[:, 0] * (3 * band_ratio - 1), inverse[:, -1] * (2 * band_ratio)


class Level:
    def __init__(self, whole, count, following):
        self.count, self.fine = count, whole // count
        self.n = self.fine // 2
        self.product, self.first, self.last = dense(whole)
        self.following = following
        self.kept = following.functional_count if following else 0
        self.functional_count = 4 + 2 * self.kept
        self.even = np.zeros((self.n, self.fine))
        self.even[np.arange(self.n), 2 * np.arange(self.n)] = 1.0
        self.v = [self.towards(i, i * self.n - 1) for i in range(count)]
        self.w = [self.towards(i, (i + 1) * self.n) for i in range(count)]
        self.functionals = []
        for i in range(count):
            own = np.zeros((4, self.fine))
            own[0, 0] = own[1, self.fine - 2] = 1.0
            own[2], own[3] = self.v[i], self.w[i]
            if following:
                inner = following.functionals[i]
                own = np.concatenate([own, inner @ self.even, inner @ self.block(i, i)])
            self.functionals.append(own)

    def rows(self, i):
        return slice(i * self.n, (i + 1) * self.n)

    def block(self, i, j):
        return self.product[self.rows(i), j * self.fine : (j + 1) * self.fine]

    def towards(self, i, row):
        if not 0 <= row < self.count * self.n:
            return np.zeros(self.fine)
        values = self.product[row, i * self.fine : (i + 1) * self.fine]
        return values / np.abs(values).max()

    def reach(self, i, j):
        side = self.v[j] if j > i else self.w[j]
        best = np.argmax(np.abs(side))
        return self.block(i, j)[:, best] / side[best]

    def side(self, i, j):
        return 2 if j > i else 3

    def tables(self, j):
        own, kept, many, n, fine = self.n, self.kept, self.functional_count, self.n, self.fine
        others = [j ^ k for k in range(1, self.count)]
        shape = (own + kept * len(others), fine + many * len(others))
        product, even = np.zeros(shape), np.zeros(shape)
        at = {i: fine + many * place for place, i in enumerate(others)}
        product[:n, :fine] = self.block(j, j)
        even[:n, :fine] = self.even
        first, last = [self.first[self.rows(j)]], [self.last[self.rows(j)]]
        for i in others:
            product[:n, at[i] + self.side(j, i)] = self.reach(j, i)
        for place, i in enumerate(others):
            if not kept:
                break
            inner = self.following.functionals[i]
            target = n + kept * place + np.arange(kept)
            product[target, :fine] = inner @ self.block(i, j)
            product[target, at[i] + 4 + kept + np.arange(kept)] = 1.0
            even[target, at[i] + 4 + np.arange(kept)] = 1.0
            for other in others:
                if other != i:
                    product[target, at[other] + self.side(i, other)] = inner @ self.reach(i, other)
            first.append(inner @ self.first[self.rows(i)])
            last.append(inner @ self.last[self.rows(i)])
        around = even.copy()
        around[:, 0 if j == 0 else at[0]] += np.concatenate(first)
        end = self.count - 1
        around[:, fine - 2 if j == end else at[end] + 1] += np.concatenate(last)
        return product, even, around

    def next_first(self, j, stride):
        if j == self.count - 1:
            return self.fine - 2
        return self.fine + stride * ((j ^ (j + 1)) - 1)


def interpolation(level, j, inputs, stride, coarse):
    table = np.zeros((level.fine, inputs))
    if coarse:
        places = list(range(level.n))
        last = level.n - 1 if j == level.count - 1 else level.n + stride * ((j ^ (j + 1)) - 1)
    else:
        places = [2 * c for c in range(level.n)]
        last = level.next_first(j, stride)
    places.append(last)
    for c in range(level.n):
        table[2 * c, places[c]] = 1.0
        table[2 * c + 1, places[c]] += 0.5
        table[2 * c + 1, places[c + 1]] += 0.5
    return table


def chain(whole, count, levels):
    made = None
    for depth in reversed(range(levels)):
        made = Level(whole >> depth, count, made)
    return made


def padded(table, rows, cols):
    out = np.zeros((rows, cols))
    out[: table.shape[0], : table.shape[1]] = table
    return out


highest = lax.Precision.HIGHEST


def dot(a, b, dims=((1,), (0,))):
    return lax.dot_general(a, b, (dims, ((), ())), precision=highest, preferred_element_type=jnp.float32)


def kernel_call(body, outs, arrays, scratch=(), left=(), left_out=(), aliases={}):
    space = lambda place, where: pl.BlockSpec(memory_space=pl.ANY if place in where else pltpu.VMEM)
    return pl.pallas_call(
        body,
        out_shape=[jax.ShapeDtypeStruct(shape, jnp.float32) for shape in outs],
        in_specs=[space(i, left) for i in range(len(arrays))],
        out_specs=[space(i, left_out) for i in range(len(outs))],
        scratch_shapes=list(scratch),
        input_output_aliases=aliases,
        compiler_params=pltpu.CompilerParams(vmem_limit_bytes=40 << 20),
    )(*arrays)


def swapped(value, axis):
    count = lax.axis_size(axis)
    return [lax.ppermute(value, axis, [(i, i ^ k) for i in range(count)]) for k in range(1, count)]


def chosen_by(values, j):
    chosen = float(values[0])
    for place in range(1, len(values)):
        if any(values[place] != values[0] for place in range(len(values))):
            chosen = jnp.where(j == place, f32(values[place]), chosen)
    return chosen


def iota(shape, dim):
    return lax.broadcasted_iota(jnp.int32, shape, dim)


def shards(counts, field):
    dz, dx, dy = counts
    lz, lx, ly = field.shape
    nz, nx, ny = lz * dz, lx * dx, ly * dy

    yone = chain(ny, dy, 3)
    ytwo, ythree = yone.following, yone.following.following
    xone = chain(nx, dx, 1)
    xtwo = chain(nx // 2, dx, 2)
    xthree = xtwo.following
    zone = Level(nz, dz, None)

    ky, ky2, ky3 = yone.kept, ytwo.kept, ythree.kept
    kya = round_up(ky + 3, 16)
    kys = round_up(ky + 2, 16)
    wide1 = yone.n + ky * (dy - 1)
    wide2 = ytwo.n + ky2 * (dy - 1)
    wide = packed = round_up(max(wide1 + 1, 3 * wide2, wide2 + wide1), 128)
    kx = round_up(xtwo.functional_count, 8)
    rowsx = xtwo.fine + kx * (dx - 1)
    tall = round_up(xtwo.n + xtwo.kept * (dx - 1), 8)

    fya = np.zeros((dy, kya, ly))
    fys = np.zeros((dy, kys, ly))
    ta = np.zeros((dy, ly, wide))
    wa = np.zeros((dy, max(dy - 1, 1) * kya, wide))
    tsm = np.zeros((dy, ly, 2 * wide))
    wsm = np.zeros((dy, max(dy - 1, 1) * kys, 2 * wide))
    for j in range(dy):
        pick_a = [2, 3] + list(range(4 + ky, 4 + 2 * ky)) + [0]
        pick_s = [0, 1] + list(range(4, 4 + ky))
        fya[j, : len(pick_a)] = yone.functionals[j][pick_a]
        fys[j, : len(pick_s)] = yone.functionals[j][pick_s]
        product, even, around = yone.tables(j)
        used = product.shape[0]
        for source, to, across, pick, k in (
            (product, ta[j], wa[j], pick_a[:-1], kya),
            (even, tsm[j][:, :wide], wsm[j][:, :wide], pick_s, kys),
            (around, tsm[j][:, wide:], wsm[j][:, wide:], pick_s, kys),
        ):
            to[:, :used] = source[:, :ly].T
            for place in range(dy - 1):
                begin = ly + yone.functional_count * place
                part = source[:, begin : begin + yone.functional_count].T[pick]
                across[k * place : k * place + len(pick), :used] = part
        if j == dy - 1:
            ta[j, ly - 2, wide - 1] = 0.5
        else:
            wa[j, kya * ((j ^ (j + 1)) - 1) + len(pick_a) - 1, wide - 1] = 0.5

    fx = np.zeros((dx, lx, 8))
    txa = np.zeros((dx, xone.n, lx + 8 * (dx - 1)))
    txm = np.zeros((dx, xone.n, xone.n + 8 * (dx - 1)))
    for j in range(dx):
        fx[j, :, :2] = xone.functionals[j][2:4].T
        product, even, around = xone.tables(j)
        txa[j, :, :lx] = product[:, :lx]
        txm[j, :, : xone.n] = around[:, :lx:2]
        for place in range(dx - 1):
            txa[j, :, lx + 8 * place : lx + 8 * place + 2] = product[:, lx + 4 * place + 2 : lx + 4 * place + 4]
            begin = xone.n + 8 * place
            txm[j, :, begin + 2 : begin + 4] = around[:, lx + 4 * place : lx + 4 * place + 2]

    zn = zone.n
    zs = np.zeros((dz, 2 * lz + 2 + zn * (lz + dz + 1)))
    for j in range(dz):
        cv, cw = zone.v[j], zone.w[j]
        k_last = (zone.last[zone.rows(0)] / zone.reach(0, j))[0] if 0 < j == dz - 1 else 0.0
        k_first = (zone.first[zone.rows(dz - 1)] / zone.reach(dz - 1, j))[-1] if j == 0 and dz > 1 else 0.0
        parts = [cv, cw, [k_last, k_first], zone.block(j, j).reshape(-1)]
        parts += [zone.reach(j, j ^ k) for k in range(1, dz)]
        parts += [zone.first[zone.rows(j)] * (j == 0), zone.last[zone.rows(j)] * (j == dz - 1)]
        zs[j] = np.concatenate([np.asarray(p, np.float64) for p in parts])
    at_local = 2 * lz + 2
    at_reach = at_local + zn * lz
    at_first = at_reach + zn * (dz - 1)
    at_last = at_first + zn

    f2x = np.stack([padded(xtwo.functionals[j], kx, xtwo.fine) for j in range(dx)])
    tx2 = np.zeros((dx, 3 * tall, rowsx))
    qx2 = np.zeros((dx, xtwo.fine, rowsx))
    tx3 = np.zeros((dx, 3 * xthree.n, tall))
    qx3 = np.zeros((dx, xthree.fine, tall))
    px3 = np.zeros((dx, xtwo.fine, tall))
    for j in range(dx):
        for c, table in enumerate(xtwo.tables(j)):
            tx2[j, c * tall : c * tall + table.shape[0], : xtwo.fine] = table[:, : xtwo.fine]
            for place in range(dx - 1):
                begin = xtwo.fine + xtwo.functional_count * place
                target = xtwo.fine + kx * place
                tx2[j, c * tall : c * tall + table.shape[0], target : target + xtwo.functional_count] = table[
                    :, begin : begin + xtwo.functional_count
                ]
        qx2[j] = interpolation(xtwo, j, rowsx, kx, False)
        for c, table in enumerate(xthree.tables(j)):
            tx3[j, c * xthree.n : (c + 1) * xthree.n, : table.shape[1]] = table
        qx3[j] = interpolation(xthree, j, tall, xthree.functional_count, False)
        px3[j] = interpolation(xtwo, j, tall, xtwo.kept, True)

    ty2 = np.zeros((dy, 3 * wide, packed))
    qy2 = np.zeros((dy, wide, round_up(ytwo.fine, 128)))
    ty3 = np.zeros((dy, 3 * packed, 128))
    qy3 = np.zeros((dy, packed, 128))
    py3 = np.zeros((dy, packed, round_up(ytwo.fine, 128)))
    px1 = np.zeros((lx, 2 * tall))
    py1 = np.zeros((dy, packed, ly))
    for j in range(dy):
        for c, table in enumerate(ytwo.tables(j)):
            ty2[j, c * wide : c * wide + table.shape[1], c * wide2 : c * wide2 + wide2] = table.T
        qy2[j, :, : ytwo.fine] = interpolation(ytwo, j, wide, ky, False).T
        for c, table in enumerate(ythree.tables(j)):
            ty3[j, c * packed : c * packed + table.shape[1], : ythree.n] = (-1.0 if c == 2 else 1.0) * table.T
        qy3[j, :, : ythree.fine] = interpolation(ythree, j, packed, ky2, False).T
        py1[j, wide2:] = interpolation(yone, j, packed - wide2, ky, True).T
        py3[j, wide2:, : ytwo.fine] = interpolation(ytwo, j, packed - wide2, ky2, True).T
    for c in range(xone.n):
        begin = c if c < xtwo.n else tall + c - xtwo.n
        px1[2 * c, begin] = 1.0
        px1[2 * c + 1, begin : begin + 2] = 0.5
    az2, first2, last2 = (t.tolist() for t in dense(nz // 2))
    az3, first3, last3 = dense(nz // 4)
    z2, z3 = nz // 2, nz // 4
    lz2, lz3 = lz // 2, lz // 4
    zt = np.concatenate([az3, first3[:, None], last3[:, None]], axis=1)
    zt = zt.reshape(dz, (lz // 8) * (z3 + 2))
    lz4 = lz // 8

    to32 = lambda *tables: [jnp.asarray(t, jnp.float32) for t in tables]
    hz, hx1 = lz // 2, lx // 2

    def y_messages(u_ref, fya_ref, fys_ref, out_ref):
        j = lax.axis_index("gy")
        nt = ((1,), (1,))
        out_ref[:kya, : lz * lx] = dot(fya_ref[j], u_ref[...].reshape(lz * lx, ly), nt)
        even = jnp.concatenate([u_ref[2 * z, pl.ds(0, hx1, stride=2), :] for z in range(hz)], axis=0)
        out_ref[:kys, lz * lx :] = dot(fys_ref[j], even, nt)

    def y_apply(*refs):
        u_ref, came = refs[0], refs[1:dy]
        ta_ref, wa_ref, tsm_ref, wsm_ref, fx_ref, ta_out, tsm_out, iy_out, xm_out = refs[dy:]
        j, jx = lax.axis_index("gy"), lax.axis_index("gx")
        tn = ((0,), (0,))
        ta_all = dot(u_ref[...].reshape(lz * lx, ly), ta_ref[j])
        even = jnp.concatenate([u_ref[2 * z, pl.ds(0, hx1, stride=2), :] for z in range(hz)], axis=0)
        tsm_all = dot(even, tsm_ref[j])
        for k, ref in enumerate(came):
            ta_all += dot(ref[:kya, : lz * lx], wa_ref[j, kya * k : kya * (k + 1), :], tn)
            tsm_all += dot(ref[:kys, lz * lx :], wsm_ref[j, kys * k : kys * (k + 1), :], tn)
        ta_out[...] = ta_all
        tsm_out[...] = tsm_all
        xm_out[...] = jnp.zeros_like(xm_out)
        lane = iota((lx, ly), 1)
        weights = [jnp.broadcast_to(fx_ref[jx, :, c : c + 1], (lx, wide)) for c in range(2)]
        xm_out[0, 5:6, :wide] = tsm_all[0:1, :wide]
        for z in range(lz):
            part = ta_all[z * lx : (z + 1) * lx]
            for c in range(2):
                xm_out[z, c : c + 1, :wide] = jnp.sum(part * weights[c], axis=0, keepdims=True)
            if z % 2 == 0:
                half = z // 2
                tm = tsm_all[half * hx1 : (half + 1) * hx1, wide:]
                xm_out[z, 2:3, :wide] = tm[0:1]
                xm_out[z, 3:4, :wide] = tm[hx1 - 1 : hx1]
                u = u_ref[z]
                before, after = pltpu.roll(u, 1, 1), pltpu.roll(u, ly - 1, 1)
                middle = 0.5 * (before + after)
                edge = 0.5 * before + jnp.broadcast_to(part[:, wide - 1 : wide], (lx, ly))
                iy = jnp.where(lane == ly - 1, edge, jnp.where(lane % 2 == 1, middle, u))
                iy_out[half] = iy
                xm_out[z, 4:5, :ly] = iy[0:1]

    def x_apply(*refs):
        ta_ref, tsm_ref, iy_ref, own_ref = refs[:4]
        came = refs[4 : 3 + dx]
        txa_ref, txm_ref, ixy_out, zc_out, u1_out = refs[3 + dx : 8 + dx]
        planes_out = refs[8 + dx :]
        jx, jz = lax.axis_index("gx"), lax.axis_index("gz")
        xa, xm, diff = [], [], []
        def from_next(own, rows):
            for k, rest in enumerate(rows):
                own = jnp.where((jx ^ (k + 1)) == jx + 1, rest, own)
            return own

        for z in range(0, lz, 2):
            pair = jnp.concatenate([ta_ref[z * lx : (z + 1) * lx, :], ta_ref[(z + 1) * lx : (z + 2) * lx, :]], axis=1)
            rest = [jnp.concatenate([r[z, :, :wide], r[z + 1, :, :wide]], axis=1) for r in came]
            both = dot(txa_ref[jx], jnp.concatenate([pair] + rest, axis=0))
            xa += [both[:, :wide], both[:, wide:]]
        zc_out[...] = jnp.zeros_like(zc_out)
        zc_out[:hx1] = tsm_ref[:hx1, :wide]
        zc_out[hx1 : hx1 + 1] = from_next(tsm_ref[hx1 - 1 : hx1, :wide], [r[0, 5:6, :wide] for r in came])
        row = iota((lx, ly), 0)
        for half in range(hz):
            part = tsm_ref[half * hx1 : (half + 1) * hx1, :]
            stacked = jnp.concatenate([part[:, wide:]] + [r[2 * half, :, :wide] for r in came], axis=0)
            xm.append(dot(txm_ref[jx], stacked))
            diff.append(part[:, :wide] - xm[-1])
            iy = iy_ref[half]
            halo = from_next(iy[lx - 2 : lx - 1], [r[2 * half, 4:5, :ly] for r in came])
            before, after = pltpu.roll(iy, 1, 0), pltpu.roll(iy, lx - 1, 0)
            after = jnp.where(row == lx - 1, jnp.broadcast_to(halo, (lx, ly)), after)
            ixy = jnp.where(row % 2 == 1, 0.5 * (before + after), iy)
            ixy_out[half] = ixy
        scalar = lambda place: chosen_by(zs[:, place], jz)
        for zc in range(zn):
            total = diff[zc] - scalar(at_first + zc) * xm[0] - scalar(at_last + zc) * xm[hz - 1]
            for z in range(lz):
                total += scalar(at_local + zc * lz + z) * xa[z]
            u1_out[zc] = total
        v = -scalar(2 * lz) * xm[hz - 1]
        w = -scalar(2 * lz + 1) * xm[0]
        for z in range(lz):
            v += scalar(z) * xa[z]
            w += scalar(lz + z) * xa[z]
        for k, out in enumerate(planes_out):
            out[...] = jnp.where((jz ^ (k + 1)) > jz, w, v)

    def z_apply(*refs):
        part_ref, came = refs[0], refs[1:dz]
        f2x_ref, u1_out, xt_out = refs[dz:]
        jx, jz = lax.axis_index("gx"), lax.axis_index("gz")
        for zc in range(zn):
            total = part_ref[zc]
            for k, r in enumerate(came):
                total += chosen_by(zs[:, at_reach + k * zn + zc], jz) * r[...]
            u1_out[zc] = total
            xt_out[:, zc * wide : (zc + 1) * wide] = dot(f2x_ref[jx], total)

    def fine_coefficients(u_ref, ixy_ref, out_ref):
        for half in range(hz):
            here = ixy_ref[half]
            out_ref[2 * half] = u_ref[2 * half] - here
            if half + 1 < hz:
                out_ref[2 * half + 1] = u_ref[2 * half + 1] - 0.5 * (here + ixy_ref[half + 1])

    def second_apply(*refs):
        u1_ref, zc_ref, came = refs[0], refs[1], refs[2 : dx + 1]
        tx2_ref, qx2_ref, ty2_ref, qy2_ref, zt_out, i2_out = refs[dx + 1 :]
        jx, jy = lax.axis_index("gx"), lax.axis_index("gy")
        own = jnp.concatenate([u1_ref[z] for z in range(lz2)], axis=1)
        state = jnp.concatenate([own] + [r[...] for r in came], axis=0)
        across = dot(tx2_ref[jx], state)
        spread = dot(qx2_ref[jx], state)
        for z in range(lz2):
            cut = across[:, z * wide : (z + 1) * wide]
            if z % 2 == 1:
                moved = dot(cut[:tall], ty2_ref[jy, :wide])
                if z < 4:
                    begin = xtwo.n * (z // 2)
                    moved += pltpu.roll(zc_ref[begin : begin + tall], wide2, 1)
                zt_out[z] = moved
            else:
                joined = jnp.concatenate([cut[c * tall : (c + 1) * tall] for c in range(3)], axis=1)
                zt_out[z] = dot(joined, ty2_ref[jy])
                i2_out[z // 2] = dot(spread[:, z * wide : (z + 1) * wide], qy2_ref[jy])

    def third_apply(*refs):
        u1_ref, i2_ref, u_ref, ixy_ref, _, own_ref = refs[:6]
        came = refs[6 : 5 + dz]
        px1_ref, py1_ref, px3_ref, py3_ref, tx3_ref, ty3_ref, qx3_ref, qy3_ref = refs[5 + dz : 13 + dz]
        fine_out, middle_out, coarse_out, coarsest_out, zbuf, ubuf, last, sem = refs[13 + dz :]
        jx, jy, jz = lax.axis_index("gx"), lax.axis_index("gy"), lax.axis_index("gz")
        zbuf[pl.ds(jz * lz2, lz2)] = own_ref[...]
        for k, r in enumerate(came):
            zbuf[pl.ds((jz ^ (k + 1)) * lz2, lz2)] = r[...]
        at = jnp.minimum(jz + 1, dz - 1) * lz2
        first = jnp.concatenate([zbuf[at + 1], zbuf[at + 3]], axis=0)
        halo = dot(dot(px1_ref[...], first), py1_ref[jy])
        here = ixy_ref[hz - 1]
        last[...] = u_ref[lz - 1] - 0.5 * (here + jnp.where(jz == dz - 1, here, halo))
        copy = pltpu.make_async_copy(last, fine_out.at[lz - 1], sem)
        copy.start()
        at = jnp.minimum((jz + 1) * lz2, z2 - 2)
        halo = dot(dot(px3_ref[jx], zbuf[at]), py3_ref[jy])
        fy = ytwo.fine
        for half in range(lz2 // 2):
            here = i2_ref[half]
            after = i2_ref[half + 1] if half + 1 < lz2 // 2 else halo
            middle_out[2 * half] = (u1_ref[2 * half][:, :fy] - here[:, :fy])
            middle_out[2 * half + 1] = u1_ref[2 * half + 1][:, :fy] - (0.5 * (here + after))[:, :fy]
        everything = [zbuf[z] for z in range(z2)]
        evens = [pltpu.roll(everything[z], packed - wide2, 1) for z in range(0, z2, 2)]
        arounds = [pltpu.roll(everything[z], packed - 2 * wide2, 1) for z in range(0, z2, 2)]
        for zc in range(z3):
            total = evens[zc] - arounds[zc] - first2[zc] * arounds[0] - last2[zc] * arounds[-1]
            for z in range(z2):
                total += az2[zc][z] * everything[z]
            ubuf[zc] = total
        fy3 = ythree.fine
        spread = []
        for half in range(lz3 // 2 + 1):
            at = jnp.minimum(jz * lz3 + 2 * half, z3 - 2)
            spread.append(dot(dot(qx3_ref[jx], ubuf[at]), qy3_ref[jy])[:, :fy3])
        for half in range(lz3 // 2):
            at = jz * lz3 + 2 * half
            coarse_out[2 * half] = ubuf[at][: xthree.fine, :fy3] - spread[half]
            coarse_out[2 * half + 1] = ubuf[at + 1][: xthree.fine, :fy3] - 0.5 * (spread[half] + spread[half + 1])
        n3 = xthree.n
        for zc in range(lz4):
            base = zc * (z3 + 2)
            along = chosen_by(zt[:, base], jz) * ubuf[0]
            for z in range(1, z3):
                along += chosen_by(zt[:, base + z], jz) * ubuf[z]
            even = ubuf[2 * (jz * lz4 + zc)]
            around = even + chosen_by(zt[:, base + z3], jz) * ubuf[0] + chosen_by(zt[:, base + z3 + 1], jz) * ubuf[z3 - 2]
            joined = jnp.concatenate(
                [
                    dot(tx3_ref[jx, c * n3 : (c + 1) * n3, :], plane)
                    for c, plane in enumerate((along, even, around))
                ],
                axis=1,
            )
            coarsest_out[zc] = dot(joined, ty3_ref[jy])[:, : ythree.n]
        copy.wait()

    (ym,) = kernel_call(y_messages, [(max(kya, kys), lz * lx + hz * hx1)], [field, *to32(fya, fys)])
    ycame = swapped(ym, "gy")
    xw = max(wide, ly)
    ta_v, tsm_v, iy, xm = kernel_call(
        y_apply,
        [(lz * lx, wide), (hz * hx1, 2 * wide), (hz, lx, ly), (lz, 8, xw)],
        [field, *ycame, *to32(ta, wa, tsm, wsm, fx)],
    )
    xcame = swapped(xm, "gx")
    ixy, zc, u1_part, *planes = kernel_call(
        x_apply,
        [(hz, lx, ly), (xtwo.n + tall, wide), (zn, xone.n, wide)] + [(xone.n, wide)] * (dz - 1),
        [ta_v, tsm_v, iy, xm, *xcame, *to32(txa, txm)],
    )
    zcame = [
        lax.ppermute(plane, "gz", [(i, i ^ (k + 1)) for i in range(dz)]) for k, plane in enumerate(planes)
    ]
    u1, xt = kernel_call(z_apply, [(zn, xone.n, wide), (kx, zn * wide)], [u1_part, *zcame, *to32(f2x)])
    xtcame = swapped(xt, "gx")
    zmsg, i2 = kernel_call(
        second_apply,
        [(lz2, tall, packed), (lz2 // 2, xtwo.fine, round_up(ytwo.fine, 128))],
        [u1, zc, *xtcame, *to32(tx2, qx2, ty2, qy2)],
    )
    ztcame = swapped(zmsg, "gz")
    (fine,) = kernel_call(fine_coefficients, [(lz, lx, ly)], [field, ixy])
    return kernel_call(
        third_apply,
        [(lz, lx, ly), (lz2, xtwo.fine, ytwo.fine), (lz3, xthree.fine, ythree.fine), (lz4, xthree.n, ythree.n)],
        [u1, i2, field, ixy, fine, zmsg, *ztcame, *to32(px1, py1, px3, py3, tx3, ty3, qx3, qy3)],
        scratch=[
            pltpu.VMEM((z2, tall, packed), jnp.float32),
            pltpu.VMEM((z3, tall, packed), jnp.float32),
            pltpu.VMEM((lx, ly), jnp.float32),
            pltpu.SemaphoreType.DMA,
        ],
        left=(4,),
        left_out=(0,),
        aliases={4: 0},
    )


def solution(mesh):
    spec = P("gz", "gx", "gy")
    counts = tuple(mesh.shape[a] for a in ("gz", "gx", "gy"))
    return jax.shard_map(
        functools.partial(shards, counts), mesh=mesh, in_specs=(spec,), out_specs=(spec,) * 4, check_vma=False
    )
```

```python
import functools
import math

import jax
import jax.numpy as jnp
import numpy as np
from jax import lax
from jax.experimental import pallas as pl
from jax.experimental.pallas import tpu as pltpu
from jax.sharding import PartitionSpec as P

band_ratio = 2.0 - math.sqrt(3.0)
f32 = np.float32


def round_up(value, unit):
    return -(-value // unit) * unit


def dense(fine):
    n = fine // 2
    steps = np.arange(n)[:, None] - np.arange(n)[None, :]
    lower = np.where(steps >= 0, (-band_ratio) ** np.maximum(steps, 0), 0.0)
    inverse = lower.T @ lower
    mass = 4.0 * np.eye(fine) + np.eye(fine, k=1) + np.eye(fine, k=-1)
    weights = np.where(np.arange(n) == n - 1, 1.0, 0.5)[:, None]
    earlier = np.concatenate([np.zeros((1, fine)), mass[1::2][:-1]])
    product = inverse @ (0.5 * band_ratio * (mass[0::2] + weights * mass[1::2] + 0.5 * earlier))
    return product, inverse[:, 0] * (3 * band_ratio - 1), inverse[:, -1] * (2 * band_ratio)


class Level:
    def __init__(self, whole, count, following):
        self.count, self.fine = count, whole // count
        self.n = self.fine // 2
        self.product, self.first, self.last = dense(whole)
        self.following = following
        self.kept = following.functional_count if following else 0
        self.functional_count = 4 + 2 * self.kept
        self.even = np.zeros((self.n, self.fine))
        self.even[np.arange(self.n), 2 * np.arange(self.n)] = 1.0
        self.v = [self.towards(i, i * self.n - 1) for i in range(count)]
        self.w = [self.towards(i, (i + 1) * self.n) for i in range(count)]
        self.functionals = []
        for i in range(count):
            own = np.zeros((4, self.fine))
            own[0, 0] = own[1, self.fine - 2] = 1.0
            own[2], own[3] = self.v[i], self.w[i]
            if following:
                inner = following.functionals[i]
                own = np.concatenate([own, inner @ self.even, inner @ self.block(i, i)])
            self.functionals.append(own)

    def rows(self, i):
        return slice(i * self.n, (i + 1) * self.n)

    def block(self, i, j):
        return self.product[self.rows(i), j * self.fine : (j + 1) * self.fine]

    def towards(self, i, row):
        if not 0 <= row < self.count * self.n:
            return np.zeros(self.fine)
        values = self.product[row, i * self.fine : (i + 1) * self.fine]
        return values / np.abs(values).max()

    def reach(self, i, j):
        side = self.v[j] if j > i else self.w[j]
        best = np.argmax(np.abs(side))
        return self.block(i, j)[:, best] / side[best]

    def side(self, i, j):
        return 2 if j > i else 3

    def tables(self, j):
        own, kept, many, n, fine = self.n, self.kept, self.functional_count, self.n, self.fine
        others = [j ^ k for k in range(1, self.count)]
        shape = (own + kept * len(others), fine + many * len(others))
        product, even = np.zeros(shape), np.zeros(shape)
        at = {i: fine + many * place for place, i in enumerate(others)}
        product[:n, :fine] = self.block(j, j)
        even[:n, :fine] = self.even
        first, last = [self.first[self.rows(j)]], [self.last[self.rows(j)]]
        for i in others:
            product[:n, at[i] + self.side(j, i)] = self.reach(j, i)
        for place, i in enumerate(others):
            if not kept:
                break
            inner = self.following.functionals[i]
            target = n + kept * place + np.arange(kept)
            product[target, :fine] = inner @ self.block(i, j)
            product[target, at[i] + 4 + kept + np.arange(kept)] = 1.0
            even[target, at[i] + 4 + np.arange(kept)] = 1.0
            for other in others:
                if other != i:
                    product[target, at[other] + self.side(i, other)] = inner @ self.reach(i, other)
            first.append(inner @ self.first[self.rows(i)])
            last.append(inner @ self.last[self.rows(i)])
        around = even.copy()
        around[:, 0 if j == 0 else at[0]] += np.concatenate(first)
        end = self.count - 1
        around[:, fine - 2 if j == end else at[end] + 1] += np.concatenate(last)
        return product, even, around

    def next_first(self, j, stride):
        if j == self.count - 1:
            return self.fine - 2
        return self.fine + stride * ((j ^ (j + 1)) - 1)


def interpolation(level, j, inputs, stride, coarse):
    table = np.zeros((level.fine, inputs))
    if coarse:
        places = list(range(level.n))
        last = level.n - 1 if j == level.count - 1 else level.n + stride * ((j ^ (j + 1)) - 1)
    else:
        places = [2 * c for c in range(level.n)]
        last = level.next_first(j, stride)
    places.append(last)
    for c in range(level.n):
        table[2 * c, places[c]] = 1.0
        table[2 * c + 1, places[c]] += 0.5
        table[2 * c + 1, places[c + 1]] += 0.5
    return table


def chain(whole, count, levels):
    made = None
    for depth in reversed(range(levels)):
        made = Level(whole >> depth, count, made)
    return made


def padded(table, rows, cols):
    out = np.zeros((rows, cols))
    out[: table.shape[0], : table.shape[1]] = table
    return out


highest = lax.Precision.HIGHEST


def dot(a, b, dims=((1,), (0,))):
    return lax.dot_general(a, b, (dims, ((), ())), precision=highest, preferred_element_type=jnp.float32)


def kernel_call(body, outs, arrays, scratch=(), left=(), left_out=(), aliases={}):
    space = lambda place, where: pl.BlockSpec(memory_space=pl.ANY if place in where else pltpu.VMEM)
    return pl.pallas_call(
        body,
        out_shape=[jax.ShapeDtypeStruct(shape, jnp.float32) for shape in outs],
        in_specs=[space(i, left) for i in range(len(arrays))],
        out_specs=[space(i, left_out) for i in range(len(outs))],
        scratch_shapes=list(scratch),
        input_output_aliases=aliases,
        compiler_params=pltpu.CompilerParams(vmem_limit_bytes=40 << 20),
    )(*arrays)


def swapped(value, axis):
    count = lax.axis_size(axis)
    return [lax.ppermute(value, axis, [(i, i ^ k) for i in range(count)]) for k in range(1, count)]


def gathered(value, axis):
    count = lax.axis_size(axis)
    if count != 4:
        return swapped(value, axis)
    by = lambda k, what: lax.ppermute(what, axis, [(i, i ^ k) for i in range(count)])
    far = by(2, value)
    return [by(1, value), far, by(1, far)]


def chosen_by(values, j):
    chosen = float(values[0])
    for place in range(1, len(values)):
        if any(values[place] != values[0] for place in range(len(values))):
            chosen = jnp.where(j == place, f32(values[place]), chosen)
    return chosen


def iota(shape, dim):
    return lax.broadcasted_iota(jnp.int32, shape, dim)


def shards(counts, field):
    dz, dx, dy = counts
    lz, lx, ly = field.shape
    nz, nx, ny = lz * dz, lx * dx, ly * dy

    yone = chain(ny, dy, 3)
    ytwo, ythree = yone.following, yone.following.following
    xone = chain(nx, dx, 1)
    xtwo = chain(nx // 2, dx, 2)
    xthree = xtwo.following
    zone = Level(nz, dz, None)

    ky, ky2, ky3 = yone.kept, ytwo.kept, ythree.kept
    kya = round_up(ky + 3, 16)
    kys = round_up(ky + 2, 16)
    wide1 = yone.n + ky * (dy - 1)
    wide2 = ytwo.n + ky2 * (dy - 1)
    wide = packed = round_up(max(wide1 + 1, 3 * wide2, wide2 + wide1), 128)
    kx = round_up(xtwo.functional_count, 8)
    rowsx = xtwo.fine + kx * (dx - 1)
    tall = round_up(xtwo.n + xtwo.kept * (dx - 1), 8)

    fya = np.zeros((dy, kya, ly))
    fys = np.zeros((dy, kys, ly))
    ta = np.zeros((dy, ly, wide))
    wa = np.zeros((dy, max(dy - 1, 1) * kya, wide))
    tsm = np.zeros((dy, ly, 2 * wide))
    wsm = np.zeros((dy, max(dy - 1, 1) * kys, 2 * wide))
    for j in range(dy):
        pick_a = [2, 3] + list(range(4 + ky, 4 + 2 * ky)) + [0]
        pick_s = [0, 1] + list(range(4, 4 + ky))
        fya[j, : len(pick_a)] = yone.functionals[j][pick_a]
        fys[j, : len(pick_s)] = yone.functionals[j][pick_s]
        product, even, around = yone.tables(j)
        used = product.shape[0]
        for source, to, across, pick, k in (
            (product, ta[j], wa[j], pick_a[:-1], kya),
            (even, tsm[j][:, :wide], wsm[j][:, :wide], pick_s, kys),
            (around, tsm[j][:, wide:], wsm[j][:, wide:], pick_s, kys),
        ):
            to[:, :used] = source[:, :ly].T
            for place in range(dy - 1):
                begin = ly + yone.functional_count * place
                part = source[:, begin : begin + yone.functional_count].T[pick]
                across[k * place : k * place + len(pick), :used] = part
        if j == dy - 1:
            ta[j, ly - 2, wide - 1] = 0.5
        else:
            wa[j, kya * ((j ^ (j + 1)) - 1) + len(pick_a) - 1, wide - 1] = 0.5

    fx = np.zeros((dx, lx, 8))
    txa = np.zeros((dx, xone.n, lx + 8 * (dx - 1)))
    txm = np.zeros((dx, xone.n, xone.n + 8 * (dx - 1)))
    for j in range(dx):
        fx[j, :, :2] = xone.functionals[j][2:4].T
        product, even, around = xone.tables(j)
        txa[j, :, :lx] = product[:, :lx]
        txm[j, :, : xone.n] = around[:, :lx:2]
        for place in range(dx - 1):
            txa[j, :, lx + 8 * place : lx + 8 * place + 2] = product[:, lx + 4 * place + 2 : lx + 4 * place + 4]
            begin = xone.n + 8 * place
            txm[j, :, begin + 2 : begin + 4] = around[:, lx + 4 * place : lx + 4 * place + 2]

    zn = zone.n
    zs = np.zeros((dz, 2 * lz + 2 + zn * (lz + dz + 1)))
    for j in range(dz):
        cv, cw = zone.v[j], zone.w[j]
        k_last = (zone.last[zone.rows(0)] / zone.reach(0, j))[0] if 0 < j == dz - 1 else 0.0
        k_first = (zone.first[zone.rows(dz - 1)] / zone.reach(dz - 1, j))[-1] if j == 0 and dz > 1 else 0.0
        parts = [cv, cw, [k_last, k_first], zone.block(j, j).reshape(-1)]
        parts += [zone.reach(j, j ^ k) for k in range(1, dz)]
        parts += [zone.first[zone.rows(j)] * (j == 0), zone.last[zone.rows(j)] * (j == dz - 1)]
        zs[j] = np.concatenate([np.asarray(p, np.float64) for p in parts])
    at_local = 2 * lz + 2
    at_reach = at_local + zn * lz
    at_first = at_reach + zn * (dz - 1)
    at_last = at_first + zn

    f2x = np.stack([padded(xtwo.functionals[j], kx, xtwo.fine) for j in range(dx)])
    tx2 = np.zeros((dx, 3 * tall, rowsx))
    qx2 = np.zeros((dx, xtwo.fine, rowsx))
    tx3 = np.zeros((dx, 3 * xthree.n, tall))
    qx3 = np.zeros((dx, xthree.fine, tall))
    px3 = np.zeros((dx, xtwo.fine, tall))
    for j in range(dx):
        for c, table in enumerate(xtwo.tables(j)):
            tx2[j, c * tall : c * tall + table.shape[0], : xtwo.fine] = table[:, : xtwo.fine]
            for place in range(dx - 1):
                begin = xtwo.fine + xtwo.functional_count * place
                target = xtwo.fine + kx * place
                tx2[j, c * tall : c * tall + table.shape[0], target : target + xtwo.functional_count] = table[
                    :, begin : begin + xtwo.functional_count
                ]
        qx2[j] = interpolation(xtwo, j, rowsx, kx, False)
        for c, table in enumerate(xthree.tables(j)):
            tx3[j, c * xthree.n : (c + 1) * xthree.n, : table.shape[1]] = table
        qx3[j] = interpolation(xthree, j, tall, xthree.functional_count, False)
        px3[j] = interpolation(xtwo, j, tall, xtwo.kept, True)

    ty2 = np.zeros((dy, 3 * wide, packed))
    qy2 = np.zeros((dy, wide, round_up(ytwo.fine, 128)))
    ty3 = np.zeros((dy, 3 * packed, 128))
    qy3 = np.zeros((dy, packed, 128))
    py3 = np.zeros((dy, packed, round_up(ytwo.fine, 128)))
    px1 = np.zeros((lx, 2 * tall))
    py1 = np.zeros((dy, packed, ly))
    for j in range(dy):
        for c, table in enumerate(ytwo.tables(j)):
            ty2[j, c * wide : c * wide + table.shape[1], c * wide2 : c * wide2 + wide2] = table.T
        qy2[j, :, : ytwo.fine] = interpolation(ytwo, j, wide, ky, False).T
        for c, table in enumerate(ythree.tables(j)):
            ty3[j, c * packed : c * packed + table.shape[1], : ythree.n] = (-1.0 if c == 2 else 1.0) * table.T
        qy3[j, :, : ythree.fine] = interpolation(ythree, j, packed, ky2, False).T
        py1[j, wide2:] = interpolation(yone, j, packed - wide2, ky, True).T
        py3[j, wide2:, : ytwo.fine] = interpolation(ytwo, j, packed - wide2, ky2, True).T
    for c in range(xone.n):
        begin = c if c < xtwo.n else tall + c - xtwo.n
        px1[2 * c, begin] = 1.0
        px1[2 * c + 1, begin : begin + 2] = 0.5
    az2, first2, last2 = (t.tolist() for t in dense(nz // 2))
    az3, first3, last3 = dense(nz // 4)
    z2, z3 = nz // 2, nz // 4
    lz2, lz3 = lz // 2, lz // 4
    zt = np.concatenate([az3, first3[:, None], last3[:, None]], axis=1)
    zt = zt.reshape(dz, (lz // 8) * (z3 + 2))
    lz4 = lz // 8

    to32 = lambda table: jnp.asarray(table, jnp.float32)

    def stacked(*tables):
        cols = max(t.shape[2] for t in tables)
        starts = np.cumsum([0] + [round_up(t.shape[1], 8) for t in tables])
        out = np.zeros((tables[0].shape[0], starts[-1], cols))
        for t, begin in zip(tables, starts):
            out[:, begin : begin + t.shape[1], : t.shape[2]] = t
        return to32(out), [int(v) for v in starts]

    messages_y, _ = stacked(fya, fys)
    tables_y, _ = stacked(np.concatenate([ta, tsm], axis=2), np.concatenate([wa, np.zeros((dy, wa.shape[1], 2 * wide))], axis=2),
                          np.concatenate([np.zeros((dy, wsm.shape[1], wide)), wsm], axis=2))
    tables_x, _ = stacked(txa, txm)
    tables_x2, _ = stacked(tx2, qx2)
    tables_y2, _ = stacked(ty2, qy2)
    tables_x3, at_x3 = stacked(tx3, qx3, px3)
    tables_y3, at_y3 = stacked(ty3, qy3, py3, py1)
    hz, hx1 = lz // 2, lx // 2

    def y_messages(u_hbm, table_hbm, out_ref, u_ref, table, sems):
        j = lax.axis_index("gy")
        nt = ((1,), (1,))
        copies = [pltpu.make_async_copy(table_hbm.at[j], table, sems.at[lz])]
        copies += [pltpu.make_async_copy(u_hbm.at[z], u_ref.at[z], sems.at[z]) for z in range(lz)]
        for copy in copies:
            copy.start()
        copies[0].wait()
        for z in range(lz):
            copies[z + 1].wait()
            out_ref[:kya, z * lx : (z + 1) * lx] = dot(table[:kya], u_ref[z], nt)
        even = jnp.concatenate([u_ref[2 * z, pl.ds(0, hx1, stride=2), :] for z in range(hz)], axis=0)
        out_ref[:kys, lz * lx :] = dot(table[kya : kya + kys], even, nt)

    def y_apply(*refs):
        u_ref, came = refs[0], refs[1:dy]
        ty_ref, fx_ref, ta_out, tsm_out, iy_out, xm_out = refs[dy:]
        j, jx = lax.axis_index("gy"), lax.axis_index("gx")
        tn = ((0,), (0,))
        ta_all = dot(u_ref[...].reshape(lz * lx, ly), ty_ref[j, :ly, :wide])
        even = jnp.concatenate([u_ref[2 * z, pl.ds(0, hx1, stride=2), :] for z in range(hz)], axis=0)
        tsm_all = dot(even, ty_ref[j, :ly, wide:])
        for k, ref in enumerate(came):
            begin = ly + kya * k
            ta_all += dot(ref[:kya, : lz * lx], ty_ref[j, begin : begin + kya, :wide], tn)
            begin = ly + kya * (dy - 1) + kys * k
            tsm_all += dot(ref[:kys, lz * lx :], ty_ref[j, begin : begin + kys, wide:], tn)
        ta_out[...] = ta_all
        tsm_out[...] = tsm_all
        xm_out[...] = jnp.zeros_like(xm_out)
        lane = iota((lx, ly), 1)
        weights = [jnp.broadcast_to(fx_ref[jx, :, c : c + 1], (lx, wide)) for c in range(2)]
        xm_out[0, 5:6, :wide] = tsm_all[0:1, :wide]
        for z in range(lz):
            part = ta_all[z * lx : (z + 1) * lx]
            for c in range(2):
                xm_out[z, c : c + 1, :wide] = jnp.sum(part * weights[c], axis=0, keepdims=True)
            if z % 2 == 0:
                half = z // 2
                tm = tsm_all[half * hx1 : (half + 1) * hx1, wide:]
                xm_out[z, 2:3, :wide] = tm[0:1]
                xm_out[z, 3:4, :wide] = tm[hx1 - 1 : hx1]
                u = u_ref[z]
                before, after = pltpu.roll(u, 1, 1), pltpu.roll(u, ly - 1, 1)
                middle = 0.5 * (before + after)
                edge = 0.5 * before + jnp.broadcast_to(part[:, wide - 1 : wide], (lx, ly))
                iy = jnp.where(lane == ly - 1, edge, jnp.where(lane % 2 == 1, middle, u))
                iy_out[half] = iy
                xm_out[z, 4:5, :ly] = iy[0:1]

    def x_apply(*refs):
        ta_ref, tsm_ref, iy_ref, own_ref = refs[:4]
        came = refs[4 : 3 + dx]
        tx_ref, ixy_out, zc_out, u1_out = refs[3 + dx : 7 + dx]
        planes_out = refs[7 + dx :]
        jx, jz = lax.axis_index("gx"), lax.axis_index("gz")
        xa, xm, diff = [], [], []
        def from_next(own, rows):
            for k, rest in enumerate(rows):
                own = jnp.where((jx ^ (k + 1)) == jx + 1, rest, own)
            return own

        for z in range(0, lz, 2):
            pair = jnp.concatenate([ta_ref[z * lx : (z + 1) * lx, :], ta_ref[(z + 1) * lx : (z + 2) * lx, :]], axis=1)
            rest = [jnp.concatenate([r[z, :, :wide], r[z + 1, :, :wide]], axis=1) for r in came]
            both = dot(tx_ref[jx, : xone.n], jnp.concatenate([pair] + rest, axis=0))
            xa += [both[:, :wide], both[:, wide:]]
        zc_out[...] = jnp.zeros_like(zc_out)
        zc_out[:hx1] = tsm_ref[:hx1, :wide]
        zc_out[hx1 : hx1 + 1] = from_next(tsm_ref[hx1 - 1 : hx1, :wide], [r[0, 5:6, :wide] for r in came])
        row = iota((lx, ly), 0)
        for half in range(hz):
            part = tsm_ref[half * hx1 : (half + 1) * hx1, :]
            stacked = jnp.concatenate([part[:, wide:]] + [r[2 * half, :, :wide] for r in came], axis=0)
            xm.append(dot(tx_ref[jx, xone.n :, : xone.n + 8 * (dx - 1)], stacked))
            diff.append(part[:, :wide] - xm[-1])
            iy = iy_ref[half]
            halo = from_next(iy[lx - 2 : lx - 1], [r[2 * half, 4:5, :ly] for r in came])
            before, after = pltpu.roll(iy, 1, 0), pltpu.roll(iy, lx - 1, 0)
            after = jnp.where(row == lx - 1, jnp.broadcast_to(halo, (lx, ly)), after)
            ixy = jnp.where(row % 2 == 1, 0.5 * (before + after), iy)
            ixy_out[half] = ixy
        scalar = lambda place: chosen_by(zs[:, place], jz)
        for zc in range(zn):
            total = diff[zc] - scalar(at_first + zc) * xm[0] - scalar(at_last + zc) * xm[hz - 1]
            for z in range(lz):
                total += scalar(at_local + zc * lz + z) * xa[z]
            u1_out[zc] = total
        v = -scalar(2 * lz) * xm[hz - 1]
        w = -scalar(2 * lz + 1) * xm[0]
        for z in range(lz):
            v += scalar(z) * xa[z]
            w += scalar(lz + z) * xa[z]
        for k, out in enumerate(planes_out):
            out[...] = jnp.where((jz ^ (k + 1)) > jz, w, v)

    def z_apply(*refs):
        part_ref, came = refs[0], refs[1:dz]
        f2x_ref, u1_out, xt_out = refs[dz:]
        jx, jz = lax.axis_index("gx"), lax.axis_index("gz")
        for zc in range(zn):
            total = part_ref[zc]
            for k, r in enumerate(came):
                total += chosen_by(zs[:, at_reach + k * zn + zc], jz) * r[...]
            u1_out[zc] = total
            xt_out[:, zc * wide : (zc + 1) * wide] = dot(f2x_ref[jx], total)

    def fine_coefficients(u_ref, ixy_ref, out_ref):
        for half in range(hz):
            here = ixy_ref[half]
            out_ref[2 * half] = u_ref[2 * half] - here
            if half + 1 < hz:
                out_ref[2 * half + 1] = u_ref[2 * half + 1] - 0.5 * (here + ixy_ref[half + 1])

    def second_apply(*refs):
        u1_ref, zc_ref, came = refs[0], refs[1], refs[2 : dx + 1]
        tx2_ref, ty2_ref, zt_out, i2_out = refs[dx + 1 :]
        jx, jy = lax.axis_index("gx"), lax.axis_index("gy")
        own = jnp.concatenate([u1_ref[z] for z in range(lz2)], axis=1)
        state = jnp.concatenate([own] + [r[...] for r in came], axis=0)
        across = dot(tx2_ref[jx], state)
        spread = across[3 * tall :]
        for z in range(lz2):
            cut = across[:, z * wide : (z + 1) * wide]
            if z % 2 == 1:
                moved = dot(cut[:tall], ty2_ref[jy, :wide])
                if z < 4:
                    begin = xtwo.n * (z // 2)
                    moved += pltpu.roll(zc_ref[begin : begin + tall], wide2, 1)
                zt_out[z] = moved
            else:
                joined = jnp.concatenate([cut[c * tall : (c + 1) * tall] for c in range(3)], axis=1)
                zt_out[z] = dot(joined, ty2_ref[jy, : 3 * wide])
                i2_out[z // 2] = dot(spread[:, z * wide : (z + 1) * wide], ty2_ref[jy, 3 * wide :, : round_up(ytwo.fine, 128)])

    def third_apply(*refs):
        u1_ref, i2_ref, u_ref, ixy_ref, _, own_ref = refs[:6]
        came = refs[6 : 5 + dz]
        px1_ref, tx_ref, ty_ref, fine_out, middle_out, coarse_out, coarsest_out = refs[5 + dz : 12 + dz]
        zbuf, ubuf, last, middle, sems = refs[12 + dz :]
        part = lambda ref, j, starts, which: ref[j, starts[which] : starts[which + 1]]
        jx, jy, jz = lax.axis_index("gx"), lax.axis_index("gy"), lax.axis_index("gz")
        zbuf[pl.ds(jz * lz2, lz2)] = own_ref[...]
        for k, r in enumerate(came):
            zbuf[pl.ds((jz ^ (k + 1)) * lz2, lz2)] = r[...]
        at = jnp.minimum(jz + 1, dz - 1) * lz2
        first = jnp.concatenate([zbuf[at + 1], zbuf[at + 3]], axis=0)
        halo = dot(dot(px1_ref[...], first), part(ty_ref, jy, at_y3, 3))
        here = ixy_ref[hz - 1]
        last[...] = u_ref[lz - 1] - 0.5 * (here + jnp.where(jz == dz - 1, here, halo))
        copies = [pltpu.make_async_copy(last, fine_out.at[lz - 1], sems.at[0])]
        copies[0].start()
        fy = ytwo.fine
        at = jnp.minimum((jz + 1) * lz2, z2 - 2)
        halo = dot(dot(part(tx_ref, jx, at_x3, 2), zbuf[at]), part(ty_ref, jy, at_y3, 2))[:, :fy]
        for half in range(lz2 // 2):
            here = i2_ref[half][:, :fy]
            after = i2_ref[half + 1][:, :fy] if half + 1 < lz2 // 2 else halo
            middle[2 * half] = u1_ref[2 * half][:, :fy] - here
            middle[2 * half + 1] = u1_ref[2 * half + 1][:, :fy] - 0.5 * (here + after)
        copies.append(pltpu.make_async_copy(middle, middle_out, sems.at[1]))
        copies[1].start()
        everything = [zbuf[z] for z in range(z2)]
        evens = [pltpu.roll(everything[z], packed - wide2, 1) for z in range(0, z2, 2)]
        arounds = [pltpu.roll(everything[z], packed - 2 * wide2, 1) for z in range(0, z2, 2)]
        for zc in range(z3):
            total = evens[zc] - arounds[zc] - first2[zc] * arounds[0] - last2[zc] * arounds[-1]
            for z in range(z2):
                total += az2[zc][z] * everything[z]
            ubuf[zc] = total
        fy3 = ythree.fine
        spread = []
        for half in range(lz3 // 2 + 1):
            at = jnp.minimum(jz * lz3 + 2 * half, z3 - 2)
            spread.append(dot(dot(part(tx_ref, jx, at_x3, 1), ubuf[at]), part(ty_ref, jy, at_y3, 1))[:, :fy3])
        for half in range(lz3 // 2):
            at = jz * lz3 + 2 * half
            coarse_out[2 * half] = ubuf[at][: xthree.fine, :fy3] - spread[half]
            coarse_out[2 * half + 1] = ubuf[at + 1][: xthree.fine, :fy3] - 0.5 * (spread[half] + spread[half + 1])
        n3 = xthree.n
        for zc in range(lz4):
            base = zc * (z3 + 2)
            along = chosen_by(zt[:, base], jz) * ubuf[0]
            for z in range(1, z3):
                along += chosen_by(zt[:, base + z], jz) * ubuf[z]
            even = ubuf[2 * (jz * lz4 + zc)]
            around = even + chosen_by(zt[:, base + z3], jz) * ubuf[0] + chosen_by(zt[:, base + z3 + 1], jz) * ubuf[z3 - 2]
            joined = jnp.concatenate(
                [
                    dot(tx_ref[jx, c * n3 : (c + 1) * n3, :], plane)
                    for c, plane in enumerate((along, even, around))
                ],
                axis=1,
            )
            coarsest_out[zc] = dot(joined, part(ty_ref, jy, at_y3, 0))[:, : ythree.n]
        for copy in copies:
            copy.wait()

    ym, u = kernel_call(
        y_messages,
        [(max(kya, kys), lz * lx + hz * hx1), (lz, lx, ly)],
        [field, messages_y],
        scratch=[pltpu.VMEM((kya + kys, ly), jnp.float32), pltpu.SemaphoreType.DMA((lz + 1,))],
        left=(0, 1),
    )
    ycame = swapped(ym, "gy")
    xw = max(wide, ly)
    ta_v, tsm_v, iy, xm = kernel_call(
        y_apply,
        [(lz * lx, wide), (hz * hx1, 2 * wide), (hz, lx, ly), (lz, 8, xw)],
        [u, *ycame, tables_y, to32(fx)],
    )
    xcame = swapped(xm, "gx")
    ixy, zc, u1_part, *planes = kernel_call(
        x_apply,
        [(hz, lx, ly), (xtwo.n + tall, wide), (zn, xone.n, wide)] + [(xone.n, wide)] * (dz - 1),
        [ta_v, tsm_v, iy, xm, *xcame, tables_x],
    )
    zcame = [
        lax.ppermute(plane, "gz", [(i, i ^ (k + 1)) for i in range(dz)]) for k, plane in enumerate(planes)
    ]
    u1, xt = kernel_call(z_apply, [(zn, xone.n, wide), (kx, zn * wide)], [u1_part, *zcame, to32(f2x)])
    xtcame = swapped(xt, "gx")
    zmsg, i2 = kernel_call(
        second_apply,
        [(lz2, tall, packed), (lz2 // 2, xtwo.fine, round_up(ytwo.fine, 128))],
        [u1, zc, *xtcame, tables_x2, tables_y2],
    )
    ztcame = gathered(zmsg, "gz")
    (fine,) = kernel_call(fine_coefficients, [(lz, lx, ly)], [u, ixy])
    return kernel_call(
        third_apply,
        [(lz, lx, ly), (lz2, xtwo.fine, ytwo.fine), (lz3, xthree.fine, ythree.fine), (lz4, xthree.n, ythree.n)],
        [u1, i2, u, ixy, fine, zmsg, *ztcame, to32(px1), tables_x3, tables_y3],
        scratch=[
            pltpu.VMEM((z2, tall, packed), jnp.float32),
            pltpu.VMEM((z3, tall, packed), jnp.float32),
            pltpu.VMEM((lx, ly), jnp.float32),
            pltpu.VMEM((lz2, xtwo.fine, ytwo.fine), jnp.float32),
            pltpu.SemaphoreType.DMA((2,)),
        ],
        left=(4,),
        left_out=(0, 1),
        aliases={4: 0},
    )


def solution(mesh):
    spec = P("gz", "gx", "gy")
    counts = tuple(mesh.shape[a] for a in ("gz", "gx", "gy"))
    return jax.shard_map(
        functools.partial(shards, counts), mesh=mesh, in_specs=(spec,), out_specs=(spec,) * 4, check_vma=False
    )
```

```python
import functools
import math

import jax
import jax.numpy as jnp
import numpy as np
from jax import lax
from jax.experimental import pallas as pl
from jax.experimental.pallas import tpu as pltpu
from jax.sharding import PartitionSpec as P

band_ratio = 2.0 - math.sqrt(3.0)
f32 = np.float32


def round_up(value, unit):
    return -(-value // unit) * unit


def dense(fine):
    n = fine // 2
    steps = np.arange(n)[:, None] - np.arange(n)[None, :]
    lower = np.where(steps >= 0, (-band_ratio) ** np.maximum(steps, 0), 0.0)
    inverse = lower.T @ lower
    mass = 4.0 * np.eye(fine) + np.eye(fine, k=1) + np.eye(fine, k=-1)
    weights = np.where(np.arange(n) == n - 1, 1.0, 0.5)[:, None]
    earlier = np.concatenate([np.zeros((1, fine)), mass[1::2][:-1]])
    product = inverse @ (0.5 * band_ratio * (mass[0::2] + weights * mass[1::2] + 0.5 * earlier))
    return product, inverse[:, 0] * (3 * band_ratio - 1), inverse[:, -1] * (2 * band_ratio)


class Level:
    def __init__(self, whole, count, following):
        self.count, self.fine = count, whole // count
        self.n = self.fine // 2
        self.product, self.first, self.last = dense(whole)
        self.following = following
        self.kept = following.functional_count if following else 0
        self.functional_count = 4 + 2 * self.kept
        self.even = np.zeros((self.n, self.fine))
        self.even[np.arange(self.n), 2 * np.arange(self.n)] = 1.0
        self.v = [self.towards(i, i * self.n - 1) for i in range(count)]
        self.w = [self.towards(i, (i + 1) * self.n) for i in range(count)]
        self.functionals = []
        for i in range(count):
            own = np.zeros((4, self.fine))
            own[0, 0] = own[1, self.fine - 2] = 1.0
            own[2], own[3] = self.v[i], self.w[i]
            if following:
                inner = following.functionals[i]
                own = np.concatenate([own, inner @ self.even, inner @ self.block(i, i)])
            self.functionals.append(own)

    def rows(self, i):
        return slice(i * self.n, (i + 1) * self.n)

    def block(self, i, j):
        return self.product[self.rows(i), j * self.fine : (j + 1) * self.fine]

    def towards(self, i, row):
        if not 0 <= row < self.count * self.n:
            return np.zeros(self.fine)
        values = self.product[row, i * self.fine : (i + 1) * self.fine]
        return values / np.abs(values).max()

    def reach(self, i, j):
        side = self.v[j] if j > i else self.w[j]
        best = np.argmax(np.abs(side))
        return self.block(i, j)[:, best] / side[best]

    def side(self, i, j):
        return 2 if j > i else 3

    def tables(self, j):
        own, kept, many, n, fine = self.n, self.kept, self.functional_count, self.n, self.fine
        others = [j ^ k for k in range(1, self.count)]
        shape = (own + kept * len(others), fine + many * len(others))
        product, even = np.zeros(shape), np.zeros(shape)
        at = {i: fine + many * place for place, i in enumerate(others)}
        product[:n, :fine] = self.block(j, j)
        even[:n, :fine] = self.even
        first, last = [self.first[self.rows(j)]], [self.last[self.rows(j)]]
        for i in others:
            product[:n, at[i] + self.side(j, i)] = self.reach(j, i)
        for place, i in enumerate(others):
            if not kept:
                break
            inner = self.following.functionals[i]
            target = n + kept * place + np.arange(kept)
            product[target, :fine] = inner @ self.block(i, j)
            product[target, at[i] + 4 + kept + np.arange(kept)] = 1.0
            even[target, at[i] + 4 + np.arange(kept)] = 1.0
            for other in others:
                if other != i:
                    product[target, at[other] + self.side(i, other)] = inner @ self.reach(i, other)
            first.append(inner @ self.first[self.rows(i)])
            last.append(inner @ self.last[self.rows(i)])
        around = even.copy()
        around[:, 0 if j == 0 else at[0]] += np.concatenate(first)
        end = self.count - 1
        around[:, fine - 2 if j == end else at[end] + 1] += np.concatenate(last)
        return product, even, around

    def next_first(self, j, stride):
        if j == self.count - 1:
            return self.fine - 2
        return self.fine + stride * ((j ^ (j + 1)) - 1)


def interpolation(level, j, inputs, stride, coarse):
    table = np.zeros((level.fine, inputs))
    if coarse:
        places = list(range(level.n))
        last = level.n - 1 if j == level.count - 1 else level.n + stride * ((j ^ (j + 1)) - 1)
    else:
        places = [2 * c for c in range(level.n)]
        last = level.next_first(j, stride)
    places.append(last)
    for c in range(level.n):
        table[2 * c, places[c]] = 1.0
        table[2 * c + 1, places[c]] += 0.5
        table[2 * c + 1, places[c + 1]] += 0.5
    return table


def chain(whole, count, levels):
    made = None
    for depth in reversed(range(levels)):
        made = Level(whole >> depth, count, made)
    return made


def padded(table, rows, cols):
    out = np.zeros((rows, cols))
    out[: table.shape[0], : table.shape[1]] = table
    return out


highest = lax.Precision.HIGHEST


def dot(a, b, dims=((1,), (0,))):
    return lax.dot_general(a, b, (dims, ((), ())), precision=highest, preferred_element_type=jnp.float32)


def kernel_call(body, outs, arrays, scratch=(), left=(), left_out=(), aliases={}):
    space = lambda place, where: pl.BlockSpec(memory_space=pltpu.HBM if place in where else pltpu.VMEM)
    return pl.pallas_call(
        body,
        out_shape=[jax.ShapeDtypeStruct(shape, jnp.float32) for shape in outs],
        in_specs=[space(i, left) for i in range(len(arrays))],
        out_specs=[space(i, left_out) for i in range(len(outs))],
        scratch_shapes=list(scratch),
        input_output_aliases=aliases,
        compiler_params=pltpu.CompilerParams(vmem_limit_bytes=40 << 20),
    )(*(pltpu.with_memory_space_constraint(a, pltpu.HBM) if i in left else a for i, a in enumerate(arrays)))


def swapped(value, axis):
    count = lax.axis_size(axis)
    return [lax.ppermute(value, axis, [(i, i ^ k) for i in range(count)]) for k in range(1, count)]


def gathered(value, axis, beside):
    count = lax.axis_size(axis)
    if count != 4:
        return swapped(value, axis), beside
    by = lambda k, what: lax.ppermute(what, axis, [(i, i ^ k) for i in range(count)])
    far, beside = lax.optimization_barrier((by(2, value), beside))
    return [by(1, value), far, by(1, far)], beside


def chosen_by(values, j):
    chosen = float(values[0])
    for place in range(1, len(values)):
        if any(values[place] != values[0] for place in range(len(values))):
            chosen = jnp.where(j == place, f32(values[place]), chosen)
    return chosen


def iota(shape, dim):
    return lax.broadcasted_iota(jnp.int32, shape, dim)


def shards(counts, field):
    dz, dx, dy = counts
    lz, lx, ly = field.shape
    nz, nx, ny = lz * dz, lx * dx, ly * dy

    yone = chain(ny, dy, 3)
    ytwo, ythree = yone.following, yone.following.following
    xone = chain(nx, dx, 1)
    xtwo = chain(nx // 2, dx, 2)
    xthree = xtwo.following
    zone = Level(nz, dz, None)

    ky, ky2, ky3 = yone.kept, ytwo.kept, ythree.kept
    kya = round_up(ky + 3, 16)
    kys = round_up(ky + 2, 16)
    wide1 = yone.n + ky * (dy - 1)
    wide2 = ytwo.n + ky2 * (dy - 1)
    wide = packed = round_up(max(wide1 + 1, 3 * wide2, wide2 + wide1), 128)
    kx = round_up(xtwo.functional_count, 8)
    rowsx = xtwo.fine + kx * (dx - 1)
    tall = round_up(xtwo.n + xtwo.kept * (dx - 1), 8)

    fya = np.zeros((dy, kya, ly))
    fys = np.zeros((dy, kys, ly))
    ta = np.zeros((dy, ly, wide))
    wa = np.zeros((dy, max(dy - 1, 1) * kya, wide))
    tsm = np.zeros((dy, ly, 2 * wide))
    wsm = np.zeros((dy, max(dy - 1, 1) * kys, 2 * wide))
    for j in range(dy):
        pick_a = [2, 3] + list(range(4 + ky, 4 + 2 * ky)) + [0]
        pick_s = [0, 1] + list(range(4, 4 + ky))
        fya[j, : len(pick_a)] = yone.functionals[j][pick_a]
        fys[j, : len(pick_s)] = yone.functionals[j][pick_s]
        product, even, around = yone.tables(j)
        used = product.shape[0]
        for source, to, across, pick, k in (
            (product, ta[j], wa[j], pick_a[:-1], kya),
            (even, tsm[j][:, :wide], wsm[j][:, :wide], pick_s, kys),
            (around, tsm[j][:, wide:], wsm[j][:, wide:], pick_s, kys),
        ):
            to[:, :used] = source[:, :ly].T
            for place in range(dy - 1):
                begin = ly + yone.functional_count * place
                part = source[:, begin : begin + yone.functional_count].T[pick]
                across[k * place : k * place + len(pick), :used] = part
        if j == dy - 1:
            ta[j, ly - 2, wide - 1] = 0.5
        else:
            wa[j, kya * ((j ^ (j + 1)) - 1) + len(pick_a) - 1, wide - 1] = 0.5

    fx = np.zeros((dx, lx, 8))
    txa = np.zeros((dx, xone.n, lx + 8 * (dx - 1)))
    txm = np.zeros((dx, xone.n, xone.n + 8 * (dx - 1)))
    for j in range(dx):
        fx[j, :, :2] = xone.functionals[j][2:4].T
        product, even, around = xone.tables(j)
        txa[j, :, :lx] = product[:, :lx]
        txm[j, :, : xone.n] = around[:, :lx:2]
        for place in range(dx - 1):
            txa[j, :, lx + 8 * place : lx + 8 * place + 2] = product[:, lx + 4 * place + 2 : lx + 4 * place + 4]
            begin = xone.n + 8 * place
            txm[j, :, begin + 2 : begin + 4] = around[:, lx + 4 * place : lx + 4 * place + 2]

    zn = zone.n
    zs = np.zeros((dz, 2 * lz + 2 + zn * (lz + dz + 1)))
    for j in range(dz):
        cv, cw = zone.v[j], zone.w[j]
        k_last = (zone.last[zone.rows(0)] / zone.reach(0, j))[0] if 0 < j == dz - 1 else 0.0
        k_first = (zone.first[zone.rows(dz - 1)] / zone.reach(dz - 1, j))[-1] if j == 0 and dz > 1 else 0.0
        parts = [cv, cw, [k_last, k_first], zone.block(j, j).reshape(-1)]
        parts += [zone.reach(j, j ^ k) for k in range(1, dz)]
        parts += [zone.first[zone.rows(j)] * (j == 0), zone.last[zone.rows(j)] * (j == dz - 1)]
        zs[j] = np.concatenate([np.asarray(p, np.float64) for p in parts])
    at_local = 2 * lz + 2
    at_reach = at_local + zn * lz
    at_first = at_reach + zn * (dz - 1)
    at_last = at_first + zn

    f2x = np.stack([padded(xtwo.functionals[j], kx, xtwo.fine) for j in range(dx)])
    tx2 = np.zeros((dx, 3 * tall, rowsx))
    qx2 = np.zeros((dx, xtwo.fine, rowsx))
    tx3 = np.zeros((dx, 3 * xthree.n, tall))
    qx3 = np.zeros((dx, xthree.fine, tall))
    px3 = np.zeros((dx, xtwo.fine, tall))
    for j in range(dx):
        for c, table in enumerate(xtwo.tables(j)):
            tx2[j, c * tall : c * tall + table.shape[0], : xtwo.fine] = table[:, : xtwo.fine]
            for place in range(dx - 1):
                begin = xtwo.fine + xtwo.functional_count * place
                target = xtwo.fine + kx * place
                tx2[j, c * tall : c * tall + table.shape[0], target : target + xtwo.functional_count] = table[
                    :, begin : begin + xtwo.functional_count
                ]
        qx2[j] = interpolation(xtwo, j, rowsx, kx, False)
        for c, table in enumerate(xthree.tables(j)):
            tx3[j, c * xthree.n : (c + 1) * xthree.n, : table.shape[1]] = table
        qx3[j] = interpolation(xthree, j, tall, xthree.functional_count, False)
        px3[j] = interpolation(xtwo, j, tall, xtwo.kept, True)

    ty2 = np.zeros((dy, 3 * wide, packed))
    qy2 = np.zeros((dy, wide, round_up(ytwo.fine, 128)))
    ty3 = np.zeros((dy, 3 * packed, 128))
    qy3 = np.zeros((dy, packed, 128))
    py3 = np.zeros((dy, packed, round_up(ytwo.fine, 128)))
    px1 = np.zeros((lx, 2 * tall))
    py1 = np.zeros((dy, packed, ly))
    for j in range(dy):
        for c, table in enumerate(ytwo.tables(j)):
            ty2[j, c * wide : c * wide + table.shape[1], c * wide2 : c * wide2 + wide2] = table.T
        qy2[j, :, : ytwo.fine] = interpolation(ytwo, j, wide, ky, False).T
        for c, table in enumerate(ythree.tables(j)):
            ty3[j, c * packed : c * packed + table.shape[1], : ythree.n] = (-1.0 if c == 2 else 1.0) * table.T
        qy3[j, :, : ythree.fine] = interpolation(ythree, j, packed, ky2, False).T
        py1[j, wide2:] = interpolation(yone, j, packed - wide2, ky, True).T
        py3[j, wide2:, : ytwo.fine] = interpolation(ytwo, j, packed - wide2, ky2, True).T
    for c in range(xone.n):
        begin = c if c < xtwo.n else tall + c - xtwo.n
        px1[2 * c, begin] = 1.0
        px1[2 * c + 1, begin : begin + 2] = 0.5
    az2, first2, last2 = (t.tolist() for t in dense(nz // 2))
    az3, first3, last3 = dense(nz // 4)
    z2, z3 = nz // 2, nz // 4
    lz2, lz3 = lz // 2, lz // 4
    zt = np.concatenate([az3, first3[:, None], last3[:, None]], axis=1)
    zt = zt.reshape(dz, (lz // 8) * (z3 + 2))
    lz4 = lz // 8

    to32 = lambda table: jnp.asarray(table, jnp.float32)

    def stacked(*tables):
        cols = max(t.shape[2] for t in tables)
        starts = np.cumsum([0] + [round_up(t.shape[1], 8) for t in tables])
        out = np.zeros((tables[0].shape[0], starts[-1], cols))
        for t, begin in zip(tables, starts):
            out[:, begin : begin + t.shape[1], : t.shape[2]] = t
        return to32(out), [int(v) for v in starts]

    messages_y, _ = stacked(fya, fys)
    tables_y, _ = stacked(np.concatenate([ta, tsm], axis=2), np.concatenate([wa, np.zeros((dy, wa.shape[1], 2 * wide))], axis=2),
                          np.concatenate([np.zeros((dy, wsm.shape[1], wide)), wsm], axis=2))
    tables_x, _ = stacked(txa, txm)
    tables_x2, _ = stacked(tx2, qx2)
    tables_y2, _ = stacked(ty2, qy2)
    tables_x3, at_x3 = stacked(tx3, qx3, px3)
    tables_y3, at_y3 = stacked(ty3, qy3, py3, py1)
    hz, hx1 = lz // 2, lx // 2

    def y_messages(u_hbm, table_hbm, ty_hbm, fx_hbm, out_ref, u_ref, ty_ref, fx_ref, table, sems):
        j = lax.axis_index("gy")
        nt = ((1,), (1,))
        copies = [pltpu.make_async_copy(table_hbm.at[j], table, sems.at[0])]
        copies.append(pltpu.make_async_copy(u_hbm, u_ref, sems.at[1]))
        copies.append(pltpu.make_async_copy(ty_hbm.at[j], ty_ref, sems.at[2]))
        copies.append(pltpu.make_async_copy(fx_hbm.at[lax.axis_index("gx")], fx_ref, sems.at[3]))
        for copy in copies:
            copy.start()
        for copy in copies[:2]:
            copy.wait()
        out_ref[:kya, : lz * lx] = dot(table[:kya], u_ref[...].reshape(lz * lx, ly), nt)
        even = jnp.concatenate([u_ref[2 * z, pl.ds(0, hx1, stride=2), :] for z in range(hz)], axis=0)
        out_ref[:kys, lz * lx :] = dot(table[kya : kya + kys], even, nt)
        for copy in copies[2:]:
            copy.wait()

    def y_apply(*refs):
        u_ref, came = refs[0], refs[1:dy]
        ty_ref, fx_ref, ta_out, tsm_out, iy_out, xm_out = refs[dy:]
        tn = ((0,), (0,))
        ta_all = dot(u_ref[...].reshape(lz * lx, ly), ty_ref[:ly, :wide])
        even = jnp.concatenate([u_ref[2 * z, pl.ds(0, hx1, stride=2), :] for z in range(hz)], axis=0)
        tsm_all = dot(even, ty_ref[:ly, wide:])
        for k, ref in enumerate(came):
            begin = ly + kya * k
            ta_all += dot(ref[:kya, : lz * lx], ty_ref[begin : begin + kya, :wide], tn)
            begin = ly + kya * (dy - 1) + kys * k
            tsm_all += dot(ref[:kys, lz * lx :], ty_ref[begin : begin + kys, wide:], tn)
        ta_out[...] = ta_all
        tsm_out[...] = tsm_all
        xm_out[...] = jnp.zeros_like(xm_out)
        lane = iota((lx, ly), 1)
        weights = [jnp.broadcast_to(fx_ref[:, c : c + 1], (lx, wide)) for c in range(2)]
        xm_out[0, 5:6, :wide] = tsm_all[0:1, :wide]
        for z in range(lz):
            part = ta_all[z * lx : (z + 1) * lx]
            for c in range(2):
                xm_out[z, c : c + 1, :wide] = jnp.sum(part * weights[c], axis=0, keepdims=True)
            if z % 2 == 0:
                half = z // 2
                tm = tsm_all[half * hx1 : (half + 1) * hx1, wide:]
                xm_out[z, 2:3, :wide] = tm[0:1]
                xm_out[z, 3:4, :wide] = tm[hx1 - 1 : hx1]
                u = u_ref[z]
                before, after = pltpu.roll(u, 1, 1), pltpu.roll(u, ly - 1, 1)
                middle = 0.5 * (before + after)
                edge = 0.5 * before + jnp.broadcast_to(part[:, wide - 1 : wide], (lx, ly))
                iy = jnp.where(lane == ly - 1, edge, jnp.where(lane % 2 == 1, middle, u))
                iy_out[half] = iy
                xm_out[z, 4:5, :ly] = iy[0:1]

    def x_apply(*refs):
        ta_ref, tsm_ref, iy_ref, own_ref = refs[:4]
        came = refs[4 : 3 + dx]
        tx_ref, ixy_out, zc_out, u1_out = refs[3 + dx : 7 + dx]
        planes_out = refs[7 + dx :]
        jx, jz = lax.axis_index("gx"), lax.axis_index("gz")
        xa, xm, diff = [], [], []
        def from_next(own, rows):
            for k, rest in enumerate(rows):
                own = jnp.where((jx ^ (k + 1)) == jx + 1, rest, own)
            return own

        for z in range(0, lz, 2):
            pair = jnp.concatenate([ta_ref[z * lx : (z + 1) * lx, :], ta_ref[(z + 1) * lx : (z + 2) * lx, :]], axis=1)
            rest = [jnp.concatenate([r[z, :, :wide], r[z + 1, :, :wide]], axis=1) for r in came]
            both = dot(tx_ref[jx, : xone.n], jnp.concatenate([pair] + rest, axis=0))
            xa += [both[:, :wide], both[:, wide:]]
        zc_out[...] = jnp.zeros_like(zc_out)
        zc_out[:hx1] = tsm_ref[:hx1, :wide]
        zc_out[hx1 : hx1 + 1] = from_next(tsm_ref[hx1 - 1 : hx1, :wide], [r[0, 5:6, :wide] for r in came])
        row = iota((lx, ly), 0)
        for half in range(hz):
            part = tsm_ref[half * hx1 : (half + 1) * hx1, :]
            stacked = jnp.concatenate([part[:, wide:]] + [r[2 * half, :, :wide] for r in came], axis=0)
            xm.append(dot(tx_ref[jx, xone.n :, : xone.n + 8 * (dx - 1)], stacked))
            diff.append(part[:, :wide] - xm[-1])
            iy = iy_ref[half]
            halo = from_next(iy[lx - 2 : lx - 1], [r[2 * half, 4:5, :ly] for r in came])
            before, after = pltpu.roll(iy, 1, 0), pltpu.roll(iy, lx - 1, 0)
            after = jnp.where(row == lx - 1, jnp.broadcast_to(halo, (lx, ly)), after)
            ixy = jnp.where(row % 2 == 1, 0.5 * (before + after), iy)
            ixy_out[half] = ixy
        scalar = lambda place: chosen_by(zs[:, place], jz)
        for zc in range(zn):
            total = diff[zc] - scalar(at_first + zc) * xm[0] - scalar(at_last + zc) * xm[hz - 1]
            for z in range(lz):
                total += scalar(at_local + zc * lz + z) * xa[z]
            u1_out[zc] = total
        v = -scalar(2 * lz) * xm[hz - 1]
        w = -scalar(2 * lz + 1) * xm[0]
        for z in range(lz):
            v += scalar(z) * xa[z]
            w += scalar(lz + z) * xa[z]
        for k, out in enumerate(planes_out):
            out[...] = jnp.where((jz ^ (k + 1)) > jz, w, v)

    def z_apply(*refs):
        part_ref, came = refs[0], refs[1:dz]
        f2x_ref, u1_out, xt_out = refs[dz:]
        jx, jz = lax.axis_index("gx"), lax.axis_index("gz")
        for zc in range(zn):
            total = part_ref[zc]
            for k, r in enumerate(came):
                total += chosen_by(zs[:, at_reach + k * zn + zc], jz) * r[...]
            u1_out[zc] = total
            xt_out[:, zc * wide : (zc + 1) * wide] = dot(f2x_ref[jx], total)

    def fine_coefficients(u_ref, ixy_ref, out_ref):
        for half in range(hz):
            here = ixy_ref[half]
            out_ref[2 * half] = u_ref[2 * half] - here
            if half + 1 < hz:
                out_ref[2 * half + 1] = u_ref[2 * half + 1] - 0.5 * (here + ixy_ref[half + 1])

    def second_apply(*refs):
        u1_ref, zc_ref, came = refs[0], refs[1], refs[2 : dx + 1]
        tx2_ref, ty2_ref, zt_out, i2_out = refs[dx + 1 :]
        jx, jy = lax.axis_index("gx"), lax.axis_index("gy")
        own = jnp.concatenate([u1_ref[z] for z in range(lz2)], axis=1)
        state = jnp.concatenate([own] + [r[...] for r in came], axis=0)
        across = dot(tx2_ref[jx], state)
        spread = across[3 * tall :]
        for z in range(lz2):
            cut = across[:, z * wide : (z + 1) * wide]
            if z % 2 == 1:
                moved = dot(cut[:tall], ty2_ref[jy, :wide])
                if z < 4:
                    begin = xtwo.n * (z // 2)
                    moved += pltpu.roll(zc_ref[begin : begin + tall], wide2, 1)
                zt_out[z] = moved
            else:
                joined = jnp.concatenate([cut[c * tall : (c + 1) * tall] for c in range(3)], axis=1)
                zt_out[z] = dot(joined, ty2_ref[jy, : 3 * wide])
                i2_out[z // 2] = dot(spread[:, z * wide : (z + 1) * wide], ty2_ref[jy, 3 * wide :, : round_up(ytwo.fine, 128)])

    def third_apply(*refs):
        u1_ref, i2_ref, u_ref, ixy_ref, _, own_ref = refs[:6]
        came = refs[6 : 5 + dz]
        px1_ref, tx_ref, ty_ref, fine_out, middle_out, coarse_out, coarsest_out = refs[5 + dz : 12 + dz]
        zbuf, ubuf, last, middle, sems = refs[12 + dz :]
        part = lambda ref, j, starts, which: ref[j, starts[which] : starts[which + 1]]
        jx, jy, jz = lax.axis_index("gx"), lax.axis_index("gy"), lax.axis_index("gz")
        zbuf[pl.ds(jz * lz2, lz2)] = own_ref[...]
        for k, r in enumerate(came):
            zbuf[pl.ds((jz ^ (k + 1)) * lz2, lz2)] = r[...]
        at = jnp.minimum(jz + 1, dz - 1) * lz2
        first = jnp.concatenate([zbuf[at + 1], zbuf[at + 3]], axis=0)
        halo = dot(dot(px1_ref[...], first), part(ty_ref, jy, at_y3, 3))
        here = ixy_ref[hz - 1]
        last[...] = u_ref[lz - 1] - 0.5 * (here + jnp.where(jz == dz - 1, here, halo))
        copies = [pltpu.make_async_copy(last, fine_out.at[lz - 1], sems.at[0])]
        copies[0].start()
        fy = ytwo.fine
        at = jnp.minimum((jz + 1) * lz2, z2 - 2)
        halo = dot(dot(part(tx_ref, jx, at_x3, 2), zbuf[at]), part(ty_ref, jy, at_y3, 2))[:, :fy]
        for half in range(lz2 // 2):
            here = i2_ref[half][:, :fy]
            after = i2_ref[half + 1][:, :fy] if half + 1 < lz2 // 2 else halo
            middle[2 * half] = u1_ref[2 * half][:, :fy] - here
            middle[2 * half + 1] = u1_ref[2 * half + 1][:, :fy] - 0.5 * (here + after)
        copies.append(pltpu.make_async_copy(middle, middle_out, sems.at[1]))
        copies[1].start()
        everything = [zbuf[z] for z in range(z2)]
        evens = [pltpu.roll(everything[z], packed - wide2, 1) for z in range(0, z2, 2)]
        arounds = [pltpu.roll(everything[z], packed - 2 * wide2, 1) for z in range(0, z2, 2)]
        for zc in range(z3):
            total = evens[zc] - arounds[zc] - first2[zc] * arounds[0] - last2[zc] * arounds[-1]
            for z in range(z2):
                total += az2[zc][z] * everything[z]
            ubuf[zc] = total
        fy3 = ythree.fine
        spread = []
        for half in range(lz3 // 2 + 1):
            at = jnp.minimum(jz * lz3 + 2 * half, z3 - 2)
            spread.append(dot(dot(part(tx_ref, jx, at_x3, 1), ubuf[at]), part(ty_ref, jy, at_y3, 1))[:, :fy3])
        for half in range(lz3 // 2):
            at = jz * lz3 + 2 * half
            coarse_out[2 * half] = ubuf[at][: xthree.fine, :fy3] - spread[half]
            coarse_out[2 * half + 1] = ubuf[at + 1][: xthree.fine, :fy3] - 0.5 * (spread[half] + spread[half + 1])
        n3 = xthree.n
        for zc in range(lz4):
            base = zc * (z3 + 2)
            along = chosen_by(zt[:, base], jz) * ubuf[0]
            for z in range(1, z3):
                along += chosen_by(zt[:, base + z], jz) * ubuf[z]
            even = ubuf[2 * (jz * lz4 + zc)]
            around = even + chosen_by(zt[:, base + z3], jz) * ubuf[0] + chosen_by(zt[:, base + z3 + 1], jz) * ubuf[z3 - 2]
            joined = jnp.concatenate(
                [
                    dot(tx_ref[jx, c * n3 : (c + 1) * n3, :], plane)
                    for c, plane in enumerate((along, even, around))
                ],
                axis=1,
            )
            coarsest_out[zc] = dot(joined, part(ty_ref, jy, at_y3, 0))[:, : ythree.n]
        for copy in copies:
            copy.wait()

    ym, u, own_ty, own_fx = kernel_call(
        y_messages,
        [(max(kya, kys), lz * lx + hz * hx1), (lz, lx, ly), tables_y.shape[1:], fx.shape[1:]],
        [field, messages_y, tables_y, to32(fx)],
        scratch=[pltpu.VMEM((kya + kys, ly), jnp.float32), pltpu.SemaphoreType.DMA((4,))],
        left=(0, 1, 2, 3),
    )
    ycame = swapped(ym, "gy")
    xw = max(wide, ly)
    ta_v, tsm_v, iy, xm = kernel_call(
        y_apply,
        [(lz * lx, wide), (hz * hx1, 2 * wide), (hz, lx, ly), (lz, 8, xw)],
        [u, *ycame, own_ty, own_fx],
    )
    xcame = swapped(xm, "gx")
    ixy, zc, u1_part, *planes = kernel_call(
        x_apply,
        [(hz, lx, ly), (xtwo.n + tall, wide), (zn, xone.n, wide)] + [(xone.n, wide)] * (dz - 1),
        [ta_v, tsm_v, iy, xm, *xcame, tables_x],
    )
    zcame = [
        lax.ppermute(plane, "gz", [(i, i ^ (k + 1)) for i in range(dz)]) for k, plane in enumerate(planes)
    ]
    u1, xt = kernel_call(z_apply, [(zn, xone.n, wide), (kx, zn * wide)], [u1_part, *zcame, to32(f2x)])
    xtcame = swapped(xt, "gx")
    zmsg, i2 = kernel_call(
        second_apply,
        [(lz2, tall, packed), (lz2 // 2, xtwo.fine, round_up(ytwo.fine, 128))],
        [u1, zc, *xtcame, tables_x2, tables_y2],
    )
    (fine,) = kernel_call(fine_coefficients, [(lz, lx, ly)], [u, ixy])
    ztcame, fine = gathered(zmsg, "gz", fine)
    return kernel_call(
        third_apply,
        [(lz, lx, ly), (lz2, xtwo.fine, ytwo.fine), (lz3, xthree.fine, ythree.fine), (lz4, xthree.n, ythree.n)],
        [u1, i2, u, ixy, fine, zmsg, *ztcame, to32(px1), tables_x3, tables_y3],
        scratch=[
            pltpu.VMEM((z2, tall, packed), jnp.float32),
            pltpu.VMEM((z3, tall, packed), jnp.float32),
            pltpu.VMEM((lx, ly), jnp.float32),
            pltpu.VMEM((lz2, xtwo.fine, ytwo.fine), jnp.float32),
            pltpu.SemaphoreType.DMA((2,)),
        ],
        left=(4,),
        left_out=(0, 1),
        aliases={4: 0},
    )


def solution(mesh):
    spec = P("gz", "gx", "gy")
    counts = tuple(mesh.shape[a] for a in ("gz", "gx", "gy"))
    return jax.shard_map(
        functools.partial(shards, counts), mesh=mesh, in_specs=(spec,), out_specs=(spec,) * 4, check_vma=False
    )
```

```python
import functools
import math

import jax
import jax.numpy as jnp
import numpy as np
from jax import lax
from jax.experimental import pallas as pl
from jax.experimental.pallas import tpu as pltpu
from jax.sharding import PartitionSpec as P

band_ratio = 2.0 - math.sqrt(3.0)
f32 = np.float32


def round_up(value, unit):
    return -(-value // unit) * unit


def dense(fine):
    n = fine // 2
    steps = np.arange(n)[:, None] - np.arange(n)[None, :]
    lower = np.where(steps >= 0, (-band_ratio) ** np.maximum(steps, 0), 0.0)
    inverse = lower.T @ lower
    mass = 4.0 * np.eye(fine) + np.eye(fine, k=1) + np.eye(fine, k=-1)
    weights = np.where(np.arange(n) == n - 1, 1.0, 0.5)[:, None]
    earlier = np.concatenate([np.zeros((1, fine)), mass[1::2][:-1]])
    product = inverse @ (0.5 * band_ratio * (mass[0::2] + weights * mass[1::2] + 0.5 * earlier))
    return product, inverse[:, 0] * (3 * band_ratio - 1), inverse[:, -1] * (2 * band_ratio)


class Level:
    def __init__(self, whole, count, following):
        self.count, self.fine = count, whole // count
        self.n = self.fine // 2
        self.product, self.first, self.last = dense(whole)
        self.following = following
        self.kept = following.functional_count if following else 0
        self.functional_count = 4 + 2 * self.kept
        self.even = np.zeros((self.n, self.fine))
        self.even[np.arange(self.n), 2 * np.arange(self.n)] = 1.0
        self.v = [self.towards(i, i * self.n - 1) for i in range(count)]
        self.w = [self.towards(i, (i + 1) * self.n) for i in range(count)]
        self.functionals = []
        for i in range(count):
            own = np.zeros((4, self.fine))
            own[0, 0] = own[1, self.fine - 2] = 1.0
            own[2], own[3] = self.v[i], self.w[i]
            if following:
                inner = following.functionals[i]
                own = np.concatenate([own, inner @ self.even, inner @ self.block(i, i)])
            self.functionals.append(own)
        built = [self.build(j) for j in range(count)]
        self.needs = [needs for needs, _ in built]
        self.tables = [tables for _, tables in built]

    def rows(self, i):
        return slice(i * self.n, (i + 1) * self.n)

    def block(self, i, j):
        return self.product[self.rows(i), j * self.fine : (j + 1) * self.fine]

    def towards(self, i, row):
        if not 0 <= row < self.count * self.n:
            return np.zeros(self.fine)
        values = self.product[row, i * self.fine : (i + 1) * self.fine]
        return values / np.abs(values).max()

    def reach(self, i, j):
        side = self.v[j] if j > i else self.w[j]
        best = np.argmax(np.abs(side))
        return self.block(i, j)[:, best] / side[best]

    def side(self, i, j):
        return 2 if j > i else 3

    def through_even(self, f):
        return 4 + f if f else 0

    def build(self, j):
        n, fine, many, end = self.n, self.fine, self.functional_count, self.count - 1
        targets = self.following.needs[j] if self.following else []
        others = [j ^ k for k in range(1, self.count)]
        at = lambda i, f: fine + many * ((i ^ j) - 1) + f
        product = np.zeros((n + len(targets), fine + many * len(others)))
        even, used = np.zeros_like(product), np.zeros(product.shape[1], bool)
        used[:fine] = True
        product[:n, :fine] = self.block(j, j)
        even[:n, :fine] = self.even
        first, last = [self.first[self.rows(j)]], [self.last[self.rows(j)]]
        for i in others:
            product[:n, at(i, self.side(j, i))] = self.reach(j, i)
            used[at(i, self.side(j, i))] = True
        for row, (i, f) in enumerate(targets, n):
            inner = self.following.functionals[i][f]
            product[row, :fine] = inner @ self.block(i, j)
            product[row, at(i, 4 + self.kept + f)] = 1.0
            even[row, at(i, self.through_even(f))] = 1.0
            used[at(i, 4 + self.kept + f)] = used[at(i, self.through_even(f))] = True
            for other in others:
                if other != i:
                    product[row, at(other, self.side(i, other))] = inner @ self.reach(i, other)
                    used[at(other, self.side(i, other))] = True
            first.append([inner @ self.first[self.rows(i)]])
            last.append([inner @ self.last[self.rows(i)]])
        around = even.copy()
        from_first, from_last = 0 if j == 0 else at(0, 0), fine - 2 if j == end else at(end, 1)
        around[:, from_first] += np.concatenate(first)
        around[:, from_last] += np.concatenate(last)
        used[from_first] = used[from_last] = True
        if j < end:
            used[at(j + 1, 0)] = True
        needs = [(j ^ (1 + place // many), place % many) for place in np.flatnonzero(used[fine:])]
        return needs, (product[:, used], even[:, used], around[:, used])

    def sent(self, i, k):
        return [f for block, f in self.needs[i ^ k] if block == i]

    def most_sent(self):
        return max([len(self.sent(i, k)) for i in range(self.count) for k in range(1, self.count)] + [1])

    def most_needed(self):
        return max(len(needs) for needs in self.needs)

    def next_first(self, j, own, fallback):
        return fallback if j == self.count - 1 else own + self.needs[j].index((j + 1, 0))


def interpolation(level, j, inputs, coarse=False):
    table = np.zeros((level.fine, inputs))
    if coarse:
        places = list(range(level.n))
        last = level.following.next_first(j, level.n, level.n - 1)
    else:
        places = [2 * c for c in range(level.n)]
        last = level.next_first(j, level.fine, level.fine - 2)
    places.append(last)
    for c in range(level.n):
        table[2 * c, places[c]] = 1.0
        table[2 * c + 1, places[c]] += 0.5
        table[2 * c + 1, places[c + 1]] += 0.5
    return table


def chain(whole, count, levels):
    made = None
    for depth in reversed(range(levels)):
        made = Level(whole >> depth, count, made)
    return made


def padded(table, rows, cols):
    out = np.zeros((rows, cols))
    out[: table.shape[0], : table.shape[1]] = table
    return out


highest = lax.Precision.HIGHEST


def dot(a, b, dims=((1,), (0,))):
    return lax.dot_general(a, b, (dims, ((), ())), precision=highest, preferred_element_type=jnp.float32)


def kernel_call(body, outs, arrays, scratch=(), left=(), left_out=(), aliases={}):
    space = lambda place, where: pl.BlockSpec(memory_space=pltpu.HBM if place in where else pltpu.VMEM)
    return pl.pallas_call(
        body,
        out_shape=[jax.ShapeDtypeStruct(shape, jnp.float32) for shape in outs],
        in_specs=[space(i, left) for i in range(len(arrays))],
        out_specs=[space(i, left_out) for i in range(len(outs))],
        scratch_shapes=list(scratch),
        input_output_aliases=aliases,
        compiler_params=pltpu.CompilerParams(vmem_limit_bytes=40 << 20),
    )(*(pltpu.with_memory_space_constraint(a, pltpu.HBM) if i in left else a for i, a in enumerate(arrays)))


def swapped(values, axis):
    count = lax.axis_size(axis)
    return [lax.ppermute(v, axis, [(i, i ^ k) for i in range(count)]) for k, v in enumerate(values, 1)]


def gathered(value, axis, beside):
    count = lax.axis_size(axis)
    if count != 4:
        return swapped([value] * (count - 1), axis), beside
    by = lambda k, what: lax.ppermute(what, axis, [(i, i ^ k) for i in range(count)])
    far, beside = lax.optimization_barrier((by(2, value), beside))
    return [by(1, value), far, by(1, far)], beside


def chosen_by(values, j):
    chosen = float(values[0])
    for place in range(1, len(values)):
        if any(values[place] != values[0] for place in range(len(values))):
            chosen = jnp.where(j == place, f32(values[place]), chosen)
    return chosen


def iota(shape, dim):
    return lax.broadcasted_iota(jnp.int32, shape, dim)


def shards(counts, field):
    dz, dx, dy = counts
    lz, lx, ly = field.shape
    nz, nx, ny = lz * dz, lx * dx, ly * dy

    yone = chain(ny, dy, 3)
    ytwo, ythree = yone.following, yone.following.following
    xone = chain(nx, dx, 1)
    xtwo = chain(nx // 2, dx, 2)
    xthree = xtwo.following
    zone = Level(nz, dz, None)

    points_a = lambda fs: [f for f in fs if f in (2, 3) or f >= 4 + yone.kept]
    points_s = lambda fs: [f for f in fs if f not in (2, 3) and f < 4 + yone.kept]
    pairs_y = [(i, k) for i in range(dy) for k in range(1, dy)]
    sa = max([len(points_a(yone.sent(i, k))) for i, k in pairs_y] + [0]) + 1
    ss = max([len(points_s(yone.sent(i, k))) for i, k in pairs_y] + [1])
    per_row = (lz * lx) // ((lz // 2) * (lx // 2))
    rowsy = round_up(sa + -(-ss // per_row), 8)
    sa8, ss8 = round_up(sa, 8), round_up(ss, 8)
    wide1 = yone.n + ytwo.most_needed()
    wide2 = ytwo.n + ythree.most_needed()
    wide = packed = round_up(max(wide1 + 1, 3 * wide2, wide2 + wide1), 128)
    kx = round_up(xtwo.most_sent(), 8)
    rowsx = xtwo.fine + kx * (dx - 1)
    tall = round_up(max(xtwo.n + xthree.most_needed(), xone.n // 2 + 1), 8)

    others_y = max(dy - 1, 1)
    fya = np.zeros((dy, others_y * sa8, ly))
    fys = np.zeros((dy, others_y * ss8, ly))
    ta = np.zeros((dy, ly, wide))
    wa = np.zeros((dy, others_y * rowsy, wide))
    tsm = np.zeros((dy, ly, 2 * wide))
    wsm = np.zeros((dy, others_y * ss8, 2 * wide))
    for j in range(dy):
        product, even, around = yone.tables[j]
        used = product.shape[0]
        ta[j, :, :used] = product[:, :ly].T
        tsm[j, :, :used] = even[:, :ly].T
        tsm[j, :, wide : wide + used] = around[:, :ly].T
        for k in range(1, dy):
            mine = yone.sent(j, k)
            fya[j, (k - 1) * sa8 :][: len(points_a(mine))] = yone.functionals[j][points_a(mine)]
            fya[j, (k - 1) * sa8 + sa - 1] = yone.functionals[j][0]
            fys[j, (k - 1) * ss8 :][: len(points_s(mine))] = yone.functionals[j][points_s(mine)]
            came = yone.sent(j ^ k, k)
            for f in came:
                column = ly + yone.needs[j].index((j ^ k, f))
                if f in points_a(came):
                    wa[j, (k - 1) * rowsy + points_a(came).index(f), :used] = product[:, column]
                else:
                    row = (k - 1) * ss8 + points_s(came).index(f)
                    wsm[j, row, :used] = even[:, column]
                    wsm[j, row, wide : wide + used] = around[:, column]
        if j == dy - 1:
            ta[j, ly - 2, wide - 1] = 0.5
        else:
            wa[j, rowsy * ((j ^ (j + 1)) - 1) + sa - 1, wide - 1] = 0.5

    ext = round_up(max(dx - 1, 1), 8)
    fx = np.zeros((dx, lx, 8))
    txa = np.zeros((dx, xone.n, lx + ext))
    txm = np.zeros((dx, xone.n, xone.n + ext))
    for j in range(dx):
        fx[j, :, :2] = xone.functionals[j][2:4].T
        product, even, around = xone.tables[j]
        txa[j, :, :lx] = product[:, :lx]
        txm[j, :, : xone.n] = around[:, :lx:2]
        for column, (i, f) in enumerate(xone.needs[j], lx):
            if f in (2, 3):
                txa[j, :, lx + (i ^ j) - 1] = product[:, column]
            else:
                txm[j, :, xone.n + (i ^ j) - 1] += around[:, column] * ((f == 0 and i == 0) or (f == 1 and i == dx - 1))

    zn = zone.n
    zs = np.zeros((dz, 2 * lz + 2 + zn * (lz + dz + 1)))
    for j in range(dz):
        cv, cw = zone.v[j], zone.w[j]
        k_last = (zone.last[zone.rows(0)] / zone.reach(0, j))[0] if 0 < j == dz - 1 else 0.0
        k_first = (zone.first[zone.rows(dz - 1)] / zone.reach(dz - 1, j))[-1] if j == 0 and dz > 1 else 0.0
        parts = [cv, cw, [k_last, k_first], zone.block(j, j).reshape(-1)]
        parts += [zone.reach(j, j ^ k) for k in range(1, dz)]
        parts += [zone.first[zone.rows(j)] * (j == 0), zone.last[zone.rows(j)] * (j == dz - 1)]
        zs[j] = np.concatenate([np.asarray(p, np.float64) for p in parts])
    at_local = 2 * lz + 2
    at_reach = at_local + zn * lz
    at_first = at_reach + zn * (dz - 1)
    at_last = at_first + zn

    f2x = np.zeros((dx, max(dx - 1, 1) * kx, xtwo.fine))
    tx2 = np.zeros((dx, 3 * tall, rowsx))
    qx2 = np.zeros((dx, xtwo.fine, rowsx))
    tx3 = np.zeros((dx, 3 * xthree.n, tall))
    qx3 = np.zeros((dx, xthree.fine, tall))
    px3 = np.zeros((dx, xtwo.fine, tall))
    for j in range(dx):
        columns = list(range(xtwo.fine))
        for i, f in xtwo.needs[j]:
            columns.append(xtwo.fine + kx * ((i ^ j) - 1) + xtwo.sent(i, i ^ j).index(f))
        for c, table in enumerate(xtwo.tables[j]):
            tx2[j, c * tall : c * tall + table.shape[0], columns] = table.T
        qx2[j][:, columns] = interpolation(xtwo, j, len(columns))
        for k in range(1, dx):
            mine = xtwo.sent(j, k)
            f2x[j, (k - 1) * kx :][: len(mine)] = xtwo.functionals[j][mine]
        for c, table in enumerate(xthree.tables[j]):
            tx3[j, c * xthree.n : (c + 1) * xthree.n, : table.shape[1]] = table
        qx3[j] = interpolation(xthree, j, tall)
        px3[j] = interpolation(xtwo, j, tall, True)

    ty2 = np.zeros((dy, 3 * wide, packed))
    qy2 = np.zeros((dy, wide, round_up(ytwo.fine, 128)))
    ty3 = np.zeros((dy, 3 * packed, 128))
    qy3 = np.zeros((dy, packed, 128))
    py3 = np.zeros((dy, packed, round_up(ytwo.fine, 128)))
    px1 = np.zeros((lx, 2 * tall))
    py1 = np.zeros((dy, packed, ly))
    for j in range(dy):
        for c, table in enumerate(ytwo.tables[j]):
            ty2[j, c * wide : c * wide + table.shape[1], c * wide2 : c * wide2 + table.shape[0]] = table.T
        qy2[j, :, : ytwo.fine] = interpolation(ytwo, j, wide).T
        for c, table in enumerate(ythree.tables[j]):
            ty3[j, c * packed : c * packed + table.shape[1], : ythree.n] = (-1.0 if c == 2 else 1.0) * table.T
        qy3[j, :, : ythree.fine] = interpolation(ythree, j, packed).T
        py1[j, wide2:] = interpolation(yone, j, packed - wide2, True).T
        py3[j, wide2:, : ytwo.fine] = interpolation(ytwo, j, packed - wide2, True).T
    for c in range(xone.n):
        begin = c if c < xtwo.n else tall + c - xtwo.n
        px1[2 * c, begin] = 1.0
        px1[2 * c + 1, begin : begin + 2] = 0.5
    az2, first2, last2 = (t.tolist() for t in dense(nz // 2))
    az3, first3, last3 = dense(nz // 4)
    z2, z3 = nz // 2, nz // 4
    lz2, lz3 = lz // 2, lz // 4
    zt = np.concatenate([az3, first3[:, None], last3[:, None]], axis=1)
    zt = zt.reshape(dz, (lz // 8) * (z3 + 2))
    lz4 = lz // 8

    to32 = lambda table: jnp.asarray(table, jnp.float32)

    def stacked(*tables):
        cols = max(t.shape[2] for t in tables)
        starts = np.cumsum([0] + [round_up(t.shape[1], 8) for t in tables])
        out = np.zeros((tables[0].shape[0], starts[-1], cols))
        for t, begin in zip(tables, starts):
            out[:, begin : begin + t.shape[1], : t.shape[2]] = t
        return to32(out), [int(v) for v in starts]

    messages_y, _ = stacked(fya, fys)
    tables_y, _ = stacked(np.concatenate([ta, tsm], axis=2), np.concatenate([wa, np.zeros((dy, wa.shape[1], 2 * wide))], axis=2),
                          np.concatenate([np.zeros((dy, wsm.shape[1], wide)), wsm], axis=2))
    tables_x, _ = stacked(txa, txm)
    tables_x2, _ = stacked(tx2, qx2)
    tables_y2, _ = stacked(ty2, qy2)
    tables_x3, at_x3 = stacked(tx3, qx3, px3)
    tables_y3, at_y3 = stacked(ty3, qy3, py3, py1)
    hz, hx1 = lz // 2, lx // 2

    def y_messages(u_hbm, table_hbm, ty_hbm, fx_hbm, u_ref, ty_ref, fx_ref, *refs):
        outs, (table, sems) = refs[:-2], refs[-2:]
        j = lax.axis_index("gy")
        nt = ((1,), (1,))
        copies = [
            pltpu.make_async_copy(table_hbm.at[j], table, sems.at[0]),
            pltpu.make_async_copy(u_hbm, u_ref, sems.at[1]),
            pltpu.make_async_copy(ty_hbm.at[j], ty_ref, sems.at[2]),
            pltpu.make_async_copy(fx_hbm.at[lax.axis_index("gx")], fx_ref, sems.at[3]),
        ]
        for copy in copies:
            copy.start()
        for copy in copies[:2]:
            copy.wait()
        lines = dot(table[: others_y * sa8], u_ref[...].reshape(lz * lx, ly), nt)
        even = jnp.concatenate([u_ref[2 * z, pl.ds(0, hx1, stride=2), :] for z in range(hz)], axis=0)
        points = dot(table[others_y * sa8 :], even, nt)
        for k, out in enumerate(outs):
            out[: min(sa8, rowsy)] = lines[k * sa8 : k * sa8 + min(sa8, rowsy)]
            if rowsy > sa8:
                out[sa8:] = jnp.zeros_like(out[sa8:])
            for f in range(ss):
                begin = hz * hx1 * (f % per_row)
                row = sa + f // per_row
                out[row : row + 1, begin : begin + hz * hx1] = points[k * ss8 + f : k * ss8 + f + 1]
        for copy in copies[2:]:
            copy.wait()

    def y_apply(*refs):
        u_ref, came = refs[0], refs[1:dy]
        ty_ref, fx_ref, ta_out, tsm_out, iy_out = refs[dy : dy + 5]
        xm_outs, points = refs[dy + 5 : -1], refs[-1]
        jx = lax.axis_index("gx")
        tn = ((0,), (0,))
        ta_all = dot(u_ref[...].reshape(lz * lx, ly), ty_ref[:ly, :wide])
        even = jnp.concatenate([u_ref[2 * z, pl.ds(0, hx1, stride=2), :] for z in range(hz)], axis=0)
        tsm_all = dot(even, ty_ref[:ly, wide:])
        for k, ref in enumerate(came):
            begin = ly + rowsy * k
            ta_all += dot(ref[...], ty_ref[begin : begin + rowsy, :wide], tn)
            points[...] = jnp.zeros_like(points)
            for f in range(ss):
                begin = hz * hx1 * (f % per_row)
                row = sa + f // per_row
                points[f : f + 1] = ref[row : row + 1, begin : begin + hz * hx1]
            begin = ly + rowsy * (dy - 1) + ss8 * k
            tsm_all += dot(points[...], ty_ref[begin : begin + ss8, wide:], tn)
        ta_out[...] = ta_all
        tsm_out[...] = tsm_all
        lane = iota((lx, ly), 1)
        weights = [jnp.broadcast_to(fx_ref[:, c : c + 1], (lx, wide)) for c in range(2)]
        for out in xm_outs:
            out[lz + 2 * hz :] = jnp.zeros_like(out[lz + 2 * hz :])
            out[lz + 2 * hz : lz + 2 * hz + 1, :wide] = tsm_all[0:1, :wide]
        for z in range(lz):
            part = ta_all[z * lx : (z + 1) * lx]
            v, w = (jnp.sum(part * weight, axis=0, keepdims=True) for weight in weights)
            for k, out in enumerate(xm_outs):
                out[z : z + 1, :wide] = jnp.where((jx ^ (k + 1)) < jx, v, w)
            if z % 2 == 0:
                half = z // 2
                tm = tsm_all[half * hx1 : (half + 1) * hx1, wide:]
                u = u_ref[z]
                before, after = pltpu.roll(u, 1, 1), pltpu.roll(u, ly - 1, 1)
                middle = 0.5 * (before + after)
                edge = 0.5 * before + jnp.broadcast_to(part[:, wide - 1 : wide], (lx, ly))
                iy = jnp.where(lane == ly - 1, edge, jnp.where(lane % 2 == 1, middle, u))
                iy_out[half] = iy
                for out in xm_outs:
                    out[lz + half : lz + half + 1, :wide] = jnp.where(jx == 0, tm[0:1], tm[hx1 - 1 : hx1])
                    out[lz + hz + half : lz + hz + half + 1, :ly] = iy[0:1]

    def x_apply(*refs):
        ta_ref, tsm_ref, iy_ref = refs[:3]
        came = refs[3 : 2 + dx][::-1]
        tx_ref, ixy_out, zc_out, u1_out = refs[2 + dx : 6 + dx]
        planes_out, rest = refs[6 + dx : -1], refs[-1]
        jx, jz = lax.axis_index("gx"), lax.axis_index("gz")
        xa, xm, diff = [], [], []

        def from_next(own, rows):
            for k, other in enumerate(rows):
                own = jnp.where((jx ^ (k + 1)) == jx + 1, other, own)
            return own

        rest[...] = jnp.zeros_like(rest)
        for k, r in enumerate(came):
            for z in range(lz):
                rest[z, k : k + 1, :wide] = r[z : z + 1, :wide]
            for half in range(hz):
                rest[half, k : k + 1, wide:] = r[lz + half : lz + half + 1, :wide]
        for z in range(0, lz, 2):
            pair = jnp.concatenate([ta_ref[z * lx : (z + 1) * lx, :], ta_ref[(z + 1) * lx : (z + 2) * lx, :]], axis=1)
            more = jnp.concatenate([rest[z, :, :wide], rest[z + 1, :, :wide]], axis=1)
            both = dot(tx_ref[jx, : xone.n], jnp.concatenate([pair, more], axis=0))
            xa += [both[:, :wide], both[:, wide:]]
        zc_out[...] = jnp.zeros_like(zc_out)
        zc_out[:hx1] = tsm_ref[:hx1, :wide]
        begin = lz + 2 * hz
        zc_out[hx1 : hx1 + 1] = from_next(tsm_ref[hx1 - 1 : hx1, :wide], [r[begin : begin + 1, :wide] for r in came])
        row = iota((lx, ly), 0)
        for half in range(0, hz, 2):
            pair = jnp.concatenate([tsm_ref[h * hx1 : (h + 1) * hx1, wide:] for h in (half, half + 1)], axis=1)
            more = jnp.concatenate([rest[half, :, wide:], rest[half + 1, :, wide:]], axis=1)
            both = dot(tx_ref[jx, xone.n :, : xone.n + ext], jnp.concatenate([pair, more], axis=0))
            xm += [both[:, :wide], both[:, wide:]]
        for half in range(hz):
            diff.append(tsm_ref[half * hx1 : (half + 1) * hx1, :wide] - xm[half])
            iy = iy_ref[half]
            begin = lz + hz + half
            halo = from_next(iy[lx - 2 : lx - 1], [r[begin : begin + 1, :ly] for r in came])
            before, after = pltpu.roll(iy, 1, 0), pltpu.roll(iy, lx - 1, 0)
            after = jnp.where(row == lx - 1, jnp.broadcast_to(halo, (lx, ly)), after)
            ixy_out[half] = jnp.where(row % 2 == 1, 0.5 * (before + after), iy)
        scalar = lambda place: chosen_by(zs[:, place], jz)
        for zc in range(zn):
            total = diff[zc] - scalar(at_first + zc) * xm[0] - scalar(at_last + zc) * xm[hz - 1]
            for z in range(lz):
                total += scalar(at_local + zc * lz + z) * xa[z]
            u1_out[zc] = total
        v = -scalar(2 * lz) * xm[hz - 1]
        w = -scalar(2 * lz + 1) * xm[0]
        for z in range(lz):
            v += scalar(z) * xa[z]
            w += scalar(lz + z) * xa[z]
        for k, out in enumerate(planes_out):
            out[...] = jnp.where((jz ^ (k + 1)) > jz, w, v)

    def z_apply(*refs):
        part_ref, came = refs[0], refs[1:dz][::-1]
        f2x_ref, u1_out, xt_outs = refs[dz], refs[dz + 1], refs[dz + 2 :]
        jx, jz = lax.axis_index("gx"), lax.axis_index("gz")
        totals = []
        for zc in range(zn):
            total = part_ref[zc]
            for k, r in enumerate(came):
                total += chosen_by(zs[:, at_reach + k * zn + zc], jz) * r[...]
            u1_out[zc] = total
            totals.append(total)
        sent = dot(f2x_ref[jx], jnp.concatenate(totals, axis=1))
        for k, out in enumerate(xt_outs):
            out[...] = sent[k * kx : (k + 1) * kx]

    def fine_coefficients(u_ref, ixy_ref, out_ref):
        for half in range(hz):
            here = ixy_ref[half]
            out_ref[2 * half] = u_ref[2 * half] - here
            if half + 1 < hz:
                out_ref[2 * half + 1] = u_ref[2 * half + 1] - 0.5 * (here + ixy_ref[half + 1])

    def second_apply(*refs):
        u1_ref, zc_ref, came = refs[0], refs[1], refs[2 : dx + 1][::-1]
        tx2_ref, ty2_ref, zt_out, i2_out = refs[dx + 1 :]
        jx, jy = lax.axis_index("gx"), lax.axis_index("gy")
        own = jnp.concatenate([u1_ref[z] for z in range(lz2)], axis=1)
        state = jnp.concatenate([own] + [r[...] for r in came], axis=0)
        across = dot(tx2_ref[jx], state)
        spread = across[3 * tall :]
        for z in range(lz2):
            cut = across[:, z * wide : (z + 1) * wide]
            if z % 2 == 1:
                moved = dot(cut[:tall], ty2_ref[jy, :wide])
                if z < 4:
                    begin = xtwo.n * (z // 2)
                    moved += pltpu.roll(zc_ref[begin : begin + tall], wide2, 1)
                zt_out[z] = moved
            else:
                joined = jnp.concatenate([cut[c * tall : (c + 1) * tall] for c in range(3)], axis=1)
                zt_out[z] = dot(joined, ty2_ref[jy, : 3 * wide])
                i2_out[z // 2] = dot(spread[:, z * wide : (z + 1) * wide], ty2_ref[jy, 3 * wide :, : round_up(ytwo.fine, 128)])

    def third_apply(*refs):
        u1_ref, i2_ref, u_ref, ixy_ref, _, own_ref = refs[:6]
        came = refs[6 : 5 + dz]
        px1_ref, tx_ref, ty_ref, fine_out, middle_out, coarse_out, coarsest_out = refs[5 + dz : 12 + dz]
        zbuf, ubuf, last, middle, sems = refs[12 + dz :]
        part = lambda ref, j, starts, which: ref[j, starts[which] : starts[which + 1]]
        jx, jy, jz = lax.axis_index("gx"), lax.axis_index("gy"), lax.axis_index("gz")
        zbuf[pl.ds(jz * lz2, lz2)] = own_ref[...]
        for k, r in enumerate(came):
            zbuf[pl.ds((jz ^ (k + 1)) * lz2, lz2)] = r[...]
        at = jnp.minimum(jz + 1, dz - 1) * lz2
        first = jnp.concatenate([zbuf[at + 1], zbuf[at + 3]], axis=0)
        halo = dot(dot(px1_ref[...], first), part(ty_ref, jy, at_y3, 3))
        here = ixy_ref[hz - 1]
        last[...] = u_ref[lz - 1] - 0.5 * (here + jnp.where(jz == dz - 1, here, halo))
        copies = [pltpu.make_async_copy(last, fine_out.at[lz - 1], sems.at[0])]
        copies[0].start()
        fy = ytwo.fine
        at = jnp.minimum((jz + 1) * lz2, z2 - 2)
        halo = dot(dot(part(tx_ref, jx, at_x3, 2), zbuf[at]), part(ty_ref, jy, at_y3, 2))[:, :fy]
        for half in range(lz2 // 2):
            here = i2_ref[half][:, :fy]
            after = i2_ref[half + 1][:, :fy] if half + 1 < lz2 // 2 else halo
            middle[2 * half] = u1_ref[2 * half][:, :fy] - here
            middle[2 * half + 1] = u1_ref[2 * half + 1][:, :fy] - 0.5 * (here + after)
        copies.append(pltpu.make_async_copy(middle, middle_out, sems.at[1]))
        copies[1].start()
        everything = [zbuf[z] for z in range(z2)]
        evens = [pltpu.roll(everything[z], packed - wide2, 1) for z in range(0, z2, 2)]
        arounds = [pltpu.roll(everything[z], packed - 2 * wide2, 1) for z in range(0, z2, 2)]
        for zc in range(z3):
            total = evens[zc] - arounds[zc] - first2[zc] * arounds[0] - last2[zc] * arounds[-1]
            for z in range(z2):
                total += az2[zc][z] * everything[z]
            ubuf[zc] = total
        fy3 = ythree.fine
        spread = []
        for half in range(lz3 // 2 + 1):
            at = jnp.minimum(jz * lz3 + 2 * half, z3 - 2)
            spread.append(dot(dot(part(tx_ref, jx, at_x3, 1), ubuf[at]), part(ty_ref, jy, at_y3, 1))[:, :fy3])
        for half in range(lz3 // 2):
            at = jz * lz3 + 2 * half
            coarse_out[2 * half] = ubuf[at][: xthree.fine, :fy3] - spread[half]
            coarse_out[2 * half + 1] = ubuf[at + 1][: xthree.fine, :fy3] - 0.5 * (spread[half] + spread[half + 1])
        n3 = xthree.n
        for zc in range(lz4):
            base = zc * (z3 + 2)
            along = chosen_by(zt[:, base], jz) * ubuf[0]
            for z in range(1, z3):
                along += chosen_by(zt[:, base + z], jz) * ubuf[z]
            even = ubuf[2 * (jz * lz4 + zc)]
            around = even + chosen_by(zt[:, base + z3], jz) * ubuf[0] + chosen_by(zt[:, base + z3 + 1], jz) * ubuf[z3 - 2]
            joined = jnp.concatenate(
                [
                    dot(tx_ref[jx, c * n3 : (c + 1) * n3, :], plane)
                    for c, plane in enumerate((along, even, around))
                ],
                axis=1,
            )
            coarsest_out[zc] = dot(joined, part(ty_ref, jy, at_y3, 0))[:, : ythree.n]
        for copy in copies:
            copy.wait()

    u, own_ty, own_fx, *ym = kernel_call(
        y_messages,
        [(lz, lx, ly), tables_y.shape[1:], fx.shape[1:]] + [(rowsy, lz * lx)] * (dy - 1),
        [field, messages_y, tables_y, to32(fx)],
        scratch=[pltpu.VMEM(messages_y.shape[1:], jnp.float32), pltpu.SemaphoreType.DMA((4,))],
        left=(0, 1, 2, 3),
    )
    ycame = swapped(ym, "gy")
    ta_v, tsm_v, iy, *xm = kernel_call(
        y_apply,
        [(lz * lx, wide), (hz * hx1, 2 * wide), (hz, lx, ly)]
        + [(round_up(lz + 2 * hz + 1, 8), max(wide, ly))] * (dx - 1),
        [u, *ycame, own_ty, own_fx],
        scratch=[pltpu.VMEM((ss8, hz * hx1), jnp.float32)],
    )
    xcame = swapped(xm, "gx")
    ixy, zc, u1_part, *planes = kernel_call(
        x_apply,
        [(hz, lx, ly), (xtwo.n + tall, wide), (zn, xone.n, wide)] + [(xone.n, wide)] * (dz - 1),
        [ta_v, tsm_v, iy, *xcame[::-1], tables_x],
        scratch=[pltpu.VMEM((lz, ext, 2 * wide), jnp.float32)],
    )
    zcame = swapped(planes, "gz")
    u1, *xt = kernel_call(
        z_apply,
        [(zn, xone.n, wide)] + [(kx, zn * wide)] * (dx - 1),
        [u1_part, *zcame[::-1], to32(f2x)],
    )
    xtcame = swapped(xt, "gx")
    zmsg, i2 = kernel_call(
        second_apply,
        [(lz2, tall, packed), (lz2 // 2, xtwo.fine, round_up(ytwo.fine, 128))],
        [u1, zc, *xtcame[::-1], tables_x2, tables_y2],
    )
    (fine,) = kernel_call(fine_coefficients, [(lz, lx, ly)], [u, ixy])
    ztcame, fine = gathered(zmsg, "gz", fine)
    return kernel_call(
        third_apply,
        [(lz, lx, ly), (lz2, xtwo.fine, ytwo.fine), (lz3, xthree.fine, ythree.fine), (lz4, xthree.n, ythree.n)],
        [u1, i2, u, ixy, fine, zmsg, *ztcame, to32(px1), tables_x3, tables_y3],
        scratch=[
            pltpu.VMEM((z2, tall, packed), jnp.float32),
            pltpu.VMEM((z3, tall, packed), jnp.float32),
            pltpu.VMEM((lx, ly), jnp.float32),
            pltpu.VMEM((lz2, xtwo.fine, ytwo.fine), jnp.float32),
            pltpu.SemaphoreType.DMA((2,)),
        ],
        left=(4,),
        left_out=(0, 1),
        aliases={4: 0},
    )


def solution(mesh):
    spec = P("gz", "gx", "gy")
    counts = tuple(mesh.shape[a] for a in ("gz", "gx", "gy"))
    return jax.shard_map(
        functools.partial(shards, counts), mesh=mesh, in_specs=(spec,), out_specs=(spec,) * 4, check_vma=False
    )
```

```python
import functools
import math

import jax
import jax.numpy as jnp
import numpy as np
from jax import lax
from jax.experimental import pallas as pl
from jax.experimental.pallas import tpu as pltpu
from jax.sharding import PartitionSpec as P

band_ratio = 2.0 - math.sqrt(3.0)
f32 = np.float32


def round_up(value, unit):
    return -(-value // unit) * unit


def dense(fine):
    n = fine // 2
    steps = np.arange(n)[:, None] - np.arange(n)[None, :]
    lower = np.where(steps >= 0, (-band_ratio) ** np.maximum(steps, 0), 0.0)
    inverse = lower.T @ lower
    mass = 4.0 * np.eye(fine) + np.eye(fine, k=1) + np.eye(fine, k=-1)
    weights = np.where(np.arange(n) == n - 1, 1.0, 0.5)[:, None]
    earlier = np.concatenate([np.zeros((1, fine)), mass[1::2][:-1]])
    product = inverse @ (0.5 * band_ratio * (mass[0::2] + weights * mass[1::2] + 0.5 * earlier))
    return product, inverse[:, 0] * (3 * band_ratio - 1), inverse[:, -1] * (2 * band_ratio)


class Level:
    def __init__(self, whole, count, following):
        self.count, self.fine = count, whole // count
        self.n = self.fine // 2
        self.product, self.first, self.last = dense(whole)
        self.following = following
        self.kept = following.functional_count if following else 0
        self.functional_count = 4 + 2 * self.kept
        self.even = np.zeros((self.n, self.fine))
        self.even[np.arange(self.n), 2 * np.arange(self.n)] = 1.0
        self.v = [self.towards(i, i * self.n - 1) for i in range(count)]
        self.w = [self.towards(i, (i + 1) * self.n) for i in range(count)]
        self.functionals = []
        for i in range(count):
            own = np.zeros((4, self.fine))
            own[0, 0] = own[1, self.fine - 2] = 1.0
            own[2], own[3] = self.v[i], self.w[i]
            if following:
                inner = following.functionals[i]
                own = np.concatenate([own, inner @ self.even, inner @ self.block(i, i)])
            self.functionals.append(own)
        built = [self.build(j) for j in range(count)]
        self.needs = [needs for needs, _ in built]
        self.tables = [tables for _, tables in built]

    def rows(self, i):
        return slice(i * self.n, (i + 1) * self.n)

    def block(self, i, j):
        return self.product[self.rows(i), j * self.fine : (j + 1) * self.fine]

    def towards(self, i, row):
        if not 0 <= row < self.count * self.n:
            return np.zeros(self.fine)
        values = self.product[row, i * self.fine : (i + 1) * self.fine]
        return values / np.abs(values).max()

    def reach(self, i, j):
        side = self.v[j] if j > i else self.w[j]
        best = np.argmax(np.abs(side))
        return self.block(i, j)[:, best] / side[best]

    def side(self, i, j):
        return 2 if j > i else 3

    def through_even(self, f):
        return 4 + f if f else 0

    def build(self, j):
        n, fine, many, end = self.n, self.fine, self.functional_count, self.count - 1
        targets = self.following.needs[j] if self.following else []
        others = [j ^ k for k in range(1, self.count)]
        at = lambda i, f: fine + many * ((i ^ j) - 1) + f
        product = np.zeros((n + len(targets), fine + many * len(others)))
        even, used = np.zeros_like(product), np.zeros(product.shape[1], bool)
        used[:fine] = True
        product[:n, :fine] = self.block(j, j)
        even[:n, :fine] = self.even
        first, last = [self.first[self.rows(j)]], [self.last[self.rows(j)]]
        for i in others:
            product[:n, at(i, self.side(j, i))] = self.reach(j, i)
            used[at(i, self.side(j, i))] = True
        for row, (i, f) in enumerate(targets, n):
            inner = self.following.functionals[i][f]
            product[row, :fine] = inner @ self.block(i, j)
            product[row, at(i, 4 + self.kept + f)] = 1.0
            even[row, at(i, self.through_even(f))] = 1.0
            used[at(i, 4 + self.kept + f)] = used[at(i, self.through_even(f))] = True
            for other in others:
                if other != i:
                    product[row, at(other, self.side(i, other))] = inner @ self.reach(i, other)
                    used[at(other, self.side(i, other))] = True
            first.append([inner @ self.first[self.rows(i)]])
            last.append([inner @ self.last[self.rows(i)]])
        around = even.copy()
        from_first, from_last = 0 if j == 0 else at(0, 0), fine - 2 if j == end else at(end, 1)
        around[:, from_first] += np.concatenate(first)
        around[:, from_last] += np.concatenate(last)
        used[from_first] = used[from_last] = True
        if j < end:
            used[at(j + 1, 0)] = True
        needs = [(j ^ (1 + place // many), place % many) for place in np.flatnonzero(used[fine:])]
        return needs, (product[:, used], even[:, used], around[:, used])

    def sent(self, i, k):
        return [f for block, f in self.needs[i ^ k] if block == i]

    def most_sent(self):
        return max([len(self.sent(i, k)) for i in range(self.count) for k in range(1, self.count)] + [1])

    def most_needed(self):
        return max(len(needs) for needs in self.needs)

    def next_first(self, j, own, fallback):
        return fallback if j == self.count - 1 else own + self.needs[j].index((j + 1, 0))


def interpolation(level, j, inputs, coarse=False):
    table = np.zeros((level.fine, inputs))
    if coarse:
        places = list(range(level.n))
        last = level.following.next_first(j, level.n, level.n - 1)
    else:
        places = [2 * c for c in range(level.n)]
        last = level.next_first(j, level.fine, level.fine - 2)
    places.append(last)
    for c in range(level.n):
        table[2 * c, places[c]] = 1.0
        table[2 * c + 1, places[c]] += 0.5
        table[2 * c + 1, places[c + 1]] += 0.5
    return table


def chain(whole, count, levels):
    made = None
    for depth in reversed(range(levels)):
        made = Level(whole >> depth, count, made)
    return made


def padded(table, rows, cols):
    out = np.zeros((rows, cols))
    out[: table.shape[0], : table.shape[1]] = table
    return out


highest = lax.Precision.HIGHEST


def dot(a, b, dims=((1,), (0,))):
    return lax.dot_general(a, b, (dims, ((), ())), precision=highest, preferred_element_type=jnp.float32)


def kernel_call(body, outs, arrays, scratch=(), left=(), left_out=(), aliases={}):
    space = lambda place, where: pl.BlockSpec(memory_space=pltpu.HBM if place in where else pltpu.VMEM)
    return pl.pallas_call(
        body,
        out_shape=[jax.ShapeDtypeStruct(shape, jnp.float32) for shape in outs],
        in_specs=[space(i, left) for i in range(len(arrays))],
        out_specs=[space(i, left_out) for i in range(len(outs))],
        scratch_shapes=list(scratch),
        input_output_aliases=aliases,
        compiler_params=pltpu.CompilerParams(vmem_limit_bytes=40 << 20),
    )(*(pltpu.with_memory_space_constraint(a, pltpu.HBM) if i in left else a for i, a in enumerate(arrays)))


def swapped(values, axis):
    count = lax.axis_size(axis)
    return [lax.ppermute(v, axis, [(i, i ^ k) for i in range(count)]) for k, v in enumerate(values, 1)]


def gathered(value, axis, beside):
    count = lax.axis_size(axis)
    if count != 4:
        return swapped([value] * (count - 1), axis), beside
    by = lambda k, what: lax.ppermute(what, axis, [(i, i ^ k) for i in range(count)])
    far, beside = lax.optimization_barrier((by(2, value), beside))
    return [by(1, value), far, by(1, far)], beside


def chosen_by(values, j):
    chosen = float(values[0])
    for place in range(1, len(values)):
        if any(values[place] != values[0] for place in range(len(values))):
            chosen = jnp.where(j == place, f32(values[place]), chosen)
    return chosen


def iota(shape, dim):
    return lax.broadcasted_iota(jnp.int32, shape, dim)


def shards(counts, field):
    dz, dx, dy = counts
    lz, lx, ly = field.shape
    nz, nx, ny = lz * dz, lx * dx, ly * dy

    yone = chain(ny, dy, 3)
    ytwo, ythree = yone.following, yone.following.following
    xone = chain(nx, dx, 1)
    xtwo = chain(nx // 2, dx, 2)
    xthree = xtwo.following
    zone = Level(nz, dz, None)

    points_a = lambda fs: [f for f in fs if f in (2, 3) or f >= 4 + yone.kept]
    points_s = lambda fs: [f for f in fs if f not in (2, 3) and f < 4 + yone.kept]
    pairs_y = [(i, k) for i in range(dy) for k in range(1, dy)]
    sa = max([len(points_a(yone.sent(i, k))) for i, k in pairs_y] + [0]) + 1
    ss = max([len(points_s(yone.sent(i, k))) for i, k in pairs_y] + [1])
    per_row = (lz * lx) // ((lz // 2) * (lx // 2))
    rowsy = round_up(sa + -(-ss // per_row), 8)
    sa8, ss8 = round_up(sa, 8), round_up(ss, 8)
    wide1 = yone.n + ytwo.most_needed()
    wide2 = ytwo.n + ythree.most_needed()
    wide = packed = round_up(max(wide1 + 1, 3 * wide2, wide2 + wide1), 128)
    kx = round_up(xtwo.most_sent(), 8)
    rowsx = xtwo.fine + kx * (dx - 1)
    tall = round_up(max(xtwo.n + xthree.most_needed() + 1, xone.n // 2 + 1), 8)

    others_y = max(dy - 1, 1)
    fya = np.zeros((dy, others_y * sa8, ly))
    fys = np.zeros((dy, others_y * ss8, ly))
    ta = np.zeros((dy, ly, wide))
    wa = np.zeros((dy, others_y * rowsy, wide))
    tsm = np.zeros((dy, ly, 2 * wide))
    wsm = np.zeros((dy, others_y * ss8, 2 * wide))
    for j in range(dy):
        product, even, around = yone.tables[j]
        used = product.shape[0]
        ta[j, :, :used] = product[:, :ly].T
        tsm[j, :, :used] = even[:, :ly].T
        tsm[j, :, wide : wide + used] = around[:, :ly].T
        for k in range(1, dy):
            mine = yone.sent(j, k)
            fya[j, (k - 1) * sa8 :][: len(points_a(mine))] = yone.functionals[j][points_a(mine)]
            fya[j, (k - 1) * sa8 + sa - 1] = yone.functionals[j][0]
            fys[j, (k - 1) * ss8 :][: len(points_s(mine))] = yone.functionals[j][points_s(mine)]
            came = yone.sent(j ^ k, k)
            for f in came:
                column = ly + yone.needs[j].index((j ^ k, f))
                if f in points_a(came):
                    wa[j, (k - 1) * rowsy + points_a(came).index(f), :used] = product[:, column]
                else:
                    row = (k - 1) * ss8 + points_s(came).index(f)
                    wsm[j, row, :used] = even[:, column]
                    wsm[j, row, wide : wide + used] = around[:, column]
        if j == dy - 1:
            ta[j, ly - 2, wide - 1] = 0.5
        else:
            wa[j, rowsy * ((j ^ (j + 1)) - 1) + sa - 1, wide - 1] = 0.5

    ext = round_up(max(dx - 1, 1), 8)
    fx = np.zeros((dx, lx, 8))
    txa = np.zeros((dx, xone.n, lx + ext))
    txm = np.zeros((dx, xone.n, xone.n + ext))
    for j in range(dx):
        fx[j, :, :2] = xone.functionals[j][2:4].T
        product, even, around = xone.tables[j]
        txa[j, :, :lx] = product[:, :lx]
        txm[j, :, : xone.n] = around[:, :lx:2]
        for column, (i, f) in enumerate(xone.needs[j], lx):
            if f in (2, 3):
                txa[j, :, lx + (i ^ j) - 1] = product[:, column]
            else:
                txm[j, :, xone.n + (i ^ j) - 1] += around[:, column] * ((f == 0 and i == 0) or (f == 1 and i == dx - 1))

    zn = zone.n
    zs = np.zeros((dz, 2 * lz + 2 + zn * (lz + dz + 1)))
    for j in range(dz):
        cv, cw = zone.v[j], zone.w[j]
        k_last = (zone.last[zone.rows(0)] / zone.reach(0, j))[0] if 0 < j == dz - 1 else 0.0
        k_first = (zone.first[zone.rows(dz - 1)] / zone.reach(dz - 1, j))[-1] if j == 0 and dz > 1 else 0.0
        parts = [cv, cw, [k_last, k_first], zone.block(j, j).reshape(-1)]
        parts += [zone.reach(j, j ^ k) for k in range(1, dz)]
        parts += [zone.first[zone.rows(j)] * (j == 0), zone.last[zone.rows(j)] * (j == dz - 1)]
        zs[j] = np.concatenate([np.asarray(p, np.float64) for p in parts])
    at_local = 2 * lz + 2
    at_reach = at_local + zn * lz
    at_first = at_reach + zn * (dz - 1)
    at_last = at_first + zn

    f2x = np.zeros((dx, max(dx - 1, 1) * kx, xtwo.fine))
    tx2 = np.zeros((dx, 3 * tall, rowsx))
    qx2 = np.zeros((dx, xtwo.fine, rowsx))
    tx3 = np.zeros((dx, 3 * xthree.n, tall))
    qx3 = np.zeros((dx, xthree.fine, tall))
    px3 = np.zeros((dx, xtwo.fine, tall))
    for j in range(dx):
        columns = list(range(xtwo.fine))
        for i, f in xtwo.needs[j]:
            columns.append(xtwo.fine + kx * ((i ^ j) - 1) + xtwo.sent(i, i ^ j).index(f))
        for c, table in enumerate(xtwo.tables[j]):
            tx2[j, c * tall : c * tall + table.shape[0], columns] = table.T
        qx2[j][:, columns] = interpolation(xtwo, j, len(columns))
        for k in range(1, dx):
            mine = xtwo.sent(j, k)
            f2x[j, (k - 1) * kx :][: len(mine)] = xtwo.functionals[j][mine]
        for c, table in enumerate(xthree.tables[j]):
            tx3[j, c * xthree.n : (c + 1) * xthree.n, : table.shape[1]] = table
        qx3[j] = interpolation(xthree, j, tall)
        px3[j] = interpolation(xtwo, j, tall, True)

    ty2 = np.zeros((dy, 3 * wide, packed))
    qy2 = np.zeros((dy, wide, round_up(ytwo.fine, 128)))
    ty3 = np.zeros((dy, 3 * packed, 128))
    qy3 = np.zeros((dy, packed, 128))
    py3 = np.zeros((dy, packed, round_up(ytwo.fine, 128)))
    px1 = np.zeros((lx, 2 * tall))
    py1 = np.zeros((dy, packed, ly))
    for j in range(dy):
        for c, table in enumerate(ytwo.tables[j]):
            ty2[j, c * wide : c * wide + table.shape[1], c * wide2 : c * wide2 + table.shape[0]] = table.T
        qy2[j, :, : ytwo.fine] = interpolation(ytwo, j, wide).T
        for c, table in enumerate(ythree.tables[j]):
            ty3[j, c * packed : c * packed + table.shape[1], : ythree.n] = (-1.0 if c == 2 else 1.0) * table.T
        qy3[j, :, : ythree.fine] = interpolation(ythree, j, packed).T
        py1[j, wide2:] = interpolation(yone, j, packed - wide2, True).T
        py3[j, wide2:, : ytwo.fine] = interpolation(ytwo, j, packed - wide2, True).T
    for c in range(xone.n):
        begin = c if c < xtwo.n else tall + c - xtwo.n
        px1[2 * c, begin] = 1.0
        px1[2 * c + 1, begin : begin + 2] = 0.5
    az2, first2, last2 = (t.tolist() for t in dense(nz // 2))
    az3, first3, last3 = dense(nz // 4)
    z2, z3 = nz // 2, nz // 4
    lz2, lz3 = lz // 2, lz // 4
    zt = np.concatenate([az3, first3[:, None], last3[:, None]], axis=1)
    zt = zt.reshape(dz, (lz // 8) * (z3 + 2))
    lz4 = lz // 8

    to32 = lambda table: jnp.asarray(table, jnp.float32)

    def stacked(*tables):
        cols = max(t.shape[2] for t in tables)
        starts = np.cumsum([0] + [round_up(t.shape[1], 8) for t in tables])
        out = np.zeros((tables[0].shape[0], starts[-1], cols))
        for t, begin in zip(tables, starts):
            out[:, begin : begin + t.shape[1], : t.shape[2]] = t
        return to32(out), [int(v) for v in starts]

    messages_y, _ = stacked(fya, fys)
    tables_y, _ = stacked(np.concatenate([ta, tsm], axis=2), np.concatenate([wa, np.zeros((dy, wa.shape[1], 2 * wide))], axis=2),
                          np.concatenate([np.zeros((dy, wsm.shape[1], wide)), wsm], axis=2))
    tables_x, _ = stacked(txa, txm)
    tables_x2, _ = stacked(tx2, qx2)
    tables_y2, _ = stacked(ty2, qy2)
    tables_x3, at_x3 = stacked(tx3, qx3, px3)
    tables_y3, at_y3 = stacked(ty3, qy3, py3, py1)
    hz, hx1 = lz // 2, lx // 2
    ly2 = round_up(ytwo.fine, 128)

    def y_messages(u_hbm, table_hbm, ty_hbm, fx_hbm, u_ref, ty_ref, fx_ref, *refs):
        outs, (table, sems) = refs[:-2], refs[-2:]
        j = lax.axis_index("gy")
        nt = ((1,), (1,))
        copies = [
            pltpu.make_async_copy(table_hbm.at[j], table, sems.at[0]),
            pltpu.make_async_copy(u_hbm, u_ref, sems.at[1]),
            pltpu.make_async_copy(ty_hbm.at[j], ty_ref, sems.at[2]),
            pltpu.make_async_copy(fx_hbm.at[lax.axis_index("gx")], fx_ref, sems.at[3]),
        ]
        for copy in copies:
            copy.start()
        for copy in copies[:2]:
            copy.wait()
        lines = dot(table[: others_y * sa8], u_ref[...].reshape(lz * lx, ly), nt)
        even = jnp.concatenate([u_ref[2 * z, pl.ds(0, hx1, stride=2), :] for z in range(hz)], axis=0)
        points = dot(table[others_y * sa8 :], even, nt)
        for k, out in enumerate(outs):
            out[: min(sa8, rowsy)] = lines[k * sa8 : k * sa8 + min(sa8, rowsy)]
            if rowsy > sa8:
                out[sa8:] = jnp.zeros_like(out[sa8:])
            for f in range(ss):
                begin = hz * hx1 * (f % per_row)
                row = sa + f // per_row
                out[row : row + 1, begin : begin + hz * hx1] = points[k * ss8 + f : k * ss8 + f + 1]
        for copy in copies[2:]:
            copy.wait()

    def y_apply(*refs):
        u_ref, came = refs[0], refs[1:dy]
        ty_ref, fx_ref, ta_out, tsm_out, iy_out = refs[dy : dy + 5]
        xm_outs, points = refs[dy + 5 : -1], refs[-1]
        jx = lax.axis_index("gx")
        tn = ((0,), (0,))
        ta_all = dot(u_ref[...].reshape(lz * lx, ly), ty_ref[:ly, :wide])
        even = jnp.concatenate([u_ref[2 * z, pl.ds(0, hx1, stride=2), :] for z in range(hz)], axis=0)
        tsm_all = dot(even, ty_ref[:ly, wide:])
        for k, ref in enumerate(came):
            begin = ly + rowsy * k
            ta_all += dot(ref[...], ty_ref[begin : begin + rowsy, :wide], tn)
            points[...] = jnp.zeros_like(points)
            for f in range(ss):
                begin = hz * hx1 * (f % per_row)
                row = sa + f // per_row
                points[f : f + 1] = ref[row : row + 1, begin : begin + hz * hx1]
            begin = ly + rowsy * (dy - 1) + ss8 * k
            tsm_all += dot(points[...], ty_ref[begin : begin + ss8, wide:], tn)
        ta_out[...] = ta_all
        tsm_out[...] = tsm_all
        lane = iota((lx, ly), 1)
        weights = [jnp.broadcast_to(fx_ref[:, c : c + 1], (lx, wide)) for c in range(2)]
        for out in xm_outs:
            out[lz + 2 * hz :] = jnp.zeros_like(out[lz + 2 * hz :])
            out[lz + 2 * hz : lz + 2 * hz + 1, :wide] = tsm_all[0:1, :wide]
        for z in range(lz):
            part = ta_all[z * lx : (z + 1) * lx]
            v, w = (jnp.sum(part * weight, axis=0, keepdims=True) for weight in weights)
            for k, out in enumerate(xm_outs):
                out[z : z + 1, :wide] = jnp.where((jx ^ (k + 1)) < jx, v, w)
            if z % 2 == 0:
                half = z // 2
                tm = tsm_all[half * hx1 : (half + 1) * hx1, wide:]
                u = u_ref[z]
                before, after = pltpu.roll(u, 1, 1), pltpu.roll(u, ly - 1, 1)
                middle = 0.5 * (before + after)
                edge = 0.5 * before + jnp.broadcast_to(part[:, wide - 1 : wide], (lx, ly))
                iy = jnp.where(lane == ly - 1, edge, jnp.where(lane % 2 == 1, middle, u))
                iy_out[half] = iy
                for out in xm_outs:
                    out[lz + half : lz + half + 1, :wide] = jnp.where(jx == 0, tm[0:1], tm[hx1 - 1 : hx1])
                    out[lz + hz + half : lz + hz + half + 1, :ly] = iy[0:1]

    def x_apply(*refs):
        ta_ref, tsm_ref, iy_ref = refs[:3]
        came = refs[3 : 2 + dx][::-1]
        tx_ref, f2x_ref, ixy_out, zc_out, u1_out = refs[2 + dx : 7 + dx]
        planes_out, xt_outs, rest = refs[7 + dx : 6 + dx + dz], refs[6 + dx + dz : -1], refs[-1]
        jx, jz = lax.axis_index("gx"), lax.axis_index("gz")
        xa, xm, diff = [], [], []

        def from_next(own, rows):
            for k, other in enumerate(rows):
                own = jnp.where((jx ^ (k + 1)) == jx + 1, other, own)
            return own

        rest[...] = jnp.zeros_like(rest)
        for k, r in enumerate(came):
            for z in range(lz):
                rest[z, k : k + 1, :wide] = r[z : z + 1, :wide]
            for half in range(hz):
                rest[half, k : k + 1, wide:] = r[lz + half : lz + half + 1, :wide]
        for z in range(0, lz, 2):
            pair = jnp.concatenate([ta_ref[z * lx : (z + 1) * lx, :], ta_ref[(z + 1) * lx : (z + 2) * lx, :]], axis=1)
            more = jnp.concatenate([rest[z, :, :wide], rest[z + 1, :, :wide]], axis=1)
            both = dot(tx_ref[jx, : xone.n], jnp.concatenate([pair, more], axis=0))
            xa += [both[:, :wide], both[:, wide:]]
        zc_out[...] = jnp.zeros_like(zc_out)
        zc_out[:hx1] = tsm_ref[:hx1, :wide]
        begin = lz + 2 * hz
        zc_out[hx1 : hx1 + 1] = from_next(tsm_ref[hx1 - 1 : hx1, :wide], [r[begin : begin + 1, :wide] for r in came])
        row = iota((lx, ly), 0)
        for half in range(0, hz, 2):
            pair = jnp.concatenate([tsm_ref[h * hx1 : (h + 1) * hx1, wide:] for h in (half, half + 1)], axis=1)
            more = jnp.concatenate([rest[half, :, wide:], rest[half + 1, :, wide:]], axis=1)
            both = dot(tx_ref[jx, xone.n :, : xone.n + ext], jnp.concatenate([pair, more], axis=0))
            xm += [both[:, :wide], both[:, wide:]]
        for half in range(hz):
            diff.append(tsm_ref[half * hx1 : (half + 1) * hx1, :wide] - xm[half])
            iy = iy_ref[half]
            begin = lz + hz + half
            halo = from_next(iy[lx - 2 : lx - 1], [r[begin : begin + 1, :ly] for r in came])
            before, after = pltpu.roll(iy, 1, 0), pltpu.roll(iy, lx - 1, 0)
            after = jnp.where(row == lx - 1, jnp.broadcast_to(halo, (lx, ly)), after)
            ixy_out[half] = jnp.where(row % 2 == 1, 0.5 * (before + after), iy)
        scalar = lambda place: chosen_by(zs[:, place], jz)
        totals = []
        for zc in range(zn):
            total = diff[zc] - scalar(at_first + zc) * xm[0] - scalar(at_last + zc) * xm[hz - 1]
            for z in range(lz):
                total += scalar(at_local + zc * lz + z) * xa[z]
            u1_out[zc] = total
            totals.append(total)
        v = -scalar(2 * lz) * xm[hz - 1]
        w = -scalar(2 * lz + 1) * xm[0]
        for z in range(lz):
            v += scalar(z) * xa[z]
            w += scalar(lz + z) * xa[z]
        for k, out in enumerate(planes_out):
            out[...] = jnp.where((jz ^ (k + 1)) > jz, w, v)
        sent = dot(f2x_ref[jx], jnp.concatenate(totals + [v, w], axis=1))
        for k, out in enumerate(xt_outs):
            out[...] = sent[k * kx : (k + 1) * kx]

    def fine_coefficients(u_ref, ixy_ref, out_ref):
        for half in range(hz):
            here = ixy_ref[half]
            out_ref[2 * half] = u_ref[2 * half] - here
            if half + 1 < hz:
                out_ref[2 * half + 1] = u_ref[2 * half + 1] - 0.5 * (here + ixy_ref[half + 1])

    def second_apply(*refs):
        part_ref, zc_ref = refs[:2]
        xcame, zcame = refs[2 : dx + 1][::-1], refs[dx + 1 : dz + dx][::-1]
        tx2_ref, ty2_ref, u1_out, zt_out, i2_out = refs[dz + dx :]
        jx, jy, jz = lax.axis_index("gx"), lax.axis_index("gy"), lax.axis_index("gz")
        own = []
        for zc in range(zn):
            total = part_ref[zc]
            for k, r in enumerate(zcame):
                total += chosen_by(zs[:, at_reach + k * zn + zc], jz) * r[...]
            u1_out[zc] = total
            own.append(total)
        own = jnp.concatenate(own + [jnp.zeros_like(own[0])] * 2, axis=1)
        across = dot(tx2_ref[jx], jnp.concatenate([own] + [r[...] for r in xcame], axis=0))
        cut = [across[:, z * wide : (z + 1) * wide] for z in range(zn + 2)]
        whole = [z for z in range(zn + 2) if z % 2 == 0 or z >= zn]
        joined = [jnp.concatenate([cut[z][c * tall : (c + 1) * tall] for c in range(3)], axis=1) for z in whole]
        made = dot(jnp.concatenate(joined, axis=0), ty2_ref[jy, : 3 * wide])
        for place, z in enumerate(whole):
            zt_out[z] = made[place * tall : (place + 1) * tall]
        made = dot(jnp.concatenate([cut[z][:tall] for z in range(1, zn, 2)], axis=0), ty2_ref[jy, :wide])
        for z in range(1, zn, 2):
            moved = made[(z // 2) * tall : (z // 2 + 1) * tall]
            if z < 4:
                begin = xtwo.n * (z // 2)
                moved += pltpu.roll(zc_ref[begin : begin + tall], wide2, 1)
            zt_out[z] = moved
        for z in (zn, zn + 1):
            zt_out[z, tall - 1 :] = cut[z][-1:]
        made = dot(jnp.concatenate([cut[z][3 * tall :] for z in range(0, zn, 2)], axis=0), ty2_ref[jy, 3 * wide :, :ly2])
        for half in range(zn // 2):
            i2_out[half] = made[half * xtwo.fine : (half + 1) * xtwo.fine]

    def third_apply(*refs):
        u1_ref, i2_ref, u_ref, ixy_ref, _, own_ref = refs[:6]
        came = refs[6 : 5 + dz]
        px1_ref, tx_ref, ty_ref, qy2_ref, fine_out, middle_out, coarse_out, coarsest_out = refs[5 + dz : 13 + dz]
        zbuf, qbuf, ubuf, last, middle, sems = refs[13 + dz :]
        part = lambda ref, j, starts, which: ref[j, starts[which] : starts[which + 1]]
        jx, jy, jz = lax.axis_index("gx"), lax.axis_index("gy"), lax.axis_index("gz")
        for k, r in enumerate((own_ref, *came)):
            zbuf[pl.ds((jz ^ k) * lz2, lz2)] = r[:lz2]
            qbuf[pl.ds((jz ^ k) * 2, 2)] = r[lz2:]
        at = jnp.minimum(jz + 1, dz - 1) * lz2
        plane_halo = dot(px1_ref[...], jnp.concatenate([zbuf[at + 1], zbuf[at + 3]], axis=0))
        everything = []
        for j in range(dz):
            for zc in range(lz2):
                total = zbuf[j * lz2 + zc]
                for i in range(dz):
                    if i != j:
                        total += float(zone.reach(j, i)[zc]) * qbuf[2 * i + (i < j)]
                everything.append(total)
        for z in range(0, z2, lz2):
            zbuf[z] = everything[z]
        if lz2 > 2:
            zbuf[z2 - 2] = everything[z2 - 2]
        at = jnp.minimum((jz + 1) * lz2, z2 - 2)
        halo = dot(part(tx_ref, jx, at_x3, 2), zbuf[at])
        edges = [jnp.zeros((1, wide), jnp.float32)] * (lz2 // 2)
        for k, r in enumerate(came):
            line = jnp.where((jz ^ (k + 1)) > jz, r[lz2, tall - 1 :], r[lz2 + 1, tall - 1 :])
            for half in range(lz2 // 2):
                edges[half] += chosen_by(zs[:, at_reach + k * zn + 2 * half], jz) * line
        fy = ytwo.fine
        edges = dot(jnp.concatenate(edges + [jnp.zeros((8 - lz2 // 2 % 8, wide), jnp.float32)], axis=0), qy2_ref[jy, :, :ly2])
        plane_halo = dot(plane_halo, part(ty_ref, jy, at_y3, 3))
        halo = dot(halo, part(ty_ref, jy, at_y3, 2))[:, :fy]
        here = ixy_ref[hz - 1]
        last[...] = u_ref[lz - 1] - 0.5 * (here + jnp.where(jz == dz - 1, here, plane_halo))
        copies = [pltpu.make_async_copy(last, fine_out.at[lz - 1], sems.at[0])]
        copies[0].start()
        at_end = iota((xtwo.fine, fy), 0) == xtwo.fine - 1
        spread = [
            i2_ref[half][:, :fy] + jnp.where(at_end, jnp.broadcast_to(edges[half : half + 1, :fy], (xtwo.fine, fy)), 0.0)
            for half in range(lz2 // 2)
        ]
        spread.append(halo)
        for half in range(lz2 // 2):
            middle[2 * half] = u1_ref[2 * half][:, :fy] - spread[half]
            middle[2 * half + 1] = u1_ref[2 * half + 1][:, :fy] - 0.5 * (spread[half] + spread[half + 1])
        copies.append(pltpu.make_async_copy(middle, middle_out, sems.at[1]))
        copies[1].start()
        evens = [pltpu.roll(everything[z], packed - wide2, 1) for z in range(0, z2, 2)]
        arounds = [pltpu.roll(everything[z], packed - 2 * wide2, 1) for z in range(0, z2, 2)]
        second = []
        for zc in range(z3):
            total = evens[zc] - arounds[zc] - first2[zc] * arounds[0] - last2[zc] * arounds[-1]
            for z in range(z2):
                total += az2[zc][z] * everything[z]
            ubuf[zc] = total
            second.append(total)
        fy3, n3 = ythree.fine, xthree.n
        at = [jnp.minimum(jz * lz3 + 2 * half, z3 - 2) for half in range(lz3 // 2 + 1)]
        spread = dot(part(tx_ref, jx, at_x3, 1), jnp.concatenate([ubuf[a] for a in at], axis=1))
        joined = []
        for zc in range(lz4):
            base = zc * (z3 + 2)
            along = chosen_by(zt[:, base], jz) * second[0]
            for z in range(1, z3):
                along += chosen_by(zt[:, base + z], jz) * second[z]
            even = ubuf[2 * (jz * lz4 + zc)]
            around = even + chosen_by(zt[:, base + z3], jz) * second[0] + chosen_by(zt[:, base + z3 + 1], jz) * second[z3 - 2]
            parts = [dot(tx_ref[jx, c * n3 : (c + 1) * n3, :], plane) for c, plane in enumerate((along, even, around))]
            joined.append(jnp.concatenate(parts, axis=1))
        spread = jnp.concatenate([spread[:, h * packed : (h + 1) * packed] for h in range(len(at))], axis=0)
        spread = dot(spread, part(ty_ref, jy, at_y3, 1))[:, :fy3]
        coarsest = dot(jnp.concatenate(joined, axis=0), part(ty_ref, jy, at_y3, 0))[:, : ythree.n]
        for zc in range(lz4):
            coarsest_out[zc] = coarsest[zc * n3 : (zc + 1) * n3]
        spread = [spread[h * xthree.fine : (h + 1) * xthree.fine] for h in range(len(at))]
        for half in range(lz3 // 2):
            at = jz * lz3 + 2 * half
            coarse_out[2 * half] = ubuf[at][: xthree.fine, :fy3] - spread[half]
            coarse_out[2 * half + 1] = ubuf[at + 1][: xthree.fine, :fy3] - 0.5 * (spread[half] + spread[half + 1])
        for copy in copies:
            copy.wait()

    u, own_ty, own_fx, *ym = kernel_call(
        y_messages,
        [(lz, lx, ly), tables_y.shape[1:], fx.shape[1:]] + [(rowsy, lz * lx)] * (dy - 1),
        [field, messages_y, tables_y, to32(fx)],
        scratch=[pltpu.VMEM(messages_y.shape[1:], jnp.float32), pltpu.SemaphoreType.DMA((4,))],
        left=(0, 1, 2, 3),
    )
    ycame = swapped(ym, "gy")
    ta_v, tsm_v, iy, *xm = kernel_call(
        y_apply,
        [(lz * lx, wide), (hz * hx1, 2 * wide), (hz, lx, ly)]
        + [(round_up(lz + 2 * hz + 1, 8), max(wide, ly))] * (dx - 1),
        [u, *ycame, own_ty, own_fx],
        scratch=[pltpu.VMEM((ss8, hz * hx1), jnp.float32)],
    )
    xcame = swapped(xm, "gx")
    ixy, zc, u1_part, *sent = kernel_call(
        x_apply,
        [(hz, lx, ly), (xtwo.n + tall, wide), (zn, xone.n, wide)]
        + [(xone.n, wide)] * (dz - 1)
        + [(kx, (zn + 2) * wide)] * (dx - 1),
        [ta_v, tsm_v, iy, *xcame[::-1], tables_x, to32(f2x)],
        scratch=[pltpu.VMEM((lz, ext, 2 * wide), jnp.float32)],
    )
    zcame = swapped(sent[: dz - 1], "gz")
    xtcame = swapped(sent[dz - 1 :], "gx")
    u1, zmsg, i2 = kernel_call(
        second_apply,
        [(zn, xone.n, wide), (lz2 + 2, tall, packed), (lz2 // 2, xtwo.fine, ly2)],
        [u1_part, zc, *xtcame[::-1], *zcame[::-1], tables_x2, tables_y2],
    )
    (fine,) = kernel_call(fine_coefficients, [(lz, lx, ly)], [u, ixy])
    ztcame, fine = gathered(zmsg, "gz", fine)
    return kernel_call(
        third_apply,
        [(lz, lx, ly), (lz2, xtwo.fine, ytwo.fine), (lz3, xthree.fine, ythree.fine), (lz4, xthree.n, ythree.n)],
        [u1, i2, u, ixy, fine, zmsg, *ztcame, to32(px1), tables_x3, tables_y3, to32(qy2)],
        scratch=[
            pltpu.VMEM((z2, tall, packed), jnp.float32),
            pltpu.VMEM((2 * dz, tall, packed), jnp.float32),
            pltpu.VMEM((z3, tall, packed), jnp.float32),
            pltpu.VMEM((lx, ly), jnp.float32),
            pltpu.VMEM((lz2, xtwo.fine, ytwo.fine), jnp.float32),
            pltpu.SemaphoreType.DMA((2,)),
        ],
        left=(4,),
        left_out=(0, 1),
        aliases={4: 0},
    )


def solution(mesh):
    spec = P("gz", "gx", "gy")
    counts = tuple(mesh.shape[a] for a in ("gz", "gx", "gy"))
    return jax.shard_map(
        functools.partial(shards, counts), mesh=mesh, in_specs=(spec,), out_specs=(spec,) * 4, check_vma=False
    )
```

```python
import functools
import math

import jax
import jax.numpy as jnp
import numpy as np
from jax import lax
from jax.experimental import pallas as pl
from jax.experimental.pallas import tpu as pltpu
from jax.sharding import PartitionSpec as P

band_ratio = 2.0 - math.sqrt(3.0)
f32 = np.float32


def round_up(value, unit):
    return -(-value // unit) * unit


def dense(fine):
    n = fine // 2
    steps = np.arange(n)[:, None] - np.arange(n)[None, :]
    lower = np.where(steps >= 0, (-band_ratio) ** np.maximum(steps, 0), 0.0)
    inverse = lower.T @ lower
    mass = 4.0 * np.eye(fine) + np.eye(fine, k=1) + np.eye(fine, k=-1)
    weights = np.where(np.arange(n) == n - 1, 1.0, 0.5)[:, None]
    earlier = np.concatenate([np.zeros((1, fine)), mass[1::2][:-1]])
    product = inverse @ (0.5 * band_ratio * (mass[0::2] + weights * mass[1::2] + 0.5 * earlier))
    return product, inverse[:, 0] * (3 * band_ratio - 1), inverse[:, -1] * (2 * band_ratio)


class Level:
    def __init__(self, whole, count, following):
        self.count, self.fine = count, whole // count
        self.n = self.fine // 2
        self.product, self.first, self.last = dense(whole)
        self.following = following
        self.kept = following.functional_count if following else 0
        self.functional_count = 4 + 2 * self.kept
        self.even = np.zeros((self.n, self.fine))
        self.even[np.arange(self.n), 2 * np.arange(self.n)] = 1.0
        self.v = [self.towards(i, i * self.n - 1) for i in range(count)]
        self.w = [self.towards(i, (i + 1) * self.n) for i in range(count)]
        self.functionals = []
        for i in range(count):
            own = np.zeros((4, self.fine))
            own[0, 0] = own[1, self.fine - 2] = 1.0
            own[2], own[3] = self.v[i], self.w[i]
            if following:
                inner = following.functionals[i]
                own = np.concatenate([own, inner @ self.even, inner @ self.block(i, i)])
            self.functionals.append(own)
        built = [self.build(j) for j in range(count)]
        self.needs = [needs for needs, _ in built]
        self.tables = [tables for _, tables in built]

    def rows(self, i):
        return slice(i * self.n, (i + 1) * self.n)

    def block(self, i, j):
        return self.product[self.rows(i), j * self.fine : (j + 1) * self.fine]

    def towards(self, i, row):
        if not 0 <= row < self.count * self.n:
            return np.zeros(self.fine)
        values = self.product[row, i * self.fine : (i + 1) * self.fine]
        return values / np.abs(values).max()

    def reach(self, i, j):
        side = self.v[j] if j > i else self.w[j]
        best = np.argmax(np.abs(side))
        return self.block(i, j)[:, best] / side[best]

    def side(self, i, j):
        return 2 if j > i else 3

    def through_even(self, f):
        return 4 + f if f else 0

    def build(self, j):
        n, fine, many, end = self.n, self.fine, self.functional_count, self.count - 1
        targets = self.following.needs[j] if self.following else []
        others = [j ^ k for k in range(1, self.count)]
        at = lambda i, f: fine + many * ((i ^ j) - 1) + f
        product = np.zeros((n + len(targets), fine + many * len(others)))
        even, used = np.zeros_like(product), np.zeros(product.shape[1], bool)
        used[:fine] = True
        product[:n, :fine] = self.block(j, j)
        even[:n, :fine] = self.even
        first, last = [self.first[self.rows(j)]], [self.last[self.rows(j)]]
        for i in others:
            product[:n, at(i, self.side(j, i))] = self.reach(j, i)
            used[at(i, self.side(j, i))] = True
        for row, (i, f) in enumerate(targets, n):
            inner = self.following.functionals[i][f]
            product[row, :fine] = inner @ self.block(i, j)
            product[row, at(i, 4 + self.kept + f)] = 1.0
            even[row, at(i, self.through_even(f))] = 1.0
            used[at(i, 4 + self.kept + f)] = used[at(i, self.through_even(f))] = True
            for other in others:
                if other != i:
                    product[row, at(other, self.side(i, other))] = inner @ self.reach(i, other)
                    used[at(other, self.side(i, other))] = True
            first.append([inner @ self.first[self.rows(i)]])
            last.append([inner @ self.last[self.rows(i)]])
        around = even.copy()
        from_first, from_last = 0 if j == 0 else at(0, 0), fine - 2 if j == end else at(end, 1)
        around[:, from_first] += np.concatenate(first)
        around[:, from_last] += np.concatenate(last)
        used[from_first] = used[from_last] = True
        if j < end:
            used[at(j + 1, 0)] = True
        needs = [(j ^ (1 + place // many), place % many) for place in np.flatnonzero(used[fine:])]
        return needs, (product[:, used], even[:, used], around[:, used])

    def sent(self, i, k):
        return [f for block, f in self.needs[i ^ k] if block == i]

    def most_sent(self):
        return max([len(self.sent(i, k)) for i in range(self.count) for k in range(1, self.count)] + [1])

    def most_needed(self):
        return max(len(needs) for needs in self.needs)

    def next_first(self, j, own, fallback):
        return fallback if j == self.count - 1 else own + self.needs[j].index((j + 1, 0))


def interpolation(level, j, inputs, coarse=False):
    table = np.zeros((level.fine, inputs))
    if coarse:
        places = list(range(level.n))
        last = level.following.next_first(j, level.n, level.n - 1)
    else:
        places = [2 * c for c in range(level.n)]
        last = level.next_first(j, level.fine, level.fine - 2)
    places.append(last)
    for c in range(level.n):
        table[2 * c, places[c]] = 1.0
        table[2 * c + 1, places[c]] += 0.5
        table[2 * c + 1, places[c + 1]] += 0.5
    return table


def chain(whole, count, levels):
    made = None
    for depth in reversed(range(levels)):
        made = Level(whole >> depth, count, made)
    return made


def padded(table, rows, cols):
    out = np.zeros((rows, cols))
    out[: table.shape[0], : table.shape[1]] = table
    return out


highest = lax.Precision.HIGHEST


def dot(a, b, dims=((1,), (0,))):
    return lax.dot_general(a, b, (dims, ((), ())), precision=highest, preferred_element_type=jnp.float32)


def kernel_call(body, outs, arrays, scratch=(), left=(), left_out=(), aliases={}):
    space = lambda place, where: pl.BlockSpec(memory_space=pltpu.HBM if place in where else pltpu.VMEM)
    return pl.pallas_call(
        body,
        out_shape=[jax.ShapeDtypeStruct(shape, jnp.float32) for shape in outs],
        in_specs=[space(i, left) for i in range(len(arrays))],
        out_specs=[space(i, left_out) for i in range(len(outs))],
        scratch_shapes=list(scratch),
        input_output_aliases=aliases,
        compiler_params=pltpu.CompilerParams(vmem_limit_bytes=40 << 20),
    )(*(pltpu.with_memory_space_constraint(a, pltpu.HBM) if i in left else a for i, a in enumerate(arrays)))


def swapped(values, axis):
    count = lax.axis_size(axis)
    return [lax.ppermute(v, axis, [(i, i ^ k) for i in range(count)]) for k, v in enumerate(values, 1)]


def gathered(value, axis, beside):
    count = lax.axis_size(axis)
    if count != 4:
        return swapped([value] * (count - 1), axis), beside
    by = lambda k, what: lax.ppermute(what, axis, [(i, i ^ k) for i in range(count)])
    far, beside = lax.optimization_barrier((by(2, value), beside))
    return [by(1, value), far, by(1, far)], beside


def chosen_by(values, j):
    chosen = float(values[0])
    for place in range(1, len(values)):
        if any(values[place] != values[0] for place in range(len(values))):
            chosen = jnp.where(j == place, f32(values[place]), chosen)
    return chosen


def iota(shape, dim):
    return lax.broadcasted_iota(jnp.int32, shape, dim)


def shards(counts, field):
    dz, dx, dy = counts
    lz, lx, ly = field.shape
    nz, nx, ny = lz * dz, lx * dx, ly * dy

    yone = chain(ny, dy, 3)
    ytwo, ythree = yone.following, yone.following.following
    xone = chain(nx, dx, 1)
    xtwo = chain(nx // 2, dx, 2)
    xthree = xtwo.following
    zone = Level(nz, dz, None)

    points_a = lambda fs: [f for f in fs if f in (2, 3) or f >= 4 + yone.kept]
    points_s = lambda fs: [f for f in fs if f not in (2, 3) and f < 4 + yone.kept]
    pairs_y = [(i, k) for i in range(dy) for k in range(1, dy)]
    sa = max([len(points_a(yone.sent(i, k))) for i, k in pairs_y] + [0]) + 1
    ss = max([len(points_s(yone.sent(i, k))) for i, k in pairs_y] + [1])
    per_row = (lz * lx) // ((lz // 2) * (lx // 2))
    rowsy = round_up(sa + -(-ss // per_row), 8)
    sa8, ss8 = round_up(sa, 8), round_up(ss, 8)
    wide1 = yone.n + ytwo.most_needed()
    wide2 = ytwo.n + ythree.most_needed()
    wide = packed = round_up(max(wide1 + 1, 3 * wide2, wide2 + wide1), 128)
    kx = round_up(xtwo.most_sent(), 8)
    rowsx = xtwo.fine + kx * (dx - 1)
    tall = round_up(max(xtwo.n + xthree.most_needed() + 1, xone.n // 2 + 1), 8)

    others_y = max(dy - 1, 1)
    fya = np.zeros((dy, others_y * sa8, ly))
    fys = np.zeros((dy, others_y * ss8, ly))
    ta = np.zeros((dy, ly, wide))
    wa = np.zeros((dy, others_y * rowsy, wide))
    tsm = np.zeros((dy, ly, 2 * wide))
    wsm = np.zeros((dy, others_y * ss8, 2 * wide))
    for j in range(dy):
        product, even, around = yone.tables[j]
        used = product.shape[0]
        ta[j, :, :used] = product[:, :ly].T
        tsm[j, :, :used] = even[:, :ly].T
        tsm[j, :, wide : wide + used] = around[:, :ly].T
        for k in range(1, dy):
            mine = yone.sent(j, k)
            fya[j, (k - 1) * sa8 :][: len(points_a(mine))] = yone.functionals[j][points_a(mine)]
            fya[j, (k - 1) * sa8 + sa - 1] = yone.functionals[j][0]
            fys[j, (k - 1) * ss8 :][: len(points_s(mine))] = yone.functionals[j][points_s(mine)]
            came = yone.sent(j ^ k, k)
            for f in came:
                column = ly + yone.needs[j].index((j ^ k, f))
                if f in points_a(came):
                    wa[j, (k - 1) * rowsy + points_a(came).index(f), :used] = product[:, column]
                else:
                    row = (k - 1) * ss8 + points_s(came).index(f)
                    wsm[j, row, :used] = even[:, column]
                    wsm[j, row, wide : wide + used] = around[:, column]
        if j == dy - 1:
            ta[j, ly - 2, wide - 1] = 0.5
        else:
            wa[j, rowsy * ((j ^ (j + 1)) - 1) + sa - 1, wide - 1] = 0.5

    ext = round_up(max(dx - 1, 1), 8)
    fx = np.zeros((dx, lx, 8))
    txa = np.zeros((dx, xone.n, lx + ext))
    txm = np.zeros((dx, xone.n, xone.n + ext))
    for j in range(dx):
        fx[j, :, :2] = xone.functionals[j][2:4].T
        product, even, around = xone.tables[j]
        txa[j, :, :lx] = product[:, :lx]
        txm[j, :, : xone.n] = around[:, :lx:2]
        for column, (i, f) in enumerate(xone.needs[j], lx):
            if f in (2, 3):
                txa[j, :, lx + (i ^ j) - 1] = product[:, column]
            else:
                txm[j, :, xone.n + (i ^ j) - 1] += around[:, column] * ((f == 0 and i == 0) or (f == 1 and i == dx - 1))

    zn = zone.n
    zs = np.zeros((dz, 2 * lz + 2 + zn * (lz + dz + 1)))
    for j in range(dz):
        cv, cw = zone.v[j], zone.w[j]
        k_last = (zone.last[zone.rows(0)] / zone.reach(0, j))[0] if 0 < j == dz - 1 else 0.0
        k_first = (zone.first[zone.rows(dz - 1)] / zone.reach(dz - 1, j))[-1] if j == 0 and dz > 1 else 0.0
        parts = [cv, cw, [k_last, k_first], zone.block(j, j).reshape(-1)]
        parts += [zone.reach(j, j ^ k) for k in range(1, dz)]
        parts += [zone.first[zone.rows(j)] * (j == 0), zone.last[zone.rows(j)] * (j == dz - 1)]
        zs[j] = np.concatenate([np.asarray(p, np.float64) for p in parts])
    at_local = 2 * lz + 2
    at_reach = at_local + zn * lz
    at_first = at_reach + zn * (dz - 1)
    at_last = at_first + zn

    f2x = np.zeros((dx, max(dx - 1, 1) * kx, xtwo.fine))
    tx2 = np.zeros((dx, 3 * tall, rowsx))
    qx2 = np.zeros((dx, xtwo.fine, rowsx))
    tx3 = np.zeros((dx, 3 * xthree.n, tall))
    qx3 = np.zeros((dx, xthree.fine, tall))
    px3 = np.zeros((dx, xtwo.fine, tall))
    for j in range(dx):
        columns = list(range(xtwo.fine))
        for i, f in xtwo.needs[j]:
            columns.append(xtwo.fine + kx * ((i ^ j) - 1) + xtwo.sent(i, i ^ j).index(f))
        for c, table in enumerate(xtwo.tables[j]):
            tx2[j, c * tall : c * tall + table.shape[0], columns] = table.T
        qx2[j][:, columns] = interpolation(xtwo, j, len(columns))
        for k in range(1, dx):
            mine = xtwo.sent(j, k)
            f2x[j, (k - 1) * kx :][: len(mine)] = xtwo.functionals[j][mine]
        for c, table in enumerate(xthree.tables[j]):
            tx3[j, c * xthree.n : (c + 1) * xthree.n, : table.shape[1]] = table
        qx3[j] = interpolation(xthree, j, tall)
        px3[j] = interpolation(xtwo, j, tall, True)

    ty2 = np.zeros((dy, 3 * wide, packed))
    qy2 = np.zeros((dy, wide, round_up(ytwo.fine, 128)))
    ty3 = np.zeros((dy, 3 * packed, 128))
    qy3 = np.zeros((dy, packed, 128))
    py3 = np.zeros((dy, packed, round_up(ytwo.fine, 128)))
    px1 = np.zeros((lx, 2 * tall))
    py1 = np.zeros((dy, packed, ly))
    for j in range(dy):
        for c, table in enumerate(ytwo.tables[j]):
            ty2[j, c * wide : c * wide + table.shape[1], c * wide2 : c * wide2 + table.shape[0]] = table.T
        qy2[j, :, : ytwo.fine] = interpolation(ytwo, j, wide).T
        for c, table in enumerate(ythree.tables[j]):
            ty3[j, c * packed : c * packed + table.shape[1], : ythree.n] = (-1.0 if c == 2 else 1.0) * table.T
        qy3[j, :, : ythree.fine] = interpolation(ythree, j, packed).T
        py1[j, wide2:] = interpolation(yone, j, packed - wide2, True).T
        py3[j, wide2:, : ytwo.fine] = interpolation(ytwo, j, packed - wide2, True).T
    for c in range(xone.n):
        begin = c if c < xtwo.n else tall + c - xtwo.n
        px1[2 * c, begin] = 1.0
        px1[2 * c + 1, begin : begin + 2] = 0.5
    az2, first2, last2 = (t.tolist() for t in dense(nz // 2))
    az3, first3, last3 = dense(nz // 4)
    z2, z3 = nz // 2, nz // 4
    lz2, lz3 = lz // 2, lz // 4
    zt = np.concatenate([az3, first3[:, None], last3[:, None]], axis=1)
    zt = zt.reshape(dz, (lz // 8) * (z3 + 2))
    lz4 = lz // 8

    to32 = lambda table: jnp.asarray(table, jnp.float32)

    def stacked(*tables):
        cols = max(t.shape[2] for t in tables)
        starts = np.cumsum([0] + [round_up(t.shape[1], 8) for t in tables])
        out = np.zeros((tables[0].shape[0], starts[-1], cols))
        for t, begin in zip(tables, starts):
            out[:, begin : begin + t.shape[1], : t.shape[2]] = t
        return to32(out), [int(v) for v in starts]

    messages_y, _ = stacked(fya, fys)
    tables_y, _ = stacked(np.concatenate([ta, tsm], axis=2), np.concatenate([wa, np.zeros((dy, wa.shape[1], 2 * wide))], axis=2),
                          np.concatenate([np.zeros((dy, wsm.shape[1], wide)), wsm], axis=2))
    tables_x, _ = stacked(txa, txm)
    tables_x2, _ = stacked(tx2, qx2)
    tables_y2, _ = stacked(ty2, qy2)
    tables_x3, at_x3 = stacked(tx3, qx3, px3)
    tables_y3, at_y3 = stacked(ty3, qy3, py3, py1)
    hz, hx1 = lz // 2, lx // 2
    ly2 = round_up(ytwo.fine, 128)

    def y_messages(u_hbm, table_hbm, ty_hbm, fx_hbm, u_ref, ty_ref, fx_ref, *refs):
        outs, (table, sems) = refs[:-2], refs[-2:]
        j = lax.axis_index("gy")
        nt = ((1,), (1,))
        copies = [
            pltpu.make_async_copy(table_hbm.at[j], table, sems.at[0]),
            pltpu.make_async_copy(u_hbm, u_ref, sems.at[1]),
            pltpu.make_async_copy(ty_hbm.at[j], ty_ref, sems.at[2]),
            pltpu.make_async_copy(fx_hbm.at[lax.axis_index("gx")], fx_ref, sems.at[3]),
        ]
        for copy in copies:
            copy.start()
        for copy in copies[:2]:
            copy.wait()
        lines = dot(table[: others_y * sa8], u_ref[...].reshape(lz * lx, ly), nt)
        even = jnp.concatenate([u_ref[2 * z, pl.ds(0, hx1, stride=2), :] for z in range(hz)], axis=0)
        points = dot(table[others_y * sa8 :], even, nt)
        for k, out in enumerate(outs):
            out[: min(sa8, rowsy)] = lines[k * sa8 : k * sa8 + min(sa8, rowsy)]
            if rowsy > sa8:
                out[sa8:] = jnp.zeros_like(out[sa8:])
            for f in range(ss):
                begin = hz * hx1 * (f % per_row)
                row = sa + f // per_row
                out[row : row + 1, begin : begin + hz * hx1] = points[k * ss8 + f : k * ss8 + f + 1]
        for copy in copies[2:]:
            copy.wait()

    def y_apply(*refs):
        u_ref, came = refs[0], refs[1:dy]
        ty_ref, fx_ref, ta_out, tsm_out, iy_out = refs[dy : dy + 5]
        xm_outs, points = refs[dy + 5 : -1], refs[-1]
        jx = lax.axis_index("gx")
        tn = ((0,), (0,))
        ta_all = dot(u_ref[...].reshape(lz * lx, ly), ty_ref[:ly, :wide])
        even = jnp.concatenate([u_ref[2 * z, pl.ds(0, hx1, stride=2), :] for z in range(hz)], axis=0)
        tsm_all = dot(even, ty_ref[:ly, wide:])
        for k, ref in enumerate(came):
            begin = ly + rowsy * k
            ta_all += dot(ref[...], ty_ref[begin : begin + rowsy, :wide], tn)
            points[...] = jnp.zeros_like(points)
            for f in range(ss):
                begin = hz * hx1 * (f % per_row)
                row = sa + f // per_row
                points[f : f + 1] = ref[row : row + 1, begin : begin + hz * hx1]
            begin = ly + rowsy * (dy - 1) + ss8 * k
            tsm_all += dot(points[...], ty_ref[begin : begin + ss8, wide:], tn)
        ta_out[...] = ta_all
        tsm_out[...] = tsm_all
        lane = iota((lx, ly), 1)
        weights = [jnp.broadcast_to(fx_ref[:, c : c + 1], (lx, wide)) for c in range(2)]
        for out in xm_outs:
            out[lz + 2 * hz :] = jnp.zeros_like(out[lz + 2 * hz :])
            out[lz + 2 * hz : lz + 2 * hz + 1, :wide] = tsm_all[0:1, :wide]
        for z in range(lz):
            part = ta_all[z * lx : (z + 1) * lx]
            v, w = (jnp.sum(part * weight, axis=0, keepdims=True) for weight in weights)
            for k, out in enumerate(xm_outs):
                out[z : z + 1, :wide] = jnp.where((jx ^ (k + 1)) < jx, v, w)
            if z % 2 == 0:
                half = z // 2
                tm = tsm_all[half * hx1 : (half + 1) * hx1, wide:]
                u = u_ref[z]
                before, after = pltpu.roll(u, 1, 1), pltpu.roll(u, ly - 1, 1)
                middle = 0.5 * (before + after)
                edge = 0.5 * before + jnp.broadcast_to(part[:, wide - 1 : wide], (lx, ly))
                iy = jnp.where(lane == ly - 1, edge, jnp.where(lane % 2 == 1, middle, u))
                iy_out[half] = iy
                for out in xm_outs:
                    out[lz + half : lz + half + 1, :wide] = jnp.where(jx == 0, tm[0:1], tm[hx1 - 1 : hx1])
                    out[lz + hz + half : lz + hz + half + 1, :ly] = iy[0:1]

    def x_apply(*refs):
        ta_ref, tsm_ref, iy_ref = refs[:3]
        came = refs[3 : 2 + dx][::-1]
        tx_ref, f2x_ref, ixy_out, zc_out, u1_out = refs[2 + dx : 7 + dx]
        planes_out, xt_outs, rest = refs[7 + dx : 6 + dx + dz], refs[6 + dx + dz : -1], refs[-1]
        jx, jz = lax.axis_index("gx"), lax.axis_index("gz")
        xa, xm, diff = [], [], []

        def from_next(own, rows):
            for k, other in enumerate(rows):
                own = jnp.where((jx ^ (k + 1)) == jx + 1, other, own)
            return own

        rest[...] = jnp.zeros_like(rest)
        for k, r in enumerate(came):
            for z in range(lz):
                rest[z, k : k + 1, :wide] = r[z : z + 1, :wide]
            for half in range(hz):
                rest[half, k : k + 1, wide:] = r[lz + half : lz + half + 1, :wide]
        for z in range(0, lz, 2):
            pair = jnp.concatenate([ta_ref[z * lx : (z + 1) * lx, :], ta_ref[(z + 1) * lx : (z + 2) * lx, :]], axis=1)
            more = jnp.concatenate([rest[z, :, :wide], rest[z + 1, :, :wide]], axis=1)
            both = dot(tx_ref[jx, : xone.n], jnp.concatenate([pair, more], axis=0))
            xa += [both[:, :wide], both[:, wide:]]
        zc_out[...] = jnp.zeros_like(zc_out)
        zc_out[:hx1] = tsm_ref[:hx1, :wide]
        begin = lz + 2 * hz
        zc_out[hx1 : hx1 + 1] = from_next(tsm_ref[hx1 - 1 : hx1, :wide], [r[begin : begin + 1, :wide] for r in came])
        row = iota((lx, ly), 0)
        for half in range(0, hz, 2):
            pair = jnp.concatenate([tsm_ref[h * hx1 : (h + 1) * hx1, wide:] for h in (half, half + 1)], axis=1)
            more = jnp.concatenate([rest[half, :, wide:], rest[half + 1, :, wide:]], axis=1)
            both = dot(tx_ref[jx, xone.n :, : xone.n + ext], jnp.concatenate([pair, more], axis=0))
            xm += [both[:, :wide], both[:, wide:]]
        for half in range(hz):
            diff.append(tsm_ref[half * hx1 : (half + 1) * hx1, :wide] - xm[half])
            iy = iy_ref[half]
            begin = lz + hz + half
            halo = from_next(iy[lx - 2 : lx - 1], [r[begin : begin + 1, :ly] for r in came])
            before, after = pltpu.roll(iy, 1, 0), pltpu.roll(iy, lx - 1, 0)
            after = jnp.where(row == lx - 1, jnp.broadcast_to(halo, (lx, ly)), after)
            ixy_out[half] = jnp.where(row % 2 == 1, 0.5 * (before + after), iy)
        scalar = lambda place: chosen_by(zs[:, place], jz)
        totals = []
        for zc in range(zn):
            total = diff[zc] - scalar(at_first + zc) * xm[0] - scalar(at_last + zc) * xm[hz - 1]
            for z in range(lz):
                total += scalar(at_local + zc * lz + z) * xa[z]
            u1_out[zc] = total
            totals.append(total)
        v = -scalar(2 * lz) * xm[hz - 1]
        w = -scalar(2 * lz + 1) * xm[0]
        for z in range(lz):
            v += scalar(z) * xa[z]
            w += scalar(lz + z) * xa[z]
        for k, out in enumerate(planes_out):
            out[...] = jnp.where((jz ^ (k + 1)) > jz, w, v)
        sent = dot(f2x_ref[jx], jnp.concatenate(totals + [v, w], axis=1))
        for k, out in enumerate(xt_outs):
            out[...] = sent[k * kx : (k + 1) * kx]

    def fine_coefficients(u_ref, ixy_ref, out_ref):
        for half in range(hz):
            here = ixy_ref[half]
            out_ref[2 * half] = u_ref[2 * half] - here
            if half + 1 < hz:
                out_ref[2 * half + 1] = u_ref[2 * half + 1] - 0.5 * (here + ixy_ref[half + 1])

    def second_apply(*refs):
        part_ref, zc_ref = refs[:2]
        xcame, zcame = refs[2 : dx + 1][::-1], refs[dx + 1 : dz + dx][::-1]
        tx2_ref, ty2_ref, u1_out, zt_out, i2_out = refs[dz + dx :]
        jx, jy, jz = lax.axis_index("gx"), lax.axis_index("gy"), lax.axis_index("gz")
        own = []
        for zc in range(zn):
            total = part_ref[zc]
            for k, r in enumerate(zcame):
                total += chosen_by(zs[:, at_reach + k * zn + zc], jz) * r[...]
            u1_out[zc] = total
            own.append(total)
        own = jnp.concatenate(own + [jnp.zeros_like(own[0])] * 2, axis=1)
        across = dot(tx2_ref[jx], jnp.concatenate([own] + [r[...] for r in xcame], axis=0))
        cut = [across[:, z * wide : (z + 1) * wide] for z in range(zn + 2)]
        whole = [z for z in range(zn + 2) if z % 2 == 0 or z >= zn]
        joined = [jnp.concatenate([cut[z][c * tall : (c + 1) * tall] for c in range(3)], axis=1) for z in whole]
        made = dot(jnp.concatenate(joined, axis=0), ty2_ref[jy, : 3 * wide])
        for place, z in enumerate(whole):
            zt_out[z] = made[place * tall : (place + 1) * tall]
        made = dot(jnp.concatenate([cut[z][:tall] for z in range(1, zn, 2)], axis=0), ty2_ref[jy, :wide])
        for z in range(1, zn, 2):
            moved = made[(z // 2) * tall : (z // 2 + 1) * tall]
            if z < 4:
                begin = xtwo.n * (z // 2)
                moved += pltpu.roll(zc_ref[begin : begin + tall], wide2, 1)
            zt_out[z] = moved
        for z in (zn, zn + 1):
            zt_out[z, tall - 1 :] = cut[z][-1:]
        made = dot(jnp.concatenate([cut[z][3 * tall :] for z in range(0, zn, 2)], axis=0), ty2_ref[jy, 3 * wide :, :ly2])
        for half in range(zn // 2):
            i2_out[half] = made[half * xtwo.fine : (half + 1) * xtwo.fine]

    def third_apply(*refs):
        u1_ref, i2_ref, u_ref, ixy_ref, _, own_ref = refs[:6]
        came = refs[6 : 5 + dz]
        px1_ref, tx_ref, ty_ref, qy2_ref, fine_out, middle_out, coarse_out, coarsest_out = refs[5 + dz : 13 + dz]
        zbuf, qbuf, ubuf, last, middle, sems = refs[13 + dz :]
        part = lambda ref, j, starts, which: ref[j, starts[which] : starts[which + 1]]
        jx, jy, jz = lax.axis_index("gx"), lax.axis_index("gy"), lax.axis_index("gz")
        for k, r in enumerate((own_ref, *came)):
            zbuf[pl.ds((jz ^ k) * lz2, lz2)] = r[:lz2]
            qbuf[pl.ds((jz ^ k) * 2, 2)] = r[lz2:]
        at = jnp.minimum(jz + 1, dz - 1) * lz2
        plane_halo = dot(px1_ref[...], jnp.concatenate([zbuf[at + 1], zbuf[at + 3]], axis=0))
        everything = []
        for j in range(dz):
            for zc in range(lz2):
                total = zbuf[j * lz2 + zc]
                for i in range(dz):
                    if i != j:
                        total += float(zone.reach(j, i)[zc]) * qbuf[2 * i + (i < j)]
                everything.append(total)
        for z in range(0, z2, lz2):
            zbuf[z] = everything[z]
        if lz2 > 2:
            zbuf[z2 - 2] = everything[z2 - 2]
        at = jnp.minimum((jz + 1) * lz2, z2 - 2)
        halo = dot(part(tx_ref, jx, at_x3, 2), zbuf[at])
        edges = [jnp.zeros((1, wide), jnp.float32)] * (lz2 // 2)
        for k, r in enumerate(came):
            line = jnp.where((jz ^ (k + 1)) > jz, r[lz2, tall - 1 :], r[lz2 + 1, tall - 1 :])
            for half in range(lz2 // 2):
                edges[half] += chosen_by(zs[:, at_reach + k * zn + 2 * half], jz) * line
        fy = ytwo.fine
        edges = dot(jnp.concatenate(edges + [jnp.zeros((8 - lz2 // 2 % 8, wide), jnp.float32)], axis=0), qy2_ref[jy, :, :ly2])
        plane_halo = dot(plane_halo, part(ty_ref, jy, at_y3, 3))
        halo = dot(halo, part(ty_ref, jy, at_y3, 2))[:, :fy]
        here = ixy_ref[hz - 1]
        last[...] = u_ref[lz - 1] - 0.5 * (here + jnp.where(jz == dz - 1, here, plane_halo))
        copies = [pltpu.make_async_copy(last, fine_out.at[lz - 1], sems.at[0])]
        copies[0].start()
        at_end = iota((xtwo.fine, fy), 0) == xtwo.fine - 1
        spread = [
            i2_ref[half][:, :fy] + jnp.where(at_end, jnp.broadcast_to(edges[half : half + 1, :fy], (xtwo.fine, fy)), 0.0)
            for half in range(lz2 // 2)
        ]
        spread.append(halo)
        for half in range(lz2 // 2):
            middle[2 * half] = u1_ref[2 * half][:, :fy] - spread[half]
            middle[2 * half + 1] = u1_ref[2 * half + 1][:, :fy] - 0.5 * (spread[half] + spread[half + 1])
        copies.append(pltpu.make_async_copy(middle, middle_out, sems.at[1]))
        copies[1].start()
        evens = [pltpu.roll(everything[z], packed - wide2, 1) for z in range(0, z2, 2)]
        arounds = [pltpu.roll(everything[z], packed - 2 * wide2, 1) for z in range(0, z2, 2)]
        second = []
        for zc in range(z3):
            total = evens[zc] - arounds[zc] - first2[zc] * arounds[0] - last2[zc] * arounds[-1]
            for z in range(z2):
                total += az2[zc][z] * everything[z]
            ubuf[zc] = total
            second.append(total)
        fy3, n3 = ythree.fine, xthree.n
        at = [jnp.minimum(jz * lz3 + 2 * half, z3 - 2) for half in range(lz3 // 2 + 1)]
        spread = dot(part(tx_ref, jx, at_x3, 1), jnp.concatenate([ubuf[a] for a in at], axis=1))
        joined = []
        for zc in range(lz4):
            base = zc * (z3 + 2)
            along = chosen_by(zt[:, base], jz) * second[0]
            for z in range(1, z3):
                along += chosen_by(zt[:, base + z], jz) * second[z]
            even = ubuf[2 * (jz * lz4 + zc)]
            around = even + chosen_by(zt[:, base + z3], jz) * second[0] + chosen_by(zt[:, base + z3 + 1], jz) * second[z3 - 2]
            parts = [dot(tx_ref[jx, c * n3 : (c + 1) * n3, :], plane) for c, plane in enumerate((along, even, around))]
            joined.append(jnp.concatenate(parts, axis=1))
        spread = jnp.concatenate([spread[:, h * packed : (h + 1) * packed] for h in range(len(at))], axis=0)
        spread = dot(spread, part(ty_ref, jy, at_y3, 1))[:, :fy3]
        coarsest = dot(jnp.concatenate(joined, axis=0), part(ty_ref, jy, at_y3, 0))[:, : ythree.n]
        for zc in range(lz4):
            coarsest_out[zc] = coarsest[zc * n3 : (zc + 1) * n3]
        spread = [spread[h * xthree.fine : (h + 1) * xthree.fine] for h in range(len(at))]
        for half in range(lz3 // 2):
            at = jz * lz3 + 2 * half
            coarse_out[2 * half] = ubuf[at][: xthree.fine, :fy3] - spread[half]
            coarse_out[2 * half + 1] = ubuf[at + 1][: xthree.fine, :fy3] - 0.5 * (spread[half] + spread[half + 1])
        for copy in copies:
            copy.wait()

    u, own_ty, own_fx, *ym = kernel_call(
        y_messages,
        [(lz, lx, ly), tables_y.shape[1:], fx.shape[1:]] + [(rowsy, lz * lx)] * (dy - 1),
        [field, messages_y, tables_y, to32(fx)],
        scratch=[pltpu.VMEM(messages_y.shape[1:], jnp.float32), pltpu.SemaphoreType.DMA((4,))],
        left=(0, 1, 2, 3),
    )
    ycame = swapped(ym, "gy")
    ta_v, tsm_v, iy, *xm = kernel_call(
        y_apply,
        [(lz * lx, wide), (hz * hx1, 2 * wide), (hz, lx, ly)]
        + [(round_up(lz + 2 * hz + 1, 8), max(wide, ly))] * (dx - 1),
        [u, *ycame, own_ty, own_fx],
        scratch=[pltpu.VMEM((ss8, hz * hx1), jnp.float32)],
    )
    xcame = swapped(xm, "gx")
    ixy, zc, u1_part, *sent = kernel_call(
        x_apply,
        [(hz, lx, ly), (xtwo.n + tall, wide), (zn, xone.n, wide)]
        + [(xone.n, wide)] * (dz - 1)
        + [(kx, (zn + 2) * wide)] * (dx - 1),
        [ta_v, tsm_v, iy, *xcame[::-1], tables_x, to32(f2x)],
        scratch=[pltpu.VMEM((lz, ext, 2 * wide), jnp.float32)],
    )
    tails = sent[dz - 1 :]
    zcame = swapped(sent[: dz - 1], "gz")
    if dz > 1 and dx > 1:
        zcame[0], tails[0] = lax.optimization_barrier((zcame[0], tails[0]))
    xtcame = swapped(tails, "gx")
    u1, zmsg, i2 = kernel_call(
        second_apply,
        [(zn, xone.n, wide), (lz2 + 2, tall, packed), (lz2 // 2, xtwo.fine, ly2)],
        [u1_part, zc, *xtcame[::-1], *zcame[::-1], tables_x2, tables_y2],
    )
    (fine,) = kernel_call(fine_coefficients, [(lz, lx, ly)], [u, ixy])
    ztcame, fine = gathered(zmsg, "gz", fine)
    return kernel_call(
        third_apply,
        [(lz, lx, ly), (lz2, xtwo.fine, ytwo.fine), (lz3, xthree.fine, ythree.fine), (lz4, xthree.n, ythree.n)],
        [u1, i2, u, ixy, fine, zmsg, *ztcame, to32(px1), tables_x3, tables_y3, to32(qy2)],
        scratch=[
            pltpu.VMEM((z2, tall, packed), jnp.float32),
            pltpu.VMEM((2 * dz, tall, packed), jnp.float32),
            pltpu.VMEM((z3, tall, packed), jnp.float32),
            pltpu.VMEM((lx, ly), jnp.float32),
            pltpu.VMEM((lz2, xtwo.fine, ytwo.fine), jnp.float32),
            pltpu.SemaphoreType.DMA((2,)),
        ],
        left=(4,),
        left_out=(0, 1),
        aliases={4: 0},
    )


def solution(mesh):
    spec = P("gz", "gx", "gy")
    counts = tuple(mesh.shape[a] for a in ("gz", "gx", "gy"))
    return jax.shard_map(
        functools.partial(shards, counts), mesh=mesh, in_specs=(spec,), out_specs=(spec,) * 4, check_vma=False
    )
```

```python
import functools
import math

import jax
import jax.numpy as jnp
import numpy as np
from jax import lax
from jax.experimental import pallas as pl
from jax.experimental.pallas import tpu as pltpu
from jax.sharding import PartitionSpec as P

band_ratio = 2.0 - math.sqrt(3.0)
f32 = np.float32


def round_up(value, unit):
    return -(-value // unit) * unit


def dense(fine):
    n = fine // 2
    steps = np.arange(n)[:, None] - np.arange(n)[None, :]
    lower = np.where(steps >= 0, (-band_ratio) ** np.maximum(steps, 0), 0.0)
    inverse = lower.T @ lower
    mass = 4.0 * np.eye(fine) + np.eye(fine, k=1) + np.eye(fine, k=-1)
    weights = np.where(np.arange(n) == n - 1, 1.0, 0.5)[:, None]
    earlier = np.concatenate([np.zeros((1, fine)), mass[1::2][:-1]])
    product = inverse @ (0.5 * band_ratio * (mass[0::2] + weights * mass[1::2] + 0.5 * earlier))
    return product, inverse[:, 0] * (3 * band_ratio - 1), inverse[:, -1] * (2 * band_ratio)


class Level:
    def __init__(self, whole, count, following):
        self.count, self.fine = count, whole // count
        self.n = self.fine // 2
        self.product, self.first, self.last = dense(whole)
        self.following = following
        self.kept = following.functional_count if following else 0
        self.functional_count = 4 + 2 * self.kept
        self.even = np.zeros((self.n, self.fine))
        self.even[np.arange(self.n), 2 * np.arange(self.n)] = 1.0
        self.v = [self.towards(i, i * self.n - 1) for i in range(count)]
        self.w = [self.towards(i, (i + 1) * self.n) for i in range(count)]
        self.functionals = []
        for i in range(count):
            own = np.zeros((4, self.fine))
            own[0, 0] = own[1, self.fine - 2] = 1.0
            own[2], own[3] = self.v[i], self.w[i]
            if following:
                inner = following.functionals[i]
                own = np.concatenate([own, inner @ self.even, inner @ self.block(i, i)])
            self.functionals.append(own)
        built = [self.build(j) for j in range(count)]
        self.needs = [needs for needs, _ in built]
        self.tables = [tables for _, tables in built]

    def rows(self, i):
        return slice(i * self.n, (i + 1) * self.n)

    def block(self, i, j):
        return self.product[self.rows(i), j * self.fine : (j + 1) * self.fine]

    def towards(self, i, row):
        if not 0 <= row < self.count * self.n:
            return np.zeros(self.fine)
        values = self.product[row, i * self.fine : (i + 1) * self.fine]
        return values / np.abs(values).max()

    def reach(self, i, j):
        side = self.v[j] if j > i else self.w[j]
        best = np.argmax(np.abs(side))
        return self.block(i, j)[:, best] / side[best]

    def side(self, i, j):
        return 2 if j > i else 3

    def through_even(self, f):
        return 4 + f if f else 0

    def build(self, j):
        n, fine, many, end = self.n, self.fine, self.functional_count, self.count - 1
        targets = self.following.needs[j] if self.following else []
        others = [j ^ k for k in range(1, self.count)]
        at = lambda i, f: fine + many * ((i ^ j) - 1) + f
        product = np.zeros((n + len(targets), fine + many * len(others)))
        even, used = np.zeros_like(product), np.zeros(product.shape[1], bool)
        used[:fine] = True
        product[:n, :fine] = self.block(j, j)
        even[:n, :fine] = self.even
        first, last = [self.first[self.rows(j)]], [self.last[self.rows(j)]]
        for i in others:
            product[:n, at(i, self.side(j, i))] = self.reach(j, i)
            used[at(i, self.side(j, i))] = True
        for row, (i, f) in enumerate(targets, n):
            inner = self.following.functionals[i][f]
            product[row, :fine] = inner @ self.block(i, j)
            product[row, at(i, 4 + self.kept + f)] = 1.0
            even[row, at(i, self.through_even(f))] = 1.0
            used[at(i, 4 + self.kept + f)] = used[at(i, self.through_even(f))] = True
            for other in others:
                if other != i:
                    product[row, at(other, self.side(i, other))] = inner @ self.reach(i, other)
                    used[at(other, self.side(i, other))] = True
            first.append([inner @ self.first[self.rows(i)]])
            last.append([inner @ self.last[self.rows(i)]])
        around = even.copy()
        from_first, from_last = 0 if j == 0 else at(0, 0), fine - 2 if j == end else at(end, 1)
        around[:, from_first] += np.concatenate(first)
        around[:, from_last] += np.concatenate(last)
        used[from_first] = used[from_last] = True
        if j < end:
            used[at(j + 1, 0)] = True
        needs = [(j ^ (1 + place // many), place % many) for place in np.flatnonzero(used[fine:])]
        return needs, (product[:, used], even[:, used], around[:, used])

    def sent(self, i, k):
        return [f for block, f in self.needs[i ^ k] if block == i]

    def most_sent(self):
        return max([len(self.sent(i, k)) for i in range(self.count) for k in range(1, self.count)] + [1])

    def most_needed(self):
        return max(len(needs) for needs in self.needs)

    def next_first(self, j, own, fallback):
        return fallback if j == self.count - 1 else own + self.needs[j].index((j + 1, 0))


def interpolation(level, j, inputs, coarse=False):
    table = np.zeros((level.fine, inputs))
    if coarse:
        places = list(range(level.n))
        last = level.following.next_first(j, level.n, level.n - 1)
    else:
        places = [2 * c for c in range(level.n)]
        last = level.next_first(j, level.fine, level.fine - 2)
    places.append(last)
    for c in range(level.n):
        table[2 * c, places[c]] = 1.0
        table[2 * c + 1, places[c]] += 0.5
        table[2 * c + 1, places[c + 1]] += 0.5
    return table


def chain(whole, count, levels):
    made = None
    for depth in reversed(range(levels)):
        made = Level(whole >> depth, count, made)
    return made


def padded(table, rows, cols):
    out = np.zeros((rows, cols))
    out[: table.shape[0], : table.shape[1]] = table
    return out


highest = lax.Precision.HIGHEST


def dot(a, b, dims=((1,), (0,))):
    return lax.dot_general(a, b, (dims, ((), ())), precision=highest, preferred_element_type=jnp.float32)


def kernel_call(body, outs, arrays, scratch=(), left=(), left_out=(), aliases={}):
    space = lambda place, where: pl.BlockSpec(memory_space=pltpu.HBM if place in where else pltpu.VMEM)
    return pl.pallas_call(
        body,
        out_shape=[jax.ShapeDtypeStruct(shape, jnp.float32) for shape in outs],
        in_specs=[space(i, left) for i in range(len(arrays))],
        out_specs=[space(i, left_out) for i in range(len(outs))],
        scratch_shapes=list(scratch),
        input_output_aliases=aliases,
        compiler_params=pltpu.CompilerParams(vmem_limit_bytes=40 << 20),
    )(*(pltpu.with_memory_space_constraint(a, pltpu.HBM) if i in left else a for i, a in enumerate(arrays)))


def swapped(values, axis):
    count = lax.axis_size(axis)
    return [lax.ppermute(v, axis, [(i, i ^ k) for i in range(count)]) for k, v in enumerate(values, 1)]


def gathered(value, axis, beside):
    count = lax.axis_size(axis)
    if count != 4:
        return swapped([value] * (count - 1), axis), beside
    by = lambda k, what: lax.ppermute(what, axis, [(i, i ^ k) for i in range(count)])
    far, beside = lax.optimization_barrier((by(2, value), beside))
    return [by(1, value), far, by(1, far)], beside


def chosen_by(values, j):
    chosen = float(values[0])
    for place in range(1, len(values)):
        if any(values[place] != values[0] for place in range(len(values))):
            chosen = jnp.where(j == place, f32(values[place]), chosen)
    return chosen


def iota(shape, dim):
    return lax.broadcasted_iota(jnp.int32, shape, dim)


def shards(counts, field):
    dz, dx, dy = counts
    lz, lx, ly = field.shape
    nz, nx, ny = lz * dz, lx * dx, ly * dy

    yone = chain(ny, dy, 3)
    ytwo, ythree = yone.following, yone.following.following
    xone = chain(nx, dx, 1)
    xtwo = chain(nx // 2, dx, 2)
    xthree = xtwo.following
    zone = Level(nz, dz, None)

    points_a = lambda fs: [f for f in fs if f in (2, 3) or f >= 4 + yone.kept]
    points_s = lambda fs: [f for f in fs if f not in (2, 3) and f < 4 + yone.kept]
    pairs_y = [(i, k) for i in range(dy) for k in range(1, dy)]
    sa = max([len(points_a(yone.sent(i, k))) for i, k in pairs_y] + [0]) + 1
    ss = max([len(points_s(yone.sent(i, k))) for i, k in pairs_y] + [1])
    per_row = (lz * lx) // ((lz // 2) * (lx // 2))
    rowsy = round_up(sa + -(-ss // per_row), 8)
    sa8, ss8 = round_up(sa, 8), round_up(ss, 8)
    wide1 = yone.n + ytwo.most_needed()
    wide2 = ytwo.n + ythree.most_needed()
    wide = packed = round_up(max(wide1 + 1, 3 * wide2, wide2 + wide1), 128)
    kx = round_up(xtwo.most_sent(), 8)
    rowsx = xtwo.fine + kx * (dx - 1)
    tall = round_up(max(xtwo.n + xthree.most_needed() + 1, xone.n // 2 + 1), 8)

    others_y = max(dy - 1, 1)
    fya = np.zeros((dy, others_y * sa8, ly))
    fys = np.zeros((dy, others_y * ss8, ly))
    ta = np.zeros((dy, ly, wide))
    wa = np.zeros((dy, others_y * rowsy, wide))
    tsm = np.zeros((dy, ly, 2 * wide))
    wsm = np.zeros((dy, others_y * ss8, 2 * wide))
    for j in range(dy):
        product, even, around = yone.tables[j]
        used = product.shape[0]
        ta[j, :, :used] = product[:, :ly].T
        tsm[j, :, :used] = even[:, :ly].T
        tsm[j, :, wide : wide + used] = around[:, :ly].T
        for k in range(1, dy):
            mine = yone.sent(j, k)
            fya[j, (k - 1) * sa8 :][: len(points_a(mine))] = yone.functionals[j][points_a(mine)]
            fya[j, (k - 1) * sa8 + sa - 1] = yone.functionals[j][0]
            fys[j, (k - 1) * ss8 :][: len(points_s(mine))] = yone.functionals[j][points_s(mine)]
            came = yone.sent(j ^ k, k)
            for f in came:
                column = ly + yone.needs[j].index((j ^ k, f))
                if f in points_a(came):
                    wa[j, (k - 1) * rowsy + points_a(came).index(f), :used] = product[:, column]
                else:
                    row = (k - 1) * ss8 + points_s(came).index(f)
                    wsm[j, row, :used] = even[:, column]
                    wsm[j, row, wide : wide + used] = around[:, column]
        if j == dy - 1:
            ta[j, ly - 2, wide - 1] = 0.5
        else:
            wa[j, rowsy * ((j ^ (j + 1)) - 1) + sa - 1, wide - 1] = 0.5

    ext = round_up(max(dx - 1, 1), 8)
    fx = np.zeros((dx, lx, 8))
    txa = np.zeros((dx, xone.n, lx + ext))
    txm = np.zeros((dx, xone.n, xone.n + ext))
    for j in range(dx):
        fx[j, :, :2] = xone.functionals[j][2:4].T
        product, even, around = xone.tables[j]
        txa[j, :, :lx] = product[:, :lx]
        txm[j, :, : xone.n] = around[:, :lx:2]
        for column, (i, f) in enumerate(xone.needs[j], lx):
            if f in (2, 3):
                txa[j, :, lx + (i ^ j) - 1] = product[:, column]
            else:
                txm[j, :, xone.n + (i ^ j) - 1] += around[:, column] * ((f == 0 and i == 0) or (f == 1 and i == dx - 1))

    zn = zone.n
    zs = np.zeros((dz, 2 * lz + 2 + zn * (lz + dz + 1)))
    for j in range(dz):
        cv, cw = zone.v[j], zone.w[j]
        k_last = (zone.last[zone.rows(0)] / zone.reach(0, j))[0] if 0 < j == dz - 1 else 0.0
        k_first = (zone.first[zone.rows(dz - 1)] / zone.reach(dz - 1, j))[-1] if j == 0 and dz > 1 else 0.0
        parts = [cv, cw, [k_last, k_first], zone.block(j, j).reshape(-1)]
        parts += [zone.reach(j, j ^ k) for k in range(1, dz)]
        parts += [zone.first[zone.rows(j)] * (j == 0), zone.last[zone.rows(j)] * (j == dz - 1)]
        zs[j] = np.concatenate([np.asarray(p, np.float64) for p in parts])
    at_local = 2 * lz + 2
    at_reach = at_local + zn * lz
    at_first = at_reach + zn * (dz - 1)
    at_last = at_first + zn

    f2x = np.zeros((dx, max(dx - 1, 1) * kx, xtwo.fine))
    tx2 = np.zeros((dx, 3 * tall, rowsx))
    qx2 = np.zeros((dx, xtwo.fine, rowsx))
    tx3 = np.zeros((dx, 3 * xthree.n, tall))
    qx3 = np.zeros((dx, xthree.fine, tall))
    px3 = np.zeros((dx, xtwo.fine, tall))
    for j in range(dx):
        columns = list(range(xtwo.fine))
        for i, f in xtwo.needs[j]:
            columns.append(xtwo.fine + kx * ((i ^ j) - 1) + xtwo.sent(i, i ^ j).index(f))
        for c, table in enumerate(xtwo.tables[j]):
            tx2[j, c * tall : c * tall + table.shape[0], columns] = table.T
        qx2[j][:, columns] = interpolation(xtwo, j, len(columns))
        tx2[j, tall - 1, xtwo.fine :] = qx2[j, -1, xtwo.fine :]
        for k in range(1, dx):
            mine = xtwo.sent(j, k)
            f2x[j, (k - 1) * kx :][: len(mine)] = xtwo.functionals[j][mine]
        for c, table in enumerate(xthree.tables[j]):
            tx3[j, c * xthree.n : (c + 1) * xthree.n, : table.shape[1]] = table
        qx3[j] = interpolation(xthree, j, tall)
        px3[j] = interpolation(xtwo, j, tall, True)

    ty2 = np.zeros((dy, 3 * wide, packed))
    qy2 = np.zeros((dy, wide, round_up(ytwo.fine, 128)))
    ty3 = np.zeros((dy, 3 * packed, 128))
    qy3 = np.zeros((dy, packed, 128))
    py3 = np.zeros((dy, packed, round_up(ytwo.fine, 128)))
    px1 = np.zeros((lx, 2 * tall))
    py1 = np.zeros((dy, packed, ly))
    for j in range(dy):
        for c, table in enumerate(ytwo.tables[j]):
            ty2[j, c * wide : c * wide + table.shape[1], c * wide2 : c * wide2 + table.shape[0]] = table.T
        qy2[j, :, : ytwo.fine] = interpolation(ytwo, j, wide).T
        for c, table in enumerate(ythree.tables[j]):
            ty3[j, c * packed : c * packed + table.shape[1], : ythree.n] = (-1.0 if c == 2 else 1.0) * table.T
        qy3[j, :, : ythree.fine] = interpolation(ythree, j, packed).T
        py1[j, wide2:] = interpolation(yone, j, packed - wide2, True).T
        py3[j, wide2:, : ytwo.fine] = interpolation(ytwo, j, packed - wide2, True).T
    for c in range(xone.n):
        begin = c if c < xtwo.n else tall + c - xtwo.n
        px1[2 * c, begin] = 1.0
        px1[2 * c + 1, begin : begin + 2] = 0.5
    az2, first2, last2 = (t.tolist() for t in dense(nz // 2))
    az3, first3, last3 = dense(nz // 4)
    z2, z3 = nz // 2, nz // 4
    lz2, lz3 = lz // 2, lz // 4
    zt = np.concatenate([az3, first3[:, None], last3[:, None]], axis=1)
    zt = zt.reshape(dz, (lz // 8) * (z3 + 2))
    lz4 = lz // 8

    to32 = lambda table: jnp.asarray(table, jnp.float32)

    def stacked(*tables):
        cols = max(t.shape[2] for t in tables)
        starts = np.cumsum([0] + [round_up(t.shape[1], 8) for t in tables])
        out = np.zeros((tables[0].shape[0], starts[-1], cols))
        for t, begin in zip(tables, starts):
            out[:, begin : begin + t.shape[1], : t.shape[2]] = t
        return to32(out), [int(v) for v in starts]

    messages_y, _ = stacked(fya, fys)
    tables_y, _ = stacked(np.concatenate([ta, tsm], axis=2), np.concatenate([wa, np.zeros((dy, wa.shape[1], 2 * wide))], axis=2),
                          np.concatenate([np.zeros((dy, wsm.shape[1], wide)), wsm], axis=2))
    tables_x, _ = stacked(txa, txm)
    tables_x3, at_x3 = stacked(tx3, qx3, px3)
    tables_y3, at_y3 = stacked(ty3, qy3, py3, py1)
    hz, hx1 = lz // 2, lx // 2
    ly2 = round_up(ytwo.fine, 128)

    def y_messages(u_hbm, table_hbm, ty_hbm, fx_hbm, u_ref, ty_ref, fx_ref, *refs):
        outs, (table, sems) = refs[:-2], refs[-2:]
        j = lax.axis_index("gy")
        nt = ((1,), (1,))
        copies = [
            pltpu.make_async_copy(table_hbm.at[j], table, sems.at[0]),
            pltpu.make_async_copy(u_hbm, u_ref, sems.at[1]),
            pltpu.make_async_copy(ty_hbm.at[j], ty_ref, sems.at[2]),
            pltpu.make_async_copy(fx_hbm.at[lax.axis_index("gx")], fx_ref, sems.at[3]),
        ]
        for copy in copies:
            copy.start()
        for copy in copies[:2]:
            copy.wait()
        lines = dot(table[: others_y * sa8], u_ref[...].reshape(lz * lx, ly), nt)
        even = jnp.concatenate([u_ref[2 * z, pl.ds(0, hx1, stride=2), :] for z in range(hz)], axis=0)
        points = dot(table[others_y * sa8 :], even, nt)
        for k, out in enumerate(outs):
            out[: min(sa8, rowsy)] = lines[k * sa8 : k * sa8 + min(sa8, rowsy)]
            if rowsy > sa8:
                out[sa8:] = jnp.zeros_like(out[sa8:])
            for f in range(ss):
                begin = hz * hx1 * (f % per_row)
                row = sa + f // per_row
                out[row : row + 1, begin : begin + hz * hx1] = points[k * ss8 + f : k * ss8 + f + 1]
        for copy in copies[2:]:
            copy.wait()

    def along_y(u, half_halo):
        lane = iota(u.shape, 1)
        before, after = pltpu.roll(u, 1, 1), pltpu.roll(u, ly - 1, 1)
        edge = 0.5 * before + jnp.broadcast_to(half_halo, u.shape)
        return jnp.where(lane == ly - 1, edge, jnp.where(lane % 2 == 1, 0.5 * (before + after), u))

    def from_next(jx, own, rows):
        for k, other in enumerate(rows):
            own = jnp.where((jx ^ (k + 1)) == jx + 1, other, own)
        return own

    def y_apply(*refs):
        u_ref, came = refs[0], refs[1:dy]
        ty_ref, fx_ref, ta_out, tsm_out = refs[dy : dy + 4]
        xm_outs, points = refs[dy + 4 : -1], refs[-1]
        jx = lax.axis_index("gx")
        tn = ((0,), (0,))
        ta_all = dot(u_ref[...].reshape(lz * lx, ly), ty_ref[:ly, :wide])
        even = jnp.concatenate([u_ref[2 * z, pl.ds(0, hx1, stride=2), :] for z in range(hz)], axis=0)
        tsm_all = dot(even, ty_ref[:ly, wide:])
        for k, ref in enumerate(came):
            begin = ly + rowsy * k
            ta_all += dot(ref[...], ty_ref[begin : begin + rowsy, :wide], tn)
            points[...] = jnp.zeros_like(points)
            for f in range(ss):
                begin = hz * hx1 * (f % per_row)
                row = sa + f // per_row
                points[f : f + 1] = ref[row : row + 1, begin : begin + hz * hx1]
            begin = ly + rowsy * (dy - 1) + ss8 * k
            tsm_all += dot(points[...], ty_ref[begin : begin + ss8, wide:], tn)
        ta_out[...] = ta_all
        tsm_out[...] = tsm_all
        weights = [jnp.broadcast_to(fx_ref[:, c : c + 1], (lx, wide)) for c in range(2)]
        for out in xm_outs:
            out[lz + 2 * hz :] = jnp.zeros_like(out[lz + 2 * hz :])
            out[lz + 2 * hz : lz + 2 * hz + 1, :wide] = tsm_all[0:1, :wide]
        for z in range(lz):
            part = ta_all[z * lx : (z + 1) * lx]
            v, w = (jnp.sum(part * weight, axis=0, keepdims=True) for weight in weights)
            for k, out in enumerate(xm_outs):
                out[z : z + 1, :wide] = jnp.where((jx ^ (k + 1)) < jx, v, w)
            if z % 2 == 0:
                half = z // 2
                tm = tsm_all[half * hx1 : (half + 1) * hx1, wide:]
                iy = along_y(u_ref[z, :8], part[:8, wide - 1 :])
                for out in xm_outs:
                    out[lz + half : lz + half + 1, :wide] = jnp.where(jx == 0, tm[0:1], tm[hx1 - 1 : hx1])
                    out[lz + hz + half : lz + hz + half + 1, :ly] = iy[0:1]

    def x_apply(*refs):
        ta_ref, tsm_ref = refs[:2]
        came = refs[2 : 1 + dx][::-1]
        tx_ref, f2x_ref, zc_out, u1_out = refs[1 + dx : 5 + dx]
        planes_out, xt_outs, rest = refs[5 + dx : 4 + dx + dz], refs[4 + dx + dz : -1], refs[-1]
        jx, jz = lax.axis_index("gx"), lax.axis_index("gz")
        xa, xm, diff = [], [], []

        rest[...] = jnp.zeros_like(rest)
        for k, r in enumerate(came):
            for z in range(lz):
                rest[z, k : k + 1, :wide] = r[z : z + 1, :wide]
            for half in range(hz):
                rest[half, k : k + 1, wide:] = r[lz + half : lz + half + 1, :wide]
        for z in range(0, lz, 2):
            pair = jnp.concatenate([ta_ref[z * lx : (z + 1) * lx, :], ta_ref[(z + 1) * lx : (z + 2) * lx, :]], axis=1)
            more = jnp.concatenate([rest[z, :, :wide], rest[z + 1, :, :wide]], axis=1)
            both = dot(tx_ref[jx, : xone.n], jnp.concatenate([pair, more], axis=0))
            xa += [both[:, :wide], both[:, wide:]]
        zc_out[...] = jnp.zeros_like(zc_out)
        zc_out[:hx1] = tsm_ref[:hx1, :wide]
        begin = lz + 2 * hz
        zc_out[hx1 : hx1 + 1] = from_next(jx, tsm_ref[hx1 - 1 : hx1, :wide], [r[begin : begin + 1, :wide] for r in came])
        for half in range(0, hz, 2):
            pair = jnp.concatenate([tsm_ref[h * hx1 : (h + 1) * hx1, wide:] for h in (half, half + 1)], axis=1)
            more = jnp.concatenate([rest[half, :, wide:], rest[half + 1, :, wide:]], axis=1)
            both = dot(tx_ref[jx, xone.n :, : xone.n + ext], jnp.concatenate([pair, more], axis=0))
            xm += [both[:, :wide], both[:, wide:]]
        for half in range(hz):
            diff.append(tsm_ref[half * hx1 : (half + 1) * hx1, :wide] - xm[half])
        scalar = lambda place: chosen_by(zs[:, place], jz)
        totals = []
        for zc in range(zn):
            total = diff[zc] - scalar(at_first + zc) * xm[0] - scalar(at_last + zc) * xm[hz - 1]
            for z in range(lz):
                total += scalar(at_local + zc * lz + z) * xa[z]
            u1_out[zc] = total
            totals.append(total)
        v = -scalar(2 * lz) * xm[hz - 1]
        w = -scalar(2 * lz + 1) * xm[0]
        for z in range(lz):
            v += scalar(z) * xa[z]
            w += scalar(lz + z) * xa[z]
        for k, out in enumerate(planes_out):
            out[...] = jnp.where((jz ^ (k + 1)) > jz, w, v)
        sent = dot(f2x_ref[jx], jnp.concatenate(totals + [v, w], axis=1))
        for k, out in enumerate(xt_outs):
            out[...] = sent[k * kx : (k + 1) * kx]

    def interpolate(*refs):
        u_ref, ta_ref, u1_ref = refs[:3]
        came, xcame = refs[3 : 2 + dx][::-1], refs[2 + dx : 1 + 2 * dx][::-1]
        qx2_ref, qy2_ref, fine_out, ixy_out, i2_out = refs[1 + 2 * dx :]
        jx, jy = lax.axis_index("gx"), lax.axis_index("gy")
        row = iota((lx, ly), 0)
        planes = []
        for half in range(hz):
            iy = along_y(u_ref[2 * half], ta_ref[2 * half * lx : (2 * half + 1) * lx, wide - 1 :])
            begin = lz + hz + half
            halo = from_next(jx, iy[lx - 2 : lx - 1], [r[begin : begin + 1, :ly] for r in came])
            before, after = pltpu.roll(iy, 1, 0), pltpu.roll(iy, lx - 1, 0)
            after = jnp.where(row == lx - 1, jnp.broadcast_to(halo, (lx, ly)), after)
            planes.append(jnp.where(row % 2 == 1, 0.5 * (before + after), iy))
        for half in range(hz):
            fine_out[2 * half] = u_ref[2 * half] - planes[half]
            if half + 1 < hz:
                fine_out[2 * half + 1] = u_ref[2 * half + 1] - 0.5 * (planes[half] + planes[half + 1])
        ixy_out[...] = planes[-1]
        evens = range(0, zn, 2)
        state = [jnp.concatenate([u1_ref[z] for z in evens], axis=1)]
        state += [jnp.concatenate([r[:, z * wide : (z + 1) * wide] for z in evens], axis=1) for r in xcame]
        spread = dot(qx2_ref[jx], jnp.concatenate(state, axis=0))
        spread = jnp.concatenate([spread[:, half * wide : (half + 1) * wide] for half in range(zn // 2)], axis=0)
        spread = dot(spread, qy2_ref[jy])
        for half in range(zn // 2):
            i2_out[half] = spread[half * xtwo.fine : (half + 1) * xtwo.fine]

    def second_apply(*refs):
        part_ref, zc_ref = refs[:2]
        xcame, zcame = refs[2 : dx + 1][::-1], refs[dx + 1 : dz + dx][::-1]
        tx2_ref, ty2_ref, u1_out, zt_out = refs[dz + dx :]
        jx, jy, jz = lax.axis_index("gx"), lax.axis_index("gy"), lax.axis_index("gz")
        own = []
        for zc in range(zn):
            total = part_ref[zc]
            for k, r in enumerate(zcame):
                total += chosen_by(zs[:, at_reach + k * zn + zc], jz) * r[...]
            u1_out[zc] = total
            own.append(total)
        own = jnp.concatenate(own + [jnp.zeros_like(own[0])] * 2, axis=1)
        across = dot(tx2_ref[jx], jnp.concatenate([own] + [r[...] for r in xcame], axis=0))
        cut = [across[:, z * wide : (z + 1) * wide] for z in range(zn + 2)]
        whole = [z for z in range(zn + 2) if z % 2 == 0 or z >= zn]
        joined = [jnp.concatenate([cut[z][c * tall : (c + 1) * tall] for c in range(3)], axis=1) for z in whole]
        made = dot(jnp.concatenate(joined, axis=0), ty2_ref[jy])
        for place, z in enumerate(whole):
            zt_out[z] = made[place * tall : (place + 1) * tall]
        made = dot(jnp.concatenate([cut[z][:tall] for z in range(1, zn, 2)], axis=0), ty2_ref[jy, :wide])
        for z in range(1, zn, 2):
            moved = made[(z // 2) * tall : (z // 2 + 1) * tall]
            if z < 4:
                begin = xtwo.n * (z // 2)
                moved += pltpu.roll(zc_ref[begin : begin + tall], wide2, 1)
            zt_out[z] = moved
        for z in (zn, zn + 1):
            zt_out[z, tall - 1 :] = cut[z][tall - 1 : tall]

    def third_apply(*refs):
        u1_ref, i2_ref, u_ref, ixy_ref, _, own_ref = refs[:6]
        came = refs[6 : 5 + dz]
        px1_ref, tx_ref, ty_ref, qy2_ref, fine_out, middle_out, coarse_out, coarsest_out = refs[5 + dz : 13 + dz]
        zbuf, qbuf, ubuf, last, middle, sems = refs[13 + dz :]
        part = lambda ref, j, starts, which: ref[j, starts[which] : starts[which + 1]]
        jx, jy, jz = lax.axis_index("gx"), lax.axis_index("gy"), lax.axis_index("gz")
        for k, r in enumerate((own_ref, *came)):
            zbuf[pl.ds((jz ^ k) * lz2, lz2)] = r[:lz2]
            qbuf[pl.ds((jz ^ k) * 2, 2)] = r[lz2:]
        at = jnp.minimum(jz + 1, dz - 1) * lz2
        plane_halo = dot(px1_ref[...], jnp.concatenate([zbuf[at + 1], zbuf[at + 3]], axis=0))
        everything = []
        for j in range(dz):
            for zc in range(lz2):
                total = zbuf[j * lz2 + zc]
                for i in range(dz):
                    if i != j:
                        total += float(zone.reach(j, i)[zc]) * qbuf[2 * i + (i < j)]
                everything.append(total)
        for z in range(0, z2, lz2):
            zbuf[z] = everything[z]
        if lz2 > 2:
            zbuf[z2 - 2] = everything[z2 - 2]
        at = jnp.minimum((jz + 1) * lz2, z2 - 2)
        halo = dot(part(tx_ref, jx, at_x3, 2), zbuf[at])
        edges = [jnp.zeros((1, wide), jnp.float32)] * (lz2 // 2)
        for k, r in enumerate(came):
            line = jnp.where((jz ^ (k + 1)) > jz, r[lz2, tall - 1 :], r[lz2 + 1, tall - 1 :])
            for half in range(lz2 // 2):
                edges[half] += chosen_by(zs[:, at_reach + k * zn + 2 * half], jz) * line
        fy = ytwo.fine
        edges = dot(jnp.concatenate(edges + [jnp.zeros((8 - lz2 // 2 % 8, wide), jnp.float32)], axis=0), qy2_ref[jy])
        plane_halo = dot(plane_halo, part(ty_ref, jy, at_y3, 3))
        halo = dot(halo, part(ty_ref, jy, at_y3, 2))[:, :fy]
        here = ixy_ref[...]
        last[...] = u_ref[lz - 1] - 0.5 * (here + jnp.where(jz == dz - 1, here, plane_halo))
        copies = [pltpu.make_async_copy(last, fine_out.at[lz - 1], sems.at[0])]
        copies[0].start()
        at_end = iota((xtwo.fine, fy), 0) == xtwo.fine - 1
        spread = [
            i2_ref[half][:, :fy] + jnp.where(at_end, jnp.broadcast_to(edges[half : half + 1, :fy], (xtwo.fine, fy)), 0.0)
            for half in range(lz2 // 2)
        ]
        spread.append(halo)
        for half in range(lz2 // 2):
            middle[2 * half] = u1_ref[2 * half][:, :fy] - spread[half]
            middle[2 * half + 1] = u1_ref[2 * half + 1][:, :fy] - 0.5 * (spread[half] + spread[half + 1])
        copies.append(pltpu.make_async_copy(middle, middle_out, sems.at[1]))
        copies[1].start()
        evens = [pltpu.roll(everything[z], packed - wide2, 1) for z in range(0, z2, 2)]
        arounds = [pltpu.roll(everything[z], packed - 2 * wide2, 1) for z in range(0, z2, 2)]
        second = []
        for zc in range(z3):
            total = evens[zc] - arounds[zc] - first2[zc] * arounds[0] - last2[zc] * arounds[-1]
            for z in range(z2):
                total += az2[zc][z] * everything[z]
            ubuf[zc] = total
            second.append(total)
        fy3, n3 = ythree.fine, xthree.n
        at = [jnp.minimum(jz * lz3 + 2 * half, z3 - 2) for half in range(lz3 // 2 + 1)]
        spread = dot(part(tx_ref, jx, at_x3, 1), jnp.concatenate([ubuf[a] for a in at], axis=1))
        joined = []
        for zc in range(lz4):
            base = zc * (z3 + 2)
            along = chosen_by(zt[:, base], jz) * second[0]
            for z in range(1, z3):
                along += chosen_by(zt[:, base + z], jz) * second[z]
            even = ubuf[2 * (jz * lz4 + zc)]
            around = even + chosen_by(zt[:, base + z3], jz) * second[0] + chosen_by(zt[:, base + z3 + 1], jz) * second[z3 - 2]
            parts = [dot(tx_ref[jx, c * n3 : (c + 1) * n3, :], plane) for c, plane in enumerate((along, even, around))]
            joined.append(jnp.concatenate(parts, axis=1))
        spread = jnp.concatenate([spread[:, h * packed : (h + 1) * packed] for h in range(len(at))], axis=0)
        spread = dot(spread, part(ty_ref, jy, at_y3, 1))[:, :fy3]
        coarsest = dot(jnp.concatenate(joined, axis=0), part(ty_ref, jy, at_y3, 0))[:, : ythree.n]
        for zc in range(lz4):
            coarsest_out[zc] = coarsest[zc * n3 : (zc + 1) * n3]
        spread = [spread[h * xthree.fine : (h + 1) * xthree.fine] for h in range(len(at))]
        for half in range(lz3 // 2):
            at = jz * lz3 + 2 * half
            coarse_out[2 * half] = ubuf[at][: xthree.fine, :fy3] - spread[half]
            coarse_out[2 * half + 1] = ubuf[at + 1][: xthree.fine, :fy3] - 0.5 * (spread[half] + spread[half + 1])
        for copy in copies:
            copy.wait()

    u, own_ty, own_fx, *ym = kernel_call(
        y_messages,
        [(lz, lx, ly), tables_y.shape[1:], fx.shape[1:]] + [(rowsy, lz * lx)] * (dy - 1),
        [field, messages_y, tables_y, to32(fx)],
        scratch=[pltpu.VMEM(messages_y.shape[1:], jnp.float32), pltpu.SemaphoreType.DMA((4,))],
        left=(0, 1, 2, 3),
    )
    ycame = swapped(ym, "gy")
    ta_v, tsm_v, *xm = kernel_call(
        y_apply,
        [(lz * lx, wide), (hz * hx1, 2 * wide)] + [(round_up(lz + 2 * hz + 1, 8), max(wide, ly))] * (dx - 1),
        [u, *ycame, own_ty, own_fx],
        scratch=[pltpu.VMEM((ss8, hz * hx1), jnp.float32)],
    )
    xcame = swapped(xm, "gx")
    zc, u1_part, *sent = kernel_call(
        x_apply,
        [(xtwo.n + tall, wide), (zn, xone.n, wide)]
        + [(xone.n, wide)] * (dz - 1)
        + [(kx, (zn + 2) * wide)] * (dx - 1),
        [ta_v, tsm_v, *xcame[::-1], tables_x, to32(f2x)],
        scratch=[pltpu.VMEM((lz, ext, 2 * wide), jnp.float32)],
    )
    tails = sent[dz - 1 :]
    zcame = swapped(sent[: dz - 1], "gz")
    if dz > 1 and dx > 1:
        zcame[0], tails[0] = lax.optimization_barrier((zcame[0], tails[0]))
    xtcame = swapped(tails, "gx")
    u1, zmsg = kernel_call(
        second_apply,
        [(zn, xone.n, wide), (lz2 + 2, tall, packed)],
        [u1_part, zc, *xtcame[::-1], *zcame[::-1], to32(tx2), to32(ty2)],
    )
    beside = kernel_call(
        interpolate,
        [(lz, lx, ly), (lx, ly), (lz2 // 2, xtwo.fine, ly2)],
        [u, ta_v, u1, *xcame[::-1], *xtcame[::-1], to32(qx2), to32(qy2)],
    )
    ztcame, (fine, ixy, i2) = gathered(zmsg, "gz", beside)
    return kernel_call(
        third_apply,
        [(lz, lx, ly), (lz2, xtwo.fine, ytwo.fine), (lz3, xthree.fine, ythree.fine), (lz4, xthree.n, ythree.n)],
        [u1, i2, u, ixy, fine, zmsg, *ztcame, to32(px1), tables_x3, tables_y3, to32(qy2)],
        scratch=[
            pltpu.VMEM((z2, tall, packed), jnp.float32),
            pltpu.VMEM((2 * dz, tall, packed), jnp.float32),
            pltpu.VMEM((z3, tall, packed), jnp.float32),
            pltpu.VMEM((lx, ly), jnp.float32),
            pltpu.VMEM((lz2, xtwo.fine, ytwo.fine), jnp.float32),
            pltpu.SemaphoreType.DMA((2,)),
        ],
        left=(4,),
        left_out=(0, 1),
        aliases={4: 0},
    )


def solution(mesh):
    spec = P("gz", "gx", "gy")
    counts = tuple(mesh.shape[a] for a in ("gz", "gx", "gy"))
    return jax.shard_map(
        functools.partial(shards, counts), mesh=mesh, in_specs=(spec,), out_specs=(spec,) * 4, check_vma=False
    )
```

```python
import functools
import math

import jax
import jax.numpy as jnp
import numpy as np
from jax import lax
from jax.experimental import pallas as pl
from jax.experimental.pallas import tpu as pltpu
from jax.sharding import PartitionSpec as P

band_ratio = 2.0 - math.sqrt(3.0)
f32 = np.float32


def round_up(value, unit):
    return -(-value // unit) * unit


def dense(fine):
    n = fine // 2
    steps = np.arange(n)[:, None] - np.arange(n)[None, :]
    lower = np.where(steps >= 0, (-band_ratio) ** np.maximum(steps, 0), 0.0)
    inverse = lower.T @ lower
    mass = 4.0 * np.eye(fine) + np.eye(fine, k=1) + np.eye(fine, k=-1)
    weights = np.where(np.arange(n) == n - 1, 1.0, 0.5)[:, None]
    earlier = np.concatenate([np.zeros((1, fine)), mass[1::2][:-1]])
    product = inverse @ (0.5 * band_ratio * (mass[0::2] + weights * mass[1::2] + 0.5 * earlier))
    return product, inverse[:, 0] * (3 * band_ratio - 1), inverse[:, -1] * (2 * band_ratio)


class Level:
    def __init__(self, whole, count, following):
        self.count, self.fine = count, whole // count
        self.n = self.fine // 2
        self.product, self.first, self.last = dense(whole)
        self.following = following
        self.kept = following.functional_count if following else 0
        self.functional_count = 4 + 2 * self.kept
        self.even = np.zeros((self.n, self.fine))
        self.even[np.arange(self.n), 2 * np.arange(self.n)] = 1.0
        self.v = [self.towards(i, i * self.n - 1) for i in range(count)]
        self.w = [self.towards(i, (i + 1) * self.n) for i in range(count)]
        self.functionals = []
        for i in range(count):
            own = np.zeros((4, self.fine))
            own[0, 0] = own[1, self.fine - 2] = 1.0
            own[2], own[3] = self.v[i], self.w[i]
            if following:
                inner = following.functionals[i]
                own = np.concatenate([own, inner @ self.even, inner @ self.block(i, i)])
            self.functionals.append(own)
        built = [self.build(j) for j in range(count)]
        self.needs = [needs for needs, _ in built]
        self.tables = [tables for _, tables in built]

    def rows(self, i):
        return slice(i * self.n, (i + 1) * self.n)

    def block(self, i, j):
        return self.product[self.rows(i), j * self.fine : (j + 1) * self.fine]

    def towards(self, i, row):
        if not 0 <= row < self.count * self.n:
            return np.zeros(self.fine)
        values = self.product[row, i * self.fine : (i + 1) * self.fine]
        return values / np.abs(values).max()

    def reach(self, i, j):
        side = self.v[j] if j > i else self.w[j]
        best = np.argmax(np.abs(side))
        return self.block(i, j)[:, best] / side[best]

    def side(self, i, j):
        return 2 if j > i else 3

    def through_even(self, f):
        return 4 + f if f else 0

    def build(self, j):
        n, fine, many, end = self.n, self.fine, self.functional_count, self.count - 1
        targets = self.following.needs[j] if self.following else []
        others = [j ^ k for k in range(1, self.count)]
        at = lambda i, f: fine + many * ((i ^ j) - 1) + f
        product = np.zeros((n + len(targets), fine + many * len(others)))
        even, used = np.zeros_like(product), np.zeros(product.shape[1], bool)
        used[:fine] = True
        product[:n, :fine] = self.block(j, j)
        even[:n, :fine] = self.even
        first, last = [self.first[self.rows(j)]], [self.last[self.rows(j)]]
        for i in others:
            product[:n, at(i, self.side(j, i))] = self.reach(j, i)
            used[at(i, self.side(j, i))] = True
        for row, (i, f) in enumerate(targets, n):
            inner = self.following.functionals[i][f]
            product[row, :fine] = inner @ self.block(i, j)
            product[row, at(i, 4 + self.kept + f)] = 1.0
            even[row, at(i, self.through_even(f))] = 1.0
            used[at(i, 4 + self.kept + f)] = used[at(i, self.through_even(f))] = True
            for other in others:
                if other != i:
                    product[row, at(other, self.side(i, other))] = inner @ self.reach(i, other)
                    used[at(other, self.side(i, other))] = True
            first.append([inner @ self.first[self.rows(i)]])
            last.append([inner @ self.last[self.rows(i)]])
        around = even.copy()
        from_first, from_last = 0 if j == 0 else at(0, 0), fine - 2 if j == end else at(end, 1)
        around[:, from_first] += np.concatenate(first)
        around[:, from_last] += np.concatenate(last)
        used[from_first] = used[from_last] = True
        if j < end:
            used[at(j + 1, 0)] = True
        needs = [(j ^ (1 + place // many), place % many) for place in np.flatnonzero(used[fine:])]
        return needs, (product[:, used], even[:, used], around[:, used])

    def sent(self, i, k):
        return [f for block, f in self.needs[i ^ k] if block == i]

    def most_sent(self):
        return max([len(self.sent(i, k)) for i in range(self.count) for k in range(1, self.count)] + [1])

    def most_needed(self):
        return max(len(needs) for needs in self.needs)

    def next_first(self, j, own, fallback):
        return fallback if j == self.count - 1 else own + self.needs[j].index((j + 1, 0))


def interpolation(level, j, inputs, coarse=False):
    table = np.zeros((level.fine, inputs))
    if coarse:
        places = list(range(level.n))
        last = level.following.next_first(j, level.n, level.n - 1)
    else:
        places = [2 * c for c in range(level.n)]
        last = level.next_first(j, level.fine, level.fine - 2)
    places.append(last)
    for c in range(level.n):
        table[2 * c, places[c]] = 1.0
        table[2 * c + 1, places[c]] += 0.5
        table[2 * c + 1, places[c + 1]] += 0.5
    return table


def chain(whole, count, levels):
    made = None
    for depth in reversed(range(levels)):
        made = Level(whole >> depth, count, made)
    return made


def padded(table, rows, cols):
    out = np.zeros((rows, cols))
    out[: table.shape[0], : table.shape[1]] = table
    return out


highest = lax.Precision.HIGHEST


def dot(a, b, dims=((1,), (0,))):
    return lax.dot_general(a, b, (dims, ((), ())), precision=highest, preferred_element_type=jnp.float32)


def kernel_call(body, outs, arrays, scratch=(), left=(), left_out=(), aliases={}):
    space = lambda place, where: pl.BlockSpec(memory_space=pltpu.HBM if place in where else pltpu.VMEM)
    return pl.pallas_call(
        body,
        out_shape=[jax.ShapeDtypeStruct(shape, jnp.float32) for shape in outs],
        in_specs=[space(i, left) for i in range(len(arrays))],
        out_specs=[space(i, left_out) for i in range(len(outs))],
        scratch_shapes=list(scratch),
        input_output_aliases=aliases,
        compiler_params=pltpu.CompilerParams(vmem_limit_bytes=40 << 20),
    )(*(pltpu.with_memory_space_constraint(a, pltpu.HBM) if i in left else a for i, a in enumerate(arrays)))


def swapped(values, axis):
    count = lax.axis_size(axis)
    return [lax.ppermute(v, axis, [(i, i ^ k) for i in range(count)]) for k, v in enumerate(values, 1)]


def gathered(value, axis, beside):
    count = lax.axis_size(axis)
    if count != 4:
        return swapped([value] * (count - 1), axis), beside
    by = lambda k, what: lax.ppermute(what, axis, [(i, i ^ k) for i in range(count)])
    far, beside = lax.optimization_barrier((by(2, value), beside))
    return [by(1, value), far, by(1, far)], beside


def chosen_by(values, j):
    chosen = float(values[0])
    for place in range(1, len(values)):
        if any(values[place] != values[0] for place in range(len(values))):
            chosen = jnp.where(j == place, f32(values[place]), chosen)
    return chosen


def iota(shape, dim):
    return lax.broadcasted_iota(jnp.int32, shape, dim)


def shards(counts, field):
    dz, dx, dy = counts
    lz, lx, ly = field.shape
    nz, nx, ny = lz * dz, lx * dx, ly * dy

    yone = chain(ny, dy, 3)
    ytwo, ythree = yone.following, yone.following.following
    xone = chain(nx, dx, 1)
    xtwo = chain(nx // 2, dx, 2)
    xthree = xtwo.following
    zone = Level(nz, dz, None)

    points_a = lambda fs: [f for f in fs if f in (2, 3) or f >= 4 + yone.kept]
    points_s = lambda fs: [f for f in fs if f not in (2, 3) and f < 4 + yone.kept]
    pairs_y = [(i, k) for i in range(dy) for k in range(1, dy)]
    sa = max([len(points_a(yone.sent(i, k))) for i, k in pairs_y] + [0]) + 1
    ss = max([len(points_s(yone.sent(i, k))) for i, k in pairs_y] + [1])
    per_row = (lz * lx) // ((lz // 2) * (lx // 2))
    rowsy = round_up(sa + -(-ss // per_row), 8)
    sa8, ss8 = round_up(sa, 8), round_up(ss, 8)
    wide1 = yone.n + ytwo.most_needed()
    wide2 = ytwo.n + ythree.most_needed()
    wide = packed = round_up(max(wide1 + 1, 3 * wide2, wide2 + wide1), 128)
    kx = round_up(xtwo.most_sent(), 8)
    rowsx = xtwo.fine + kx * (dx - 1)
    tall = round_up(max(xtwo.n + xthree.most_needed() + 1, xone.n // 2 + 1), 8)

    others_y = max(dy - 1, 1)
    fya = np.zeros((dy, others_y * sa8, ly))
    fys = np.zeros((dy, others_y * ss8, ly))
    ta = np.zeros((dy, ly, wide))
    wa = np.zeros((dy, others_y * rowsy, wide))
    tsm = np.zeros((dy, ly, 2 * wide))
    wsm = np.zeros((dy, others_y * ss8, 2 * wide))
    for j in range(dy):
        product, even, around = yone.tables[j]
        used = product.shape[0]
        ta[j, :, :used] = product[:, :ly].T
        tsm[j, :, :used] = even[:, :ly].T
        tsm[j, :, wide : wide + used] = around[:, :ly].T
        for k in range(1, dy):
            mine = yone.sent(j, k)
            fya[j, (k - 1) * sa8 :][: len(points_a(mine))] = yone.functionals[j][points_a(mine)]
            fya[j, (k - 1) * sa8 + sa - 1] = yone.functionals[j][0]
            fys[j, (k - 1) * ss8 :][: len(points_s(mine))] = yone.functionals[j][points_s(mine)]
            came = yone.sent(j ^ k, k)
            for f in came:
                column = ly + yone.needs[j].index((j ^ k, f))
                if f in points_a(came):
                    wa[j, (k - 1) * rowsy + points_a(came).index(f), :used] = product[:, column]
                else:
                    row = (k - 1) * ss8 + points_s(came).index(f)
                    wsm[j, row, :used] = even[:, column]
                    wsm[j, row, wide : wide + used] = around[:, column]
        if j == dy - 1:
            ta[j, ly - 2, wide - 1] = 0.5
        else:
            wa[j, rowsy * ((j ^ (j + 1)) - 1) + sa - 1, wide - 1] = 0.5

    ext = round_up(max(dx - 1, 1), 8)
    fx = np.zeros((dx, lx, 8))
    heads = round_up(2 * lz + lz // 2, 8)
    sums = np.zeros((dx, heads, lz * lx))
    txa = np.zeros((dx, xone.n, lx + ext))
    txm = np.zeros((dx, xone.n, xone.n + ext))
    for j in range(dx):
        fx[j, :, :2] = xone.functionals[j][2:4].T
        for z in range(lz):
            sums[j, 2 * z : 2 * z + 2, z * lx : (z + 1) * lx] = xone.functionals[j][2:4]
        for half in range(lz // 2):
            sums[j, 2 * lz + half, 2 * half * lx] = 1.0
        product, even, around = xone.tables[j]
        txa[j, :, :lx] = product[:, :lx]
        txm[j, :, : xone.n] = around[:, :lx:2]
        for column, (i, f) in enumerate(xone.needs[j], lx):
            if f in (2, 3):
                txa[j, :, lx + (i ^ j) - 1] = product[:, column]
            else:
                txm[j, :, xone.n + (i ^ j) - 1] += around[:, column] * ((f == 0 and i == 0) or (f == 1 and i == dx - 1))

    zn = zone.n
    zs = np.zeros((dz, 2 * lz + 2 + zn * (lz + dz + 1)))
    for j in range(dz):
        cv, cw = zone.v[j], zone.w[j]
        k_last = (zone.last[zone.rows(0)] / zone.reach(0, j))[0] if 0 < j == dz - 1 else 0.0
        k_first = (zone.first[zone.rows(dz - 1)] / zone.reach(dz - 1, j))[-1] if j == 0 and dz > 1 else 0.0
        parts = [cv, cw, [k_last, k_first], zone.block(j, j).reshape(-1)]
        parts += [zone.reach(j, j ^ k) for k in range(1, dz)]
        parts += [zone.first[zone.rows(j)] * (j == 0), zone.last[zone.rows(j)] * (j == dz - 1)]
        zs[j] = np.concatenate([np.asarray(p, np.float64) for p in parts])
    at_local = 2 * lz + 2
    at_reach = at_local + zn * lz
    at_first = at_reach + zn * (dz - 1)
    at_last = at_first + zn

    f2x = np.zeros((dx, max(dx - 1, 1) * kx, xtwo.fine))
    tx2 = np.zeros((dx, 3 * tall, rowsx))
    qx2 = np.zeros((dx, xtwo.fine, rowsx))
    tx3 = np.zeros((dx, 3 * xthree.n, tall))
    qx3 = np.zeros((dx, xthree.fine, tall))
    px3 = np.zeros((dx, xtwo.fine, tall))
    for j in range(dx):
        columns = list(range(xtwo.fine))
        for i, f in xtwo.needs[j]:
            columns.append(xtwo.fine + kx * ((i ^ j) - 1) + xtwo.sent(i, i ^ j).index(f))
        for c, table in enumerate(xtwo.tables[j]):
            tx2[j, c * tall : c * tall + table.shape[0], columns] = table.T
        qx2[j][:, columns] = interpolation(xtwo, j, len(columns))
        tx2[j, tall - 1, xtwo.fine :] = qx2[j, -1, xtwo.fine :]
        for k in range(1, dx):
            mine = xtwo.sent(j, k)
            f2x[j, (k - 1) * kx :][: len(mine)] = xtwo.functionals[j][mine]
        for c, table in enumerate(xthree.tables[j]):
            tx3[j, c * xthree.n : (c + 1) * xthree.n, : table.shape[1]] = table
        qx3[j] = interpolation(xthree, j, tall)
        px3[j] = interpolation(xtwo, j, tall, True)

    ty2 = np.zeros((dy, 3 * wide, packed))
    qy2 = np.zeros((dy, wide, round_up(ytwo.fine, 128)))
    ty3 = np.zeros((dy, 3 * packed, 128))
    qy3 = np.zeros((dy, packed, 128))
    py3 = np.zeros((dy, packed, round_up(ytwo.fine, 128)))
    px1 = np.zeros((lx, 2 * tall))
    py1 = np.zeros((dy, packed, ly))
    for j in range(dy):
        for c, table in enumerate(ytwo.tables[j]):
            ty2[j, c * wide : c * wide + table.shape[1], c * wide2 : c * wide2 + table.shape[0]] = table.T
        qy2[j, :, : ytwo.fine] = interpolation(ytwo, j, wide).T
        for c, table in enumerate(ythree.tables[j]):
            ty3[j, c * packed : c * packed + table.shape[1], : ythree.n] = (-1.0 if c == 2 else 1.0) * table.T
        qy3[j, :, : ythree.fine] = interpolation(ythree, j, packed).T
        py1[j, wide2:] = interpolation(yone, j, packed - wide2, True).T
        py3[j, wide2:, : ytwo.fine] = interpolation(ytwo, j, packed - wide2, True).T
    for c in range(xone.n):
        begin = c if c < xtwo.n else tall + c - xtwo.n
        px1[2 * c, begin] = 1.0
        px1[2 * c + 1, begin : begin + 2] = 0.5
    az2, first2, last2 = (t.tolist() for t in dense(nz // 2))
    az3, first3, last3 = dense(nz // 4)
    z2, z3 = nz // 2, nz // 4
    lz2, lz3 = lz // 2, lz // 4
    zt = np.concatenate([az3, first3[:, None], last3[:, None]], axis=1)
    zt = zt.reshape(dz, (lz // 8) * (z3 + 2))
    lz4 = lz // 8

    to32 = lambda table: jnp.asarray(table, jnp.float32)

    def stacked(*tables):
        cols = max(t.shape[2] for t in tables)
        starts = np.cumsum([0] + [round_up(t.shape[1], 8) for t in tables])
        out = np.zeros((tables[0].shape[0], starts[-1], cols))
        for t, begin in zip(tables, starts):
            out[:, begin : begin + t.shape[1], : t.shape[2]] = t
        return to32(out), [int(v) for v in starts]

    messages_y, _ = stacked(fya, fys)
    tables_y, _ = stacked(np.concatenate([ta, tsm], axis=2), np.concatenate([wa, np.zeros((dy, wa.shape[1], 2 * wide))], axis=2),
                          np.concatenate([np.zeros((dy, wsm.shape[1], wide)), wsm], axis=2))
    tables_x, _ = stacked(txa, txm)
    tables_x3, at_x3 = stacked(tx3, qx3, px3)
    tables_y3, at_y3 = stacked(ty3, qy3, py3, py1)
    hz, hx1 = lz // 2, lx // 2
    ly2 = round_up(ytwo.fine, 128)

    def y_messages(u_hbm, table_hbm, ty_hbm, fx_hbm, sums_hbm, u_ref, ty_ref, fx_ref, sums_ref, *refs):
        outs, (table, sems) = refs[:-2], refs[-2:]
        j = lax.axis_index("gy")
        nt = ((1,), (1,))
        copies = [
            pltpu.make_async_copy(table_hbm.at[j], table, sems.at[0]),
            pltpu.make_async_copy(u_hbm, u_ref, sems.at[1]),
            pltpu.make_async_copy(ty_hbm.at[j], ty_ref, sems.at[2]),
            pltpu.make_async_copy(fx_hbm.at[lax.axis_index("gx")], fx_ref, sems.at[3]),
            pltpu.make_async_copy(sums_hbm.at[lax.axis_index("gx")], sums_ref, sems.at[4]),
        ]
        for copy in copies:
            copy.start()
        for copy in copies[:2]:
            copy.wait()
        lines = dot(table[: others_y * sa8], u_ref[...].reshape(lz * lx, ly), nt)
        even = jnp.concatenate([u_ref[2 * z, pl.ds(0, hx1, stride=2), :] for z in range(hz)], axis=0)
        points = dot(table[others_y * sa8 :], even, nt)
        for k, out in enumerate(outs):
            out[: min(sa8, rowsy)] = lines[k * sa8 : k * sa8 + min(sa8, rowsy)]
            if rowsy > sa8:
                out[sa8:] = jnp.zeros_like(out[sa8:])
            for f in range(ss):
                begin = hz * hx1 * (f % per_row)
                row = sa + f // per_row
                out[row : row + 1, begin : begin + hz * hx1] = points[k * ss8 + f : k * ss8 + f + 1]
        for copy in copies[2:]:
            copy.wait()

    def along_y(u, half_halo):
        lane = iota(u.shape, 1)
        before, after = pltpu.roll(u, 1, 1), pltpu.roll(u, ly - 1, 1)
        edge = 0.5 * before + jnp.broadcast_to(half_halo, u.shape)
        return jnp.where(lane == ly - 1, edge, jnp.where(lane % 2 == 1, 0.5 * (before + after), u))

    def from_next(jx, own, rows):
        for k, other in enumerate(rows):
            own = jnp.where((jx ^ (k + 1)) == jx + 1, other, own)
        return own

    def y_own(u_ref, ty_ref, fx_ref, ta_out, tsm_out, heads_out, points_out):
        jx = lax.axis_index("gx")
        ta_all = dot(u_ref[...].reshape(lz * lx, ly), ty_ref[:ly, :wide])
        even = jnp.concatenate([u_ref[2 * z, pl.ds(0, hx1, stride=2), :] for z in range(hz)], axis=0)
        tsm_all = dot(even, ty_ref[:ly, wide:])
        ta_out[...] = ta_all
        tsm_out[...] = tsm_all
        weights = [jnp.broadcast_to(fx_ref[:, c : c + 1], (lx, wide)) for c in range(2)]
        heads_out[...] = jnp.zeros_like(heads_out)
        points_out[...] = jnp.zeros_like(points_out)
        for z in range(lz):
            part = ta_all[z * lx : (z + 1) * lx]
            for c in range(2):
                heads_out[2 * z + c : 2 * z + c + 1] = jnp.sum(part * weights[c], axis=0, keepdims=True)
        for half in range(hz):
            heads_out[2 * lz + half : 2 * lz + half + 1] = ta_all[2 * half * lx : 2 * half * lx + 1]
            tm = tsm_all[half * hx1 : (half + 1) * hx1]
            points_out[half : half + 1] = jnp.where(jx == 0, tm[0:1], tm[hx1 - 1 : hx1])
        points_out[hz : hz + 1] = tsm_all[0:1]

    def came_points(ref, points):
        points[...] = jnp.zeros_like(points)
        for f in range(ss):
            begin = hz * hx1 * (f % per_row)
            row = sa + f // per_row
            points[f : f + 1] = ref[row : row + 1, begin : begin + hz * hx1]
        return points[...]

    def x_messages(*refs):
        u_ref, came = refs[0], refs[1:dy]
        ty_ref, sums_ref, heads_ref, points_ref = refs[dy : dy + 4]
        xm_outs, points = refs[dy + 4 : -1], refs[-1]
        jx = lax.axis_index("gx")
        nt = ((1,), (1,))
        head, point = heads_ref[...], points_ref[...]
        shape = (point.shape[0], hz * hx1)
        row, lane = iota(shape, 0), iota(shape, 1)
        line = jnp.where(row == hz, 0, row * hx1 + jnp.where(jx == 0, 0, hx1 - 1))
        one = jnp.where((lane == line) & (row <= hz), 1.0, 0.0)
        for k, ref in enumerate(came):
            begin = ly + rowsy * k
            head += dot(dot(sums_ref[...], ref[...], nt), ty_ref[begin : begin + rowsy, :wide])
            begin = ly + rowsy * (dy - 1) + ss8 * k
            point += dot(dot(one, came_points(ref, points), nt), ty_ref[begin : begin + ss8, wide:])
        for out in xm_outs:
            out[lz + 2 * hz :] = jnp.zeros_like(out[lz + 2 * hz :])
            out[lz + 2 * hz : lz + 2 * hz + 1, :wide] = point[hz : hz + 1, :wide]
        for z in range(lz):
            for k, out in enumerate(xm_outs):
                out[z : z + 1, :wide] = jnp.where((jx ^ (k + 1)) < jx, head[2 * z : 2 * z + 1], head[2 * z + 1 : 2 * z + 2])
        for half in range(hz):
            first = head[2 * lz + half : 2 * lz + half + 1, wide - 1 :]
            iy = along_y(u_ref[2 * half, :8], jnp.broadcast_to(first, (8, 1)))
            for out in xm_outs:
                out[lz + half : lz + half + 1, :wide] = point[half : half + 1, wide:]
                out[lz + hz + half : lz + hz + half + 1, :ly] = iy[0:1]

    def y_apply(*refs):
        came = refs[: dy - 1]
        ty_ref, ta_ref, tsm_ref, ta_out, tsm_out, points = refs[dy - 1 :]
        tn = ((0,), (0,))
        ta_all, tsm_all = ta_ref[...], tsm_ref[...]
        for k, ref in enumerate(came):
            begin = ly + rowsy * k
            ta_all += dot(ref[...], ty_ref[begin : begin + rowsy, :wide], tn)
            begin = ly + rowsy * (dy - 1) + ss8 * k
            tsm_all += dot(came_points(ref, points), ty_ref[begin : begin + ss8, wide:], tn)
        ta_out[...] = ta_all
        tsm_out[...] = tsm_all

    def x_apply(*refs):
        ta_ref, tsm_ref = refs[:2]
        came = refs[2 : 1 + dx][::-1]
        tx_ref, f2x_ref, zc_out, u1_out = refs[1 + dx : 5 + dx]
        planes_out, xt_outs, rest = refs[5 + dx : 4 + dx + dz], refs[4 + dx + dz : -1], refs[-1]
        jx, jz = lax.axis_index("gx"), lax.axis_index("gz")
        xa, xm, diff = [], [], []

        rest[...] = jnp.zeros_like(rest)
        for k, r in enumerate(came):
            for z in range(lz):
                rest[z, k : k + 1, :wide] = r[z : z + 1, :wide]
            for half in range(hz):
                rest[half, k : k + 1, wide:] = r[lz + half : lz + half + 1, :wide]
        for z in range(0, lz, 2):
            pair = jnp.concatenate([ta_ref[z * lx : (z + 1) * lx, :], ta_ref[(z + 1) * lx : (z + 2) * lx, :]], axis=1)
            more = jnp.concatenate([rest[z, :, :wide], rest[z + 1, :, :wide]], axis=1)
            both = dot(tx_ref[jx, : xone.n], jnp.concatenate([pair, more], axis=0))
            xa += [both[:, :wide], both[:, wide:]]
        zc_out[...] = jnp.zeros_like(zc_out)
        zc_out[:hx1] = tsm_ref[:hx1, :wide]
        begin = lz + 2 * hz
        zc_out[hx1 : hx1 + 1] = from_next(jx, tsm_ref[hx1 - 1 : hx1, :wide], [r[begin : begin + 1, :wide] for r in came])
        for half in range(0, hz, 2):
            pair = jnp.concatenate([tsm_ref[h * hx1 : (h + 1) * hx1, wide:] for h in (half, half + 1)], axis=1)
            more = jnp.concatenate([rest[half, :, wide:], rest[half + 1, :, wide:]], axis=1)
            both = dot(tx_ref[jx, xone.n :, : xone.n + ext], jnp.concatenate([pair, more], axis=0))
            xm += [both[:, :wide], both[:, wide:]]
        for half in range(hz):
            diff.append(tsm_ref[half * hx1 : (half + 1) * hx1, :wide] - xm[half])
        scalar = lambda place: chosen_by(zs[:, place], jz)
        totals = []
        for zc in range(zn):
            total = diff[zc] - scalar(at_first + zc) * xm[0] - scalar(at_last + zc) * xm[hz - 1]
            for z in range(lz):
                total += scalar(at_local + zc * lz + z) * xa[z]
            u1_out[zc] = total
            totals.append(total)
        v = -scalar(2 * lz) * xm[hz - 1]
        w = -scalar(2 * lz + 1) * xm[0]
        for z in range(lz):
            v += scalar(z) * xa[z]
            w += scalar(lz + z) * xa[z]
        for k, out in enumerate(planes_out):
            out[...] = jnp.where((jz ^ (k + 1)) > jz, w, v)
        sent = dot(f2x_ref[jx], jnp.concatenate(totals + [v, w], axis=1))
        for k, out in enumerate(xt_outs):
            out[...] = sent[k * kx : (k + 1) * kx]

    def interpolate(*refs):
        u_ref, ta_ref, u1_ref = refs[:3]
        came, xcame = refs[3 : 2 + dx][::-1], refs[2 + dx : 1 + 2 * dx][::-1]
        qx2_ref, qy2_ref, fine_out, ixy_out, i2_out = refs[1 + 2 * dx :]
        jx, jy = lax.axis_index("gx"), lax.axis_index("gy")
        row = iota((lx, ly), 0)
        planes = []
        for half in range(hz):
            iy = along_y(u_ref[2 * half], ta_ref[2 * half * lx : (2 * half + 1) * lx, wide - 1 :])
            begin = lz + hz + half
            halo = from_next(jx, iy[lx - 2 : lx - 1], [r[begin : begin + 1, :ly] for r in came])
            before, after = pltpu.roll(iy, 1, 0), pltpu.roll(iy, lx - 1, 0)
            after = jnp.where(row == lx - 1, jnp.broadcast_to(halo, (lx, ly)), after)
            planes.append(jnp.where(row % 2 == 1, 0.5 * (before + after), iy))
        for half in range(hz):
            fine_out[2 * half] = u_ref[2 * half] - planes[half]
            if half + 1 < hz:
                fine_out[2 * half + 1] = u_ref[2 * half + 1] - 0.5 * (planes[half] + planes[half + 1])
        ixy_out[...] = planes[-1]
        evens = range(0, zn, 2)
        state = [jnp.concatenate([u1_ref[z] for z in evens], axis=1)]
        state += [jnp.concatenate([r[:, z * wide : (z + 1) * wide] for z in evens], axis=1) for r in xcame]
        spread = dot(qx2_ref[jx], jnp.concatenate(state, axis=0))
        spread = jnp.concatenate([spread[:, half * wide : (half + 1) * wide] for half in range(zn // 2)], axis=0)
        spread = dot(spread, qy2_ref[jy])
        for half in range(zn // 2):
            i2_out[half] = spread[half * xtwo.fine : (half + 1) * xtwo.fine]

    def second_apply(*refs):
        part_ref, zc_ref = refs[:2]
        xcame, zcame = refs[2 : dx + 1][::-1], refs[dx + 1 : dz + dx][::-1]
        tx2_ref, ty2_ref, u1_out, zt_out = refs[dz + dx :]
        jx, jy, jz = lax.axis_index("gx"), lax.axis_index("gy"), lax.axis_index("gz")
        own = []
        for zc in range(zn):
            total = part_ref[zc]
            for k, r in enumerate(zcame):
                total += chosen_by(zs[:, at_reach + k * zn + zc], jz) * r[...]
            u1_out[zc] = total
            own.append(total)
        own = jnp.concatenate(own + [jnp.zeros_like(own[0])] * 2, axis=1)
        across = dot(tx2_ref[jx], jnp.concatenate([own] + [r[...] for r in xcame], axis=0))
        cut = [across[:, z * wide : (z + 1) * wide] for z in range(zn + 2)]
        whole = [z for z in range(zn + 2) if z % 2 == 0 or z >= zn]
        joined = [jnp.concatenate([cut[z][c * tall : (c + 1) * tall] for c in range(3)], axis=1) for z in whole]
        made = dot(jnp.concatenate(joined, axis=0), ty2_ref[jy])
        for place, z in enumerate(whole):
            zt_out[z] = made[place * tall : (place + 1) * tall]
        made = dot(jnp.concatenate([cut[z][:tall] for z in range(1, zn, 2)], axis=0), ty2_ref[jy, :wide])
        for z in range(1, zn, 2):
            moved = made[(z // 2) * tall : (z // 2 + 1) * tall]
            if z < 4:
                begin = xtwo.n * (z // 2)
                moved += pltpu.roll(zc_ref[begin : begin + tall], wide2, 1)
            zt_out[z] = moved
        for z in (zn, zn + 1):
            zt_out[z, tall - 1 :] = cut[z][tall - 1 : tall]

    def third_apply(*refs):
        u1_ref, i2_ref, u_ref, ixy_ref, _, own_ref = refs[:6]
        came = refs[6 : 5 + dz]
        px1_ref, tx_ref, ty_ref, qy2_ref, fine_out, middle_out, coarse_out, coarsest_out = refs[5 + dz : 13 + dz]
        zbuf, qbuf, ubuf, last, middle, sems = refs[13 + dz :]
        part = lambda ref, j, starts, which: ref[j, starts[which] : starts[which + 1]]
        jx, jy, jz = lax.axis_index("gx"), lax.axis_index("gy"), lax.axis_index("gz")
        for k, r in enumerate((own_ref, *came)):
            zbuf[pl.ds((jz ^ k) * lz2, lz2)] = r[:lz2]
            qbuf[pl.ds((jz ^ k) * 2, 2)] = r[lz2:]
        at = jnp.minimum(jz + 1, dz - 1) * lz2
        plane_halo = dot(px1_ref[...], jnp.concatenate([zbuf[at + 1], zbuf[at + 3]], axis=0))
        everything = []
        for j in range(dz):
            for zc in range(lz2):
                total = zbuf[j * lz2 + zc]
                for i in range(dz):
                    if i != j:
                        total += float(zone.reach(j, i)[zc]) * qbuf[2 * i + (i < j)]
                everything.append(total)
        for z in range(0, z2, lz2):
            zbuf[z] = everything[z]
        if lz2 > 2:
            zbuf[z2 - 2] = everything[z2 - 2]
        at = jnp.minimum((jz + 1) * lz2, z2 - 2)
        halo = dot(part(tx_ref, jx, at_x3, 2), zbuf[at])
        edges = [jnp.zeros((1, wide), jnp.float32)] * (lz2 // 2)
        for k, r in enumerate(came):
            line = jnp.where((jz ^ (k + 1)) > jz, r[lz2, tall - 1 :], r[lz2 + 1, tall - 1 :])
            for half in range(lz2 // 2):
                edges[half] += chosen_by(zs[:, at_reach + k * zn + 2 * half], jz) * line
        fy = ytwo.fine
        edges = dot(jnp.concatenate(edges + [jnp.zeros((8 - lz2 // 2 % 8, wide), jnp.float32)], axis=0), qy2_ref[jy])
        plane_halo = dot(plane_halo, part(ty_ref, jy, at_y3, 3))
        halo = dot(halo, part(ty_ref, jy, at_y3, 2))[:, :fy]
        here = ixy_ref[...]
        last[...] = u_ref[lz - 1] - 0.5 * (here + jnp.where(jz == dz - 1, here, plane_halo))
        copies = [pltpu.make_async_copy(last, fine_out.at[lz - 1], sems.at[0])]
        copies[0].start()
        at_end = iota((xtwo.fine, fy), 0) == xtwo.fine - 1
        spread = [
            i2_ref[half][:, :fy] + jnp.where(at_end, jnp.broadcast_to(edges[half : half + 1, :fy], (xtwo.fine, fy)), 0.0)
            for half in range(lz2 // 2)
        ]
        spread.append(halo)
        for half in range(lz2 // 2):
            middle[2 * half] = u1_ref[2 * half][:, :fy] - spread[half]
            middle[2 * half + 1] = u1_ref[2 * half + 1][:, :fy] - 0.5 * (spread[half] + spread[half + 1])
        copies.append(pltpu.make_async_copy(middle, middle_out, sems.at[1]))
        copies[1].start()
        evens = [pltpu.roll(everything[z], packed - wide2, 1) for z in range(0, z2, 2)]
        arounds = [pltpu.roll(everything[z], packed - 2 * wide2, 1) for z in range(0, z2, 2)]
        second = []
        for zc in range(z3):
            total = evens[zc] - arounds[zc] - first2[zc] * arounds[0] - last2[zc] * arounds[-1]
            for z in range(z2):
                total += az2[zc][z] * everything[z]
            ubuf[zc] = total
            second.append(total)
        fy3, n3 = ythree.fine, xthree.n
        at = [jnp.minimum(jz * lz3 + 2 * half, z3 - 2) for half in range(lz3 // 2 + 1)]
        spread = dot(part(tx_ref, jx, at_x3, 1), jnp.concatenate([ubuf[a] for a in at], axis=1))
        joined = []
        for zc in range(lz4):
            base = zc * (z3 + 2)
            along = chosen_by(zt[:, base], jz) * second[0]
            for z in range(1, z3):
                along += chosen_by(zt[:, base + z], jz) * second[z]
            even = ubuf[2 * (jz * lz4 + zc)]
            around = even + chosen_by(zt[:, base + z3], jz) * second[0] + chosen_by(zt[:, base + z3 + 1], jz) * second[z3 - 2]
            parts = [dot(tx_ref[jx, c * n3 : (c + 1) * n3, :], plane) for c, plane in enumerate((along, even, around))]
            joined.append(jnp.concatenate(parts, axis=1))
        spread = jnp.concatenate([spread[:, h * packed : (h + 1) * packed] for h in range(len(at))], axis=0)
        spread = dot(spread, part(ty_ref, jy, at_y3, 1))[:, :fy3]
        coarsest = dot(jnp.concatenate(joined, axis=0), part(ty_ref, jy, at_y3, 0))[:, : ythree.n]
        for zc in range(lz4):
            coarsest_out[zc] = coarsest[zc * n3 : (zc + 1) * n3]
        spread = [spread[h * xthree.fine : (h + 1) * xthree.fine] for h in range(len(at))]
        for half in range(lz3 // 2):
            at = jz * lz3 + 2 * half
            coarse_out[2 * half] = ubuf[at][: xthree.fine, :fy3] - spread[half]
            coarse_out[2 * half + 1] = ubuf[at + 1][: xthree.fine, :fy3] - 0.5 * (spread[half] + spread[half + 1])
        for copy in copies:
            copy.wait()

    u, own_ty, own_fx, own_sums, *ym = kernel_call(
        y_messages,
        [(lz, lx, ly), tables_y.shape[1:], fx.shape[1:], sums.shape[1:]] + [(rowsy, lz * lx)] * (dy - 1),
        [field, messages_y, tables_y, to32(fx), to32(sums)],
        scratch=[pltpu.VMEM(messages_y.shape[1:], jnp.float32), pltpu.SemaphoreType.DMA((5,))],
        left=(0, 1, 2, 3, 4),
    )
    ycame = swapped(ym, "gy")
    ta_own, tsm_own, head, point = kernel_call(
        y_own,
        [(lz * lx, wide), (hz * hx1, 2 * wide), (heads, wide), (round_up(hz + 1, 8), 2 * wide)],
        [u, own_ty, own_fx],
    )
    xm = kernel_call(
        x_messages,
        [(round_up(lz + 2 * hz + 1, 8), max(wide, ly))] * (dx - 1),
        [u, *ycame, own_ty, own_sums, head, point],
        scratch=[pltpu.VMEM((ss8, hz * hx1), jnp.float32)],
    )
    xcame = swapped(xm, "gx")
    ta_v, tsm_v = kernel_call(
        y_apply,
        [(lz * lx, wide), (hz * hx1, 2 * wide)],
        [*ycame, own_ty, ta_own, tsm_own],
        scratch=[pltpu.VMEM((ss8, hz * hx1), jnp.float32)],
    )
    zc, u1_part, *sent = kernel_call(
        x_apply,
        [(xtwo.n + tall, wide), (zn, xone.n, wide)]
        + [(xone.n, wide)] * (dz - 1)
        + [(kx, (zn + 2) * wide)] * (dx - 1),
        [ta_v, tsm_v, *xcame[::-1], tables_x, to32(f2x)],
        scratch=[pltpu.VMEM((lz, ext, 2 * wide), jnp.float32)],
    )
    tails = sent[dz - 1 :]
    zcame = swapped(sent[: dz - 1], "gz")
    if dz > 1 and dx > 1:
        zcame[0], tails[0] = lax.optimization_barrier((zcame[0], tails[0]))
    xtcame = swapped(tails, "gx")
    u1, zmsg = kernel_call(
        second_apply,
        [(zn, xone.n, wide), (lz2 + 2, tall, packed)],
        [u1_part, zc, *xtcame[::-1], *zcame[::-1], to32(tx2), to32(ty2)],
    )
    beside = kernel_call(
        interpolate,
        [(lz, lx, ly), (lx, ly), (lz2 // 2, xtwo.fine, ly2)],
        [u, ta_v, u1, *xcame[::-1], *xtcame[::-1], to32(qx2), to32(qy2)],
    )
    ztcame, (fine, ixy, i2) = gathered(zmsg, "gz", beside)
    return kernel_call(
        third_apply,
        [(lz, lx, ly), (lz2, xtwo.fine, ytwo.fine), (lz3, xthree.fine, ythree.fine), (lz4, xthree.n, ythree.n)],
        [u1, i2, u, ixy, fine, zmsg, *ztcame, to32(px1), tables_x3, tables_y3, to32(qy2)],
        scratch=[
            pltpu.VMEM((z2, tall, packed), jnp.float32),
            pltpu.VMEM((2 * dz, tall, packed), jnp.float32),
            pltpu.VMEM((z3, tall, packed), jnp.float32),
            pltpu.VMEM((lx, ly), jnp.float32),
            pltpu.VMEM((lz2, xtwo.fine, ytwo.fine), jnp.float32),
            pltpu.SemaphoreType.DMA((2,)),
        ],
        left=(4,),
        left_out=(0, 1),
        aliases={4: 0},
    )


def solution(mesh):
    spec = P("gz", "gx", "gy")
    counts = tuple(mesh.shape[a] for a in ("gz", "gx", "gy"))
    return jax.shard_map(
        functools.partial(shards, counts), mesh=mesh, in_specs=(spec,), out_specs=(spec,) * 4, check_vma=False
    )
```

```python
import functools
import math

import jax
import jax.numpy as jnp
import numpy as np
from jax import lax
from jax.experimental import pallas as pl
from jax.experimental.pallas import tpu as pltpu
from jax.sharding import PartitionSpec as P

band_ratio = 2.0 - math.sqrt(3.0)
f32 = np.float32


def round_up(value, unit):
    return -(-value // unit) * unit


def dense(fine):
    n = fine // 2
    steps = np.arange(n)[:, None] - np.arange(n)[None, :]
    lower = np.where(steps >= 0, (-band_ratio) ** np.maximum(steps, 0), 0.0)
    inverse = lower.T @ lower
    mass = 4.0 * np.eye(fine) + np.eye(fine, k=1) + np.eye(fine, k=-1)
    weights = np.where(np.arange(n) == n - 1, 1.0, 0.5)[:, None]
    earlier = np.concatenate([np.zeros((1, fine)), mass[1::2][:-1]])
    product = inverse @ (0.5 * band_ratio * (mass[0::2] + weights * mass[1::2] + 0.5 * earlier))
    return product, inverse[:, 0] * (3 * band_ratio - 1), inverse[:, -1] * (2 * band_ratio)


class Level:
    def __init__(self, whole, count, following):
        self.count, self.fine = count, whole // count
        self.n = self.fine // 2
        self.product, self.first, self.last = dense(whole)
        self.following = following
        self.kept = following.functional_count if following else 0
        self.functional_count = 4 + 2 * self.kept
        self.even = np.zeros((self.n, self.fine))
        self.even[np.arange(self.n), 2 * np.arange(self.n)] = 1.0
        self.v = [self.towards(i, i * self.n - 1) for i in range(count)]
        self.w = [self.towards(i, (i + 1) * self.n) for i in range(count)]
        self.functionals = []
        for i in range(count):
            own = np.zeros((4, self.fine))
            own[0, 0] = own[1, self.fine - 2] = 1.0
            own[2], own[3] = self.v[i], self.w[i]
            if following:
                inner = following.functionals[i]
                own = np.concatenate([own, inner @ self.even, inner @ self.block(i, i)])
            self.functionals.append(own)
        built = [self.build(j) for j in range(count)]
        self.needs = [needs for needs, _ in built]
        self.tables = [tables for _, tables in built]

    def rows(self, i):
        return slice(i * self.n, (i + 1) * self.n)

    def block(self, i, j):
        return self.product[self.rows(i), j * self.fine : (j + 1) * self.fine]

    def towards(self, i, row):
        if not 0 <= row < self.count * self.n:
            return np.zeros(self.fine)
        values = self.product[row, i * self.fine : (i + 1) * self.fine]
        return values / np.abs(values).max()

    def reach(self, i, j):
        side = self.v[j] if j > i else self.w[j]
        best = np.argmax(np.abs(side))
        return self.block(i, j)[:, best] / side[best]

    def side(self, i, j):
        return 2 if j > i else 3

    def through_even(self, f):
        return 4 + f if f else 0

    def build(self, j):
        n, fine, many, end = self.n, self.fine, self.functional_count, self.count - 1
        targets = self.following.needs[j] if self.following else []
        others = [j ^ k for k in range(1, self.count)]
        at = lambda i, f: fine + many * ((i ^ j) - 1) + f
        product = np.zeros((n + len(targets), fine + many * len(others)))
        even, used = np.zeros_like(product), np.zeros(product.shape[1], bool)
        used[:fine] = True
        product[:n, :fine] = self.block(j, j)
        even[:n, :fine] = self.even
        first, last = [self.first[self.rows(j)]], [self.last[self.rows(j)]]
        for i in others:
            product[:n, at(i, self.side(j, i))] = self.reach(j, i)
            used[at(i, self.side(j, i))] = True
        for row, (i, f) in enumerate(targets, n):
            inner = self.following.functionals[i][f]
            product[row, :fine] = inner @ self.block(i, j)
            product[row, at(i, 4 + self.kept + f)] = 1.0
            even[row, at(i, self.through_even(f))] = 1.0
            used[at(i, 4 + self.kept + f)] = used[at(i, self.through_even(f))] = True
            for other in others:
                if other != i:
                    product[row, at(other, self.side(i, other))] = inner @ self.reach(i, other)
                    used[at(other, self.side(i, other))] = True
            first.append([inner @ self.first[self.rows(i)]])
            last.append([inner @ self.last[self.rows(i)]])
        around = even.copy()
        from_first, from_last = 0 if j == 0 else at(0, 0), fine - 2 if j == end else at(end, 1)
        around[:, from_first] += np.concatenate(first)
        around[:, from_last] += np.concatenate(last)
        used[from_first] = used[from_last] = True
        if j < end:
            used[at(j + 1, 0)] = True
        needs = [(j ^ (1 + place // many), place % many) for place in np.flatnonzero(used[fine:])]
        return needs, (product[:, used], even[:, used], around[:, used])

    def sent(self, i, k):
        return [f for block, f in self.needs[i ^ k] if block == i]

    def most_sent(self):
        return max([len(self.sent(i, k)) for i in range(self.count) for k in range(1, self.count)] + [1])

    def most_needed(self):
        return max(len(needs) for needs in self.needs)

    def next_first(self, j, own, fallback):
        return fallback if j == self.count - 1 else own + self.needs[j].index((j + 1, 0))


def interpolation(level, j, inputs, coarse=False):
    table = np.zeros((level.fine, inputs))
    if coarse:
        places = list(range(level.n))
        last = level.following.next_first(j, level.n, level.n - 1)
    else:
        places = [2 * c for c in range(level.n)]
        last = level.next_first(j, level.fine, level.fine - 2)
    places.append(last)
    for c in range(level.n):
        table[2 * c, places[c]] = 1.0
        table[2 * c + 1, places[c]] += 0.5
        table[2 * c + 1, places[c + 1]] += 0.5
    return table


def chain(whole, count, levels):
    made = None
    for depth in reversed(range(levels)):
        made = Level(whole >> depth, count, made)
    return made


def padded(table, rows, cols):
    out = np.zeros((rows, cols))
    out[: table.shape[0], : table.shape[1]] = table
    return out


highest = lax.Precision.HIGHEST


def dot(a, b, dims=((1,), (0,))):
    return lax.dot_general(a, b, (dims, ((), ())), precision=highest, preferred_element_type=jnp.float32)


def kernel_call(body, outs, arrays, scratch=(), left=(), left_out=(), aliases={}):
    space = lambda place, where: pl.BlockSpec(memory_space=pltpu.HBM if place in where else pltpu.VMEM)
    return pl.pallas_call(
        body,
        out_shape=[jax.ShapeDtypeStruct(shape, jnp.float32) for shape in outs],
        in_specs=[space(i, left) for i in range(len(arrays))],
        out_specs=[space(i, left_out) for i in range(len(outs))],
        scratch_shapes=list(scratch),
        input_output_aliases=aliases,
        compiler_params=pltpu.CompilerParams(vmem_limit_bytes=40 << 20),
    )(*(pltpu.with_memory_space_constraint(a, pltpu.HBM) if i in left else a for i, a in enumerate(arrays)))


def swapped(values, axis):
    count = lax.axis_size(axis)
    return [lax.ppermute(v, axis, [(i, i ^ k) for i in range(count)]) for k, v in enumerate(values, 1)]


def gathered(value, axis, beside):
    count = lax.axis_size(axis)
    if count != 4:
        return swapped([value] * (count - 1), axis), beside
    by = lambda k, what: lax.ppermute(what, axis, [(i, i ^ k) for i in range(count)])
    far, beside = lax.optimization_barrier((by(2, value), beside))
    return [by(1, value), far, by(1, far)], beside


def chosen_by(values, j):
    chosen = float(values[0])
    for place in range(1, len(values)):
        if any(values[place] != values[0] for place in range(len(values))):
            chosen = jnp.where(j == place, f32(values[place]), chosen)
    return chosen


def iota(shape, dim):
    return lax.broadcasted_iota(jnp.int32, shape, dim)


def shards(counts, field):
    dz, dx, dy = counts
    lz, lx, ly = field.shape
    nz, nx, ny = lz * dz, lx * dx, ly * dy

    yone = chain(ny, dy, 3)
    ytwo, ythree = yone.following, yone.following.following
    xone = chain(nx, dx, 1)
    xtwo = chain(nx // 2, dx, 2)
    xthree = xtwo.following
    zone = Level(nz, dz, None)

    points_a = lambda fs: [f for f in fs if f in (2, 3) or f >= 4 + yone.kept]
    points_s = lambda fs: [f for f in fs if f not in (2, 3) and f < 4 + yone.kept]
    pairs_y = [(i, k) for i in range(dy) for k in range(1, dy)]
    sa = max([len(points_a(yone.sent(i, k))) for i, k in pairs_y] + [0]) + 1
    ss = max([len(points_s(yone.sent(i, k))) for i, k in pairs_y] + [1])
    per_row = (lz * lx) // ((lz // 2) * (lx // 2))
    rowsy = round_up(sa + -(-ss // per_row), 8)
    sa8, ss8 = round_up(sa, 8), round_up(ss, 8)
    wide1 = yone.n + ytwo.most_needed()
    wide2 = ytwo.n + ythree.most_needed()
    wide = packed = round_up(max(wide1 + 1, 3 * wide2, wide2 + wide1), 128)
    kx = round_up(xtwo.most_sent(), 8)
    rowsx = xtwo.fine + kx * (dx - 1)
    tall = round_up(max(xtwo.n + xthree.most_needed() + 1, xone.n // 2 + 1), 8)

    others_y = max(dy - 1, 1)
    fya = np.zeros((dy, others_y * sa8, ly))
    fys = np.zeros((dy, others_y * ss8, ly))
    ta = np.zeros((dy, ly, wide))
    wa = np.zeros((dy, others_y * rowsy, wide))
    tsm = np.zeros((dy, ly, 2 * wide))
    wsm = np.zeros((dy, others_y * ss8, 2 * wide))
    for j in range(dy):
        product, even, around = yone.tables[j]
        used = product.shape[0]
        ta[j, :, :used] = product[:, :ly].T
        tsm[j, :, :used] = even[:, :ly].T
        tsm[j, :, wide : wide + used] = around[:, :ly].T
        for k in range(1, dy):
            mine = yone.sent(j, k)
            fya[j, (k - 1) * sa8 :][: len(points_a(mine))] = yone.functionals[j][points_a(mine)]
            fya[j, (k - 1) * sa8 + sa - 1] = yone.functionals[j][0]
            fys[j, (k - 1) * ss8 :][: len(points_s(mine))] = yone.functionals[j][points_s(mine)]
            came = yone.sent(j ^ k, k)
            for f in came:
                column = ly + yone.needs[j].index((j ^ k, f))
                if f in points_a(came):
                    wa[j, (k - 1) * rowsy + points_a(came).index(f), :used] = product[:, column]
                else:
                    row = (k - 1) * ss8 + points_s(came).index(f)
                    wsm[j, row, :used] = even[:, column]
                    wsm[j, row, wide : wide + used] = around[:, column]
        if j == dy - 1:
            ta[j, ly - 2, wide - 1] = 0.5
        else:
            wa[j, rowsy * ((j ^ (j + 1)) - 1) + sa - 1, wide - 1] = 0.5

    ext = round_up(max(dx - 1, 1), 8)
    fx = np.zeros((dx, lx, 8))
    heads = round_up(2 * lz + lz // 2, 8)
    sums = np.zeros((dx, heads, lz * lx))
    txa = np.zeros((dx, xone.n, lx + ext))
    txm = np.zeros((dx, xone.n, xone.n + ext))
    for j in range(dx):
        fx[j, :, :2] = xone.functionals[j][2:4].T
        for z in range(lz):
            sums[j, 2 * z : 2 * z + 2, z * lx : (z + 1) * lx] = xone.functionals[j][2:4]
        for half in range(lz // 2):
            sums[j, 2 * lz + half, 2 * half * lx] = 1.0
        product, even, around = xone.tables[j]
        txa[j, :, :lx] = product[:, :lx]
        txm[j, :, : xone.n] = around[:, :lx:2]
        for column, (i, f) in enumerate(xone.needs[j], lx):
            if f in (2, 3):
                txa[j, :, lx + (i ^ j) - 1] = product[:, column]
            else:
                txm[j, :, xone.n + (i ^ j) - 1] += around[:, column] * ((f == 0 and i == 0) or (f == 1 and i == dx - 1))

    zn = zone.n
    zs = np.zeros((dz, 2 * lz + 2 + zn * (lz + dz + 1)))
    for j in range(dz):
        cv, cw = zone.v[j], zone.w[j]
        k_last = (zone.last[zone.rows(0)] / zone.reach(0, j))[0] if 0 < j == dz - 1 else 0.0
        k_first = (zone.first[zone.rows(dz - 1)] / zone.reach(dz - 1, j))[-1] if j == 0 and dz > 1 else 0.0
        parts = [cv, cw, [k_last, k_first], zone.block(j, j).reshape(-1)]
        parts += [zone.reach(j, j ^ k) for k in range(1, dz)]
        parts += [zone.first[zone.rows(j)] * (j == 0), zone.last[zone.rows(j)] * (j == dz - 1)]
        zs[j] = np.concatenate([np.asarray(p, np.float64) for p in parts])
    at_local = 2 * lz + 2
    at_reach = at_local + zn * lz
    at_first = at_reach + zn * (dz - 1)
    at_last = at_first + zn

    f2x = np.zeros((dx, max(dx - 1, 1) * kx, xtwo.fine))
    tx2 = np.zeros((dx, 3 * tall, rowsx))
    qx2 = np.zeros((dx, xtwo.fine, rowsx))
    tx3 = np.zeros((dx, 3 * xthree.n, tall))
    qx3 = np.zeros((dx, xthree.fine, tall))
    px3 = np.zeros((dx, xtwo.fine, tall))
    for j in range(dx):
        columns = list(range(xtwo.fine))
        for i, f in xtwo.needs[j]:
            columns.append(xtwo.fine + kx * ((i ^ j) - 1) + xtwo.sent(i, i ^ j).index(f))
        for c, table in enumerate(xtwo.tables[j]):
            tx2[j, c * tall : c * tall + table.shape[0], columns] = table.T
        qx2[j][:, columns] = interpolation(xtwo, j, len(columns))
        tx2[j, tall - 1, xtwo.fine :] = qx2[j, -1, xtwo.fine :]
        for k in range(1, dx):
            mine = xtwo.sent(j, k)
            f2x[j, (k - 1) * kx :][: len(mine)] = xtwo.functionals[j][mine]
        for c, table in enumerate(xthree.tables[j]):
            tx3[j, c * xthree.n : (c + 1) * xthree.n, : table.shape[1]] = table
        qx3[j] = interpolation(xthree, j, tall)
        px3[j] = interpolation(xtwo, j, tall, True)

    ty2 = np.zeros((dy, 3 * wide, packed))
    qy2 = np.zeros((dy, wide, round_up(ytwo.fine, 128)))
    ty3 = np.zeros((dy, 3 * packed, 128))
    qy3 = np.zeros((dy, packed, 128))
    py3 = np.zeros((dy, packed, round_up(ytwo.fine, 128)))
    px1 = np.zeros((lx, 2 * tall))
    py1 = np.zeros((dy, packed, ly))
    for j in range(dy):
        for c, table in enumerate(ytwo.tables[j]):
            ty2[j, c * wide : c * wide + table.shape[1], c * wide2 : c * wide2 + table.shape[0]] = table.T
        qy2[j, :, : ytwo.fine] = interpolation(ytwo, j, wide).T
        for c, table in enumerate(ythree.tables[j]):
            ty3[j, c * packed : c * packed + table.shape[1], : ythree.n] = (-1.0 if c == 2 else 1.0) * table.T
        qy3[j, :, : ythree.fine] = interpolation(ythree, j, packed).T
        py1[j, wide2:] = interpolation(yone, j, packed - wide2, True).T
        py3[j, wide2:, : ytwo.fine] = interpolation(ytwo, j, packed - wide2, True).T
    for c in range(xone.n):
        begin = c if c < xtwo.n else tall + c - xtwo.n
        px1[2 * c, begin] = 1.0
        px1[2 * c + 1, begin : begin + 2] = 0.5
    az2, first2, last2 = (t.tolist() for t in dense(nz // 2))
    az3, first3, last3 = dense(nz // 4)
    z2, z3 = nz // 2, nz // 4
    lz2, lz3 = lz // 2, lz // 4
    zt = np.concatenate([az3, first3[:, None], last3[:, None]], axis=1)
    zt = zt.reshape(dz, (lz // 8) * (z3 + 2))
    lz4 = lz // 8

    to32 = lambda table: jnp.asarray(table, jnp.float32)

    def stacked(*tables):
        cols = max(t.shape[2] for t in tables)
        starts = np.cumsum([0] + [round_up(t.shape[1], 8) for t in tables])
        out = np.zeros((tables[0].shape[0], starts[-1], cols))
        for t, begin in zip(tables, starts):
            out[:, begin : begin + t.shape[1], : t.shape[2]] = t
        return to32(out), [int(v) for v in starts]

    messages_y, _ = stacked(fya, fys)
    tables_y, _ = stacked(np.concatenate([ta, tsm], axis=2), np.concatenate([wa, np.zeros((dy, wa.shape[1], 2 * wide))], axis=2),
                          np.concatenate([np.zeros((dy, wsm.shape[1], wide)), wsm], axis=2))
    tables_x, _ = stacked(txa[:, :, :lx], txm[:, :, : xone.n])
    rows_x = np.concatenate([txa[:, :, lx:], txm[:, :, xone.n :]], axis=2)
    rows_x = np.concatenate([rows_x, f2x @ rows_x], axis=1)
    tables_x3, at_x3 = stacked(tx3, qx3, px3)
    tables_y3, at_y3 = stacked(ty3, qy3, py3, py1)
    hz, hx1 = lz // 2, lx // 2
    ly2 = round_up(ytwo.fine, 128)

    def y_messages(u_hbm, table_hbm, ty_hbm, fx_hbm, sums_hbm, u_ref, ty_ref, fx_ref, sums_ref, *refs):
        outs, (table, sems) = refs[:-2], refs[-2:]
        j = lax.axis_index("gy")
        nt = ((1,), (1,))
        copies = [
            pltpu.make_async_copy(table_hbm.at[j], table, sems.at[0]),
            pltpu.make_async_copy(u_hbm, u_ref, sems.at[1]),
            pltpu.make_async_copy(ty_hbm.at[j], ty_ref, sems.at[2]),
            pltpu.make_async_copy(fx_hbm.at[lax.axis_index("gx")], fx_ref, sems.at[3]),
            pltpu.make_async_copy(sums_hbm.at[lax.axis_index("gx")], sums_ref, sems.at[4]),
        ]
        for copy in copies:
            copy.start()
        for copy in copies[:2]:
            copy.wait()
        lines = dot(table[: others_y * sa8], u_ref[...].reshape(lz * lx, ly), nt)
        even = jnp.concatenate([u_ref[2 * z, pl.ds(0, hx1, stride=2), :] for z in range(hz)], axis=0)
        points = dot(table[others_y * sa8 :], even, nt)
        for k, out in enumerate(outs):
            out[: min(sa8, rowsy)] = lines[k * sa8 : k * sa8 + min(sa8, rowsy)]
            if rowsy > sa8:
                out[sa8:] = jnp.zeros_like(out[sa8:])
            for f in range(ss):
                begin = hz * hx1 * (f % per_row)
                row = sa + f // per_row
                out[row : row + 1, begin : begin + hz * hx1] = points[k * ss8 + f : k * ss8 + f + 1]
        for copy in copies[2:]:
            copy.wait()

    def along_y(u, half_halo):
        lane = iota(u.shape, 1)
        before, after = pltpu.roll(u, 1, 1), pltpu.roll(u, ly - 1, 1)
        edge = 0.5 * before + jnp.broadcast_to(half_halo, u.shape)
        return jnp.where(lane == ly - 1, edge, jnp.where(lane % 2 == 1, 0.5 * (before + after), u))

    def from_next(jx, own, rows):
        for k, other in enumerate(rows):
            own = jnp.where((jx ^ (k + 1)) == jx + 1, other, own)
        return own

    def y_own(u_ref, ty_ref, fx_ref, ta_out, tsm_out, heads_out, points_out):
        jx = lax.axis_index("gx")
        ta_all = dot(u_ref[...].reshape(lz * lx, ly), ty_ref[:ly, :wide])
        even = jnp.concatenate([u_ref[2 * z, pl.ds(0, hx1, stride=2), :] for z in range(hz)], axis=0)
        tsm_all = dot(even, ty_ref[:ly, wide:])
        ta_out[...] = ta_all
        tsm_out[...] = tsm_all
        weights = [jnp.broadcast_to(fx_ref[:, c : c + 1], (lx, wide)) for c in range(2)]
        heads_out[...] = jnp.zeros_like(heads_out)
        points_out[...] = jnp.zeros_like(points_out)
        for z in range(lz):
            part = ta_all[z * lx : (z + 1) * lx]
            for c in range(2):
                heads_out[2 * z + c : 2 * z + c + 1] = jnp.sum(part * weights[c], axis=0, keepdims=True)
        for half in range(hz):
            heads_out[2 * lz + half : 2 * lz + half + 1] = ta_all[2 * half * lx : 2 * half * lx + 1]
            tm = tsm_all[half * hx1 : (half + 1) * hx1]
            points_out[half : half + 1] = jnp.where(jx == 0, tm[0:1], tm[hx1 - 1 : hx1])
        points_out[hz : hz + 1] = tsm_all[0:1]

    def came_points(ref, points):
        points[...] = jnp.zeros_like(points)
        for f in range(ss):
            begin = hz * hx1 * (f % per_row)
            row = sa + f // per_row
            points[f : f + 1] = ref[row : row + 1, begin : begin + hz * hx1]
        return points[...]

    def x_messages(*refs):
        u_ref, came = refs[0], refs[1:dy]
        ty_ref, sums_ref, heads_ref, points_ref = refs[dy : dy + 4]
        xm_outs, points = refs[dy + 4 : -1], refs[-1]
        jx = lax.axis_index("gx")
        nt = ((1,), (1,))
        head, point = heads_ref[...], points_ref[...]
        shape = (point.shape[0], hz * hx1)
        row, lane = iota(shape, 0), iota(shape, 1)
        line = jnp.where(row == hz, 0, row * hx1 + jnp.where(jx == 0, 0, hx1 - 1))
        one = jnp.where((lane == line) & (row <= hz), 1.0, 0.0)
        for k, ref in enumerate(came):
            begin = ly + rowsy * k
            head += dot(dot(sums_ref[...], ref[...], nt), ty_ref[begin : begin + rowsy, :wide])
            begin = ly + rowsy * (dy - 1) + ss8 * k
            point += dot(dot(one, came_points(ref, points), nt), ty_ref[begin : begin + ss8, wide:])
        for out in xm_outs:
            out[lz + 2 * hz :] = jnp.zeros_like(out[lz + 2 * hz :])
            out[lz + 2 * hz : lz + 2 * hz + 1, :wide] = point[hz : hz + 1, :wide]
        for z in range(lz):
            for k, out in enumerate(xm_outs):
                out[z : z + 1, :wide] = jnp.where((jx ^ (k + 1)) < jx, head[2 * z : 2 * z + 1], head[2 * z + 1 : 2 * z + 2])
        for half in range(hz):
            first = head[2 * lz + half : 2 * lz + half + 1, wide - 1 :]
            iy = along_y(u_ref[2 * half, :8], jnp.broadcast_to(first, (8, 1)))
            for out in xm_outs:
                out[lz + half : lz + half + 1, :wide] = point[half : half + 1, wide:]
                out[lz + hz + half : lz + hz + half + 1, :ly] = iy[0:1]

    def y_apply(*refs):
        came = refs[: dy - 1]
        ty_ref, ta_ref, tsm_ref, tx_ref, f2x_ref, ta_out, zc_out, six_out, sent_out, points = refs[dy - 1 :]
        jx, jz = lax.axis_index("gx"), lax.axis_index("gz")
        tn = ((0,), (0,))
        ta_all, tsm_all = ta_ref[...], tsm_ref[...]
        for k, ref in enumerate(came):
            begin = ly + rowsy * k
            ta_all += dot(ref[...], ty_ref[begin : begin + rowsy, :wide], tn)
            begin = ly + rowsy * (dy - 1) + ss8 * k
            tsm_all += dot(came_points(ref, points), ty_ref[begin : begin + ss8, wide:], tn)
        ta_out[...] = ta_all
        zc_out[...] = jnp.zeros_like(zc_out)
        zc_out[:hx1] = tsm_all[:hx1, :wide]
        xa, xm = [], []
        for z in range(0, lz, 2):
            pair = jnp.concatenate([ta_all[z * lx : (z + 1) * lx], ta_all[(z + 1) * lx : (z + 2) * lx]], axis=1)
            both = dot(tx_ref[jx, : xone.n], pair)
            xa += [both[:, :wide], both[:, wide:]]
        for half in range(0, hz, 2):
            pair = jnp.concatenate([tsm_all[h * hx1 : (h + 1) * hx1, wide:] for h in (half, half + 1)], axis=1)
            both = dot(tx_ref[jx, xone.n :, : xone.n], pair)
            xm += [both[:, :wide], both[:, wide:]]
        six = along_planes(jz, xa, xm)
        for half in range(hz):
            six[half] += tsm_all[half * hx1 : (half + 1) * hx1, :wide]
        six = jnp.concatenate(six, axis=1)
        six_out[...] = six
        sent_out[...] = dot(f2x_ref[jx], six)

    def along_planes(jz, xa, xm):
        scalar = lambda place: chosen_by(zs[:, place], jz)
        made = []
        for zc in range(zn):
            total = -xm[zc] - scalar(at_first + zc) * xm[0] - scalar(at_last + zc) * xm[hz - 1]
            for z in range(lz):
                total += scalar(at_local + zc * lz + z) * xa[z]
            made.append(total)
        v = -scalar(2 * lz) * xm[hz - 1]
        w = -scalar(2 * lz + 1) * xm[0]
        for z in range(lz):
            v += scalar(z) * xa[z]
            w += scalar(lz + z) * xa[z]
        return made + [v, w]

    def x_apply(*refs):
        own_zc_ref, six_ref, own_sent_ref = refs[:3]
        came = refs[3 : 2 + dx][::-1]
        rows_ref, zc_out, u1_out = refs[2 + dx : 5 + dx]
        planes_out, xt_outs, rest = refs[5 + dx : 4 + dx + dz], refs[4 + dx + dz : -1], refs[-1]
        jx, jz = lax.axis_index("gx"), lax.axis_index("gz")
        rest[...] = jnp.zeros_like(rest)
        for k, r in enumerate(came):
            for z in range(lz + hz):
                rest[z, k : k + 1] = r[z : z + 1, :wide]
        zero = [jnp.zeros_like(rest[0])]
        lines_a = along_planes(jz, [rest[z] for z in range(lz)], zero * hz)
        lines_m = along_planes(jz, zero * lz, [rest[lz + half] for half in range(hz)])
        lines = jnp.concatenate([jnp.concatenate(lines_a, axis=1), jnp.concatenate(lines_m, axis=1)], axis=0)
        added = dot(rows_ref[jx], lines)
        six = six_ref[...] + added[: xone.n]
        sent = own_sent_ref[...] + added[xone.n :]
        zc_out[...] = own_zc_ref[...]
        begin = lz + 2 * hz
        zc_out[hx1 : hx1 + 1] = from_next(jx, own_zc_ref[hx1 - 1 : hx1], [r[begin : begin + 1, :wide] for r in came])
        for zc in range(zn):
            u1_out[zc] = six[:, zc * wide : (zc + 1) * wide]
        v, w = six[:, zn * wide : (zn + 1) * wide], six[:, (zn + 1) * wide :]
        for k, out in enumerate(planes_out):
            out[...] = jnp.where((jz ^ (k + 1)) > jz, w, v)
        for k, out in enumerate(xt_outs):
            out[...] = sent[k * kx : (k + 1) * kx]

    def interpolate(*refs):
        u_ref, ta_ref, u1_ref = refs[:3]
        came, xcame = refs[3 : 2 + dx][::-1], refs[2 + dx : 1 + 2 * dx][::-1]
        qx2_ref, qy2_ref, fine_out, ixy_out, i2_out = refs[1 + 2 * dx :]
        jx, jy = lax.axis_index("gx"), lax.axis_index("gy")
        row = iota((lx, ly), 0)
        planes = []
        for half in range(hz):
            iy = along_y(u_ref[2 * half], ta_ref[2 * half * lx : (2 * half + 1) * lx, wide - 1 :])
            begin = lz + hz + half
            halo = from_next(jx, iy[lx - 2 : lx - 1], [r[begin : begin + 1, :ly] for r in came])
            before, after = pltpu.roll(iy, 1, 0), pltpu.roll(iy, lx - 1, 0)
            after = jnp.where(row == lx - 1, jnp.broadcast_to(halo, (lx, ly)), after)
            planes.append(jnp.where(row % 2 == 1, 0.5 * (before + after), iy))
        for half in range(hz):
            fine_out[2 * half] = u_ref[2 * half] - planes[half]
            if half + 1 < hz:
                fine_out[2 * half + 1] = u_ref[2 * half + 1] - 0.5 * (planes[half] + planes[half + 1])
        ixy_out[...] = planes[-1]
        evens = range(0, zn, 2)
        state = [jnp.concatenate([u1_ref[z] for z in evens], axis=1)]
        state += [jnp.concatenate([r[:, z * wide : (z + 1) * wide] for z in evens], axis=1) for r in xcame]
        spread = dot(qx2_ref[jx], jnp.concatenate(state, axis=0))
        spread = jnp.concatenate([spread[:, half * wide : (half + 1) * wide] for half in range(zn // 2)], axis=0)
        spread = dot(spread, qy2_ref[jy])
        for half in range(zn // 2):
            i2_out[half] = spread[half * xtwo.fine : (half + 1) * xtwo.fine]

    def second_apply(*refs):
        part_ref, zc_ref = refs[:2]
        xcame, zcame = refs[2 : dx + 1][::-1], refs[dx + 1 : dz + dx][::-1]
        tx2_ref, ty2_ref, u1_out, zt_out = refs[dz + dx :]
        jx, jy, jz = lax.axis_index("gx"), lax.axis_index("gy"), lax.axis_index("gz")
        own = []
        for zc in range(zn):
            total = part_ref[zc]
            for k, r in enumerate(zcame):
                total += chosen_by(zs[:, at_reach + k * zn + zc], jz) * r[...]
            u1_out[zc] = total
            own.append(total)
        own = jnp.concatenate(own + [jnp.zeros_like(own[0])] * 2, axis=1)
        across = dot(tx2_ref[jx], jnp.concatenate([own] + [r[...] for r in xcame], axis=0))
        cut = [across[:, z * wide : (z + 1) * wide] for z in range(zn + 2)]
        whole = [z for z in range(zn + 2) if z % 2 == 0 or z >= zn]
        joined = [jnp.concatenate([cut[z][c * tall : (c + 1) * tall] for c in range(3)], axis=1) for z in whole]
        made = dot(jnp.concatenate(joined, axis=0), ty2_ref[jy])
        for place, z in enumerate(whole):
            zt_out[z] = made[place * tall : (place + 1) * tall]
        made = dot(jnp.concatenate([cut[z][:tall] for z in range(1, zn, 2)], axis=0), ty2_ref[jy, :wide])
        for z in range(1, zn, 2):
            moved = made[(z // 2) * tall : (z // 2 + 1) * tall]
            if z < 4:
                begin = xtwo.n * (z // 2)
                moved += pltpu.roll(zc_ref[begin : begin + tall], wide2, 1)
            zt_out[z] = moved
        for z in (zn, zn + 1):
            zt_out[z, tall - 1 :] = cut[z][tall - 1 : tall]

    def third_apply(*refs):
        u1_ref, i2_ref, u_ref, ixy_ref, _, own_ref = refs[:6]
        came = refs[6 : 5 + dz]
        px1_ref, tx_ref, ty_ref, qy2_ref, fine_out, middle_out, coarse_out, coarsest_out = refs[5 + dz : 13 + dz]
        zbuf, qbuf, ubuf, last, middle, sems = refs[13 + dz :]
        part = lambda ref, j, starts, which: ref[j, starts[which] : starts[which + 1]]
        jx, jy, jz = lax.axis_index("gx"), lax.axis_index("gy"), lax.axis_index("gz")
        for k, r in enumerate((own_ref, *came)):
            zbuf[pl.ds((jz ^ k) * lz2, lz2)] = r[:lz2]
            qbuf[pl.ds((jz ^ k) * 2, 2)] = r[lz2:]
        at = jnp.minimum(jz + 1, dz - 1) * lz2
        plane_halo = dot(px1_ref[...], jnp.concatenate([zbuf[at + 1], zbuf[at + 3]], axis=0))
        everything = []
        for j in range(dz):
            for zc in range(lz2):
                total = zbuf[j * lz2 + zc]
                for i in range(dz):
                    if i != j:
                        total += float(zone.reach(j, i)[zc]) * qbuf[2 * i + (i < j)]
                everything.append(total)
        for z in range(0, z2, lz2):
            zbuf[z] = everything[z]
        if lz2 > 2:
            zbuf[z2 - 2] = everything[z2 - 2]
        at = jnp.minimum((jz + 1) * lz2, z2 - 2)
        halo = dot(part(tx_ref, jx, at_x3, 2), zbuf[at])
        edges = [jnp.zeros((1, wide), jnp.float32)] * (lz2 // 2)
        for k, r in enumerate(came):
            line = jnp.where((jz ^ (k + 1)) > jz, r[lz2, tall - 1 :], r[lz2 + 1, tall - 1 :])
            for half in range(lz2 // 2):
                edges[half] += chosen_by(zs[:, at_reach + k * zn + 2 * half], jz) * line
        fy = ytwo.fine
        edges = dot(jnp.concatenate(edges + [jnp.zeros((8 - lz2 // 2 % 8, wide), jnp.float32)], axis=0), qy2_ref[jy])
        plane_halo = dot(plane_halo, part(ty_ref, jy, at_y3, 3))
        halo = dot(halo, part(ty_ref, jy, at_y3, 2))[:, :fy]
        here = ixy_ref[...]
        last[...] = u_ref[lz - 1] - 0.5 * (here + jnp.where(jz == dz - 1, here, plane_halo))
        copies = [pltpu.make_async_copy(last, fine_out.at[lz - 1], sems.at[0])]
        copies[0].start()
        at_end = iota((xtwo.fine, fy), 0) == xtwo.fine - 1
        spread = [
            i2_ref[half][:, :fy] + jnp.where(at_end, jnp.broadcast_to(edges[half : half + 1, :fy], (xtwo.fine, fy)), 0.0)
            for half in range(lz2 // 2)
        ]
        spread.append(halo)
        for half in range(lz2 // 2):
            middle[2 * half] = u1_ref[2 * half][:, :fy] - spread[half]
            middle[2 * half + 1] = u1_ref[2 * half + 1][:, :fy] - 0.5 * (spread[half] + spread[half + 1])
        copies.append(pltpu.make_async_copy(middle, middle_out, sems.at[1]))
        copies[1].start()
        evens = [pltpu.roll(everything[z], packed - wide2, 1) for z in range(0, z2, 2)]
        arounds = [pltpu.roll(everything[z], packed - 2 * wide2, 1) for z in range(0, z2, 2)]
        second = []
        for zc in range(z3):
            total = evens[zc] - arounds[zc] - first2[zc] * arounds[0] - last2[zc] * arounds[-1]
            for z in range(z2):
                total += az2[zc][z] * everything[z]
            ubuf[zc] = total
            second.append(total)
        fy3, n3 = ythree.fine, xthree.n
        at = [jnp.minimum(jz * lz3 + 2 * half, z3 - 2) for half in range(lz3 // 2 + 1)]
        spread = dot(part(tx_ref, jx, at_x3, 1), jnp.concatenate([ubuf[a] for a in at], axis=1))
        joined = []
        for zc in range(lz4):
            base = zc * (z3 + 2)
            along = chosen_by(zt[:, base], jz) * second[0]
            for z in range(1, z3):
                along += chosen_by(zt[:, base + z], jz) * second[z]
            even = ubuf[2 * (jz * lz4 + zc)]
            around = even + chosen_by(zt[:, base + z3], jz) * second[0] + chosen_by(zt[:, base + z3 + 1], jz) * second[z3 - 2]
            parts = [dot(tx_ref[jx, c * n3 : (c + 1) * n3, :], plane) for c, plane in enumerate((along, even, around))]
            joined.append(jnp.concatenate(parts, axis=1))
        spread = jnp.concatenate([spread[:, h * packed : (h + 1) * packed] for h in range(len(at))], axis=0)
        spread = dot(spread, part(ty_ref, jy, at_y3, 1))[:, :fy3]
        coarsest = dot(jnp.concatenate(joined, axis=0), part(ty_ref, jy, at_y3, 0))[:, : ythree.n]
        for zc in range(lz4):
            coarsest_out[zc] = coarsest[zc * n3 : (zc + 1) * n3]
        spread = [spread[h * xthree.fine : (h + 1) * xthree.fine] for h in range(len(at))]
        for half in range(lz3 // 2):
            at = jz * lz3 + 2 * half
            coarse_out[2 * half] = ubuf[at][: xthree.fine, :fy3] - spread[half]
            coarse_out[2 * half + 1] = ubuf[at + 1][: xthree.fine, :fy3] - 0.5 * (spread[half] + spread[half + 1])
        for copy in copies:
            copy.wait()

    u, own_ty, own_fx, own_sums, *ym = kernel_call(
        y_messages,
        [(lz, lx, ly), tables_y.shape[1:], fx.shape[1:], sums.shape[1:]] + [(rowsy, lz * lx)] * (dy - 1),
        [field, messages_y, tables_y, to32(fx), to32(sums)],
        scratch=[pltpu.VMEM(messages_y.shape[1:], jnp.float32), pltpu.SemaphoreType.DMA((5,))],
        left=(0, 1, 2, 3, 4),
    )
    ycame = swapped(ym, "gy")
    ta_own, tsm_own, head, point = kernel_call(
        y_own,
        [(lz * lx, wide), (hz * hx1, 2 * wide), (heads, wide), (round_up(hz + 1, 8), 2 * wide)],
        [u, own_ty, own_fx],
    )
    xm = kernel_call(
        x_messages,
        [(round_up(lz + 2 * hz + 1, 8), max(wide, ly))] * (dx - 1),
        [u, *ycame, own_ty, own_sums, head, point],
        scratch=[pltpu.VMEM((ss8, hz * hx1), jnp.float32)],
    )
    xcame = swapped(xm, "gx")
    six_cols = (zn + 2) * wide
    ta_v, own_zc, six, own_sent = kernel_call(
        y_apply,
        [(lz * lx, wide), (xtwo.n + tall, wide), (xone.n, six_cols), (f2x.shape[1], six_cols)],
        [*ycame, own_ty, ta_own, tsm_own, tables_x, to32(f2x)],
        scratch=[pltpu.VMEM((ss8, hz * hx1), jnp.float32)],
    )
    zc, u1_part, *sent = kernel_call(
        x_apply,
        [(xtwo.n + tall, wide), (zn, xone.n, wide)] + [(xone.n, wide)] * (dz - 1) + [(kx, six_cols)] * (dx - 1),
        [own_zc, six, own_sent, *xcame[::-1], to32(rows_x)],
        scratch=[pltpu.VMEM((lz + hz, ext, wide), jnp.float32)],
    )
    tails = sent[dz - 1 :]
    zcame = swapped(sent[: dz - 1], "gz")
    if dz > 1 and dx > 1:
        zcame[0], tails[0] = lax.optimization_barrier((zcame[0], tails[0]))
    xtcame = swapped(tails, "gx")
    u1, zmsg = kernel_call(
        second_apply,
        [(zn, xone.n, wide), (lz2 + 2, tall, packed)],
        [u1_part, zc, *xtcame[::-1], *zcame[::-1], to32(tx2), to32(ty2)],
    )
    beside = kernel_call(
        interpolate,
        [(lz, lx, ly), (lx, ly), (lz2 // 2, xtwo.fine, ly2)],
        [u, ta_v, u1, *xcame[::-1], *xtcame[::-1], to32(qx2), to32(qy2)],
    )
    ztcame, (fine, ixy, i2) = gathered(zmsg, "gz", beside)
    return kernel_call(
        third_apply,
        [(lz, lx, ly), (lz2, xtwo.fine, ytwo.fine), (lz3, xthree.fine, ythree.fine), (lz4, xthree.n, ythree.n)],
        [u1, i2, u, ixy, fine, zmsg, *ztcame, to32(px1), tables_x3, tables_y3, to32(qy2)],
        scratch=[
            pltpu.VMEM((z2, tall, packed), jnp.float32),
            pltpu.VMEM((2 * dz, tall, packed), jnp.float32),
            pltpu.VMEM((z3, tall, packed), jnp.float32),
            pltpu.VMEM((lx, ly), jnp.float32),
            pltpu.VMEM((lz2, xtwo.fine, ytwo.fine), jnp.float32),
            pltpu.SemaphoreType.DMA((2,)),
        ],
        left=(4,),
        left_out=(0, 1),
        aliases={4: 0},
    )


def solution(mesh):
    spec = P("gz", "gx", "gy")
    counts = tuple(mesh.shape[a] for a in ("gz", "gx", "gy"))
    return jax.shard_map(
        functools.partial(shards, counts), mesh=mesh, in_specs=(spec,), out_specs=(spec,) * 4, check_vma=False
    )
```

```python
import functools
import math

import jax
import jax.numpy as jnp
import numpy as np
from jax import lax
from jax.experimental import pallas as pl
from jax.experimental.pallas import tpu as pltpu
from jax.sharding import PartitionSpec as P

band_ratio = 2.0 - math.sqrt(3.0)
f32 = np.float32


def round_up(value, unit):
    return -(-value // unit) * unit


def dense(fine):
    n = fine // 2
    steps = np.arange(n)[:, None] - np.arange(n)[None, :]
    lower = np.where(steps >= 0, (-band_ratio) ** np.maximum(steps, 0), 0.0)
    inverse = lower.T @ lower
    mass = 4.0 * np.eye(fine) + np.eye(fine, k=1) + np.eye(fine, k=-1)
    weights = np.where(np.arange(n) == n - 1, 1.0, 0.5)[:, None]
    earlier = np.concatenate([np.zeros((1, fine)), mass[1::2][:-1]])
    product = inverse @ (0.5 * band_ratio * (mass[0::2] + weights * mass[1::2] + 0.5 * earlier))
    return product, inverse[:, 0] * (3 * band_ratio - 1), inverse[:, -1] * (2 * band_ratio)


class Level:
    def __init__(self, whole, count, following):
        self.count, self.fine = count, whole // count
        self.n = self.fine // 2
        self.product, self.first, self.last = dense(whole)
        self.following = following
        self.kept = following.functional_count if following else 0
        self.functional_count = 4 + 2 * self.kept
        self.even = np.zeros((self.n, self.fine))
        self.even[np.arange(self.n), 2 * np.arange(self.n)] = 1.0
        self.v = [self.towards(i, i * self.n - 1) for i in range(count)]
        self.w = [self.towards(i, (i + 1) * self.n) for i in range(count)]
        self.functionals = []
        for i in range(count):
            own = np.zeros((4, self.fine))
            own[0, 0] = own[1, self.fine - 2] = 1.0
            own[2], own[3] = self.v[i], self.w[i]
            if following:
                inner = following.functionals[i]
                own = np.concatenate([own, inner @ self.even, inner @ self.block(i, i)])
            self.functionals.append(own)
        built = [self.build(j) for j in range(count)]
        self.needs = [needs for needs, _ in built]
        self.tables = [tables for _, tables in built]

    def rows(self, i):
        return slice(i * self.n, (i + 1) * self.n)

    def block(self, i, j):
        return self.product[self.rows(i), j * self.fine : (j + 1) * self.fine]

    def towards(self, i, row):
        if not 0 <= row < self.count * self.n:
            return np.zeros(self.fine)
        values = self.product[row, i * self.fine : (i + 1) * self.fine]
        return values / np.abs(values).max()

    def reach(self, i, j):
        side = self.v[j] if j > i else self.w[j]
        best = np.argmax(np.abs(side))
        return self.block(i, j)[:, best] / side[best]

    def side(self, i, j):
        return 2 if j > i else 3

    def through_even(self, f):
        return 4 + f if f else 0

    def build(self, j):
        n, fine, many, end = self.n, self.fine, self.functional_count, self.count - 1
        targets = self.following.needs[j] if self.following else []
        others = [j ^ k for k in range(1, self.count)]
        at = lambda i, f: fine + many * ((i ^ j) - 1) + f
        product = np.zeros((n + len(targets), fine + many * len(others)))
        even, used = np.zeros_like(product), np.zeros(product.shape[1], bool)
        used[:fine] = True
        product[:n, :fine] = self.block(j, j)
        even[:n, :fine] = self.even
        first, last = [self.first[self.rows(j)]], [self.last[self.rows(j)]]
        for i in others:
            product[:n, at(i, self.side(j, i))] = self.reach(j, i)
            used[at(i, self.side(j, i))] = True
        for row, (i, f) in enumerate(targets, n):
            inner = self.following.functionals[i][f]
            product[row, :fine] = inner @ self.block(i, j)
            product[row, at(i, 4 + self.kept + f)] = 1.0
            even[row, at(i, self.through_even(f))] = 1.0
            used[at(i, 4 + self.kept + f)] = used[at(i, self.through_even(f))] = True
            for other in others:
                if other != i:
                    product[row, at(other, self.side(i, other))] = inner @ self.reach(i, other)
                    used[at(other, self.side(i, other))] = True
            first.append([inner @ self.first[self.rows(i)]])
            last.append([inner @ self.last[self.rows(i)]])
        around = even.copy()
        from_first, from_last = 0 if j == 0 else at(0, 0), fine - 2 if j == end else at(end, 1)
        around[:, from_first] += np.concatenate(first)
        around[:, from_last] += np.concatenate(last)
        used[from_first] = used[from_last] = True
        if j < end:
            used[at(j + 1, 0)] = True
        needs = [(j ^ (1 + place // many), place % many) for place in np.flatnonzero(used[fine:])]
        return needs, (product[:, used], even[:, used], around[:, used])

    def sent(self, i, k):
        return [f for block, f in self.needs[i ^ k] if block == i]

    def most_sent(self):
        return max([len(self.sent(i, k)) for i in range(self.count) for k in range(1, self.count)] + [1])

    def most_needed(self):
        return max(len(needs) for needs in self.needs)

    def next_first(self, j, own, fallback):
        return fallback if j == self.count - 1 else own + self.needs[j].index((j + 1, 0))


def interpolation(level, j, inputs, coarse=False):
    table = np.zeros((level.fine, inputs))
    if coarse:
        places = list(range(level.n))
        last = level.following.next_first(j, level.n, level.n - 1)
    else:
        places = [2 * c for c in range(level.n)]
        last = level.next_first(j, level.fine, level.fine - 2)
    places.append(last)
    for c in range(level.n):
        table[2 * c, places[c]] = 1.0
        table[2 * c + 1, places[c]] += 0.5
        table[2 * c + 1, places[c + 1]] += 0.5
    return table


def chain(whole, count, levels):
    made = None
    for depth in reversed(range(levels)):
        made = Level(whole >> depth, count, made)
    return made


def padded(table, rows, cols):
    out = np.zeros((rows, cols))
    out[: table.shape[0], : table.shape[1]] = table
    return out


highest = lax.Precision.HIGHEST


def dot(a, b, dims=((1,), (0,))):
    return lax.dot_general(a, b, (dims, ((), ())), precision=highest, preferred_element_type=jnp.float32)


def kernel_call(body, outs, arrays, scratch=(), left=(), left_out=(), aliases={}):
    space = lambda place, where: pl.BlockSpec(memory_space=pltpu.HBM if place in where else pltpu.VMEM)
    return pl.pallas_call(
        body,
        out_shape=[jax.ShapeDtypeStruct(shape, jnp.float32) for shape in outs],
        in_specs=[space(i, left) for i in range(len(arrays))],
        out_specs=[space(i, left_out) for i in range(len(outs))],
        scratch_shapes=list(scratch),
        input_output_aliases=aliases,
        compiler_params=pltpu.CompilerParams(vmem_limit_bytes=40 << 20),
    )(*(pltpu.with_memory_space_constraint(a, pltpu.HBM) if i in left else a for i, a in enumerate(arrays)))


def swapped(values, axis):
    count = lax.axis_size(axis)
    return [lax.ppermute(v, axis, [(i, i ^ k) for i in range(count)]) for k, v in enumerate(values, 1)]


def gathered(value, axis, beside):
    count = lax.axis_size(axis)
    if count != 4:
        return swapped([value] * (count - 1), axis), beside
    by = lambda k, what: lax.ppermute(what, axis, [(i, i ^ k) for i in range(count)])
    far, beside = lax.optimization_barrier((by(2, value), beside))
    return [by(1, value), far, by(1, far)], beside


def chosen_by(values, j):
    chosen = float(values[0])
    for place in range(1, len(values)):
        if any(values[place] != values[0] for place in range(len(values))):
            chosen = jnp.where(j == place, f32(values[place]), chosen)
    return chosen


def iota(shape, dim):
    return lax.broadcasted_iota(jnp.int32, shape, dim)


def shards(counts, field):
    dz, dx, dy = counts
    lz, lx, ly = field.shape
    nz, nx, ny = lz * dz, lx * dx, ly * dy

    yone = chain(ny, dy, 3)
    ytwo, ythree = yone.following, yone.following.following
    xone = chain(nx, dx, 1)
    xtwo = chain(nx // 2, dx, 2)
    xthree = xtwo.following
    zone = Level(nz, dz, None)

    points_a = lambda fs: [f for f in fs if f in (2, 3) or f >= 4 + yone.kept]
    points_s = lambda fs: [f for f in fs if f not in (2, 3) and f < 4 + yone.kept]
    pairs_y = [(i, k) for i in range(dy) for k in range(1, dy)]
    sa = max([len(points_a(yone.sent(i, k))) for i, k in pairs_y] + [0]) + 1
    ss = max([len(points_s(yone.sent(i, k))) for i, k in pairs_y] + [1])
    per_row = (lz * lx) // ((lz // 2) * (lx // 2))
    rowsy = round_up(sa + -(-ss // per_row), 8)
    sa8, ss8 = round_up(sa, 8), round_up(ss, 8)
    wide1 = yone.n + ytwo.most_needed()
    wide2 = ytwo.n + ythree.most_needed()
    wide = packed = round_up(max(wide1 + 1, 3 * wide2, wide2 + wide1), 128)
    kx = round_up(xtwo.most_sent(), 8)
    rowsx = xtwo.fine + kx * (dx - 1)
    tall = round_up(max(xtwo.n + xthree.most_needed() + 1, xone.n // 2 + 1), 8)

    others_y = max(dy - 1, 1)
    fya = np.zeros((dy, others_y * sa8, ly))
    fys = np.zeros((dy, others_y * ss8, ly))
    ta = np.zeros((dy, ly, wide))
    wa = np.zeros((dy, others_y * rowsy, wide))
    tsm = np.zeros((dy, ly, 2 * wide))
    wsm = np.zeros((dy, others_y * ss8, 2 * wide))
    for j in range(dy):
        product, even, around = yone.tables[j]
        used = product.shape[0]
        ta[j, :, :used] = product[:, :ly].T
        tsm[j, :, :used] = even[:, :ly].T
        tsm[j, :, wide : wide + used] = around[:, :ly].T
        for k in range(1, dy):
            mine = yone.sent(j, k)
            fya[j, (k - 1) * sa8 :][: len(points_a(mine))] = yone.functionals[j][points_a(mine)]
            fya[j, (k - 1) * sa8 + sa - 1] = yone.functionals[j][0]
            fys[j, (k - 1) * ss8 :][: len(points_s(mine))] = yone.functionals[j][points_s(mine)]
            came = yone.sent(j ^ k, k)
            for f in came:
                column = ly + yone.needs[j].index((j ^ k, f))
                if f in points_a(came):
                    wa[j, (k - 1) * rowsy + points_a(came).index(f), :used] = product[:, column]
                else:
                    row = (k - 1) * ss8 + points_s(came).index(f)
                    wsm[j, row, :used] = even[:, column]
                    wsm[j, row, wide : wide + used] = around[:, column]
        if j == dy - 1:
            ta[j, ly - 2, wide - 1] = 0.5
        else:
            wa[j, rowsy * ((j ^ (j + 1)) - 1) + sa - 1, wide - 1] = 0.5

    ext = round_up(max(dx - 1, 1), 8)
    fx = np.zeros((dx, lx, 8))
    heads = round_up(2 * lz + lz // 2, 8)
    sums = np.zeros((dx, heads, lz * lx))
    txa = np.zeros((dx, xone.n, lx + ext))
    txm = np.zeros((dx, xone.n, xone.n + ext))
    for j in range(dx):
        fx[j, :, :2] = xone.functionals[j][2:4].T
        for z in range(lz):
            sums[j, 2 * z : 2 * z + 2, z * lx : (z + 1) * lx] = xone.functionals[j][2:4]
        for half in range(lz // 2):
            sums[j, 2 * lz + half, 2 * half * lx] = 1.0
        product, even, around = xone.tables[j]
        txa[j, :, :lx] = product[:, :lx]
        txm[j, :, : xone.n] = around[:, :lx:2]
        for column, (i, f) in enumerate(xone.needs[j], lx):
            if f in (2, 3):
                txa[j, :, lx + (i ^ j) - 1] = product[:, column]
            else:
                txm[j, :, xone.n + (i ^ j) - 1] += around[:, column] * ((f == 0 and i == 0) or (f == 1 and i == dx - 1))

    zn = zone.n
    zs = np.zeros((dz, 2 * lz + 2 + zn * (lz + dz + 1)))
    for j in range(dz):
        cv, cw = zone.v[j], zone.w[j]
        k_last = (zone.last[zone.rows(0)] / zone.reach(0, j))[0] if 0 < j == dz - 1 else 0.0
        k_first = (zone.first[zone.rows(dz - 1)] / zone.reach(dz - 1, j))[-1] if j == 0 and dz > 1 else 0.0
        parts = [cv, cw, [k_last, k_first], zone.block(j, j).reshape(-1)]
        parts += [zone.reach(j, j ^ k) for k in range(1, dz)]
        parts += [zone.first[zone.rows(j)] * (j == 0), zone.last[zone.rows(j)] * (j == dz - 1)]
        zs[j] = np.concatenate([np.asarray(p, np.float64) for p in parts])
    at_local = 2 * lz + 2
    at_reach = at_local + zn * lz
    at_first = at_reach + zn * (dz - 1)
    at_last = at_first + zn

    f2x = np.zeros((dx, max(dx - 1, 1) * kx, xtwo.fine))
    tx2 = np.zeros((dx, 3 * tall, rowsx))
    qx2 = np.zeros((dx, xtwo.fine, rowsx))
    tx3 = np.zeros((dx, 3 * xthree.n, tall))
    qx3 = np.zeros((dx, xthree.fine, tall))
    px3 = np.zeros((dx, xtwo.fine, tall))
    for j in range(dx):
        columns = list(range(xtwo.fine))
        for i, f in xtwo.needs[j]:
            columns.append(xtwo.fine + kx * ((i ^ j) - 1) + xtwo.sent(i, i ^ j).index(f))
        for c, table in enumerate(xtwo.tables[j]):
            tx2[j, c * tall : c * tall + table.shape[0], columns] = table.T
        qx2[j][:, columns] = interpolation(xtwo, j, len(columns))
        tx2[j, tall - 1, xtwo.fine :] = qx2[j, -1, xtwo.fine :]
        for k in range(1, dx):
            mine = xtwo.sent(j, k)
            f2x[j, (k - 1) * kx :][: len(mine)] = xtwo.functionals[j][mine]
        for c, table in enumerate(xthree.tables[j]):
            tx3[j, c * xthree.n : (c + 1) * xthree.n, : table.shape[1]] = table
        qx3[j] = interpolation(xthree, j, tall)
        px3[j] = interpolation(xtwo, j, tall, True)

    ty2 = np.zeros((dy, 3 * wide, packed))
    qy2 = np.zeros((dy, wide, round_up(ytwo.fine, 128)))
    ty3 = np.zeros((dy, 3 * packed, 128))
    qy3 = np.zeros((dy, packed, 128))
    py3 = np.zeros((dy, packed, round_up(ytwo.fine, 128)))
    px1 = np.zeros((lx, 2 * tall))
    py1 = np.zeros((dy, packed, ly))
    for j in range(dy):
        for c, table in enumerate(ytwo.tables[j]):
            ty2[j, c * wide : c * wide + table.shape[1], c * wide2 : c * wide2 + table.shape[0]] = table.T
        qy2[j, :, : ytwo.fine] = interpolation(ytwo, j, wide).T
        for c, table in enumerate(ythree.tables[j]):
            ty3[j, c * packed : c * packed + table.shape[1], : ythree.n] = (-1.0 if c == 2 else 1.0) * table.T
        qy3[j, :, : ythree.fine] = interpolation(ythree, j, packed).T
        py1[j, wide2:] = interpolation(yone, j, packed - wide2, True).T
        py3[j, wide2:, : ytwo.fine] = interpolation(ytwo, j, packed - wide2, True).T
    for c in range(xone.n):
        begin = c if c < xtwo.n else tall + c - xtwo.n
        px1[2 * c, begin] = 1.0
        px1[2 * c + 1, begin : begin + 2] = 0.5
    az2, first2, last2 = (t.tolist() for t in dense(nz // 2))
    az3, first3, last3 = dense(nz // 4)
    z2, z3 = nz // 2, nz // 4
    lz2, lz3 = lz // 2, lz // 4
    zt = np.concatenate([az3, first3[:, None], last3[:, None]], axis=1)
    zt = zt.reshape(dz, (lz // 8) * (z3 + 2))
    lz4 = lz // 8

    to32 = lambda table: jnp.asarray(table, jnp.float32)

    def stacked(*tables):
        cols = max(t.shape[2] for t in tables)
        starts = np.cumsum([0] + [round_up(t.shape[1], 8) for t in tables])
        out = np.zeros((tables[0].shape[0], starts[-1], cols))
        for t, begin in zip(tables, starts):
            out[:, begin : begin + t.shape[1], : t.shape[2]] = t
        return to32(out), [int(v) for v in starts]

    messages_y, _ = stacked(fya, fys)
    tables_y, _ = stacked(np.concatenate([ta, tsm], axis=2), np.concatenate([wa, np.zeros((dy, wa.shape[1], 2 * wide))], axis=2),
                          np.concatenate([np.zeros((dy, wsm.shape[1], wide)), wsm], axis=2))
    tables_x, _ = stacked(txa[:, :, :lx], txm[:, :, : xone.n])
    rows_x = np.concatenate([txa[:, :, lx:], txm[:, :, xone.n :]], axis=2)
    rows_x = np.concatenate([rows_x, f2x @ rows_x], axis=1)
    tables_x3, at_x3 = stacked(tx3, qx3, px3)
    tables_y3, at_y3 = stacked(ty3, qy3, py3, py1)
    hz, hx1 = lz // 2, lx // 2
    ly2 = round_up(ytwo.fine, 128)

    def y_messages(u_hbm, table_hbm, ty_hbm, fx_hbm, sums_hbm, u_ref, ty_ref, fx_ref, sums_ref, *refs):
        outs, (table, sems) = refs[:-2], refs[-2:]
        j = lax.axis_index("gy")
        nt = ((1,), (1,))
        copies = [
            pltpu.make_async_copy(table_hbm.at[j], table, sems.at[0]),
            pltpu.make_async_copy(u_hbm, u_ref, sems.at[1]),
            pltpu.make_async_copy(ty_hbm.at[j], ty_ref, sems.at[2]),
            pltpu.make_async_copy(fx_hbm.at[lax.axis_index("gx")], fx_ref, sems.at[3]),
            pltpu.make_async_copy(sums_hbm.at[lax.axis_index("gx")], sums_ref, sems.at[4]),
        ]
        for copy in copies:
            copy.start()
        for copy in copies[:2]:
            copy.wait()
        lines = dot(table[: others_y * sa8], u_ref[...].reshape(lz * lx, ly), nt)
        even = jnp.concatenate([u_ref[2 * z, pl.ds(0, hx1, stride=2), :] for z in range(hz)], axis=0)
        points = dot(table[others_y * sa8 :], even, nt)
        for k, out in enumerate(outs):
            out[: min(sa8, rowsy)] = lines[k * sa8 : k * sa8 + min(sa8, rowsy)]
            if rowsy > sa8:
                out[sa8:] = jnp.zeros_like(out[sa8:])
            for f in range(ss):
                begin = hz * hx1 * (f % per_row)
                row = sa + f // per_row
                out[row : row + 1, begin : begin + hz * hx1] = points[k * ss8 + f : k * ss8 + f + 1]
        for copy in copies[2:]:
            copy.wait()

    def along_y(u, half_halo):
        lane = iota(u.shape, 1)
        before, after = pltpu.roll(u, 1, 1), pltpu.roll(u, ly - 1, 1)
        edge = 0.5 * before + jnp.broadcast_to(half_halo, u.shape)
        return jnp.where(lane == ly - 1, edge, jnp.where(lane % 2 == 1, 0.5 * (before + after), u))

    def from_next(jx, own, rows):
        for k, other in enumerate(rows):
            own = jnp.where((jx ^ (k + 1)) == jx + 1, other, own)
        return own

    def y_own(u_ref, ty_ref, fx_ref, ta_out, tsm_out, heads_out, points_out):
        jx = lax.axis_index("gx")
        ta_all = dot(u_ref[...].reshape(lz * lx, ly), ty_ref[:ly, :wide])
        even = jnp.concatenate([u_ref[2 * z, pl.ds(0, hx1, stride=2), :] for z in range(hz)], axis=0)
        tsm_all = dot(even, ty_ref[:ly, wide:])
        ta_out[...] = ta_all
        tsm_out[...] = tsm_all
        weights = [jnp.broadcast_to(fx_ref[:, c : c + 1], (lx, wide)) for c in range(2)]
        heads_out[...] = jnp.zeros_like(heads_out)
        points_out[...] = jnp.zeros_like(points_out)
        for z in range(lz):
            part = ta_all[z * lx : (z + 1) * lx]
            for c in range(2):
                heads_out[2 * z + c : 2 * z + c + 1] = jnp.sum(part * weights[c], axis=0, keepdims=True)
        for half in range(hz):
            heads_out[2 * lz + half : 2 * lz + half + 1] = ta_all[2 * half * lx : 2 * half * lx + 1]
            tm = tsm_all[half * hx1 : (half + 1) * hx1]
            points_out[half : half + 1] = jnp.where(jx == 0, tm[0:1], tm[hx1 - 1 : hx1])
        points_out[hz : hz + 1] = tsm_all[0:1]

    def came_points(ref, points):
        points[...] = jnp.zeros_like(points)
        for f in range(ss):
            begin = hz * hx1 * (f % per_row)
            row = sa + f // per_row
            points[f : f + 1] = ref[row : row + 1, begin : begin + hz * hx1]
        return points[...]

    def x_messages(*refs):
        u_ref, came = refs[0], refs[1:dy]
        ty_ref, sums_ref, heads_ref, points_ref = refs[dy : dy + 4]
        xm_outs, points = refs[dy + 4 : -1], refs[-1]
        jx = lax.axis_index("gx")
        nt = ((1,), (1,))
        head, point = heads_ref[...], points_ref[...]
        shape = (point.shape[0], hz * hx1)
        row, lane = iota(shape, 0), iota(shape, 1)
        line = jnp.where(row == hz, 0, row * hx1 + jnp.where(jx == 0, 0, hx1 - 1))
        one = jnp.where((lane == line) & (row <= hz), 1.0, 0.0)
        for k, ref in enumerate(came):
            begin = ly + rowsy * k
            head += dot(dot(sums_ref[...], ref[...], nt), ty_ref[begin : begin + rowsy, :wide])
            begin = ly + rowsy * (dy - 1) + ss8 * k
            point += dot(dot(one, came_points(ref, points), nt), ty_ref[begin : begin + ss8, wide:])
        for out in xm_outs:
            out[lz + 2 * hz :] = jnp.zeros_like(out[lz + 2 * hz :])
            out[lz + 2 * hz : lz + 2 * hz + 1, :wide] = point[hz : hz + 1, :wide]
        for z in range(lz):
            for k, out in enumerate(xm_outs):
                out[z : z + 1, :wide] = jnp.where((jx ^ (k + 1)) < jx, head[2 * z : 2 * z + 1], head[2 * z + 1 : 2 * z + 2])
        for half in range(hz):
            first = head[2 * lz + half : 2 * lz + half + 1, wide - 1 :]
            iy = along_y(u_ref[2 * half, :8], jnp.broadcast_to(first, (8, 1)))
            for out in xm_outs:
                out[lz + half : lz + half + 1, :wide] = point[half : half + 1, wide:]
                out[lz + hz + half : lz + hz + half + 1, :ly] = iy[0:1]

    def y_apply(*refs):
        came = refs[: dy - 1]
        ty_ref, ta_ref, tsm_ref, tx_ref, f2x_ref, ta_out, zc_out, six_out, sent_out, points = refs[dy - 1 :]
        jx, jz = lax.axis_index("gx"), lax.axis_index("gz")
        tn = ((0,), (0,))
        ta_all, tsm_all = ta_ref[...], tsm_ref[...]
        for k, ref in enumerate(came):
            begin = ly + rowsy * k
            ta_all += dot(ref[...], ty_ref[begin : begin + rowsy, :wide], tn)
            begin = ly + rowsy * (dy - 1) + ss8 * k
            tsm_all += dot(came_points(ref, points), ty_ref[begin : begin + ss8, wide:], tn)
        ta_out[...] = ta_all
        zc_out[...] = jnp.zeros_like(zc_out)
        zc_out[:hx1] = tsm_all[:hx1, :wide]
        xa, xm = [], []
        for z in range(0, lz, 2):
            pair = jnp.concatenate([ta_all[z * lx : (z + 1) * lx], ta_all[(z + 1) * lx : (z + 2) * lx]], axis=1)
            both = dot(tx_ref[jx, : xone.n], pair)
            xa += [both[:, :wide], both[:, wide:]]
        for half in range(0, hz, 2):
            pair = jnp.concatenate([tsm_all[h * hx1 : (h + 1) * hx1, wide:] for h in (half, half + 1)], axis=1)
            both = dot(tx_ref[jx, xone.n :, : xone.n], pair)
            xm += [both[:, :wide], both[:, wide:]]
        six = along_planes(jz, xa, xm)
        for half in range(hz):
            six[half] += tsm_all[half * hx1 : (half + 1) * hx1, :wide]
        six = jnp.concatenate(six, axis=1)
        six_out[...] = six
        sent_out[...] = dot(f2x_ref[jx], six)

    def along_planes(jz, xa, xm):
        scalar = lambda place: chosen_by(zs[:, place], jz)
        made = []
        for zc in range(zn):
            total = -xm[zc] - scalar(at_first + zc) * xm[0] - scalar(at_last + zc) * xm[hz - 1]
            for z in range(lz):
                total += scalar(at_local + zc * lz + z) * xa[z]
            made.append(total)
        v = -scalar(2 * lz) * xm[hz - 1]
        w = -scalar(2 * lz + 1) * xm[0]
        for z in range(lz):
            v += scalar(z) * xa[z]
            w += scalar(lz + z) * xa[z]
        return made + [v, w]

    def x_apply(*refs):
        own_zc_ref, six_ref, own_sent_ref = refs[:3]
        came = refs[3 : 2 + dx][::-1]
        rows_ref, zc_out, u1_out = refs[2 + dx : 5 + dx]
        planes_out, xt_outs, rest = refs[5 + dx : 4 + dx + dz], refs[4 + dx + dz : -1], refs[-1]
        jx, jz = lax.axis_index("gx"), lax.axis_index("gz")
        rest[...] = jnp.zeros_like(rest)
        for k, r in enumerate(came):
            for z in range(lz + hz):
                rest[z, k : k + 1] = r[z : z + 1, :wide]
        zero = [jnp.zeros_like(rest[0])]
        lines_a = along_planes(jz, [rest[z] for z in range(lz)], zero * hz)
        lines_m = along_planes(jz, zero * lz, [rest[lz + half] for half in range(hz)])
        lines = jnp.concatenate([jnp.concatenate(lines_a, axis=1), jnp.concatenate(lines_m, axis=1)], axis=0)
        added = dot(rows_ref[jx], lines)
        six = six_ref[...] + added[: xone.n]
        sent = own_sent_ref[...] + added[xone.n :]
        zc_out[...] = own_zc_ref[...]
        begin = lz + 2 * hz
        zc_out[hx1 : hx1 + 1] = from_next(jx, own_zc_ref[hx1 - 1 : hx1], [r[begin : begin + 1, :wide] for r in came])
        for zc in range(zn):
            u1_out[zc] = six[:, zc * wide : (zc + 1) * wide]
        v, w = six[:, zn * wide : (zn + 1) * wide], six[:, (zn + 1) * wide :]
        for k, out in enumerate(planes_out):
            out[...] = jnp.where((jz ^ (k + 1)) > jz, w, v)
        for k, out in enumerate(xt_outs):
            out[...] = sent[k * kx : (k + 1) * kx]

    def interpolate(*refs):
        u_ref, ta_ref, u1_ref = refs[:3]
        came, xcame = refs[3 : 2 + dx][::-1], refs[2 + dx : 1 + 2 * dx][::-1]
        qx2_ref, qy2_ref, fine_out, ixy_out, i2_out = refs[1 + 2 * dx :]
        jx, jy = lax.axis_index("gx"), lax.axis_index("gy")
        row = iota((lx, ly), 0)
        planes = []
        for half in range(hz):
            iy = along_y(u_ref[2 * half], ta_ref[2 * half * lx : (2 * half + 1) * lx, wide - 1 :])
            begin = lz + hz + half
            halo = from_next(jx, iy[lx - 2 : lx - 1], [r[begin : begin + 1, :ly] for r in came])
            before, after = pltpu.roll(iy, 1, 0), pltpu.roll(iy, lx - 1, 0)
            after = jnp.where(row == lx - 1, jnp.broadcast_to(halo, (lx, ly)), after)
            planes.append(jnp.where(row % 2 == 1, 0.5 * (before + after), iy))
        for half in range(hz):
            fine_out[2 * half] = u_ref[2 * half] - planes[half]
            if half + 1 < hz:
                fine_out[2 * half + 1] = u_ref[2 * half + 1] - 0.5 * (planes[half] + planes[half + 1])
        ixy_out[...] = planes[-1]
        evens = range(0, zn, 2)
        state = [jnp.concatenate([u1_ref[z] for z in evens], axis=1)]
        state += [jnp.concatenate([r[:, z * wide : (z + 1) * wide] for z in evens], axis=1) for r in xcame]
        spread = dot(qx2_ref[jx], jnp.concatenate(state, axis=0))
        spread = jnp.concatenate([spread[:, half * wide : (half + 1) * wide] for half in range(zn // 2)], axis=0)
        spread = dot(spread, qy2_ref[jy])
        for half in range(zn // 2):
            i2_out[half] = spread[half * xtwo.fine : (half + 1) * xtwo.fine]

    def second_own(*refs):
        part_ref, zcame = refs[0], refs[1:dz][::-1]
        tx2_ref, u1_out, across_out = refs[dz:]
        jx, jz = lax.axis_index("gx"), lax.axis_index("gz")
        own = []
        for zc in range(zn):
            total = part_ref[zc]
            for k, r in enumerate(zcame):
                total += chosen_by(zs[:, at_reach + k * zn + zc], jz) * r[...]
            u1_out[zc] = total
            own.append(total)
        across_out[...] = dot(tx2_ref[jx, :, : xtwo.fine], jnp.concatenate(own, axis=1))

    def second_apply(across_ref, zc_ref, *refs):
        xcame, (tx2_ref, ty2_ref, zt_out) = refs[:-3][::-1], refs[-3:]
        jx, jy = lax.axis_index("gx"), lax.axis_index("gy")
        across = dot(tx2_ref[jx, :, xtwo.fine :], jnp.concatenate([r[...] for r in xcame], axis=0))
        across = jnp.concatenate([across_ref[...] + across[:, : zn * wide], across[:, zn * wide :]], axis=1)
        cut = [across[:, z * wide : (z + 1) * wide] for z in range(zn + 2)]
        whole = [z for z in range(zn + 2) if z % 2 == 0 or z >= zn]
        joined = [jnp.concatenate([cut[z][c * tall : (c + 1) * tall] for c in range(3)], axis=1) for z in whole]
        made = dot(jnp.concatenate(joined, axis=0), ty2_ref[jy])
        for place, z in enumerate(whole):
            zt_out[z] = made[place * tall : (place + 1) * tall]
        made = dot(jnp.concatenate([cut[z][:tall] for z in range(1, zn, 2)], axis=0), ty2_ref[jy, :wide])
        for z in range(1, zn, 2):
            moved = made[(z // 2) * tall : (z // 2 + 1) * tall]
            if z < 4:
                begin = xtwo.n * (z // 2)
                moved += pltpu.roll(zc_ref[begin : begin + tall], wide2, 1)
            zt_out[z] = moved
        for z in (zn, zn + 1):
            zt_out[z, tall - 1 :] = cut[z][tall - 1 : tall]

    def third_apply(*refs):
        u1_ref, i2_ref, u_ref, ixy_ref, _, own_ref = refs[:6]
        came = refs[6 : 5 + dz]
        px1_ref, tx_ref, ty_ref, qy2_ref, fine_out, middle_out, coarse_out, coarsest_out = refs[5 + dz : 13 + dz]
        zbuf, qbuf, ubuf, last, middle, sems = refs[13 + dz :]
        part = lambda ref, j, starts, which: ref[j, starts[which] : starts[which + 1]]
        jx, jy, jz = lax.axis_index("gx"), lax.axis_index("gy"), lax.axis_index("gz")
        for k, r in enumerate((own_ref, *came)):
            zbuf[pl.ds((jz ^ k) * lz2, lz2)] = r[:lz2]
            qbuf[pl.ds((jz ^ k) * 2, 2)] = r[lz2:]
        at = jnp.minimum(jz + 1, dz - 1) * lz2
        plane_halo = dot(px1_ref[...], jnp.concatenate([zbuf[at + 1], zbuf[at + 3]], axis=0))
        everything = []
        for j in range(dz):
            for zc in range(lz2):
                total = zbuf[j * lz2 + zc]
                for i in range(dz):
                    if i != j:
                        total += float(zone.reach(j, i)[zc]) * qbuf[2 * i + (i < j)]
                everything.append(total)
        for z in range(0, z2, lz2):
            zbuf[z] = everything[z]
        if lz2 > 2:
            zbuf[z2 - 2] = everything[z2 - 2]
        at = jnp.minimum((jz + 1) * lz2, z2 - 2)
        halo = dot(part(tx_ref, jx, at_x3, 2), zbuf[at])
        edges = [jnp.zeros((1, wide), jnp.float32)] * (lz2 // 2)
        for k, r in enumerate(came):
            line = jnp.where((jz ^ (k + 1)) > jz, r[lz2, tall - 1 :], r[lz2 + 1, tall - 1 :])
            for half in range(lz2 // 2):
                edges[half] += chosen_by(zs[:, at_reach + k * zn + 2 * half], jz) * line
        fy = ytwo.fine
        edges = dot(jnp.concatenate(edges + [jnp.zeros((8 - lz2 // 2 % 8, wide), jnp.float32)], axis=0), qy2_ref[jy])
        plane_halo = dot(plane_halo, part(ty_ref, jy, at_y3, 3))
        halo = dot(halo, part(ty_ref, jy, at_y3, 2))[:, :fy]
        here = ixy_ref[...]
        last[...] = u_ref[lz - 1] - 0.5 * (here + jnp.where(jz == dz - 1, here, plane_halo))
        copies = [pltpu.make_async_copy(last, fine_out.at[lz - 1], sems.at[0])]
        copies[0].start()
        at_end = iota((xtwo.fine, fy), 0) == xtwo.fine - 1
        spread = [
            i2_ref[half][:, :fy] + jnp.where(at_end, jnp.broadcast_to(edges[half : half + 1, :fy], (xtwo.fine, fy)), 0.0)
            for half in range(lz2 // 2)
        ]
        spread.append(halo)
        for half in range(lz2 // 2):
            middle[2 * half] = u1_ref[2 * half][:, :fy] - spread[half]
            middle[2 * half + 1] = u1_ref[2 * half + 1][:, :fy] - 0.5 * (spread[half] + spread[half + 1])
        copies.append(pltpu.make_async_copy(middle, middle_out, sems.at[1]))
        copies[1].start()
        evens = [pltpu.roll(everything[z], packed - wide2, 1) for z in range(0, z2, 2)]
        arounds = [pltpu.roll(everything[z], packed - 2 * wide2, 1) for z in range(0, z2, 2)]
        second = []
        for zc in range(z3):
            total = evens[zc] - arounds[zc] - first2[zc] * arounds[0] - last2[zc] * arounds[-1]
            for z in range(z2):
                total += az2[zc][z] * everything[z]
            ubuf[zc] = total
            second.append(total)
        fy3, n3 = ythree.fine, xthree.n
        at = [jnp.minimum(jz * lz3 + 2 * half, z3 - 2) for half in range(lz3 // 2 + 1)]
        spread = dot(part(tx_ref, jx, at_x3, 1), jnp.concatenate([ubuf[a] for a in at], axis=1))
        joined = []
        for zc in range(lz4):
            base = zc * (z3 + 2)
            along = chosen_by(zt[:, base], jz) * second[0]
            for z in range(1, z3):
                along += chosen_by(zt[:, base + z], jz) * second[z]
            even = ubuf[2 * (jz * lz4 + zc)]
            around = even + chosen_by(zt[:, base + z3], jz) * second[0] + chosen_by(zt[:, base + z3 + 1], jz) * second[z3 - 2]
            parts = [dot(tx_ref[jx, c * n3 : (c + 1) * n3, :], plane) for c, plane in enumerate((along, even, around))]
            joined.append(jnp.concatenate(parts, axis=1))
        spread = jnp.concatenate([spread[:, h * packed : (h + 1) * packed] for h in range(len(at))], axis=0)
        spread = dot(spread, part(ty_ref, jy, at_y3, 1))[:, :fy3]
        coarsest = dot(jnp.concatenate(joined, axis=0), part(ty_ref, jy, at_y3, 0))[:, : ythree.n]
        for zc in range(lz4):
            coarsest_out[zc] = coarsest[zc * n3 : (zc + 1) * n3]
        spread = [spread[h * xthree.fine : (h + 1) * xthree.fine] for h in range(len(at))]
        for half in range(lz3 // 2):
            at = jz * lz3 + 2 * half
            coarse_out[2 * half] = ubuf[at][: xthree.fine, :fy3] - spread[half]
            coarse_out[2 * half + 1] = ubuf[at + 1][: xthree.fine, :fy3] - 0.5 * (spread[half] + spread[half + 1])
        for copy in copies:
            copy.wait()

    u, own_ty, own_fx, own_sums, *ym = kernel_call(
        y_messages,
        [(lz, lx, ly), tables_y.shape[1:], fx.shape[1:], sums.shape[1:]] + [(rowsy, lz * lx)] * (dy - 1),
        [field, messages_y, tables_y, to32(fx), to32(sums)],
        scratch=[pltpu.VMEM(messages_y.shape[1:], jnp.float32), pltpu.SemaphoreType.DMA((5,))],
        left=(0, 1, 2, 3, 4),
    )
    ycame = swapped(ym, "gy")
    ta_own, tsm_own, head, point = kernel_call(
        y_own,
        [(lz * lx, wide), (hz * hx1, 2 * wide), (heads, wide), (round_up(hz + 1, 8), 2 * wide)],
        [u, own_ty, own_fx],
    )
    xm = kernel_call(
        x_messages,
        [(round_up(lz + 2 * hz + 1, 8), max(wide, ly))] * (dx - 1),
        [u, *ycame, own_ty, own_sums, head, point],
        scratch=[pltpu.VMEM((ss8, hz * hx1), jnp.float32)],
    )
    xcame = swapped(xm, "gx")
    six_cols = (zn + 2) * wide
    ta_v, own_zc, six, own_sent = kernel_call(
        y_apply,
        [(lz * lx, wide), (xtwo.n + tall, wide), (xone.n, six_cols), (f2x.shape[1], six_cols)],
        [*ycame, own_ty, ta_own, tsm_own, tables_x, to32(f2x)],
        scratch=[pltpu.VMEM((ss8, hz * hx1), jnp.float32)],
    )
    zc, u1_part, *sent = kernel_call(
        x_apply,
        [(xtwo.n + tall, wide), (zn, xone.n, wide)] + [(xone.n, wide)] * (dz - 1) + [(kx, six_cols)] * (dx - 1),
        [own_zc, six, own_sent, *xcame[::-1], to32(rows_x)],
        scratch=[pltpu.VMEM((lz + hz, ext, wide), jnp.float32)],
    )
    tails = sent[dz - 1 :]
    zcame = swapped(sent[: dz - 1], "gz")
    if dz > 1 and dx > 1:
        zcame[0], tails[0] = lax.optimization_barrier((zcame[0], tails[0]))
    xtcame = swapped(tails, "gx")
    tables_x2 = to32(tx2)
    u1, across = kernel_call(
        second_own, [(zn, xone.n, wide), (3 * tall, zn * wide)], [u1_part, *zcame[::-1], tables_x2]
    )
    (zmsg,) = kernel_call(
        second_apply, [(lz2 + 2, tall, packed)], [across, zc, *xtcame[::-1], tables_x2, to32(ty2)]
    )
    beside = kernel_call(
        interpolate,
        [(lz, lx, ly), (lx, ly), (lz2 // 2, xtwo.fine, ly2)],
        [u, ta_v, u1, *xcame[::-1], *xtcame[::-1], to32(qx2), to32(qy2)],
    )
    ztcame, (fine, ixy, i2) = gathered(zmsg, "gz", beside)
    return kernel_call(
        third_apply,
        [(lz, lx, ly), (lz2, xtwo.fine, ytwo.fine), (lz3, xthree.fine, ythree.fine), (lz4, xthree.n, ythree.n)],
        [u1, i2, u, ixy, fine, zmsg, *ztcame, to32(px1), tables_x3, tables_y3, to32(qy2)],
        scratch=[
            pltpu.VMEM((z2, tall, packed), jnp.float32),
            pltpu.VMEM((2 * dz, tall, packed), jnp.float32),
            pltpu.VMEM((z3, tall, packed), jnp.float32),
            pltpu.VMEM((lx, ly), jnp.float32),
            pltpu.VMEM((lz2, xtwo.fine, ytwo.fine), jnp.float32),
            pltpu.SemaphoreType.DMA((2,)),
        ],
        left=(4,),
        left_out=(0, 1),
        aliases={4: 0},
    )


def solution(mesh):
    spec = P("gz", "gx", "gy")
    counts = tuple(mesh.shape[a] for a in ("gz", "gx", "gy"))
    return jax.shard_map(
        functools.partial(shards, counts), mesh=mesh, in_specs=(spec,), out_specs=(spec,) * 4, check_vma=False
    )
```

```python
import functools
import math

import jax
import jax.numpy as jnp
import numpy as np
from jax import lax
from jax.experimental import pallas as pl
from jax.experimental.pallas import tpu as pltpu
from jax.sharding import PartitionSpec as P

band_ratio = 2.0 - math.sqrt(3.0)
f32 = np.float32


def round_up(value, unit):
    return -(-value // unit) * unit


def dense(fine):
    n = fine // 2
    steps = np.arange(n)[:, None] - np.arange(n)[None, :]
    lower = np.where(steps >= 0, (-band_ratio) ** np.maximum(steps, 0), 0.0)
    inverse = lower.T @ lower
    mass = 4.0 * np.eye(fine) + np.eye(fine, k=1) + np.eye(fine, k=-1)
    weights = np.where(np.arange(n) == n - 1, 1.0, 0.5)[:, None]
    earlier = np.concatenate([np.zeros((1, fine)), mass[1::2][:-1]])
    product = inverse @ (0.5 * band_ratio * (mass[0::2] + weights * mass[1::2] + 0.5 * earlier))
    return product, inverse[:, 0] * (3 * band_ratio - 1), inverse[:, -1] * (2 * band_ratio)


class Level:
    def __init__(self, whole, count, following):
        self.count, self.fine = count, whole // count
        self.n = self.fine // 2
        self.product, self.first, self.last = dense(whole)
        self.following = following
        self.kept = following.functional_count if following else 0
        self.functional_count = 4 + 2 * self.kept
        self.even = np.zeros((self.n, self.fine))
        self.even[np.arange(self.n), 2 * np.arange(self.n)] = 1.0
        self.v = [self.towards(i, i * self.n - 1) for i in range(count)]
        self.w = [self.towards(i, (i + 1) * self.n) for i in range(count)]
        self.functionals = []
        for i in range(count):
            own = np.zeros((4, self.fine))
            own[0, 0] = own[1, self.fine - 2] = 1.0
            own[2], own[3] = self.v[i], self.w[i]
            if following:
                inner = following.functionals[i]
                own = np.concatenate([own, inner @ self.even, inner @ self.block(i, i)])
            self.functionals.append(own)
        built = [self.build(j) for j in range(count)]
        self.needs = [needs for needs, _ in built]
        self.tables = [tables for _, tables in built]

    def rows(self, i):
        return slice(i * self.n, (i + 1) * self.n)

    def block(self, i, j):
        return self.product[self.rows(i), j * self.fine : (j + 1) * self.fine]

    def towards(self, i, row):
        if not 0 <= row < self.count * self.n:
            return np.zeros(self.fine)
        values = self.product[row, i * self.fine : (i + 1) * self.fine]
        return values / np.abs(values).max()

    def reach(self, i, j):
        side = self.v[j] if j > i else self.w[j]
        best = np.argmax(np.abs(side))
        return self.block(i, j)[:, best] / side[best]

    def side(self, i, j):
        return 2 if j > i else 3

    def through_even(self, f):
        return 4 + f if f else 0

    def build(self, j):
        n, fine, many, end = self.n, self.fine, self.functional_count, self.count - 1
        targets = self.following.needs[j] if self.following else []
        others = [j ^ k for k in range(1, self.count)]
        at = lambda i, f: fine + many * ((i ^ j) - 1) + f
        product = np.zeros((n + len(targets), fine + many * len(others)))
        even, used = np.zeros_like(product), np.zeros(product.shape[1], bool)
        used[:fine] = True
        product[:n, :fine] = self.block(j, j)
        even[:n, :fine] = self.even
        first, last = [self.first[self.rows(j)]], [self.last[self.rows(j)]]
        for i in others:
            product[:n, at(i, self.side(j, i))] = self.reach(j, i)
            used[at(i, self.side(j, i))] = True
        for row, (i, f) in enumerate(targets, n):
            inner = self.following.functionals[i][f]
            product[row, :fine] = inner @ self.block(i, j)
            product[row, at(i, 4 + self.kept + f)] = 1.0
            even[row, at(i, self.through_even(f))] = 1.0
            used[at(i, 4 + self.kept + f)] = used[at(i, self.through_even(f))] = True
            for other in others:
                if other != i:
                    product[row, at(other, self.side(i, other))] = inner @ self.reach(i, other)
                    used[at(other, self.side(i, other))] = True
            first.append([inner @ self.first[self.rows(i)]])
            last.append([inner @ self.last[self.rows(i)]])
        around = even.copy()
        from_first, from_last = 0 if j == 0 else at(0, 0), fine - 2 if j == end else at(end, 1)
        around[:, from_first] += np.concatenate(first)
        around[:, from_last] += np.concatenate(last)
        used[from_first] = used[from_last] = True
        if j < end:
            used[at(j + 1, 0)] = True
        needs = [(j ^ (1 + place // many), place % many) for place in np.flatnonzero(used[fine:])]
        return needs, (product[:, used], even[:, used], around[:, used])

    def sent(self, i, k):
        return [f for block, f in self.needs[i ^ k] if block == i]

    def most_sent(self):
        return max([len(self.sent(i, k)) for i in range(self.count) for k in range(1, self.count)] + [1])

    def most_needed(self):
        return max(len(needs) for needs in self.needs)

    def next_first(self, j, own, fallback):
        return fallback if j == self.count - 1 else own + self.needs[j].index((j + 1, 0))


def interpolation(level, j, inputs, coarse=False):
    table = np.zeros((level.fine, inputs))
    if coarse:
        places = list(range(level.n))
        last = level.following.next_first(j, level.n, level.n - 1)
    else:
        places = [2 * c for c in range(level.n)]
        last = level.next_first(j, level.fine, level.fine - 2)
    places.append(last)
    for c in range(level.n):
        table[2 * c, places[c]] = 1.0
        table[2 * c + 1, places[c]] += 0.5
        table[2 * c + 1, places[c + 1]] += 0.5
    return table


def chain(whole, count, levels):
    made = None
    for depth in reversed(range(levels)):
        made = Level(whole >> depth, count, made)
    return made


def padded(table, rows, cols):
    out = np.zeros((rows, cols))
    out[: table.shape[0], : table.shape[1]] = table
    return out


highest = lax.Precision.HIGHEST


def dot(a, b, dims=((1,), (0,))):
    return lax.dot_general(a, b, (dims, ((), ())), precision=highest, preferred_element_type=jnp.float32)


def kernel_call(body, outs, arrays, scratch=(), left=(), left_out=(), aliases={}):
    space = lambda place, where: pl.BlockSpec(memory_space=pltpu.HBM if place in where else pltpu.VMEM)
    return pl.pallas_call(
        body,
        out_shape=[jax.ShapeDtypeStruct(shape, jnp.float32) for shape in outs],
        in_specs=[space(i, left) for i in range(len(arrays))],
        out_specs=[space(i, left_out) for i in range(len(outs))],
        scratch_shapes=list(scratch),
        input_output_aliases=aliases,
        compiler_params=pltpu.CompilerParams(vmem_limit_bytes=40 << 20),
    )(*(pltpu.with_memory_space_constraint(a, pltpu.HBM) if i in left else a for i, a in enumerate(arrays)))


def swapped(values, axis):
    count = lax.axis_size(axis)
    return [lax.ppermute(v, axis, [(i, i ^ k) for i in range(count)]) for k, v in enumerate(values, 1)]


def gathered(value, axis, beside):
    count = lax.axis_size(axis)
    if count != 4:
        return swapped([value] * (count - 1), axis), beside
    by = lambda k, what: lax.ppermute(what, axis, [(i, i ^ k) for i in range(count)])
    far, beside = lax.optimization_barrier((by(2, value), beside))
    return [by(1, value), far, by(1, far)], beside


def chosen_by(values, j):
    chosen = float(values[0])
    for place in range(1, len(values)):
        if any(values[place] != values[0] for place in range(len(values))):
            chosen = jnp.where(j == place, f32(values[place]), chosen)
    return chosen


def iota(shape, dim):
    return lax.broadcasted_iota(jnp.int32, shape, dim)


def shards(counts, field):
    dz, dx, dy = counts
    lz, lx, ly = field.shape
    nz, nx, ny = lz * dz, lx * dx, ly * dy

    yone = chain(ny, dy, 3)
    ytwo, ythree = yone.following, yone.following.following
    xone = chain(nx, dx, 1)
    xtwo = chain(nx // 2, dx, 2)
    xthree = xtwo.following
    zone = Level(nz, dz, None)

    points_a = lambda fs: [f for f in fs if f in (2, 3) or f >= 4 + yone.kept]
    points_s = lambda fs: [f for f in fs if f not in (2, 3) and f < 4 + yone.kept]
    pairs_y = [(i, k) for i in range(dy) for k in range(1, dy)]
    sa = max([len(points_a(yone.sent(i, k))) for i, k in pairs_y] + [0]) + 1
    ss = max([len(points_s(yone.sent(i, k))) for i, k in pairs_y] + [1])
    per_row = (lz * lx) // ((lz // 2) * (lx // 2))
    rowsy = round_up(sa + -(-ss // per_row), 8)
    sa8, ss8 = round_up(sa, 8), round_up(ss, 8)
    wide1 = yone.n + ytwo.most_needed()
    wide2 = ytwo.n + ythree.most_needed()
    wide = packed = round_up(max(wide1 + 1, 3 * wide2, wide2 + wide1), 128)
    kx = round_up(xtwo.most_sent(), 8)
    rowsx = xtwo.fine + kx * (dx - 1)
    tall = round_up(max(xtwo.n + xthree.most_needed() + 1, xone.n // 2 + 1), 8)

    others_y = max(dy - 1, 1)
    fya = np.zeros((dy, others_y * sa8, ly))
    fys = np.zeros((dy, others_y * ss8, ly))
    ta = np.zeros((dy, ly, wide))
    wa = np.zeros((dy, others_y * rowsy, wide))
    tsm = np.zeros((dy, ly, 2 * wide))
    wsm = np.zeros((dy, others_y * ss8, 2 * wide))
    for j in range(dy):
        product, even, around = yone.tables[j]
        used = product.shape[0]
        ta[j, :, :used] = product[:, :ly].T
        tsm[j, :, :used] = even[:, :ly].T
        tsm[j, :, wide : wide + used] = around[:, :ly].T
        for k in range(1, dy):
            mine = yone.sent(j, k)
            fya[j, (k - 1) * sa8 :][: len(points_a(mine))] = yone.functionals[j][points_a(mine)]
            fya[j, (k - 1) * sa8 + sa - 1] = yone.functionals[j][0]
            fys[j, (k - 1) * ss8 :][: len(points_s(mine))] = yone.functionals[j][points_s(mine)]
            came = yone.sent(j ^ k, k)
            for f in came:
                column = ly + yone.needs[j].index((j ^ k, f))
                if f in points_a(came):
                    wa[j, (k - 1) * rowsy + points_a(came).index(f), :used] = product[:, column]
                else:
                    row = (k - 1) * ss8 + points_s(came).index(f)
                    wsm[j, row, :used] = even[:, column]
                    wsm[j, row, wide : wide + used] = around[:, column]
        if j == dy - 1:
            ta[j, ly - 2, wide - 1] = 0.5
        else:
            wa[j, rowsy * ((j ^ (j + 1)) - 1) + sa - 1, wide - 1] = 0.5

    ext = round_up(max(dx - 1, 1), 8)
    fx = np.zeros((dx, lx, 8))
    heads = round_up(2 * lz + lz // 2, 8)
    sums = np.zeros((dx, heads, lz * lx))
    txa = np.zeros((dx, xone.n, lx + ext))
    txm = np.zeros((dx, xone.n, xone.n + ext))
    for j in range(dx):
        fx[j, :, :2] = xone.functionals[j][2:4].T
        for z in range(lz):
            sums[j, 2 * z : 2 * z + 2, z * lx : (z + 1) * lx] = xone.functionals[j][2:4]
        for half in range(lz // 2):
            sums[j, 2 * lz + half, 2 * half * lx] = 1.0
        product, even, around = xone.tables[j]
        txa[j, :, :lx] = product[:, :lx]
        txm[j, :, : xone.n] = around[:, :lx:2]
        for column, (i, f) in enumerate(xone.needs[j], lx):
            if f in (2, 3):
                txa[j, :, lx + (i ^ j) - 1] = product[:, column]
            else:
                txm[j, :, xone.n + (i ^ j) - 1] += around[:, column] * ((f == 0 and i == 0) or (f == 1 and i == dx - 1))

    zn = zone.n
    zs = np.zeros((dz, 2 * lz + 2 + zn * (lz + dz + 1)))
    for j in range(dz):
        cv, cw = zone.v[j], zone.w[j]
        k_last = (zone.last[zone.rows(0)] / zone.reach(0, j))[0] if 0 < j == dz - 1 else 0.0
        k_first = (zone.first[zone.rows(dz - 1)] / zone.reach(dz - 1, j))[-1] if j == 0 and dz > 1 else 0.0
        parts = [cv, cw, [k_last, k_first], zone.block(j, j).reshape(-1)]
        parts += [zone.reach(j, j ^ k) for k in range(1, dz)]
        parts += [zone.first[zone.rows(j)] * (j == 0), zone.last[zone.rows(j)] * (j == dz - 1)]
        zs[j] = np.concatenate([np.asarray(p, np.float64) for p in parts])
    at_local = 2 * lz + 2
    at_reach = at_local + zn * lz
    at_first = at_reach + zn * (dz - 1)
    at_last = at_first + zn

    f2x = np.zeros((dx, max(dx - 1, 1) * kx, xtwo.fine))
    tx2 = np.zeros((dx, 3 * tall, rowsx))
    qx2 = np.zeros((dx, xtwo.fine, rowsx))
    tx3 = np.zeros((dx, 3 * xthree.n, tall))
    qx3 = np.zeros((dx, xthree.fine, tall))
    px3 = np.zeros((dx, xtwo.fine, tall))
    for j in range(dx):
        columns = list(range(xtwo.fine))
        for i, f in xtwo.needs[j]:
            columns.append(xtwo.fine + kx * ((i ^ j) - 1) + xtwo.sent(i, i ^ j).index(f))
        for c, table in enumerate(xtwo.tables[j]):
            tx2[j, c * tall : c * tall + table.shape[0], columns] = table.T
        qx2[j][:, columns] = interpolation(xtwo, j, len(columns))
        tx2[j, tall - 1, xtwo.fine :] = qx2[j, -1, xtwo.fine :]
        for k in range(1, dx):
            mine = xtwo.sent(j, k)
            f2x[j, (k - 1) * kx :][: len(mine)] = xtwo.functionals[j][mine]
        for c, table in enumerate(xthree.tables[j]):
            tx3[j, c * xthree.n : (c + 1) * xthree.n, : table.shape[1]] = table
        qx3[j] = interpolation(xthree, j, tall)
        px3[j] = interpolation(xtwo, j, tall, True)

    ty2 = np.zeros((dy, 3 * wide, packed))
    qy2 = np.zeros((dy, wide, round_up(ytwo.fine, 128)))
    ty3 = np.zeros((dy, 3 * packed, 128))
    qy3 = np.zeros((dy, packed, 128))
    py3 = np.zeros((dy, packed, round_up(ytwo.fine, 128)))
    px1 = np.zeros((lx, 2 * tall))
    py1 = np.zeros((dy, packed, ly))
    for j in range(dy):
        for c, table in enumerate(ytwo.tables[j]):
            ty2[j, c * wide : c * wide + table.shape[1], c * wide2 : c * wide2 + table.shape[0]] = table.T
        qy2[j, :, : ytwo.fine] = interpolation(ytwo, j, wide).T
        for c, table in enumerate(ythree.tables[j]):
            ty3[j, c * packed : c * packed + table.shape[1], : ythree.n] = (-1.0 if c == 2 else 1.0) * table.T
        qy3[j, :, : ythree.fine] = interpolation(ythree, j, packed).T
        py1[j, wide2:] = interpolation(yone, j, packed - wide2, True).T
        py3[j, wide2:, : ytwo.fine] = interpolation(ytwo, j, packed - wide2, True).T
    for c in range(xone.n):
        begin = c if c < xtwo.n else tall + c - xtwo.n
        px1[2 * c, begin] = 1.0
        px1[2 * c + 1, begin : begin + 2] = 0.5
    az2, first2, last2 = (t.tolist() for t in dense(nz // 2))
    az3, first3, last3 = dense(nz // 4)
    z2, z3 = nz // 2, nz // 4
    lz2, lz3 = lz // 2, lz // 4
    zt = np.concatenate([az3, first3[:, None], last3[:, None]], axis=1)
    zt = zt.reshape(dz, (lz // 8) * (z3 + 2))
    lz4 = lz // 8

    to32 = lambda table: jnp.asarray(table, jnp.float32)

    def stacked(*tables):
        cols = max(t.shape[2] for t in tables)
        starts = np.cumsum([0] + [round_up(t.shape[1], 8) for t in tables])
        out = np.zeros((tables[0].shape[0], starts[-1], cols))
        for t, begin in zip(tables, starts):
            out[:, begin : begin + t.shape[1], : t.shape[2]] = t
        return to32(out), [int(v) for v in starts]

    messages_y, _ = stacked(fya, fys)
    tables_y, _ = stacked(np.concatenate([ta, tsm], axis=2), np.concatenate([wa, np.zeros((dy, wa.shape[1], 2 * wide))], axis=2),
                          np.concatenate([np.zeros((dy, wsm.shape[1], wide)), wsm], axis=2))
    tables_x, _ = stacked(txa[:, :, :lx], txm[:, :, : xone.n])
    rows_x = np.concatenate([txa[:, :, lx:], txm[:, :, xone.n :]], axis=2)
    rows_x = np.concatenate([rows_x, f2x @ rows_x], axis=1)
    tables_x3, at_x3 = stacked(tx3, qx3, px3)
    tables_y3, at_y3 = stacked(ty3, qy3, py3, py1)
    hz, hx1 = lz // 2, lx // 2
    ly2 = round_up(ytwo.fine, 128)

    def y_messages(u_hbm, table_hbm, ty_hbm, fx_hbm, sums_hbm, u_ref, ty_ref, fx_ref, sums_ref, *refs):
        outs, (table, sems) = refs[:-2], refs[-2:]
        j = lax.axis_index("gy")
        nt = ((1,), (1,))
        copies = [
            pltpu.make_async_copy(table_hbm.at[j], table, sems.at[0]),
            pltpu.make_async_copy(u_hbm, u_ref, sems.at[1]),
            pltpu.make_async_copy(ty_hbm.at[j], ty_ref, sems.at[2]),
            pltpu.make_async_copy(fx_hbm.at[lax.axis_index("gx")], fx_ref, sems.at[3]),
            pltpu.make_async_copy(sums_hbm.at[lax.axis_index("gx")], sums_ref, sems.at[4]),
        ]
        for copy in copies:
            copy.start()
        for copy in copies[:2]:
            copy.wait()
        lines = dot(table[: others_y * sa8], u_ref[...].reshape(lz * lx, ly), nt)
        even = jnp.concatenate([u_ref[2 * z, pl.ds(0, hx1, stride=2), :] for z in range(hz)], axis=0)
        points = dot(table[others_y * sa8 :], even, nt)
        for k, out in enumerate(outs):
            out[: min(sa8, rowsy)] = lines[k * sa8 : k * sa8 + min(sa8, rowsy)]
            if rowsy > sa8:
                out[sa8:] = jnp.zeros_like(out[sa8:])
            for f in range(ss):
                begin = hz * hx1 * (f % per_row)
                row = sa + f // per_row
                out[row : row + 1, begin : begin + hz * hx1] = points[k * ss8 + f : k * ss8 + f + 1]
        for copy in copies[2:]:
            copy.wait()

    def along_y(u, half_halo):
        lane = iota(u.shape, 1)
        before, after = pltpu.roll(u, 1, 1), pltpu.roll(u, ly - 1, 1)
        edge = 0.5 * before + jnp.broadcast_to(half_halo, u.shape)
        return jnp.where(lane == ly - 1, edge, jnp.where(lane % 2 == 1, 0.5 * (before + after), u))

    def from_next(jx, own, rows):
        for k, other in enumerate(rows):
            own = jnp.where((jx ^ (k + 1)) == jx + 1, other, own)
        return own

    def y_own(u_ref, ty_ref, fx_ref, ta_out, tsm_out, heads_out, points_out):
        jx = lax.axis_index("gx")
        ta_all = dot(u_ref[...].reshape(lz * lx, ly), ty_ref[:ly, :wide])
        even = jnp.concatenate([u_ref[2 * z, pl.ds(0, hx1, stride=2), :] for z in range(hz)], axis=0)
        tsm_all = dot(even, ty_ref[:ly, wide:])
        ta_out[...] = ta_all
        tsm_out[...] = tsm_all
        weights = [jnp.broadcast_to(fx_ref[:, c : c + 1], (lx, wide)) for c in range(2)]
        heads_out[...] = jnp.zeros_like(heads_out)
        points_out[...] = jnp.zeros_like(points_out)
        for z in range(lz):
            part = ta_all[z * lx : (z + 1) * lx]
            for c in range(2):
                heads_out[2 * z + c : 2 * z + c + 1] = jnp.sum(part * weights[c], axis=0, keepdims=True)
        for half in range(hz):
            heads_out[2 * lz + half : 2 * lz + half + 1] = ta_all[2 * half * lx : 2 * half * lx + 1]
            tm = tsm_all[half * hx1 : (half + 1) * hx1]
            points_out[half : half + 1] = jnp.where(jx == 0, tm[0:1], tm[hx1 - 1 : hx1])
        points_out[hz : hz + 1] = tsm_all[0:1]

    def came_points(ref, points):
        points[...] = jnp.zeros_like(points)
        for f in range(ss):
            begin = hz * hx1 * (f % per_row)
            row = sa + f // per_row
            points[f : f + 1] = ref[row : row + 1, begin : begin + hz * hx1]
        return points[...]

    def x_messages(*refs):
        u_ref, came = refs[0], refs[1:dy]
        ty_ref, sums_ref, heads_ref, points_ref = refs[dy : dy + 4]
        xm_outs, points = refs[dy + 4 : -1], refs[-1]
        jx = lax.axis_index("gx")
        nt = ((1,), (1,))
        head, point = heads_ref[...], points_ref[...]
        shape = (point.shape[0], hz * hx1)
        row, lane = iota(shape, 0), iota(shape, 1)
        line = jnp.where(row == hz, 0, row * hx1 + jnp.where(jx == 0, 0, hx1 - 1))
        one = jnp.where((lane == line) & (row <= hz), 1.0, 0.0)
        for k, ref in enumerate(came):
            begin = ly + rowsy * k
            head += dot(dot(sums_ref[...], ref[...], nt), ty_ref[begin : begin + rowsy, :wide])
            begin = ly + rowsy * (dy - 1) + ss8 * k
            point += dot(dot(one, came_points(ref, points), nt), ty_ref[begin : begin + ss8, wide:])
        for out in xm_outs:
            out[lz + 2 * hz :] = jnp.zeros_like(out[lz + 2 * hz :])
            out[lz + 2 * hz : lz + 2 * hz + 1, :wide] = point[hz : hz + 1, :wide]
        for z in range(lz):
            for k, out in enumerate(xm_outs):
                out[z : z + 1, :wide] = jnp.where((jx ^ (k + 1)) < jx, head[2 * z : 2 * z + 1], head[2 * z + 1 : 2 * z + 2])
        for half in range(hz):
            first = head[2 * lz + half : 2 * lz + half + 1, wide - 1 :]
            iy = along_y(u_ref[2 * half, :8], jnp.broadcast_to(first, (8, 1)))
            for out in xm_outs:
                out[lz + half : lz + half + 1, :wide] = point[half : half + 1, wide:]
                out[lz + hz + half : lz + hz + half + 1, :ly] = iy[0:1]

    def y_apply(*refs):
        came = refs[: dy - 1]
        ty_ref, ta_ref, tsm_ref, tx_ref, f2x_ref, ta_out, zc_out, six_out, sent_out, points = refs[dy - 1 :]
        jx, jz = lax.axis_index("gx"), lax.axis_index("gz")
        tn = ((0,), (0,))
        ta_all, tsm_all = ta_ref[...], tsm_ref[...]
        for k, ref in enumerate(came):
            begin = ly + rowsy * k
            ta_all += dot(ref[...], ty_ref[begin : begin + rowsy, :wide], tn)
            begin = ly + rowsy * (dy - 1) + ss8 * k
            tsm_all += dot(came_points(ref, points), ty_ref[begin : begin + ss8, wide:], tn)
        ta_out[...] = ta_all
        zc_out[...] = jnp.zeros_like(zc_out)
        zc_out[:hx1] = tsm_all[:hx1, :wide]
        xa, xm = [], []
        for z in range(0, lz, 2):
            pair = jnp.concatenate([ta_all[z * lx : (z + 1) * lx], ta_all[(z + 1) * lx : (z + 2) * lx]], axis=1)
            both = dot(tx_ref[jx, : xone.n], pair)
            xa += [both[:, :wide], both[:, wide:]]
        for half in range(0, hz, 2):
            pair = jnp.concatenate([tsm_all[h * hx1 : (h + 1) * hx1, wide:] for h in (half, half + 1)], axis=1)
            both = dot(tx_ref[jx, xone.n :, : xone.n], pair)
            xm += [both[:, :wide], both[:, wide:]]
        six = along_planes(jz, xa, xm)
        for half in range(hz):
            six[half] += tsm_all[half * hx1 : (half + 1) * hx1, :wide]
        six = jnp.concatenate(six, axis=1)
        six_out[...] = six
        sent_out[...] = dot(f2x_ref[jx], six)

    def along_planes(jz, xa, xm):
        scalar = lambda place: chosen_by(zs[:, place], jz)
        made = []
        for zc in range(zn):
            total = -xm[zc] - scalar(at_first + zc) * xm[0] - scalar(at_last + zc) * xm[hz - 1]
            for z in range(lz):
                total += scalar(at_local + zc * lz + z) * xa[z]
            made.append(total)
        v = -scalar(2 * lz) * xm[hz - 1]
        w = -scalar(2 * lz + 1) * xm[0]
        for z in range(lz):
            v += scalar(z) * xa[z]
            w += scalar(lz + z) * xa[z]
        return made + [v, w]

    def x_apply(*refs):
        own_zc_ref, six_ref, own_sent_ref = refs[:3]
        came = refs[3 : 2 + dx][::-1]
        rows_ref, zc_out, u1_out = refs[2 + dx : 5 + dx]
        planes_out, xt_outs, rest = refs[5 + dx : 4 + dx + dz], refs[4 + dx + dz : -1], refs[-1]
        jx, jz = lax.axis_index("gx"), lax.axis_index("gz")
        rest[...] = jnp.zeros_like(rest)
        for k, r in enumerate(came):
            for z in range(lz + hz):
                rest[z, k : k + 1] = r[z : z + 1, :wide]
        zero = [jnp.zeros_like(rest[0])]
        lines_a = along_planes(jz, [rest[z] for z in range(lz)], zero * hz)
        lines_m = along_planes(jz, zero * lz, [rest[lz + half] for half in range(hz)])
        lines = jnp.concatenate([jnp.concatenate(lines_a, axis=1), jnp.concatenate(lines_m, axis=1)], axis=0)
        added = dot(rows_ref[jx], lines)
        six = six_ref[...] + added[: xone.n]
        sent = own_sent_ref[...] + added[xone.n :]
        zc_out[...] = own_zc_ref[...]
        begin = lz + 2 * hz
        zc_out[hx1 : hx1 + 1] = from_next(jx, own_zc_ref[hx1 - 1 : hx1], [r[begin : begin + 1, :wide] for r in came])
        for zc in range(zn):
            u1_out[zc] = six[:, zc * wide : (zc + 1) * wide]
        v, w = six[:, zn * wide : (zn + 1) * wide], six[:, (zn + 1) * wide :]
        for k, out in enumerate(planes_out):
            out[...] = jnp.where((jz ^ (k + 1)) > jz, w, v)
        for k, out in enumerate(xt_outs):
            out[...] = sent[k * kx : (k + 1) * kx]

    def interpolate(*refs):
        u_ref, ta_ref, u1_ref = refs[:3]
        came, xcame = refs[3 : 2 + dx][::-1], refs[2 + dx : 1 + 2 * dx][::-1]
        qx2_ref, qy2_ref, fine_out, ixy_out, i2_out = refs[1 + 2 * dx :]
        jx, jy = lax.axis_index("gx"), lax.axis_index("gy")
        row = iota((lx, ly), 0)
        planes = []
        for half in range(hz):
            iy = along_y(u_ref[2 * half], ta_ref[2 * half * lx : (2 * half + 1) * lx, wide - 1 :])
            begin = lz + hz + half
            halo = from_next(jx, iy[lx - 2 : lx - 1], [r[begin : begin + 1, :ly] for r in came])
            before, after = pltpu.roll(iy, 1, 0), pltpu.roll(iy, lx - 1, 0)
            after = jnp.where(row == lx - 1, jnp.broadcast_to(halo, (lx, ly)), after)
            planes.append(jnp.where(row % 2 == 1, 0.5 * (before + after), iy))
        for half in range(hz):
            fine_out[2 * half] = u_ref[2 * half] - planes[half]
            if half + 1 < hz:
                fine_out[2 * half + 1] = u_ref[2 * half + 1] - 0.5 * (planes[half] + planes[half + 1])
        ixy_out[...] = planes[-1]
        evens = range(0, zn, 2)
        state = [jnp.concatenate([u1_ref[z] for z in evens], axis=1)]
        state += [jnp.concatenate([r[:, z * wide : (z + 1) * wide] for z in evens], axis=1) for r in xcame]
        spread = dot(qx2_ref[jx], jnp.concatenate(state, axis=0))
        spread = jnp.concatenate([spread[:, half * wide : (half + 1) * wide] for half in range(zn // 2)], axis=0)
        spread = dot(spread, qy2_ref[jy])
        for half in range(zn // 2):
            i2_out[half] = spread[half * xtwo.fine : (half + 1) * xtwo.fine]

    def second_own(*refs):
        part_ref, zcame = refs[0], refs[1:dz][::-1]
        tx2_ref, u1_out, across_out = refs[dz:]
        jx, jz = lax.axis_index("gx"), lax.axis_index("gz")
        own = []
        for zc in range(zn):
            total = part_ref[zc]
            for k, r in enumerate(zcame):
                total += chosen_by(zs[:, at_reach + k * zn + zc], jz) * r[...]
            u1_out[zc] = total
            own.append(total)
        across_out[...] = dot(tx2_ref[jx, :, : xtwo.fine], jnp.concatenate(own, axis=1))

    def second_apply(across_ref, zc_ref, *refs):
        xcame, (tx2_ref, ty2_ref, zt_out) = refs[:-3][::-1], refs[-3:]
        jx, jy = lax.axis_index("gx"), lax.axis_index("gy")
        across = dot(tx2_ref[jx, :, xtwo.fine :], jnp.concatenate([r[...] for r in xcame], axis=0))
        across = jnp.concatenate([across_ref[...] + across[:, : zn * wide], across[:, zn * wide :]], axis=1)
        cut = [across[:, z * wide : (z + 1) * wide] for z in range(zn + 2)]
        whole = [z for z in range(zn + 2) if z % 2 == 0 or z >= zn]
        joined = [jnp.concatenate([cut[z][c * tall : (c + 1) * tall] for c in range(3)], axis=1) for z in whole]
        made = dot(jnp.concatenate(joined, axis=0), ty2_ref[jy])
        for place, z in enumerate(whole):
            zt_out[z] = made[place * tall : (place + 1) * tall]
        made = dot(jnp.concatenate([cut[z][:tall] for z in range(1, zn, 2)], axis=0), ty2_ref[jy, :wide])
        for z in range(1, zn, 2):
            moved = made[(z // 2) * tall : (z // 2 + 1) * tall]
            if z < 4:
                begin = xtwo.n * (z // 2)
                moved += pltpu.roll(zc_ref[begin : begin + tall], wide2, 1)
            zt_out[z] = moved
        for z in (zn, zn + 1):
            zt_out[z, tall - 1 :] = cut[z][tall - 1 : tall]

    def third_apply(*refs):
        u1_ref, i2_ref, u_ref, ixy_ref, _, own_ref = refs[:6]
        came = refs[6 : 5 + dz]
        px1_ref, tx_ref, ty_ref, qy2_ref, fine_out, middle_out, coarse_out, coarsest_out = refs[5 + dz : 13 + dz]
        zbuf, qbuf, ubuf, last, middle, sems = refs[13 + dz :]
        part = lambda ref, j, starts, which: ref[j, starts[which] : starts[which + 1]]
        jx, jy, jz = lax.axis_index("gx"), lax.axis_index("gy"), lax.axis_index("gz")
        for k, r in enumerate((own_ref, *came)):
            zbuf[pl.ds((jz ^ k) * lz2, lz2)] = r[:lz2]
            qbuf[pl.ds((jz ^ k) * 2, 2)] = r[lz2:]
        at = jnp.minimum(jz + 1, dz - 1) * lz2
        plane_halo = dot(px1_ref[...], jnp.concatenate([zbuf[at + 1], zbuf[at + 3]], axis=0))
        everything = []
        for j in range(dz):
            sides = []
            for near, blocks in ((j - 1, range(j)), (j + 1, range(j + 1, dz))):
                if len(blocks):
                    reach = zone.reach(j, near)
                    gain = lambda i: float(zone.reach(j, i)[0] / reach[0])
                    sides.append((reach, sum(gain(i) * qbuf[2 * i + (i < j)] for i in blocks)))
            for zc in range(lz2):
                total = zbuf[j * lz2 + zc]
                for reach, lines in sides:
                    total += float(reach[zc]) * lines
                everything.append(total)
        for z in range(0, z2, lz2):
            zbuf[z] = everything[z]
        if lz2 > 2:
            zbuf[z2 - 2] = everything[z2 - 2]
        at = jnp.minimum((jz + 1) * lz2, z2 - 2)
        halo = dot(part(tx_ref, jx, at_x3, 2), zbuf[at])
        edges = [jnp.zeros((1, wide), jnp.float32)] * (lz2 // 2)
        for k, r in enumerate(came):
            line = jnp.where((jz ^ (k + 1)) > jz, r[lz2, tall - 1 :], r[lz2 + 1, tall - 1 :])
            for half in range(lz2 // 2):
                edges[half] += chosen_by(zs[:, at_reach + k * zn + 2 * half], jz) * line
        fy = ytwo.fine
        edges = dot(jnp.concatenate(edges + [jnp.zeros((8 - lz2 // 2 % 8, wide), jnp.float32)], axis=0), qy2_ref[jy])
        plane_halo = dot(plane_halo, part(ty_ref, jy, at_y3, 3))
        halo = dot(halo, part(ty_ref, jy, at_y3, 2))[:, :fy]
        here = ixy_ref[...]
        last[...] = u_ref[lz - 1] - 0.5 * (here + jnp.where(jz == dz - 1, here, plane_halo))
        copies = [pltpu.make_async_copy(last, fine_out.at[lz - 1], sems.at[0])]
        copies[0].start()
        at_end = iota((xtwo.fine, fy), 0) == xtwo.fine - 1
        spread = [
            i2_ref[half][:, :fy] + jnp.where(at_end, jnp.broadcast_to(edges[half : half + 1, :fy], (xtwo.fine, fy)), 0.0)
            for half in range(lz2 // 2)
        ]
        spread.append(halo)
        for half in range(lz2 // 2):
            middle[2 * half] = u1_ref[2 * half][:, :fy] - spread[half]
            middle[2 * half + 1] = u1_ref[2 * half + 1][:, :fy] - 0.5 * (spread[half] + spread[half + 1])
        copies.append(pltpu.make_async_copy(middle, middle_out, sems.at[1]))
        copies[1].start()
        evens = [pltpu.roll(everything[z], packed - wide2, 1) for z in range(0, z2, 2)]
        arounds = [pltpu.roll(everything[z], packed - 2 * wide2, 1) for z in range(0, z2, 2)]
        second = []
        for zc in range(z3):
            total = evens[zc] - arounds[zc] - first2[zc] * arounds[0] - last2[zc] * arounds[-1]
            for z in range(z2):
                total += az2[zc][z] * everything[z]
            ubuf[zc] = total
            second.append(total)
        fy3, n3 = ythree.fine, xthree.n
        at = [jnp.minimum(jz * lz3 + 2 * half, z3 - 2) for half in range(lz3 // 2 + 1)]
        spread = dot(part(tx_ref, jx, at_x3, 1), jnp.concatenate([ubuf[a] for a in at], axis=1))
        joined = []
        for zc in range(lz4):
            base = zc * (z3 + 2)
            along = chosen_by(zt[:, base], jz) * second[0]
            for z in range(1, z3):
                along += chosen_by(zt[:, base + z], jz) * second[z]
            even = ubuf[2 * (jz * lz4 + zc)]
            around = even + chosen_by(zt[:, base + z3], jz) * second[0] + chosen_by(zt[:, base + z3 + 1], jz) * second[z3 - 2]
            parts = [dot(tx_ref[jx, c * n3 : (c + 1) * n3, :], plane) for c, plane in enumerate((along, even, around))]
            joined.append(jnp.concatenate(parts, axis=1))
        spread = jnp.concatenate([spread[:, h * packed : (h + 1) * packed] for h in range(len(at))], axis=0)
        spread = dot(spread, part(ty_ref, jy, at_y3, 1))[:, :fy3]
        coarsest = dot(jnp.concatenate(joined, axis=0), part(ty_ref, jy, at_y3, 0))[:, : ythree.n]
        for zc in range(lz4):
            coarsest_out[zc] = coarsest[zc * n3 : (zc + 1) * n3]
        spread = [spread[h * xthree.fine : (h + 1) * xthree.fine] for h in range(len(at))]
        for half in range(lz3 // 2):
            at = jz * lz3 + 2 * half
            coarse_out[2 * half] = ubuf[at][: xthree.fine, :fy3] - spread[half]
            coarse_out[2 * half + 1] = ubuf[at + 1][: xthree.fine, :fy3] - 0.5 * (spread[half] + spread[half + 1])
        for copy in copies:
            copy.wait()

    u, own_ty, own_fx, own_sums, *ym = kernel_call(
        y_messages,
        [(lz, lx, ly), tables_y.shape[1:], fx.shape[1:], sums.shape[1:]] + [(rowsy, lz * lx)] * (dy - 1),
        [field, messages_y, tables_y, to32(fx), to32(sums)],
        scratch=[pltpu.VMEM(messages_y.shape[1:], jnp.float32), pltpu.SemaphoreType.DMA((5,))],
        left=(0, 1, 2, 3, 4),
    )
    ycame = swapped(ym, "gy")
    ta_own, tsm_own, head, point = kernel_call(
        y_own,
        [(lz * lx, wide), (hz * hx1, 2 * wide), (heads, wide), (round_up(hz + 1, 8), 2 * wide)],
        [u, own_ty, own_fx],
    )
    xm = kernel_call(
        x_messages,
        [(round_up(lz + 2 * hz + 1, 8), max(wide, ly))] * (dx - 1),
        [u, *ycame, own_ty, own_sums, head, point],
        scratch=[pltpu.VMEM((ss8, hz * hx1), jnp.float32)],
    )
    xcame = swapped(xm, "gx")
    six_cols = (zn + 2) * wide
    ta_v, own_zc, six, own_sent = kernel_call(
        y_apply,
        [(lz * lx, wide), (xtwo.n + tall, wide), (xone.n, six_cols), (f2x.shape[1], six_cols)],
        [*ycame, own_ty, ta_own, tsm_own, tables_x, to32(f2x)],
        scratch=[pltpu.VMEM((ss8, hz * hx1), jnp.float32)],
    )
    zc, u1_part, *sent = kernel_call(
        x_apply,
        [(xtwo.n + tall, wide), (zn, xone.n, wide)] + [(xone.n, wide)] * (dz - 1) + [(kx, six_cols)] * (dx - 1),
        [own_zc, six, own_sent, *xcame[::-1], to32(rows_x)],
        scratch=[pltpu.VMEM((lz + hz, ext, wide), jnp.float32)],
    )
    tails = sent[dz - 1 :]
    zcame = swapped(sent[: dz - 1], "gz")
    if dz > 1 and dx > 1:
        zcame[0], tails[0] = lax.optimization_barrier((zcame[0], tails[0]))
    xtcame = swapped(tails, "gx")
    tables_x2 = to32(tx2)
    u1, across = kernel_call(
        second_own, [(zn, xone.n, wide), (3 * tall, zn * wide)], [u1_part, *zcame[::-1], tables_x2]
    )
    (zmsg,) = kernel_call(
        second_apply, [(lz2 + 2, tall, packed)], [across, zc, *xtcame[::-1], tables_x2, to32(ty2)]
    )
    beside = kernel_call(
        interpolate,
        [(lz, lx, ly), (lx, ly), (lz2 // 2, xtwo.fine, ly2)],
        [u, ta_v, u1, *xcame[::-1], *xtcame[::-1], to32(qx2), to32(qy2)],
    )
    ztcame, (fine, ixy, i2) = gathered(zmsg, "gz", beside)
    return kernel_call(
        third_apply,
        [(lz, lx, ly), (lz2, xtwo.fine, ytwo.fine), (lz3, xthree.fine, ythree.fine), (lz4, xthree.n, ythree.n)],
        [u1, i2, u, ixy, fine, zmsg, *ztcame, to32(px1), tables_x3, tables_y3, to32(qy2)],
        scratch=[
            pltpu.VMEM((z2, tall, packed), jnp.float32),
            pltpu.VMEM((2 * dz, tall, packed), jnp.float32),
            pltpu.VMEM((z3, tall, packed), jnp.float32),
            pltpu.VMEM((lx, ly), jnp.float32),
            pltpu.VMEM((lz2, xtwo.fine, ytwo.fine), jnp.float32),
            pltpu.SemaphoreType.DMA((2,)),
        ],
        left=(4,),
        left_out=(0, 1),
        aliases={4: 0},
    )


def solution(mesh):
    spec = P("gz", "gx", "gy")
    counts = tuple(mesh.shape[a] for a in ("gz", "gx", "gy"))
    return jax.shard_map(
        functools.partial(shards, counts), mesh=mesh, in_specs=(spec,), out_specs=(spec,) * 4, check_vma=False
    )
```
